32 devices in a mesh: seq: 4 (over y, core), dp: 8 (over z, x).
Axes of the slice: x: 2, y: 2, z: 4, core: 2. Of those that a mesh axis runs over, the one named last changes fastest.
Arguments:
- tokens: bfloat16 [8, 768, 768], P('dp', 'seq'), may hold values from -6 to 6
- lengths: int32 [8], P('dp'), may hold values from 192 to 768, as said below
- norm_one: bfloat16 [768], P(('seq', 'dp')), may hold values from 0.099609375 to 1.8984375
- query_one: bfloat16 [768, 768], P(('seq', 'dp')), may hold values from -0.21875 to 0.21875
- key_one: bfloat16 [768, 768], P(('seq', 'dp')), may hold values from -0.21875 to 0.21875
- value_one: bfloat16 [768, 768], P(('seq', 'dp')), may hold values from -0.21875 to 0.21875
- shift_taps: bfloat16 [768, 64], P(('seq', 'dp')), may hold values from -0.75 to 0.75
- decay_log: bfloat16 [768, 64], P(('seq', 'dp')), may hold values from -9 to -1.1953125
- turn_angle: bfloat16 [768, 64], P(('seq', 'dp')), may hold values from -3.140625 to 3.140625
- mix_real: bfloat16 [768, 64], P(('seq', 'dp')), may hold values from -0.059814453 to 0.059814453
- mix_imag: bfloat16 [768, 64], P(('seq', 'dp')), may hold values from -0.059814453 to 0.059814453
- skip_gain: bfloat16 [768], P(('seq', 'dp')), may hold values from -4 to 4
- out_one: bfloat16 [768, 768], P(('seq', 'dp')), may hold values from -0.21875 to 0.21875
- norm_two: bfloat16 [768], P(('seq', 'dp')), may hold values from 0.099609375 to 1.8984375
- up_one: bfloat16 [768, 3072], P(('seq', 'dp')), may hold values from -0.21875 to 0.21875
- down_one: bfloat16 [3072, 768], P(('seq', 'dp')), may hold values from -0.109375 to 0.109375
- norm_three: bfloat16 [768], P(('seq', 'dp')), may hold values from 0.099609375 to 1.8984375
- qkv_weight: bfloat16 [768, 2304], P(('seq', 'dp')), may hold values from -0.21875 to 0.21875
- out_two: bfloat16 [768, 768], P(('seq', 'dp')), may hold values from -3 to 3
- norm_four: bfloat16 [768], P(('seq', 'dp')), may hold values from 0.099609375 to 1.8984375
- up_two: bfloat16 [768, 3072], P(('seq', 'dp')), may hold values from -0.21875 to 0.21875
- down_two: bfloat16 [3072, 768], P(('seq', 'dp')), may hold values from -0.109375 to 0.109375
- cotangent: bfloat16 [8, 768, 768], P('dp', 'seq'), may hold values from -6 to 6
Outputs:
- activations: bfloat16 [8, 768, 768], P('dp', 'seq')
- input_grad: float32 [8, 768, 768], P('dp', 'seq')
- grad_norm_one: float32 [768], P(('seq', 'dp'))
- grad_query_one: float32 [768, 768], P(('seq', 'dp'))
- grad_key_one: float32 [768, 768], P(('seq', 'dp'))
- grad_value_one: float32 [768, 768], P(('seq', 'dp'))
- grad_shift_taps: float32 [768, 64], P(('seq', 'dp'))
- grad_decay_log: float32 [768, 64], P(('seq', 'dp'))
- grad_turn_angle: float32 [768, 64], P(('seq', 'dp'))
- grad_mix_real: float32 [768, 64], P(('seq', 'dp'))
- grad_mix_imag: float32 [768, 64], P(('seq', 'dp'))
- grad_skip_gain: float32 [768], P(('seq', 'dp'))
- grad_out_one: float32 [768, 768], P(('seq', 'dp'))
- grad_norm_two: float32 [768], P(('seq', 'dp'))
- grad_up_one: float32 [768, 3072], P(('seq', 'dp'))
- grad_down_one: float32 [3072, 768], P(('seq', 'dp'))
- grad_norm_three: float32 [768], P(('seq', 'dp'))
- grad_qkv_weight: float32 [768, 2304], P(('seq', 'dp'))
- grad_out_two: float32 [768, 768], P(('seq', 'dp'))
- grad_norm_four: float32 [768], P(('seq', 'dp'))
- grad_up_two: float32 [768, 3072], P(('seq', 'dp'))
- grad_down_two: float32 [3072, 768], P(('seq', 'dp'))
The draws below stay inside these ranges and needn't reach their ends.
Inputs may be any that keep to these rules, and one draw needn't show every extreme that they name: `lengths`: in each aligned run of four sequences exactly one, which one drawn from the seed, has 192 tokens and the other three have 768.
All inputs are finite; a program needn't handle non-finite values.
Results may differ from the reference program's by a relative error of at most 0.024.
Values may be sent and summed in bfloat16 or wider, within the bound.
A program may use at most 320 MiB of HBM per device.

```python
import math
import jax
import jax.numpy as jnp
from jax import lax

D = 768
FF = 3072
HEADS = 12
HDIM = 64
NSTATE = 64
SHIFT = 64
LEN = 768
GROUPS = 8


def draw_lengths(key, part):
    key = jax.random.fold_in(key, 7)
    short_slot = jax.random.randint(key, (GROUPS // 4,), 0, 4)
    slot_ids = jnp.arange(4, dtype=jnp.int32)
    is_short = slot_ids[None, :] == short_slot[:, None]
    return jnp.where(is_short, LEN // 4, LEN).reshape(GROUPS).astype(jnp.int32)


def levels(stream_key, dims, shards, low, top_value):
    def one(dim, shards_of):
        steps = jax.random.uniform(jax.random.fold_in(jax.random.fold_in(stream_key, 6), dim), (shards_of,), jnp.float32, low / len(shards), top_value / len(shards))
        return jnp.repeat(jnp.exp(steps), dims[dim] // shards_of).reshape((-1,) + (1,) * (len(dims) - dim - 1))

    loudness = one(*shards[0])
    for cut in shards[1:]:
        loudness = loudness * one(*cut)
    return loudness


def noise(own_key, dims, spread, bound, cuts=(), kind=jnp.bfloat16):
    gain = levels(own_key, dims, cuts, -0.22, 0.18) if cuts else 1.0
    drawn = jax.random.normal(own_key, dims, jnp.float32) * spread * gain
    return jnp.minimum(jnp.maximum(drawn, -bound), bound).astype(kind)


def setup_inputs(seed: int = 0) -> dict:
    arg_keys = jax.random.split(jax.random.key(seed), 24)
    return {
        "tokens": noise(arg_keys[0], (GROUPS, LEN, D), 1.0, 6.0, ((0, 8), (1, 4))),
        "lengths": draw_lengths(jax.random.fold_in(arg_keys[23], 71), 0),
        "norm_one": jnp.clip(1.0 + 0.18 * jax.random.normal(arg_keys[2], (D,), jnp.float32), 0.099609375, 1.8984375).astype(jnp.bfloat16),
        "query_one": noise(arg_keys[3], (D, D), D ** -0.5, 0.21875, ((0, 32),)),
        "key_one": noise(arg_keys[4], (D, D), D ** -0.5, 0.21875, ((0, 32),)),
        "value_one": noise(arg_keys[5], (D, D), D ** -0.5, 0.21875, ((0, 32),)),
        "shift_taps": noise(arg_keys[6], (D, SHIFT), SHIFT ** -0.5, 0.75, ((0, 32),)),
        "decay_log": jnp.clip(-9.0 + 7.8046875 * jax.random.uniform(arg_keys[7], (D, NSTATE), jnp.float32) ** levels(arg_keys[7], (D, NSTATE), ((0, 32),), -0.2, 0.2), -9.0, -1.1953125).astype(jnp.bfloat16),
        "turn_angle": jnp.clip(jax.random.uniform(arg_keys[8], (D, NSTATE), jnp.float32, -3.140625, 3.140625), -3.140625, 3.140625).astype(jnp.bfloat16),
        "mix_real": noise(arg_keys[9], (D, NSTATE), 0.01, 0.059814453, ((0, 32),)),
        "mix_imag": noise(arg_keys[10], (D, NSTATE), 0.01, 0.059814453, ((0, 32),)),
        "skip_gain": noise(arg_keys[11], (D,), 1.0, 4.0, ((0, 32),)),
        "out_one": noise(arg_keys[12], (D, D), D ** -0.5, 0.21875, ((0, 32),)),
        "norm_two": jnp.clip(1.0 + 0.18 * jax.random.normal(arg_keys[13], (D,), jnp.float32), 0.099609375, 1.8984375).astype(jnp.bfloat16),
        "up_one": noise(arg_keys[14], (D, FF), D ** -0.5, 0.21875, ((0, 32),)),
        "down_one": noise(arg_keys[15], (FF, D), FF ** -0.5, 0.109375, ((0, 32),)),
        "norm_three": jnp.clip(1.0 + 0.18 * jax.random.normal(arg_keys[16], (D,), jnp.float32), 0.099609375, 1.8984375).astype(jnp.bfloat16),
        "qkv_weight": noise(arg_keys[17], (D, 3 * D), D ** -0.5, 0.21875, ((0, 32),)),
        "out_two": noise(arg_keys[18], (D, D), 4 ** -0.5, 3.0, ((0, 32),)),
        "norm_four": jnp.clip(1.0 + 0.18 * jax.random.normal(arg_keys[19], (D,), jnp.float32), 0.099609375, 1.8984375).astype(jnp.bfloat16),
        "up_two": noise(arg_keys[20], (D, FF), D ** -0.5, 0.21875, ((0, 32),)),
        "down_two": noise(arg_keys[21], (FF, D), FF ** -0.5, 0.109375, ((0, 32),)),
        "cotangent": noise(arg_keys[22], (GROUPS, LEN, D), 1.0, 6.0, ((0, 8), (1, 4))),
    }


HIGHEST = lax.Precision.HIGHEST
EPSILON = 1e-05
MASKED = -1e+30

@jax.custom_vjp
def low(v):
    return lax.optimization_barrier(v.astype(jnp.bfloat16)).astype(jnp.float32)

@jax.custom_vjp
def low_back(v):
    return v

def low_keep(v):
    return (low(v), None)

def low_pass(kept, grad):
    return (grad,)

def back_keep(v):
    return (v, None)

def back_low(kept, grad):
    return (low(grad),)
low.defvjp(low_keep, low_pass)
low_back.defvjp(back_keep, back_low)

def layer_norm(residual, scale_gain):
    average = lax.optimization_barrier(jnp.mean(residual, axis=-1, keepdims=True))
    centered = residual - average
    variance = lax.optimization_barrier(jnp.mean(centered * centered, axis=-1, keepdims=True))
    return centered * lax.rsqrt(variance + EPSILON) * scale_gain

def matmul(left_side, right_side):
    return jnp.dot(left_side, right_side, precision=HIGHEST, preferred_element_type=jnp.float32)

def shift_conv(key_rows, tap_gains):
    seq_len = key_rows.shape[0]
    tap_count = tap_gains.shape[1]
    padded = jnp.concatenate([jnp.zeros((tap_count - 1, key_rows.shape[1]), jnp.float32), key_rows], axis=0)
    result = jnp.zeros_like(key_rows)
    for offset in range(tap_count):
        result = result + tap_gains[:, offset] * padded[tap_count - 1 - offset:tap_count - 1 - offset + seq_len]
    return result

def ssm_kernel(decay_log, turn_angle, mix_real, mix_imag, seq_len):
    decay_rate = jnp.exp(decay_log)
    piece_len = math.gcd(seq_len, 128)

    def kernel_piece(piece_index):
        offsets = (piece_index * piece_len + jnp.arange(piece_len)).astype(jnp.float32)
        scaled = offsets[:, None, None]
        magnitude = jnp.exp(-scaled * decay_rate[None])
        terms = mix_real[None] * jnp.cos(scaled * turn_angle[None]) - mix_imag[None] * jnp.sin(scaled * turn_angle[None])
        return lax.optimization_barrier(jnp.sum(magnitude * terms, axis=2))
    pieces = lax.map(jax.checkpoint(kernel_piece), jnp.arange(seq_len // piece_len))
    return pieces.reshape(seq_len, decay_log.shape[0])

def long_conv(signal, kernel):
    seq_len = signal.shape[0]
    spectrum = jnp.fft.rfft(signal, n=2 * seq_len, axis=0) * jnp.fft.rfft(kernel, n=2 * seq_len, axis=0)
    return jnp.fft.irfft(spectrum, n=2 * seq_len, axis=0)[:seq_len]

def feed_forward(residual, scale_gain, up_weight, down_weight):
    normed = low(layer_norm(residual, scale_gain))
    pre_act = low_back(matmul(normed, up_weight))
    activated = low(jax.nn.gelu(pre_act))
    return residual + low_back(matmul(activated, down_weight))

def attention(att_q, att_k, att_v, length):
    seq_len = att_q.shape[0]
    block_len = math.gcd(seq_len, 512)
    key_places = jnp.arange(seq_len, dtype=jnp.int32)

    def one_block(block_index):
        first_row = (block_index * block_len).astype(jnp.int32)
        query_rows = lax.dynamic_slice_in_dim(att_q, first_row, block_len, 0)
        raw_scores = jnp.einsum('qhd,khd->hqk', query_rows, att_k, precision=HIGHEST) * HDIM ** (-0.5)
        scores = low_back(raw_scores)
        row_places = first_row + jnp.arange(block_len, dtype=jnp.int32)
        allowed = (key_places[None, :] <= row_places[:, None]) & (key_places[None, :] < length)
        scores = jnp.where(allowed[None], scores, MASKED)
        att_weights = low(jax.nn.softmax(scores, axis=-1))
        return jnp.einsum('hqk,khd->qhd', att_weights, att_v, precision=HIGHEST)
    blocks = lax.map(jax.checkpoint(one_block), jnp.arange(seq_len // block_len, dtype=jnp.int32))
    return blocks.reshape(seq_len, HEADS * HDIM)

def forward_one(params, tokens, length):
    norm_one, query_one, key_one, value_one, shift_taps, decay_log, turn_angle, mix_real, mix_imag, skip_gain, out_one, norm_two, up_one, down_one, norm_three, qkv_weight, out_two, norm_four, up_two, down_two = params
    seq_len = tokens.shape[0]
    features = HEADS * HDIM
    live_mask = (jnp.arange(seq_len, dtype=jnp.int32) < length).astype(jnp.float32)[:, None]
    normed_one = low(layer_norm(tokens, norm_one))
    queries = low_back(matmul(normed_one, query_one))
    key_rows = low_back(matmul(normed_one, key_one))
    values = low_back(matmul(normed_one, value_one))
    signal = live_mask * shift_conv(key_rows, shift_taps) * values
    kernel = ssm_kernel(decay_log, turn_angle, mix_real, mix_imag, seq_len)
    ssm_out = long_conv(signal, kernel) + skip_gain * signal
    gated = low(queries * ssm_out)
    residual = tokens + low_back(matmul(gated, out_one))
    residual = feed_forward(residual, norm_two, up_one, down_one)
    normed_three = low(layer_norm(residual, norm_three))
    joint = low(low_back(matmul(normed_three, qkv_weight)))
    att_q = joint[:, :features].reshape(seq_len, HEADS, HDIM)
    att_k = joint[:, features:2 * features].reshape(seq_len, HEADS, HDIM)
    att_v = joint[:, 2 * features:].reshape(seq_len, HEADS, HDIM)
    attended = low(low_back(attention(att_q, att_k, att_v, length)))
    residual = residual + low_back(matmul(attended, out_two))
    residual = feed_forward(residual, norm_four, up_two, down_two)
    return live_mask * residual

def reference(tokens, lengths, norm_one, query_one, key_one, value_one, shift_taps, decay_log, turn_angle, mix_real, mix_imag, skip_gain, out_one, norm_two, up_one, down_one, norm_three, qkv_weight, out_two, norm_four, up_two, down_two, cotangent):
    weights = (norm_one.astype(jnp.float32), query_one.astype(jnp.float32), key_one.astype(jnp.float32), value_one.astype(jnp.float32), shift_taps.astype(jnp.float32), decay_log.astype(jnp.float32), turn_angle.astype(jnp.float32), mix_real.astype(jnp.float32), mix_imag.astype(jnp.float32), skip_gain.astype(jnp.float32), out_one.astype(jnp.float32), norm_two.astype(jnp.float32), up_one.astype(jnp.float32), down_one.astype(jnp.float32), norm_three.astype(jnp.float32), qkv_weight.astype(jnp.float32), out_two.astype(jnp.float32), norm_four.astype(jnp.float32), up_two.astype(jnp.float32), down_two.astype(jnp.float32))

    def one_sequence(totals, item):
        seq_tokens, length, seq_cot = item
        output, pull = jax.vjp(lambda params, inputs: forward_one(params, inputs, length), weights, seq_tokens.astype(jnp.float32))
        grad_weights, grad_tokens = pull(seq_cot.astype(jnp.float32))
        totals = jax.tree.map(lambda left_side, right_side: left_side + right_side, totals, grad_weights)
        return (totals, (output.astype(jnp.bfloat16), grad_tokens))
    empty_grads = jax.tree.map(jnp.zeros_like, weights)
    totals, (activations, input_grad) = lax.scan(one_sequence, empty_grads, (tokens, lengths, cotangent))
    grad_norm_one, grad_query_one, grad_key_one, grad_value_one, grad_shift_taps, grad_decay_log, grad_turn_angle, grad_mix_real, grad_mix_imag, grad_skip_gain, grad_out_one, grad_norm_two, grad_up_one, grad_down_one, grad_norm_three, grad_qkv_weight, grad_out_two, grad_norm_four, grad_up_two, grad_down_two = totals
    return (activations, input_grad, grad_norm_one, grad_query_one, grad_key_one, grad_value_one, grad_shift_taps, grad_decay_log, grad_turn_angle, grad_mix_real, grad_mix_imag, grad_skip_gain, grad_out_one, grad_norm_two, grad_up_one, grad_down_one, grad_norm_three, grad_qkv_weight, grad_out_two, grad_norm_four, grad_up_two, grad_down_two)
```

```python
from functools import partial

import jax
import jax.numpy as jnp
from jax import lax
from jax.experimental import pallas as pl
from jax.experimental.pallas import tpu as pltpu
from jax.sharding import PartitionSpec as P

HEADS = 12
HDIM = 64
EPSILON = 1e-05
HIGHEST = lax.Precision.HIGHEST
MASKED = -1e30
BOTH = ("seq", "dp")
MESH = pl.DeviceIdType.MESH
MIB = 1024 * 1024
F32 = jnp.float32
BF16 = jnp.bfloat16


def grouped(fast):
    return lax.axis_size("seq") == 4 and lax.axis_size("dp") == 8


def coordinates():
    seq, dp = lax.axis_index("seq"), lax.axis_index("dp")
    return seq // 2, seq % 2, dp // 2, dp % 2


def slot_of(y, c, z, x):
    return (y * 2 + c) * 8 + z * 2 + x


def device_of(y, c, z, x):
    return (y * 2 + c, z * 2 + x)


def greet(peers):
    barrier = pltpu.get_barrier_semaphore()
    for peer in peers:
        pl.semaphore_signal(barrier, inc=1, device_id=peer, device_id_type=MESH)
    pl.semaphore_wait(barrier, len(peers))


def six_peers(y, c, z, x):
    return [device_of(y, c, (z + k) % 4, x) for k in (1, 2, 3)] + [
        device_of(y, c, z, 1 - x),
        device_of(1 - y, c, z, x),
        device_of(y, 1 - c, z, x),
    ]


def gather_body(parts, count, *refs):
    sources, gathered = refs[:count], refs[count : 2 * count]
    local_sem, send_sem, recv_sem = refs[2 * count :]
    y, c, z, x = coordinates()
    greet(six_peers(y, c, z, x))
    me = slot_of(y, c, z, x)
    across_x = device_of(y, c, z, 1 - x)
    across_y = device_of(1 - y, c, z, x)
    other_core = device_of(y, 1 - c, z, x)
    own = [
        pltpu.make_async_copy(sources[i], gathered[i].at[me], local_sem.at[i])
        for i in range(count)
    ]
    for copy in own:
        copy.start()

    def place(p, slot):
        i, row, rows, column, columns, _ = parts[p]
        return gathered[i].at[slot, pl.ds(row, rows), pl.ds(column, columns)]

    def source(p):
        i, row, rows, column, columns, _ = parts[p]
        return sources[i].at[pl.ds(row, rows), pl.ds(column, columns)]

    def send(p, slot, target, first=False):
        pltpu.make_async_remote_copy(
            src_ref=source(p) if first else place(p, slot),
            dst_ref=place(p, slot),
            send_sem=send_sem.at[p],
            recv_sem=recv_sem.at[p, slot],
            device_id=target,
            device_id_type=MESH,
        ).start()

    def arrived(p, slot):
        pltpu.make_async_copy(place(p, slot), place(p, slot), recv_sem.at[p, slot]).wait()

    every = range(len(parts))
    for p in every:
        for k in (1, 3, 2):
            send(p, me, device_of(y, c, (z + k) % 4, x), True)
        send(p, me, across_x, True)
        send(p, me, across_y, True)
        send(p, me, other_core, True)

    def after_z(p):
        for k in (3, 1, 2):
            slot = slot_of(y, c, (z + k) % 4, x)
            arrived(p, slot)
            send(p, slot, across_x)
            send(p, slot, across_y)
            send(p, slot, other_core)

    def after_first(p):
        x_first = parts[p][5]
        for k in (0, 3, 1, 2):
            by_x = slot_of(y, c, (z + k) % 4, 1 - x)
            by_y = slot_of(1 - y, c, (z + k) % 4, x)
            arrived(p, by_x)
            if x_first:
                send(p, by_x, across_y)
            send(p, by_x, other_core)
            arrived(p, by_y)
            if not x_first:
                send(p, by_y, across_x)
            send(p, by_y, other_core)

    def after_second(p):
        for k in (0, 3, 1, 2):
            slot = slot_of(1 - y, c, (z + k) % 4, 1 - x)
            arrived(p, slot)
            send(p, slot, other_core)

    for p in range(len(parts) + 2):
        if p < len(parts):
            after_z(p)
        if 0 <= p - 1 < len(parts):
            after_first(p - 1)
        if 0 <= p - 2 < len(parts):
            after_second(p - 2)
    for p in every:
        for side in (0, 1):
            for zz in range(4):
                for xx in (0, 1):
                    arrived(p, slot_of(side, 1 - c, zz, xx))
    for copy in own:
        copy.wait()
    for p in every:
        i, row, rows, column, columns, _ = parts[p]
        sent = gathered[i].at[pl.ds(0, 31), pl.ds(row, rows), pl.ds(column, columns)]
        pltpu.make_async_copy(sent, sent, send_sem.at[p]).wait()


def cut(arrays):
    parts = []
    for i, (rows, columns) in enumerate(arrays):
        if columns > 1536:
            width = 1536 if columns % 1536 == 0 else 768
            pieces = [(0, rows, w, width) for w in range(0, columns, width)]
        elif rows > 48:
            pieces = [(r, 48, 0, columns) for r in range(0, rows, 48)]
        else:
            pieces = [(0, rows, 0, columns)]
        for piece in pieces:
            parts.append((i,) + piece + (len(parts) % 2 == 0,))
    return parts


def gather_all(arrays, collective_id):
    if not grouped(None):
        return [lax.all_gather(a, BOTH, axis=0) for a in arrays]
    count = len(arrays)
    parts = cut([a.shape for a in arrays])
    return pl.pallas_call(
        partial(gather_body, parts, count),
        out_shape=[jax.ShapeDtypeStruct((32,) + a.shape, a.dtype) for a in arrays],
        in_specs=[pl.BlockSpec(memory_space=pl.ANY)] * count,
        out_specs=[pl.BlockSpec(memory_space=pl.ANY)] * count,
        scratch_shapes=[
            pltpu.SemaphoreType.DMA((count,)),
            pltpu.SemaphoreType.DMA((len(parts),)),
            pltpu.SemaphoreType.DMA((len(parts), 32)),
        ],
        compiler_params=pltpu.CompilerParams(
            collective_id=collective_id, has_side_effects=True
        ),
    )(*arrays)


def reduce_body(parts, count, *refs):
    terms, totals = refs[:count], refs[count : 2 * count]
    buffers = refs[2 * count : 2 * count + 4 * len(parts)]
    send_sem, recv_sem = refs[2 * count + 4 * len(parts) :]
    y, c, z, x = coordinates()
    greet(six_peers(y, c, z, x))

    def term(p, core):
        i, row, rows, column, columns, _ = parts[p]
        return terms[i].at[:, core, :, :, pl.ds(row, rows), pl.ds(column, columns)]

    def copies(p, stage):
        one, two, three, four = buffers[4 * p : 4 * p + 4]
        x_last = parts[p][5]
        if stage == 0:
            pairs = [(term(p, 1 - c), one, device_of(y, 1 - c, z, x))]
        elif stage == 1 and x_last:
            pairs = [(one.at[1 - y], two, device_of(1 - y, c, z, x))]
        elif stage == 1:
            pairs = [(one.at[:, :, 1 - x], two, device_of(y, c, z, 1 - x))]
        elif stage == 2 and x_last:
            pairs = [(two.at[:, 1 - x], three, device_of(y, c, z, 1 - x))]
        elif stage == 2:
            pairs = [(two.at[1 - y], three, device_of(1 - y, c, z, x))]
        else:
            pairs = [
                (three.at[(z + k) % 4], four.at[k - 1], device_of(y, c, (z + k) % 4, x))
                for k in (1, 2, 3)
            ]
        return [
            pltpu.make_async_remote_copy(
                src_ref=src,
                dst_ref=dst,
                send_sem=send_sem.at[p, stage + n],
                recv_sem=recv_sem.at[p, stage + n],
                device_id=target,
                device_id_type=MESH,
            )
            for n, (src, dst, target) in enumerate(pairs)
        ]

    def add(p, stage):
        one, two, three, four = buffers[4 * p : 4 * p + 4]
        i, row, rows, column, columns, x_last = parts[p]
        total = lambda a, b: (a.astype(F32) + b.astype(F32)).astype(one.dtype)
        if stage == 0:

            def add_one(k, _):
                b, zz = k // 4, k % 4
                for xx in (0, 1):
                    mine = terms[i][b, c, zz, xx, pl.ds(row, rows), pl.ds(column, columns)]
                    one[b, zz, xx] = total(one[b, zz, xx], mine)
                return 0

            lax.fori_loop(0, 8, add_one, 0)
        elif stage == 1:

            def add_two(k, _):
                for h in (0, 1):
                    mine = one[y, k, h] if x_last else one[h, k, x]
                    if x_last:
                        two[k, h] = total(two[k, h], mine)
                    else:
                        two[h, k] = total(two[h, k], mine)
                return 0

            lax.fori_loop(0, 4, add_two, 0)
        elif stage == 2:

            def add_three(k, _):
                mine = two[k, x] if x_last else two[y, k]
                three[k] = total(three[k], mine)
                return 0

            lax.fori_loop(0, 4, add_three, 0)
        else:
            totals[i][pl.ds(row, rows), pl.ds(column, columns)] = (
                three[z].astype(F32)
                + four[0].astype(F32)
                + four[1].astype(F32)
                + four[2].astype(F32)
            )

    for p in range(len(parts)):
        for copy in copies(p, 0):
            copy.start()
    for step in range(len(parts) + 3):
        for stage in range(4):
            p = step - stage
            if 0 <= p < len(parts):
                for copy in copies(p, stage):
                    copy.wait_recv()
                add(p, stage)
                if stage < 3:
                    for copy in copies(p, stage + 1):
                        copy.start()
    for p in range(len(parts)):
        for stage in range(4):
            for copy in copies(p, stage):
                copy.wait_send()


def reduce_all(arrays, collective_id):
    if not grouped(None):
        return [
            lax.psum_scatter(a, BOTH, scatter_dimension=0, tiled=False).astype(F32)
            for a in arrays
        ]
    count = len(arrays)
    parts = cut([a.shape[1:] for a in arrays])
    scratch = []
    for i, _, rows, _, columns, x_last in parts:
        kind = arrays[i].dtype
        scratch += [
            pltpu.VMEM((2, 4, 2, rows, columns), kind),
            pltpu.VMEM(((4, 2) if x_last else (2, 4)) + (rows, columns), kind),
            pltpu.VMEM((4, rows, columns), kind),
            pltpu.VMEM((3, rows, columns), kind),
        ]
    return pl.pallas_call(
        partial(reduce_body, parts, count),
        out_shape=[jax.ShapeDtypeStruct(a.shape[1:], F32) for a in arrays],
        in_specs=[pl.BlockSpec(memory_space=pltpu.VMEM)] * count,
        out_specs=[pl.BlockSpec(memory_space=pltpu.VMEM)] * count,
        scratch_shapes=scratch
        + [
            pltpu.SemaphoreType.DMA((len(parts), 6)),
            pltpu.SemaphoreType.DMA((len(parts), 6)),
        ],
        compiler_params=pltpu.CompilerParams(
            collective_id=collective_id, has_side_effects=True, vmem_limit_bytes=58 * MIB
        ),
    )(*[a.reshape((2, 2, 4, 2) + a.shape[1:]) for a in arrays])


def swap_body(src, dst, local_sem, send_sem, recv_sem):
    rows, groups = lax.axis_size("seq"), lax.axis_size("dp")
    count = rows * groups
    me = lax.axis_index("seq") * groups + lax.axis_index("dp")
    others = [lax.rem(me + k, count) for k in range(1, count)]
    places = [(o // groups, lax.rem(o, groups)) for o in others]
    own = pltpu.make_async_copy(src.at[me], dst.at[me], local_sem)
    own.start()
    greet(places)
    for o, place in zip(others, places):
        pltpu.make_async_remote_copy(
            src_ref=src.at[o],
            dst_ref=dst.at[me],
            send_sem=send_sem,
            recv_sem=recv_sem,
            device_id=place,
            device_id_type=MESH,
        ).start()
    most = pl.ds(0, count - 1)
    pltpu.make_async_copy(src.at[most], dst.at[most], recv_sem).wait()
    pltpu.make_async_copy(src.at[most], dst.at[most], send_sem).wait()
    own.wait()


def swap_all(value, collective_id):
    if not grouped(None):
        return lax.all_to_all(value, BOTH, 0, 0, tiled=True)
    return pl.pallas_call(
        swap_body,
        out_shape=jax.ShapeDtypeStruct(value.shape, value.dtype),
        in_specs=[pl.BlockSpec(memory_space=pltpu.VMEM)],
        out_specs=pl.BlockSpec(memory_space=pltpu.VMEM),
        scratch_shapes=[pltpu.SemaphoreType.DMA(())] * 3,
        compiler_params=pltpu.CompilerParams(
            collective_id=collective_id, has_side_effects=True
        ),
    )(value)


def line_body(src, dst, local_sem, send_sem, recv_sem):
    y, c, z, x = coordinates()
    me, mate, far, last = y * 2 + c, y * 2 + 1 - c, (1 - y) * 2 + c, (1 - y) * 2 + 1 - c
    own = pltpu.make_async_copy(src, dst.at[me], local_sem)
    own.start()
    core, side = device_of(y, 1 - c, z, x), device_of(1 - y, c, z, x)
    greet([core, side])

    def copy(n, source, slot, target):
        return pltpu.make_async_remote_copy(
            src_ref=source,
            dst_ref=dst.at[slot],
            send_sem=send_sem.at[n],
            recv_sem=recv_sem.at[n],
            device_id=target,
            device_id_type=MESH,
        )

    first = copy(0, src, me, side)
    second = copy(1, src, me, core)
    third = copy(2, dst.at[far], far, core)
    first.start()
    second.start()
    first.wait_recv()
    third.start()
    second.wait_recv()
    third.wait_recv()
    for each in (first, second, third):
        each.wait_send()
    own.wait()


def gather_line(value, collective_id):
    if not grouped(None):
        return lax.all_gather(value, "seq", axis=0)
    return pl.pallas_call(
        line_body,
        out_shape=jax.ShapeDtypeStruct((4,) + value.shape, value.dtype),
        in_specs=[pl.BlockSpec(memory_space=pltpu.VMEM)],
        out_specs=pl.BlockSpec(memory_space=pltpu.VMEM),
        scratch_shapes=[
            pltpu.SemaphoreType.DMA(()),
            pltpu.SemaphoreType.DMA((3,)),
            pltpu.SemaphoreType.DMA((3,)),
        ],
        compiler_params=pltpu.CompilerParams(
            collective_id=collective_id, has_side_effects=True
        ),
    )(value)


def line_sum_body(src, dst, one, two, send_sem, recv_sem):
    y, c, z, x = coordinates()
    core, side = device_of(y, 1 - c, z, x), device_of(1 - y, c, z, x)
    greet([core, side])

    def copy(n, source, target, where):
        return pltpu.make_async_remote_copy(
            src_ref=source,
            dst_ref=where,
            send_sem=send_sem.at[n],
            recv_sem=recv_sem.at[n],
            device_id=target,
            device_id_type=MESH,
        )

    far = copy(0, src.at[1 - y, 1 - c], core, one.at[1 - y])
    near = copy(1, src.at[y, 1 - c], core, one.at[y])
    far.start()
    near.start()
    far.wait_recv()
    one[1 - y] = (one[1 - y].astype(F32) + src[1 - y, c].astype(F32)).astype(one.dtype)
    onward = copy(2, one.at[1 - y], side, two)
    onward.start()
    near.wait_recv()
    onward.wait_recv()
    dst[...] = (one[y].astype(F32) + src[y, c].astype(F32)) + two[...].astype(F32)
    for each in (far, near, onward):
        each.wait_send()


def sum_line(value, collective_id):
    if not grouped(None):
        return lax.psum_scatter(value, "seq", scatter_dimension=0).astype(F32)
    return pl.pallas_call(
        line_sum_body,
        out_shape=jax.ShapeDtypeStruct(value.shape[1:], F32),
        in_specs=[pl.BlockSpec(memory_space=pltpu.VMEM)],
        out_specs=pl.BlockSpec(memory_space=pltpu.VMEM),
        scratch_shapes=[
            pltpu.VMEM((2,) + value.shape[1:], value.dtype),
            pltpu.VMEM(value.shape[1:], value.dtype),
            pltpu.SemaphoreType.DMA((3,)),
            pltpu.SemaphoreType.DMA((3,)),
        ],
        compiler_params=pltpu.CompilerParams(
            collective_id=collective_id, has_side_effects=True, vmem_limit_bytes=32 * MIB
        ),
    )(value.reshape((2, 2) + value.shape[1:]))


def layer_norm(residual, scale_gain):
    average = jnp.mean(residual, axis=-1, keepdims=True)
    centered = residual - average
    variance = jnp.mean(centered * centered, axis=-1, keepdims=True)
    return centered * lax.rsqrt(variance + EPSILON) * scale_gain


def contract(left_side, right_side, left_dim, right_dim):
    return lax.dot_general(
        left_side,
        right_side,
        (((left_dim,), (right_dim,)), ((), ())),
        preferred_element_type=F32,
    )


def product(left_side, right_side):
    return contract(left_side, right_side, 1, 0)


def product_back(left_side, right_side):
    return contract(left_side, right_side, 1, 1)


def product_sum(left_side, right_side):
    return contract(left_side, right_side, 0, 0)


def feed_forward(residual, scale_gain, up_weight, down_weight):
    normed = layer_norm(residual, scale_gain).astype(BF16)
    pre_act = product(normed, up_weight)
    activated = jax.nn.gelu(pre_act).astype(BF16)
    return (residual + product(activated, down_weight), (normed, pre_act, activated))


def feed_back(residual, scale_gain, up_weight, down_weight, stored, grad_residual):
    normed, pre_act, activated = stored
    grad_branch = grad_residual.astype(BF16)
    grad_down = product_sum(activated, grad_branch)
    grad_activated = product_back(grad_branch, down_weight)
    gelu_pull = jax.vjp(jax.nn.gelu, pre_act)[1]
    grad_pre = gelu_pull(grad_activated)[0].astype(BF16)
    grad_up = product_sum(normed, grad_pre)
    grad_normed = product_back(grad_pre, up_weight)
    norm_pull = jax.vjp(layer_norm, residual, scale_gain)[1]
    grad_input, grad_gain = norm_pull(grad_normed)
    return (grad_residual + grad_input, grad_gain, grad_up, grad_down)


def ssm_kernel(decay_log, turn_angle, mix_real, mix_imag, length):
    rate = jnp.exp(decay_log)[:, :, None]
    angle = turn_angle[:, :, None]
    step = 32

    def powers(times):
        return (
            jnp.exp(-times * rate) * jnp.cos(times * angle),
            jnp.exp(-times * rate) * jnp.sin(times * angle),
        )

    low_real, low_imag = powers(jnp.arange(step, dtype=F32)[None, None])
    high_real, high_imag = powers(
        (step * jnp.arange(length // step, dtype=jnp.int32)).astype(F32)[None, None]
    )
    real, imag = mix_real[:, :, None], mix_imag[:, :, None]
    high = jnp.concatenate(
        [real * high_real - imag * high_imag, -(real * high_imag + imag * high_real)], axis=1
    )
    low = jnp.concatenate([low_real, low_imag], axis=1)
    kernel = jnp.einsum("cna,cnb->cab", high, low, precision=HIGHEST)
    return kernel.reshape(decay_log.shape[0], length)


def toeplitz(row, rows):
    spread = jnp.broadcast_to(row, (rows, row.shape[1]))
    return pltpu.roll(spread, 0, 1, stride=1, stride_axis=0)


def block_sum(mixed, blocks, groups, rows):
    total = mixed[:, :rows]
    for d in range(1, blocks):
        piece = mixed[: (blocks - d) * groups, d * rows : (d + 1) * rows]
        total = total + jnp.concatenate(
            [jnp.zeros((d * groups, rows), piece.dtype), piece], axis=0
        )
    return total


def block_spread(value, blocks, lags, groups, rows):
    pieces = [value]
    for d in range(1, lags):
        pieces.append(
            jnp.concatenate(
                [value[d * groups :], jnp.zeros((d * groups, rows), value.dtype)], axis=0
            )
        )
    return jnp.concatenate(pieces, axis=1)


def mixer_body(blocks, groups, rows, k_ref, v_ref, taps_ref, kernel_ref, skip_ref, shifted_ref, out_ref):
    channels = k_ref.shape[0]
    span = blocks * rows
    for ch in range(channels):
        taps = toeplitz(taps_ref[ch : ch + 1, :], rows)[:, : 2 * rows].astype(BF16)
        longer = toeplitz(kernel_ref[ch : ch + 1, :], rows)[:, :span].astype(BF16)
        near = product(k_ref[ch], taps)
        shifted = near[:, :rows] + jnp.concatenate(
            [jnp.zeros((groups, rows), F32), near[: (blocks - 1) * groups, rows:]], axis=0
        )
        signal = shifted * v_ref[ch].astype(F32)
        mixed = product(signal.astype(BF16), longer)
        total = block_sum(mixed, blocks, groups, rows)
        shifted_ref[ch] = shifted
        out_ref[ch] = (total + skip_ref[ch : ch + 1, :1] * signal).astype(BF16)


def mixer_back_body(
    blocks, groups, rows,
    grad_ref, k_ref, v_ref, shifted_ref, taps_ref, kernel_ref, skip_ref,
    grad_k_ref, grad_v_ref, kernel_grad_ref, taps_grad_ref, skip_grad_ref,
):
    channels = k_ref.shape[0]
    span = blocks * rows
    wide, narrow = kernel_ref.shape[1], taps_ref.shape[1]
    turned = (
        lax.broadcasted_iota(jnp.int32, (rows, rows), 0)
        + lax.broadcasted_iota(jnp.int32, (rows, rows), 1)
        == rows - 1
    ).astype(BF16)

    def lag_sums(earlier, spread, lanes):
        backward = product(earlier, turned).astype(BF16)
        pairs = product_sum(backward, spread)
        padded = jnp.concatenate(
            [pairs, jnp.zeros((rows, lanes - pairs.shape[1]), F32)], axis=1
        )
        return jnp.sum(
            pltpu.roll(padded, lanes - rows + 1, 1, stride=1, stride_axis=0),
            axis=0,
            keepdims=True,
        )

    for ch in range(channels):
        taps = toeplitz(taps_ref[ch : ch + 1, :], rows)[:, : 2 * rows].astype(BF16)
        longer = toeplitz(kernel_ref[ch : ch + 1, :], rows)[:, :span].astype(BF16)
        out_grad = grad_ref[ch]
        skip = skip_ref[ch : ch + 1, :1]
        values = v_ref[ch].astype(F32)
        shifted = shifted_ref[ch]
        signal = shifted * values
        wide_grad = out_grad.astype(F32)
        later = block_spread(wide_grad, blocks, blocks, groups, rows).astype(BF16)
        signal_grad = product_back(later, longer) + skip * wide_grad
        kernel_grad_ref[ch : ch + 1, :] = lag_sums(signal.astype(BF16), later, wide)
        skip_grad_ref[ch : ch + 1, :] = jnp.broadcast_to(
            jnp.sum(jnp.sum(signal * wide_grad, axis=0, keepdims=True), axis=1, keepdims=True),
            (1, 128),
        )
        shifted_grad = values * signal_grad
        grad_v_ref[ch] = (shifted * signal_grad).astype(BF16)
        next_two = block_spread(shifted_grad, blocks, 2, groups, rows).astype(BF16)
        grad_k_ref[ch] = product_back(next_two, taps).astype(BF16)
        taps_grad_ref[ch : ch + 1, :] = lag_sums(k_ref[ch], next_two, narrow)


def allowed_keys(place, length, rows, keys):
    row_places = place * rows + lax.broadcasted_iota(jnp.int32, (rows, keys), 0)
    key_places = lax.broadcasted_iota(jnp.int32, (rows, keys), 1)
    return (key_places <= row_places) & (key_places < length)


def attend_body(where_ref, q_ref, kv_ref, out_ref, log_ref):
    rows, features = q_ref.shape
    keys = kv_ref.shape[0]
    allowed = allowed_keys(where_ref[0], where_ref[1], rows, keys)
    for head in range(HEADS):
        own = slice(head * HDIM, (head + 1) * HDIM)
        values = slice(features + head * HDIM, features + (head + 1) * HDIM)
        scores = product_back(q_ref[:, own], kv_ref[:, own]) * HDIM ** (-0.5)
        scores = jnp.where(allowed, scores, MASKED)
        most = jnp.max(scores, axis=1, keepdims=True)
        powers = jnp.exp(scores - most)
        total = jnp.sum(powers, axis=1, keepdims=True)
        weights = (powers * (1.0 / total)).astype(BF16)
        out_ref[:, own] = product(weights, kv_ref[:, values]).astype(BF16)
        log_ref[:, head : head + 1] = most + jnp.log(total)


def attend_back_body(where_ref, q_ref, kv_ref, log_ref, grad_ref, grad_q_ref, grad_kv_ref):
    rows, features = q_ref.shape
    keys = kv_ref.shape[0]
    allowed = allowed_keys(where_ref[0], where_ref[1], rows, keys)
    scale = HDIM ** (-0.5)
    for head in range(HEADS):
        own = slice(head * HDIM, (head + 1) * HDIM)
        values = slice(features + head * HDIM, features + (head + 1) * HDIM)
        queries, grads = q_ref[:, own], grad_ref[:, own]
        scores = product_back(queries, kv_ref[:, own]) * scale
        probs = jnp.where(allowed, jnp.exp(scores - log_ref[:, head : head + 1]), 0.0)
        prob_grad = product_back(grads, kv_ref[:, values])
        delta = jnp.sum(probs * prob_grad, axis=1, keepdims=True)
        grad_scores = (probs * (prob_grad - delta)).astype(BF16)
        grad_q_ref[:, own] = (product(grad_scores, kv_ref[:, own]) * scale).astype(BF16)
        grad_kv_ref[:, own] = (product_sum(grad_scores, queries) * scale).astype(BF16)
        grad_kv_ref[:, values] = product_sum(probs.astype(BF16), grads).astype(BF16)


def local_call(body, out_shape, *operands, scalars=0, limit=48):
    vmem = pl.BlockSpec(memory_space=pltpu.VMEM)
    smem = pl.BlockSpec(memory_space=pltpu.SMEM)
    return pl.pallas_call(
        body,
        out_shape=out_shape,
        in_specs=[smem] * scalars + [vmem] * (len(operands) - scalars),
        out_specs=jax.tree.map(lambda _: vmem, out_shape),
        compiler_params=pltpu.CompilerParams(vmem_limit_bytes=limit * MIB),
    )(*operands)


def shards(
    tokens, lengths, norm_one, query_one, key_one, value_one, shift_taps, decay_log,
    turn_angle, mix_real, mix_imag, skip_gain, out_one, norm_two, up_one, down_one,
    norm_three, qkv_weight, out_two, norm_four, up_two, down_two, cotangent,
):
    blocks, groups = lax.axis_size("seq"), lax.axis_size("dp")
    devices = blocks * groups
    rows, features = tokens.shape[1], tokens.shape[2]
    channels = features // devices
    place = lax.axis_index("seq")
    length = lengths[0]
    row_places = place * rows + jnp.arange(rows, dtype=jnp.int32)
    live_mask = (row_places < length).astype(F32)[:, None]
    live_lane = (row_places < length).astype(F32)[None, :]

    gains = jnp.stack([norm_one, norm_two, norm_three, norm_four]).astype(F32)
    gains = jnp.pad(gains, ((0, 4), (0, 128 - channels)))
    late_up, late_down = (
        lax.all_gather(up_two, BOTH, axis=0, tiled=True),
        lax.all_gather(down_two, BOTH, axis=0, tiled=True),
    )
    everything = gather_all(
        [gains, query_one, key_one, value_one, out_one, up_one, down_one, qkv_weight, out_two], 1
    )
    gains = everything[0][:, :4, :channels].transpose(1, 0, 2).reshape(4, features)
    gain_one, gain_two, gain_three, gain_four = gains[0], gains[1], gains[2], gains[3]
    query_all, key_all, value_all, out_one_all, up_one_all, down_one_all, qkv_all, out_two_all = [
        g.reshape((-1, g.shape[2])) for g in everything[1:]
    ]

    kernel, kernel_pull = jax.vjp(
        partial(ssm_kernel, length=rows * blocks),
        *[a.astype(F32) for a in (decay_log, turn_angle, mix_real, mix_imag)],
    )
    wide = -(-(blocks + 1) * rows // 128) * 128
    kernel_row = jnp.pad(kernel, ((0, 0), (0, wide - kernel.shape[1])))
    narrow = -(-3 * rows // 128) * 128
    tap_row = jnp.pad(
        shift_taps.astype(F32), ((0, 0), (0, narrow - shift_taps.shape[1]))
    )
    skip_row = jnp.broadcast_to(skip_gain.astype(F32)[:, None], (channels, 128))

    residual_zero = tokens[0].astype(F32)
    normed_one = layer_norm(residual_zero, gain_one).astype(BF16)
    queries = product(normed_one, query_all)
    keys = contract(key_all, normed_one, 0, 1).astype(BF16)
    values = (contract(value_all, normed_one, 0, 1) * live_lane).astype(BF16)

    def to_channels(pieces, collective_id):
        sent = jnp.stack([p.reshape(devices, channels, rows) for p in pieces], axis=1)
        came = swap_all(sent, collective_id)
        came = came.transpose(1, 2, 0, 3)
        return [came[n] for n in range(len(pieces))]

    def to_rows(pieces, collective_id):
        sent = jnp.stack([p.transpose(1, 0, 2) for p in pieces], axis=1)
        came = swap_all(sent, collective_id)
        return [came[:, n].reshape(features, rows) for n in range(len(pieces))]

    k_own, v_own = to_channels([keys, values], 2)
    per_channel = (channels, devices, rows)
    shifted, mixed = local_call(
        partial(mixer_body, blocks, groups, rows),
        [jax.ShapeDtypeStruct(per_channel, F32), jax.ShapeDtypeStruct(per_channel, BF16)],
        k_own, v_own, tap_row, kernel_row, skip_row,
    )
    (ssm_out,) = to_rows([mixed], 3)
    ssm_out = ssm_out.T.astype(F32)
    gated = (queries * ssm_out).astype(BF16)
    residual_one = residual_zero + product(gated, out_one_all)
    residual_two, stored_two = feed_forward(residual_one, gain_two, up_one_all, down_one_all)
    normed_three = layer_norm(residual_two, gain_three).astype(BF16)
    joint = product(normed_three, qkv_all).astype(BF16)
    att_q = joint[:, :features]
    kv = gather_line(joint[:, features:], 4).reshape(blocks * rows, 2 * features)
    where = jnp.stack([place.astype(jnp.int32), length])
    attended, log_total = local_call(
        attend_body,
        [jax.ShapeDtypeStruct((rows, features), BF16), jax.ShapeDtypeStruct((rows, 128), F32)],
        where, att_q, kv, scalars=1,
    )
    residual_three = residual_two + product(attended, out_two_all)
    residual_four, stored_four = feed_forward(residual_three, gain_four, late_up, late_down)
    activations = (live_mask * residual_four).astype(BF16)

    grad_four = live_mask * cotangent[0].astype(F32)
    grad_three, grad_norm_four, grad_up_two, grad_down_two = feed_back(
        residual_three, gain_four, late_up, late_down, stored_four, grad_four
    )
    grad_up_two = lax.psum_scatter(
        grad_up_two.astype(BF16), BOTH, scatter_dimension=0, tiled=True
    ).astype(F32)
    grad_down_two = lax.psum_scatter(
        grad_down_two.astype(BF16), BOTH, scatter_dimension=0, tiled=True
    ).astype(F32)
    branch_three = grad_three.astype(BF16)
    grad_out_two = product_sum(attended, branch_three)
    grad_attended = product_back(branch_three, out_two_all).astype(BF16)
    grad_q, grad_kv = local_call(
        attend_back_body,
        [
            jax.ShapeDtypeStruct((rows, features), BF16),
            jax.ShapeDtypeStruct((blocks * rows, 2 * features), BF16),
        ],
        where, att_q, kv, log_total, grad_attended, scalars=1,
    )
    grad_kv = sum_line(grad_kv.reshape(blocks, rows, 2 * features), 5)
    grad_joint = jnp.concatenate([grad_q, grad_kv.astype(BF16)], axis=1)
    grad_qkv_weight = product_sum(normed_three, grad_joint)
    grad_normed_three = product_back(grad_joint, qkv_all)
    grad_from_three, grad_norm_three = jax.vjp(layer_norm, residual_two, gain_three)[1](
        grad_normed_three
    )
    grad_two = grad_three + grad_from_three
    grad_one, grad_norm_two, grad_up_one, grad_down_one = feed_back(
        residual_one, gain_two, up_one_all, down_one_all, stored_two, grad_two
    )
    branch_one = grad_one.astype(BF16)
    grad_out_one = product_sum(gated, branch_one)
    gated_grad = product_back(branch_one, out_one_all)
    grad_queries = (gated_grad * ssm_out).astype(BF16)
    ssm_grad = (gated_grad * queries).T.astype(BF16)
    (grad_own,) = to_channels([ssm_grad], 6)
    grad_k_own, grad_v_own, kernel_grad, taps_grad, skip_grad = local_call(
        partial(mixer_back_body, blocks, groups, rows),
        [
            jax.ShapeDtypeStruct(per_channel, BF16),
            jax.ShapeDtypeStruct(per_channel, BF16),
            jax.ShapeDtypeStruct((channels, wide), F32),
            jax.ShapeDtypeStruct((channels, narrow), F32),
            jax.ShapeDtypeStruct((channels, 128), F32),
        ],
        grad_own, k_own, v_own, shifted, tap_row, kernel_row, skip_row,
    )
    grad_keys, grad_values = to_rows([grad_k_own, grad_v_own], 7)
    grad_values = (grad_values.astype(F32) * live_lane).astype(BF16)
    grad_decay_log, grad_turn_angle, grad_mix_real, grad_mix_imag = kernel_pull(
        kernel_grad[:, : rows * blocks]
    )
    grad_shift_taps = taps_grad[:, : shift_taps.shape[1]]
    grad_skip_gain = skip_grad[:, 0]

    grad_query_one = product_sum(normed_one, grad_queries)
    grad_key_one = contract(normed_one, grad_keys, 0, 1)
    grad_value_one = contract(normed_one, grad_values, 0, 1)
    grad_normed_one = (
        product_back(grad_queries, query_all)
        + contract(grad_keys, key_all, 0, 1)
        + contract(grad_values, value_all, 0, 1)
    )
    grad_from_one, grad_norm_one = jax.vjp(layer_norm, residual_zero, gain_one)[1](
        grad_normed_one
    )
    input_grad = grad_one + grad_from_one

    gain_grads = jnp.stack([grad_norm_one, grad_norm_two, grad_norm_three, grad_norm_four])
    gain_grads = gain_grads.reshape(4, devices, channels).transpose(1, 0, 2)
    gain_grads = jnp.pad(gain_grads, ((0, 0), (0, 4), (0, 128 - channels)))

    def owned(grad):
        return grad.astype(BF16).reshape(devices, -1, grad.shape[1])

    sums = reduce_all(
        [gain_grads]
        + [
            owned(g)
            for g in (
                grad_up_one, grad_down_one, grad_qkv_weight, grad_out_two, grad_out_one,
                grad_query_one, grad_key_one, grad_value_one,
            )
        ],
        8,
    )
    gain_grads, grad_up_one, grad_down_one, grad_qkv_weight, grad_out_two, grad_out_one = sums[:6]
    grad_query_one, grad_key_one, grad_value_one = sums[6:]
    gain_grads = gain_grads[:4, :channels]
    return (
        activations[None], input_grad[None],
        gain_grads[0], grad_query_one, grad_key_one, grad_value_one,
        grad_shift_taps, grad_decay_log, grad_turn_angle, grad_mix_real, grad_mix_imag,
        grad_skip_gain, grad_out_one,
        gain_grads[1], grad_up_one, grad_down_one,
        gain_grads[2], grad_qkv_weight, grad_out_two,
        gain_grads[3], grad_up_two, grad_down_two,
    )


def solution(mesh):
    row, vector = P(BOTH, None), P(BOTH)
    whole = P("dp", "seq", None)
    weights = (
        vector, row, row, row, row, row, row, row, row, vector, row,
        vector, row, row, vector, row, row, vector, row, row,
    )
    return jax.shard_map(
        shards,
        mesh=mesh,
        in_specs=(whole, P("dp")) + weights + (whole,),
        out_specs=(whole, whole) + weights,
        check_vma=False,
    )
```

```python
from functools import partial

import jax
import jax.numpy as jnp
from jax import lax
from jax.experimental import pallas as pl
from jax.experimental.pallas import tpu as pltpu
from jax.sharding import PartitionSpec as P

HEADS = 12
HDIM = 64
EPSILON = 1e-05
HIGHEST = lax.Precision.HIGHEST
MASKED = -1e30
BOTH = ("seq", "dp")
MESH = pl.DeviceIdType.MESH
MIB = 1024 * 1024
F32 = jnp.float32
BF16 = jnp.bfloat16


def grouped():
    return lax.axis_size("seq") == 4 and lax.axis_size("dp") == 8


def coordinates():
    seq, dp = lax.axis_index("seq"), lax.axis_index("dp")
    return seq // 2, seq % 2, dp // 2, dp % 2


def slot_of(y, c, z, x):
    return (y * 2 + c) * 8 + z * 2 + x


def device_of(y, c, z, x):
    return (y * 2 + c, z * 2 + x)


def greet(peers):
    barrier = pltpu.get_barrier_semaphore()
    for peer in peers:
        pl.semaphore_signal(barrier, inc=1, device_id=peer, device_id_type=MESH)
    pl.semaphore_wait(barrier, len(peers))


def six_peers(y, c, z, x):
    return [device_of(y, c, (z + k) % 4, x) for k in (1, 2, 3)] + [
        device_of(y, c, z, 1 - x),
        device_of(1 - y, c, z, x),
        device_of(y, 1 - c, z, x),
    ]


class Gather:
    def __init__(self, parts, sources, gathered, local_sem, send_sem, recv_sem, ahead=4):
        self.parts, self.sources, self.gathered = parts, sources, gathered
        self.send_sem, self.recv_sem, self.ahead = send_sem, recv_sem, ahead
        self.y, self.c, self.z, self.x = y, c, z, x = coordinates()
        self.me = slot_of(y, c, z, x)
        self.across_x = device_of(y, c, z, 1 - x)
        self.across_y = device_of(1 - y, c, z, x)
        self.other_core = device_of(y, 1 - c, z, x)
        self.own = [
            pltpu.make_async_copy(sources[i], gathered[i].at[self.me], local_sem.at[i])
            for i in range(len(sources))
        ]
        self.done = 0

    def place(self, p, slot):
        i, row, rows, column, columns, _ = self.parts[p]
        return self.gathered[i].at[slot, pl.ds(row, rows), pl.ds(column, columns)]

    def send(self, p, slot, target, first=False):
        i, row, rows, column, columns, _ = self.parts[p]
        source = self.sources[i].at[pl.ds(row, rows), pl.ds(column, columns)]
        pltpu.make_async_remote_copy(
            src_ref=source if first else self.place(p, slot),
            dst_ref=self.place(p, slot),
            send_sem=self.send_sem.at[p],
            recv_sem=self.recv_sem.at[p, slot],
            device_id=target,
            device_id_type=MESH,
        ).start()

    def arrived(self, p, slot):
        place = self.place(p, slot)
        pltpu.make_async_copy(place, place, self.recv_sem.at[p, slot]).wait()

    def first(self, p):
        for k in (1, 3, 2):
            self.send(p, self.me, device_of(self.y, self.c, (self.z + k) % 4, self.x), True)
        self.send(p, self.me, self.across_x, True)
        self.send(p, self.me, self.across_y, True)
        self.send(p, self.me, self.other_core, True)

    def start(self):
        for copy in self.own:
            copy.start()
        for p in range(min(self.ahead, len(self.parts))):
            self.first(p)

    def after_z(self, p):
        for k in (3, 1, 2):
            slot = slot_of(self.y, self.c, (self.z + k) % 4, self.x)
            self.arrived(p, slot)
            self.send(p, slot, self.across_x)
            self.send(p, slot, self.across_y)
            self.send(p, slot, self.other_core)

    def after_first(self, p):
        x_first = self.parts[p][5]
        for k in (0, 3, 1, 2):
            by_x = slot_of(self.y, self.c, (self.z + k) % 4, 1 - self.x)
            by_y = slot_of(1 - self.y, self.c, (self.z + k) % 4, self.x)
            self.arrived(p, by_x)
            if x_first:
                self.send(p, by_x, self.across_y)
            self.send(p, by_x, self.other_core)
            self.arrived(p, by_y)
            if not x_first:
                self.send(p, by_y, self.across_x)
            self.send(p, by_y, self.other_core)

    def after_second(self, p):
        for k in (0, 3, 1, 2):
            slot = slot_of(1 - self.y, self.c, (self.z + k) % 4, 1 - self.x)
            self.arrived(p, slot)
            self.send(p, slot, self.other_core)

    def whole(self, p):
        for side in (0, 1):
            for zz in range(4):
                for xx in (0, 1):
                    self.arrived(p, slot_of(side, 1 - self.c, zz, xx))

    def steps(self):
        return len(self.parts) + 3

    def run(self, until):
        while self.done < min(until, self.steps()):
            s, count = self.done, len(self.parts)
            if self.ahead <= s + self.ahead < count:
                self.first(s + self.ahead)
            for stage, act in enumerate(
                (self.after_z, self.after_first, self.after_second, self.whole)
            ):
                if 0 <= s - stage < count:
                    act(s - stage)
            self.done += 1

    def own_arrived(self, indices):
        for i in indices:
            self.own[i].wait()

    def finish(self):
        self.run(self.steps())
        for p, (i, row, rows, column, columns, _) in enumerate(self.parts):
            sent = self.gathered[i].at[pl.ds(0, 31), pl.ds(row, rows), pl.ds(column, columns)]
            pltpu.make_async_copy(sent, sent, self.send_sem.at[p]).wait()


def cut(arrays):
    parts = []
    for i, (rows, columns) in enumerate(arrays):
        if columns > 1536:
            width = 1536 if columns % 1536 == 0 else 768
            pieces = [(0, rows, w, width) for w in range(0, columns, width)]
        elif rows > 48:
            pieces = [(r, 48, 0, columns) for r in range(0, rows, 48)]
        else:
            pieces = [(0, rows, 0, columns)]
        for piece in pieces:
            parts.append((i,) + piece + (len(parts) % 2 == 0,))
    return parts


def reduce_body(parts, count, *refs):
    terms, totals = refs[:count], refs[count : 2 * count]
    buffers = refs[2 * count : 2 * count + 4 * len(parts)]
    send_sem, recv_sem = refs[2 * count + 4 * len(parts) :]
    y, c, z, x = coordinates()
    greet(six_peers(y, c, z, x))

    def term(p, core):
        i, row, rows, column, columns, _ = parts[p]
        return terms[i].at[:, core, :, :, pl.ds(row, rows), pl.ds(column, columns)]

    def copies(p, stage):
        one, two, three, four = buffers[4 * p : 4 * p + 4]
        x_last = parts[p][5]
        if stage == 0:
            pairs = [(term(p, 1 - c), one, device_of(y, 1 - c, z, x))]
        elif stage == 1 and x_last:
            pairs = [(one.at[1 - y], two, device_of(1 - y, c, z, x))]
        elif stage == 1:
            pairs = [(one.at[:, :, 1 - x], two, device_of(y, c, z, 1 - x))]
        elif stage == 2 and x_last:
            pairs = [(two.at[:, 1 - x], three, device_of(y, c, z, 1 - x))]
        elif stage == 2:
            pairs = [(two.at[1 - y], three, device_of(1 - y, c, z, x))]
        else:
            pairs = [
                (three.at[(z + k) % 4], four.at[k - 1], device_of(y, c, (z + k) % 4, x))
                for k in (1, 2, 3)
            ]
        return [
            pltpu.make_async_remote_copy(
                src_ref=src,
                dst_ref=dst,
                send_sem=send_sem.at[p, stage + n],
                recv_sem=recv_sem.at[p, stage + n],
                device_id=target,
                device_id_type=MESH,
            )
            for n, (src, dst, target) in enumerate(pairs)
        ]

    def add(p, stage):
        one, two, three, four = buffers[4 * p : 4 * p + 4]
        i, row, rows, column, columns, x_last = parts[p]
        total = lambda a, b: (a.astype(F32) + b.astype(F32)).astype(one.dtype)
        if stage == 0:

            def add_one(k, _):
                b, zz = k // 4, k % 4
                for xx in (0, 1):
                    mine = terms[i][b, c, zz, xx, pl.ds(row, rows), pl.ds(column, columns)]
                    one[b, zz, xx] = total(one[b, zz, xx], mine)
                return 0

            lax.fori_loop(0, 8, add_one, 0)
        elif stage == 1:

            def add_two(k, _):
                for h in (0, 1):
                    mine = one[y, k, h] if x_last else one[h, k, x]
                    if x_last:
                        two[k, h] = total(two[k, h], mine)
                    else:
                        two[h, k] = total(two[h, k], mine)
                return 0

            lax.fori_loop(0, 4, add_two, 0)
        elif stage == 2:

            def add_three(k, _):
                mine = two[k, x] if x_last else two[y, k]
                three[k] = total(three[k], mine)
                return 0

            lax.fori_loop(0, 4, add_three, 0)
        else:
            totals[i][pl.ds(row, rows), pl.ds(column, columns)] = (
                three[z].astype(F32)
                + four[0].astype(F32)
                + four[1].astype(F32)
                + four[2].astype(F32)
            )

    for p in range(len(parts)):
        for copy in copies(p, 0):
            copy.start()
    for step in range(len(parts) + 3):
        for stage in range(4):
            p = step - stage
            if 0 <= p < len(parts):
                for copy in copies(p, stage):
                    copy.wait_recv()
                add(p, stage)
                if stage < 3:
                    for copy in copies(p, stage + 1):
                        copy.start()
    for p in range(len(parts)):
        for stage in range(4):
            for copy in copies(p, stage):
                copy.wait_send()


def reduce_all(arrays, collective_id):
    if not grouped():
        return [
            lax.psum_scatter(a, BOTH, scatter_dimension=0, tiled=False).astype(F32)
            for a in arrays
        ]
    count = len(arrays)
    parts = cut([a.shape[1:] for a in arrays])
    scratch = []
    for i, _, rows, _, columns, x_last in parts:
        kind = arrays[i].dtype
        scratch += [
            pltpu.VMEM((2, 4, 2, rows, columns), kind),
            pltpu.VMEM(((4, 2) if x_last else (2, 4)) + (rows, columns), kind),
            pltpu.VMEM((4, rows, columns), kind),
            pltpu.VMEM((3, rows, columns), kind),
        ]
    return pl.pallas_call(
        partial(reduce_body, parts, count),
        out_shape=[jax.ShapeDtypeStruct(a.shape[1:], F32) for a in arrays],
        in_specs=[pl.BlockSpec(memory_space=pltpu.VMEM)] * count,
        out_specs=[pl.BlockSpec(memory_space=pltpu.VMEM)] * count,
        scratch_shapes=scratch
        + [
            pltpu.SemaphoreType.DMA((len(parts), 6)),
            pltpu.SemaphoreType.DMA((len(parts), 6)),
        ],
        compiler_params=pltpu.CompilerParams(
            collective_id=collective_id, has_side_effects=True, vmem_limit_bytes=58 * MIB
        ),
    )(*[a.reshape((2, 2, 4, 2) + a.shape[1:]) for a in arrays])


def all_others():
    rows, groups = lax.axis_size("seq"), lax.axis_size("dp")
    count = rows * groups
    me = lax.axis_index("seq") * groups + lax.axis_index("dp")
    others = [lax.rem(me + k, count) for k in range(1, count)]
    return me, others, [(o // groups, lax.rem(o, groups)) for o in others]


class Swap:
    def __init__(self, src, dst, send_sem, recv_sem):
        self.src, self.dst, self.send_sem, self.recv_sem = src, dst, send_sem, recv_sem

    def start(self):
        me, others, places = all_others()
        for o, place in zip(others, places):
            pltpu.make_async_remote_copy(
                src_ref=self.src.at[o],
                dst_ref=self.dst.at[me],
                send_sem=self.send_sem,
                recv_sem=self.recv_sem,
                device_id=place,
                device_id_type=MESH,
            ).start()

    def wait(self):
        most = pl.ds(0, self.src.shape[0] - 1)
        me = all_others()[0]
        pltpu.make_async_copy(self.src.at[most], self.dst.at[most], self.recv_sem).wait()
        pltpu.make_async_copy(self.src.at[most], self.dst.at[most], self.send_sem).wait()
        self.dst[me] = self.src[me]


def swap_body(src, dst, send_sem, recv_sem):
    greet(all_others()[2])
    swap = Swap(src, dst, send_sem, recv_sem)
    swap.start()
    swap.wait()


def swap_all(value, collective_id):
    if not grouped():
        return lax.all_to_all(value, BOTH, 0, 0, tiled=True)
    return pl.pallas_call(
        swap_body,
        out_shape=jax.ShapeDtypeStruct(value.shape, value.dtype),
        in_specs=[pl.BlockSpec(memory_space=pltpu.VMEM)],
        out_specs=pl.BlockSpec(memory_space=pltpu.VMEM),
        scratch_shapes=[pltpu.SemaphoreType.DMA(())] * 2,
        compiler_params=pltpu.CompilerParams(
            collective_id=collective_id, has_side_effects=True
        ),
    )(value)


def line_body(src, dst, local_sem, send_sem, recv_sem):
    y, c, z, x = coordinates()
    me, mate, far, last = y * 2 + c, y * 2 + 1 - c, (1 - y) * 2 + c, (1 - y) * 2 + 1 - c
    own = pltpu.make_async_copy(src, dst.at[me], local_sem)
    own.start()
    core, side = device_of(y, 1 - c, z, x), device_of(1 - y, c, z, x)
    greet([core, side])

    def copy(n, source, slot, target):
        return pltpu.make_async_remote_copy(
            src_ref=source,
            dst_ref=dst.at[slot],
            send_sem=send_sem.at[n],
            recv_sem=recv_sem.at[n],
            device_id=target,
            device_id_type=MESH,
        )

    first = copy(0, src, me, side)
    second = copy(1, src, me, core)
    third = copy(2, dst.at[far], far, core)
    first.start()
    second.start()
    first.wait_recv()
    third.start()
    second.wait_recv()
    third.wait_recv()
    for each in (first, second, third):
        each.wait_send()
    own.wait()


def gather_line(value, collective_id):
    if not grouped():
        return lax.all_gather(value, "seq", axis=0)
    return pl.pallas_call(
        line_body,
        out_shape=jax.ShapeDtypeStruct((4,) + value.shape, value.dtype),
        in_specs=[pl.BlockSpec(memory_space=pltpu.VMEM)],
        out_specs=pl.BlockSpec(memory_space=pltpu.VMEM),
        scratch_shapes=[
            pltpu.SemaphoreType.DMA(()),
            pltpu.SemaphoreType.DMA((3,)),
            pltpu.SemaphoreType.DMA((3,)),
        ],
        compiler_params=pltpu.CompilerParams(
            collective_id=collective_id, has_side_effects=True
        ),
    )(value)


def line_sum_body(src, dst, one, two, send_sem, recv_sem):
    y, c, z, x = coordinates()
    core, side = device_of(y, 1 - c, z, x), device_of(1 - y, c, z, x)
    greet([core, side])

    def copy(n, source, target, where):
        return pltpu.make_async_remote_copy(
            src_ref=source,
            dst_ref=where,
            send_sem=send_sem.at[n],
            recv_sem=recv_sem.at[n],
            device_id=target,
            device_id_type=MESH,
        )

    far = copy(0, src.at[1 - y, 1 - c], core, one.at[1 - y])
    near = copy(1, src.at[y, 1 - c], core, one.at[y])
    far.start()
    near.start()
    far.wait_recv()
    one[1 - y] = (one[1 - y].astype(F32) + src[1 - y, c].astype(F32)).astype(one.dtype)
    onward = copy(2, one.at[1 - y], side, two)
    onward.start()
    near.wait_recv()
    onward.wait_recv()
    dst[...] = (one[y].astype(F32) + src[y, c].astype(F32)) + two[...].astype(F32)
    for each in (far, near, onward):
        each.wait_send()


def sum_line(value, collective_id):
    if not grouped():
        return lax.psum_scatter(value, "seq", scatter_dimension=0).astype(F32)
    return pl.pallas_call(
        line_sum_body,
        out_shape=jax.ShapeDtypeStruct(value.shape[1:], F32),
        in_specs=[pl.BlockSpec(memory_space=pltpu.VMEM)],
        out_specs=pl.BlockSpec(memory_space=pltpu.VMEM),
        scratch_shapes=[
            pltpu.VMEM((2,) + value.shape[1:], value.dtype),
            pltpu.VMEM(value.shape[1:], value.dtype),
            pltpu.SemaphoreType.DMA((3,)),
            pltpu.SemaphoreType.DMA((3,)),
        ],
        compiler_params=pltpu.CompilerParams(
            collective_id=collective_id, has_side_effects=True, vmem_limit_bytes=32 * MIB
        ),
    )(value.reshape((2, 2) + value.shape[1:]))


def layer_norm(residual, scale_gain):
    average = jnp.mean(residual, axis=-1, keepdims=True)
    centered = residual - average
    variance = jnp.mean(centered * centered, axis=-1, keepdims=True)
    return centered * lax.rsqrt(variance + EPSILON) * scale_gain


def contract(left_side, right_side, left_dim, right_dim):
    return lax.dot_general(
        left_side,
        right_side,
        (((left_dim,), (right_dim,)), ((), ())),
        preferred_element_type=F32,
    )


def product(left_side, right_side):
    return contract(left_side, right_side, 1, 0)


def product_back(left_side, right_side):
    return contract(left_side, right_side, 1, 1)


def product_sum(left_side, right_side):
    return contract(left_side, right_side, 0, 0)


def feed_forward(residual, scale_gain, up_weight, down_weight):
    normed = layer_norm(residual, scale_gain).astype(BF16)
    pre_act = product(normed, up_weight)
    activated = jax.nn.gelu(pre_act).astype(BF16)
    return (residual + product(activated, down_weight), (normed, pre_act, activated))


def feed_back(residual, scale_gain, up_weight, down_weight, stored, grad_residual):
    normed, pre_act, activated = stored
    grad_branch = grad_residual.astype(BF16)
    grad_down = product_sum(activated, grad_branch)
    grad_activated = product_back(grad_branch, down_weight)
    gelu_pull = jax.vjp(jax.nn.gelu, pre_act)[1]
    grad_pre = gelu_pull(grad_activated)[0].astype(BF16)
    grad_up = product_sum(normed, grad_pre)
    grad_normed = product_back(grad_pre, up_weight)
    norm_pull = jax.vjp(layer_norm, residual, scale_gain)[1]
    grad_input, grad_gain = norm_pull(grad_normed)
    return (grad_residual + grad_input, grad_gain, grad_up, grad_down)


def ssm_kernel(decay_log, turn_angle, mix_real, mix_imag, length):
    rate = jnp.exp(decay_log)[:, :, None]
    angle = turn_angle[:, :, None]
    step = 32

    def powers(times):
        return (
            jnp.exp(-times * rate) * jnp.cos(times * angle),
            jnp.exp(-times * rate) * jnp.sin(times * angle),
        )

    low_real, low_imag = powers(jnp.arange(step, dtype=F32)[None, None])
    high_real, high_imag = powers(
        (step * jnp.arange(length // step, dtype=jnp.int32)).astype(F32)[None, None]
    )
    real, imag = mix_real[:, :, None], mix_imag[:, :, None]
    high = jnp.concatenate(
        [real * high_real - imag * high_imag, -(real * high_imag + imag * high_real)], axis=1
    )
    low = jnp.concatenate([low_real, low_imag], axis=1)
    kernel = jnp.einsum("cna,cnb->cab", high, low, precision=HIGHEST)
    return kernel.reshape(decay_log.shape[0], length)


def toeplitz(row, rows):
    spread = jnp.broadcast_to(row, (rows, row.shape[1]))
    return pltpu.roll(spread, 0, 1, stride=1, stride_axis=0)


def block_sum(mixed, blocks, groups, rows):
    total = mixed[:, :rows]
    for d in range(1, blocks):
        piece = mixed[: (blocks - d) * groups, d * rows : (d + 1) * rows]
        total = total + jnp.concatenate(
            [jnp.zeros((d * groups, rows), piece.dtype), piece], axis=0
        )
    return total


def block_spread(value, blocks, lags, groups, rows):
    pieces = [value]
    for d in range(1, lags):
        pieces.append(
            jnp.concatenate(
                [value[d * groups :], jnp.zeros((d * groups, rows), value.dtype)], axis=0
            )
        )
    return jnp.concatenate(pieces, axis=1)


def mix(blocks, groups, rows, keys, values, tap_row, kernel_row, skip):
    span = blocks * rows
    taps = toeplitz(tap_row, rows)[:, : 2 * rows].astype(BF16)
    longer = toeplitz(kernel_row, rows)[:, :span].astype(BF16)
    near = product(keys, taps)
    shifted = near[:, :rows] + jnp.concatenate(
        [jnp.zeros((groups, rows), F32), near[: (blocks - 1) * groups, rows:]], axis=0
    )
    signal = shifted * values.astype(F32)
    mixed = product(signal.astype(BF16), longer)
    return shifted, block_sum(mixed, blocks, groups, rows) + skip * signal


def mixer_body(blocks, groups, rows, k_ref, v_ref, taps_ref, kernel_ref, skip_ref, shifted_ref, out_ref):
    for ch in range(k_ref.shape[0]):
        row = slice(ch, ch + 1)
        shifted_ref[ch], out = mix(
            blocks, groups, rows, k_ref[ch], v_ref[ch],
            taps_ref[row, :], kernel_ref[row, :], skip_ref[row, :1],
        )
        out_ref[ch] = out.astype(BF16)


def flat_weight(ref):
    wide = ref[...].astype(F32)
    return wide.reshape(wide.shape[0] * wide.shape[1], wide.shape[2]).astype(BF16)


def first_body(
    parts, count, *refs,
):
    sources = refs[:count]
    tokens, live, taps_ref, kernel_ref, skip_ref = refs[count : count + 5]
    refs = refs[count + 5 :]
    gathered = refs[:count]
    (
        residual_ref, standard_ref, inverse_ref, normed_ref, queries_ref, ssm_ref, gated_ref,
        k_ref, v_ref, shifted_ref,
    ) = refs[count : count + 10]
    (
        wide, sent_kv, came_kv, sent_y, came_y,
        local_sem, send_sem, recv_sem, swap_sem,
    ) = refs[count + 10 :]
    gains, key_all, value_all, query_all, out_all = gathered[:5]
    devices, channels = key_all.shape[0], key_all.shape[1]
    rows, features = tokens.shape
    blocks, groups = lax.axis_size("seq"), lax.axis_size("dp")
    greet(all_others()[2])
    gather = Gather(parts, sources, gathered, local_sem, send_sem, recv_sem)
    gather.start()

    turned = tokens[...].astype(F32).T
    centered = turned - jnp.mean(turned, axis=0, keepdims=True)
    inverse = lax.rsqrt(jnp.mean(centered * centered, axis=0, keepdims=True) + EPSILON)
    inverse_ref[...] = jnp.broadcast_to(inverse, inverse_ref.shape)
    standard_ref[...] = centered * inverse

    gather.run(8)
    gather.own_arrived(range(5))
    gain = gains[...].reshape(features, 128)[:, :1]
    normed_ref[...] = (standard_ref[...] * gain).astype(BF16)

    def projected(weight):
        return contract(flat_weight(weight), normed_ref[...], 0, 0)

    wide[:, :channels, :] = projected(key_all).reshape(devices, channels, rows)
    wide[:, channels:, :] = (projected(value_all) * live[...]).reshape(devices, channels, rows)
    sent_kv[...] = wide[...].astype(BF16)
    over = Swap(sent_kv, came_kv, swap_sem.at[0], swap_sem.at[1])
    over.start()
    queries_ref[...] = projected(query_all)
    gather.run(11)
    over.wait()
    wide[...] = came_kv[...].astype(F32)
    for ch in range(channels):
        row = slice(ch, ch + 1)
        k_ref[ch] = wide[:, ch, :].astype(BF16)
        v_ref[ch] = wide[:, channels + ch, :].astype(BF16)
        shifted_ref[ch], out = mix(
            blocks, groups, rows, k_ref[ch], v_ref[ch],
            taps_ref[row, :], kernel_ref[row, :], skip_ref[row, :1],
        )
        wide[:, ch, :] = out
        if ch == channels // 2:
            gather.run(12)
    sent_y[...] = wide[:, :channels, :].astype(BF16)
    back = Swap(sent_y, came_y, swap_sem.at[2], swap_sem.at[3])
    back.start()
    gather.run(14)
    back.wait()
    ssm = came_y[...].astype(F32).reshape(features, rows)
    ssm_ref[...] = ssm.astype(BF16)
    gated_ref[...] = (queries_ref[...] * ssm).astype(BF16)
    residual_ref[...] = tokens[...].astype(F32) + contract(
        gated_ref[...], flat_weight(out_all), 0, 0
    )
    gather.own_arrived(range(5, count))
    gather.finish()


def first_layer(weights, tokens, live, tap_row, kernel_row, skip_row, collective_id):
    count = len(weights)
    blocks, groups = lax.axis_size("seq"), lax.axis_size("dp")
    devices = blocks * groups
    rows, features = tokens.shape
    channels = features // devices
    parts = cut([a.shape for a in weights])
    vmem, anywhere = pl.BlockSpec(memory_space=pltpu.VMEM), pl.BlockSpec(memory_space=pl.ANY)
    turned = (features, rows)
    per_channel = (channels, devices, rows)
    results = [
        ((rows, features), F32), (turned, F32), ((8, rows), F32), (turned, BF16), (turned, F32),
        (turned, BF16), (turned, BF16), (per_channel, BF16), (per_channel, BF16), (per_channel, F32),
    ]
    out = pl.pallas_call(
        partial(first_body, parts, count),
        out_shape=[jax.ShapeDtypeStruct((devices,) + a.shape, a.dtype) for a in weights]
        + [jax.ShapeDtypeStruct(*r) for r in results],
        in_specs=[anywhere] * count + [vmem] * 5,
        out_specs=[vmem] * 5 + [anywhere] * (count - 5) + [vmem] * len(results),
        scratch_shapes=[
            pltpu.VMEM((devices, 2 * channels, rows), F32),
            pltpu.VMEM((devices, 2 * channels, rows), BF16),
            pltpu.VMEM((devices, 2 * channels, rows), BF16),
            pltpu.VMEM((devices, channels, rows), BF16),
            pltpu.VMEM((devices, channels, rows), BF16),
            pltpu.SemaphoreType.DMA((count,)),
            pltpu.SemaphoreType.DMA((len(parts),)),
            pltpu.SemaphoreType.DMA((len(parts), devices)),
            pltpu.SemaphoreType.DMA((4,)),
        ],
        compiler_params=pltpu.CompilerParams(
            collective_id=collective_id, has_side_effects=True, vmem_limit_bytes=48 * MIB
        ),
    )(*weights, tokens, live, tap_row, kernel_row, skip_row)
    return out[:count], out[count:]


def first_layer_apart(weights, tokens, live, tap_row, kernel_row, skip_row):
    blocks, groups = lax.axis_size("seq"), lax.axis_size("dp")
    devices = blocks * groups
    rows, features = tokens.shape
    channels = features // devices
    every = [lax.all_gather(a, BOTH, axis=0) for a in weights]
    gain = every[0][:, :, 0].reshape(features, 1)
    key_all, value_all, query_all, out_all = [a.reshape(features, -1) for a in every[1:5]]
    turned = tokens.astype(F32).T
    centered = turned - jnp.mean(turned, axis=0, keepdims=True)
    inverse = lax.rsqrt(jnp.mean(centered * centered, axis=0, keepdims=True) + EPSILON)
    standard = centered * inverse
    normed = (standard * gain).astype(BF16)
    queries = contract(query_all, normed, 0, 0)
    keys = contract(key_all, normed, 0, 0).astype(BF16)
    values = (contract(value_all, normed, 0, 0) * live).astype(BF16)
    sent = jnp.stack([a.reshape(devices, channels, rows) for a in (keys, values)], axis=1)
    k_own, v_own = lax.all_to_all(sent, BOTH, 0, 0, tiled=True).transpose(1, 2, 0, 3)
    per_channel = (channels, devices, rows)
    shifted, mixed = local_call(
        partial(mixer_body, blocks, groups, rows),
        [jax.ShapeDtypeStruct(per_channel, F32), jax.ShapeDtypeStruct(per_channel, BF16)],
        k_own, v_own, tap_row, kernel_row, skip_row,
    )
    ssm = lax.all_to_all(mixed.transpose(1, 0, 2), BOTH, 0, 0, tiled=True)
    ssm = ssm.reshape(features, rows)
    gated = (queries * ssm.astype(F32)).astype(BF16)
    residual = tokens.astype(F32) + contract(gated, out_all, 0, 0)
    inverse = jnp.broadcast_to(inverse, (8, rows))
    return every, [residual, standard, inverse, normed, queries, ssm, gated, k_own, v_own, shifted]


def mixer_back_body(
    blocks, groups, rows,
    grad_ref, k_ref, v_ref, shifted_ref, taps_ref, kernel_ref, skip_ref,
    grad_k_ref, grad_v_ref, kernel_grad_ref, taps_grad_ref, skip_grad_ref,
):
    channels = k_ref.shape[0]
    span = blocks * rows
    wide, narrow = kernel_ref.shape[1], taps_ref.shape[1]
    turned = (
        lax.broadcasted_iota(jnp.int32, (rows, rows), 0)
        + lax.broadcasted_iota(jnp.int32, (rows, rows), 1)
        == rows - 1
    ).astype(BF16)

    def lag_sums(earlier, spread, lanes):
        backward = product(earlier, turned).astype(BF16)
        pairs = product_sum(backward, spread)
        padded = jnp.concatenate(
            [pairs, jnp.zeros((rows, lanes - pairs.shape[1]), F32)], axis=1
        )
        return jnp.sum(
            pltpu.roll(padded, lanes - rows + 1, 1, stride=1, stride_axis=0),
            axis=0,
            keepdims=True,
        )

    for ch in range(channels):
        taps = toeplitz(taps_ref[ch : ch + 1, :], rows)[:, : 2 * rows].astype(BF16)
        longer = toeplitz(kernel_ref[ch : ch + 1, :], rows)[:, :span].astype(BF16)
        out_grad = grad_ref[ch]
        skip = skip_ref[ch : ch + 1, :1]
        values = v_ref[ch].astype(F32)
        shifted = shifted_ref[ch]
        signal = shifted * values
        wide_grad = out_grad.astype(F32)
        later = block_spread(wide_grad, blocks, blocks, groups, rows).astype(BF16)
        signal_grad = product_back(later, longer) + skip * wide_grad
        kernel_grad_ref[ch : ch + 1, :] = lag_sums(signal.astype(BF16), later, wide)
        skip_grad_ref[ch : ch + 1, :] = jnp.broadcast_to(
            jnp.sum(jnp.sum(signal * wide_grad, axis=0, keepdims=True), axis=1, keepdims=True),
            (1, 128),
        )
        shifted_grad = values * signal_grad
        grad_v_ref[ch] = (shifted * signal_grad).astype(BF16)
        next_two = block_spread(shifted_grad, blocks, 2, groups, rows).astype(BF16)
        grad_k_ref[ch] = product_back(next_two, taps).astype(BF16)
        taps_grad_ref[ch : ch + 1, :] = lag_sums(k_ref[ch], next_two, narrow)


def allowed_keys(place, length, rows, keys):
    row_places = place * rows + lax.broadcasted_iota(jnp.int32, (rows, keys), 0)
    key_places = lax.broadcasted_iota(jnp.int32, (rows, keys), 1)
    return (key_places <= row_places) & (key_places < length)


def attend_body(where_ref, q_ref, kv_ref, out_ref, log_ref):
    rows, features = q_ref.shape
    keys = kv_ref.shape[0]
    allowed = allowed_keys(where_ref[0], where_ref[1], rows, keys)
    for head in range(HEADS):
        own = slice(head * HDIM, (head + 1) * HDIM)
        values = slice(features + head * HDIM, features + (head + 1) * HDIM)
        scores = product_back(q_ref[:, own], kv_ref[:, own]) * HDIM ** (-0.5)
        scores = jnp.where(allowed, scores, MASKED)
        most = jnp.max(scores, axis=1, keepdims=True)
        powers = jnp.exp(scores - most)
        total = jnp.sum(powers, axis=1, keepdims=True)
        weights = (powers * (1.0 / total)).astype(BF16)
        out_ref[:, own] = product(weights, kv_ref[:, values]).astype(BF16)
        log_ref[:, head : head + 1] = most + jnp.log(total)


def attend_back_body(where_ref, q_ref, kv_ref, log_ref, grad_ref, grad_q_ref, grad_kv_ref):
    rows, features = q_ref.shape
    keys = kv_ref.shape[0]
    allowed = allowed_keys(where_ref[0], where_ref[1], rows, keys)
    scale = HDIM ** (-0.5)
    for head in range(HEADS):
        own = slice(head * HDIM, (head + 1) * HDIM)
        values = slice(features + head * HDIM, features + (head + 1) * HDIM)
        queries, grads = q_ref[:, own], grad_ref[:, own]
        scores = product_back(queries, kv_ref[:, own]) * scale
        probs = jnp.where(allowed, jnp.exp(scores - log_ref[:, head : head + 1]), 0.0)
        prob_grad = product_back(grads, kv_ref[:, values])
        delta = jnp.sum(probs * prob_grad, axis=1, keepdims=True)
        grad_scores = (probs * (prob_grad - delta)).astype(BF16)
        grad_q_ref[:, own] = (product(grad_scores, kv_ref[:, own]) * scale).astype(BF16)
        grad_kv_ref[:, own] = (product_sum(grad_scores, queries) * scale).astype(BF16)
        grad_kv_ref[:, values] = product_sum(probs.astype(BF16), grads).astype(BF16)


def local_call(body, out_shape, *operands, scalars=0, limit=48):
    vmem = pl.BlockSpec(memory_space=pltpu.VMEM)
    smem = pl.BlockSpec(memory_space=pltpu.SMEM)
    return pl.pallas_call(
        body,
        out_shape=out_shape,
        in_specs=[smem] * scalars + [vmem] * (len(operands) - scalars),
        out_specs=jax.tree.map(lambda _: vmem, out_shape),
        compiler_params=pltpu.CompilerParams(vmem_limit_bytes=limit * MIB),
    )(*operands)


def shards(
    tokens, lengths, norm_one, query_one, key_one, value_one, shift_taps, decay_log,
    turn_angle, mix_real, mix_imag, skip_gain, out_one, norm_two, up_one, down_one,
    norm_three, qkv_weight, out_two, norm_four, up_two, down_two, cotangent,
):
    blocks, groups = lax.axis_size("seq"), lax.axis_size("dp")
    devices = blocks * groups
    rows, features = tokens.shape[1], tokens.shape[2]
    channels = features // devices
    place = lax.axis_index("seq")
    length = lengths[0]
    row_places = place * rows + jnp.arange(rows, dtype=jnp.int32)
    live_mask = (row_places < length).astype(F32)[:, None]
    live_lane = (row_places < length).astype(F32)[None, :]

    kernel, kernel_pull = jax.vjp(
        partial(ssm_kernel, length=rows * blocks),
        *[a.astype(F32) for a in (decay_log, turn_angle, mix_real, mix_imag)],
    )
    wide = -(-(blocks + 1) * rows // 128) * 128
    kernel_row = jnp.pad(kernel, ((0, 0), (0, wide - kernel.shape[1])))
    narrow = -(-3 * rows // 128) * 128
    tap_row = jnp.pad(
        shift_taps.astype(F32), ((0, 0), (0, narrow - shift_taps.shape[1]))
    )
    skip_row = jnp.broadcast_to(skip_gain.astype(F32)[:, None], (channels, 128))

    gains = jnp.stack([norm_one, norm_two, norm_three, norm_four], axis=1).astype(F32)
    gains = jnp.pad(gains, ((0, 0), (0, 124)))
    weights = [
        gains, key_one, value_one, query_one, out_one, up_one, down_one, qkv_weight, out_two,
        up_two, down_two,
    ]
    mixer_rows = (tap_row, kernel_row, skip_row)
    if grouped():
        every, kept = first_layer(weights, tokens[0], live_lane, *mixer_rows, 1)
    else:
        every, kept = first_layer_apart(weights, tokens[0], live_lane, *mixer_rows)
    residual_one, standard, inverse, normed_turned, queries, ssm_out, gated, k_own, v_own, shifted = kept
    gain_one, gain_two, gain_three, gain_four = [
        every[0][:, :, n].reshape(features) for n in range(4)
    ]
    (
        key_all, value_all, query_all, out_one_all, up_one_all, down_one_all, qkv_all,
        out_two_all, late_up, late_down,
    ) = [g.reshape((-1, g.shape[2])) for g in every[1:]]
    residual_zero = tokens[0].astype(F32)

    def to_channels(pieces, collective_id):
        sent = jnp.stack([p.reshape(devices, channels, rows) for p in pieces], axis=1)
        came = swap_all(sent, collective_id)
        came = came.transpose(1, 2, 0, 3)
        return [came[n] for n in range(len(pieces))]

    def to_rows(pieces, collective_id):
        sent = jnp.stack([p.transpose(1, 0, 2) for p in pieces], axis=1)
        came = swap_all(sent, collective_id)
        return [came[:, n].reshape(features, rows) for n in range(len(pieces))]

    per_channel = (channels, devices, rows)
    residual_two, stored_two = feed_forward(residual_one, gain_two, up_one_all, down_one_all)
    normed_three = layer_norm(residual_two, gain_three).astype(BF16)
    joint = product(normed_three, qkv_all).astype(BF16)
    att_q = joint[:, :features]
    kv = gather_line(joint[:, features:], 4).reshape(blocks * rows, 2 * features)
    where = jnp.stack([place.astype(jnp.int32), length])
    attended, log_total = local_call(
        attend_body,
        [jax.ShapeDtypeStruct((rows, features), BF16), jax.ShapeDtypeStruct((rows, 128), F32)],
        where, att_q, kv, scalars=1,
    )
    residual_three = residual_two + product(attended, out_two_all)
    residual_four, stored_four = feed_forward(residual_three, gain_four, late_up, late_down)
    activations = (live_mask * residual_four).astype(BF16)

    grad_four = live_mask * cotangent[0].astype(F32)
    grad_three, grad_norm_four, grad_up_two, grad_down_two = feed_back(
        residual_three, gain_four, late_up, late_down, stored_four, grad_four
    )
    grad_up_two = lax.psum_scatter(
        grad_up_two.astype(BF16), BOTH, scatter_dimension=0, tiled=True
    ).astype(F32)
    grad_down_two = lax.psum_scatter(
        grad_down_two.astype(BF16), BOTH, scatter_dimension=0, tiled=True
    ).astype(F32)
    branch_three = grad_three.astype(BF16)
    grad_out_two = product_sum(attended, branch_three)
    grad_attended = product_back(branch_three, out_two_all).astype(BF16)
    grad_q, grad_kv = local_call(
        attend_back_body,
        [
            jax.ShapeDtypeStruct((rows, features), BF16),
            jax.ShapeDtypeStruct((blocks * rows, 2 * features), BF16),
        ],
        where, att_q, kv, log_total, grad_attended, scalars=1,
    )
    grad_kv = sum_line(grad_kv.reshape(blocks, rows, 2 * features), 5)
    grad_joint = jnp.concatenate([grad_q, grad_kv.astype(BF16)], axis=1)
    grad_qkv_weight = product_sum(normed_three, grad_joint)
    grad_normed_three = product_back(grad_joint, qkv_all)
    grad_from_three, grad_norm_three = jax.vjp(layer_norm, residual_two, gain_three)[1](
        grad_normed_three
    )
    grad_two = grad_three + grad_from_three
    grad_one, grad_norm_two, grad_up_one, grad_down_one = feed_back(
        residual_one, gain_two, up_one_all, down_one_all, stored_two, grad_two
    )
    branch_one = grad_one.astype(BF16)
    grad_out_one = product(gated, branch_one)
    gated_grad = contract(out_one_all, branch_one, 1, 1)
    grad_queries = (gated_grad * ssm_out.astype(F32)).astype(BF16)
    ssm_grad = (gated_grad * queries).astype(BF16)
    (grad_own,) = to_channels([ssm_grad], 6)
    grad_k_own, grad_v_own, kernel_grad, taps_grad, skip_grad = local_call(
        partial(mixer_back_body, blocks, groups, rows),
        [
            jax.ShapeDtypeStruct(per_channel, BF16),
            jax.ShapeDtypeStruct(per_channel, BF16),
            jax.ShapeDtypeStruct((channels, wide), F32),
            jax.ShapeDtypeStruct((channels, narrow), F32),
            jax.ShapeDtypeStruct((channels, 128), F32),
        ],
        grad_own, k_own, v_own, shifted, tap_row, kernel_row, skip_row,
    )
    grad_keys, grad_values = to_rows([grad_k_own, grad_v_own], 7)
    grad_values = (grad_values.astype(F32) * live_lane).astype(BF16)
    grad_decay_log, grad_turn_angle, grad_mix_real, grad_mix_imag = kernel_pull(
        kernel_grad[:, : rows * blocks]
    )
    grad_shift_taps = taps_grad[:, : shift_taps.shape[1]]
    grad_skip_gain = skip_grad[:, 0]

    grad_query_one = contract(normed_turned, grad_queries, 1, 1)
    grad_key_one = contract(normed_turned, grad_keys, 1, 1)
    grad_value_one = contract(normed_turned, grad_values, 1, 1)
    grad_normed_one = (
        contract(grad_queries, query_all, 0, 1)
        + contract(grad_keys, key_all, 0, 1)
        + contract(grad_values, value_all, 0, 1)
    )
    grad_from_one, grad_norm_one = jax.vjp(layer_norm, residual_zero, gain_one)[1](
        grad_normed_one
    )
    input_grad = grad_one + grad_from_one

    gain_grads = jnp.stack([grad_norm_one, grad_norm_two, grad_norm_three, grad_norm_four])
    gain_grads = gain_grads.reshape(4, devices, channels).transpose(1, 0, 2)
    gain_grads = jnp.pad(gain_grads, ((0, 0), (0, 4), (0, 128 - channels)))

    def owned(grad):
        return grad.astype(BF16).reshape(devices, -1, grad.shape[1])

    sums = reduce_all(
        [gain_grads]
        + [
            owned(g)
            for g in (
                grad_up_one, grad_down_one, grad_qkv_weight, grad_out_two, grad_out_one,
                grad_query_one, grad_key_one, grad_value_one,
            )
        ],
        8,
    )
    gain_grads, grad_up_one, grad_down_one, grad_qkv_weight, grad_out_two, grad_out_one = sums[:6]
    grad_query_one, grad_key_one, grad_value_one = sums[6:]
    gain_grads = gain_grads[:4, :channels]
    return (
        activations[None], input_grad[None],
        gain_grads[0], grad_query_one, grad_key_one, grad_value_one,
        grad_shift_taps, grad_decay_log, grad_turn_angle, grad_mix_real, grad_mix_imag,
        grad_skip_gain, grad_out_one,
        gain_grads[1], grad_up_one, grad_down_one,
        gain_grads[2], grad_qkv_weight, grad_out_two,
        gain_grads[3], grad_up_two, grad_down_two,
    )


def solution(mesh):
    row, vector = P(BOTH, None), P(BOTH)
    whole = P("dp", "seq", None)
    weights = (
        vector, row, row, row, row, row, row, row, row, vector, row,
        vector, row, row, vector, row, row, vector, row, row,
    )
    return jax.shard_map(
        shards,
        mesh=mesh,
        in_specs=(whole, P("dp")) + weights + (whole,),
        out_specs=(whole, whole) + weights,
        check_vma=False,
    )
```

```python
from functools import partial

import jax
import jax.numpy as jnp
from jax import lax
from jax.experimental import pallas as pl
from jax.experimental.pallas import tpu as pltpu
from jax.sharding import PartitionSpec as P

HEADS = 12
HDIM = 64
EPSILON = 1e-05
HIGHEST = lax.Precision.HIGHEST
MASKED = -1e30
BOTH = ("seq", "dp")
MESH = pl.DeviceIdType.MESH
MIB = 1024 * 1024
LAGS = (0, 2, 4, 6)
PLACES = (5, 6, 7, 8, 11)
RUNS = (8, 11, 12, 14)
AHEAD = 4
F32 = jnp.float32
BF16 = jnp.bfloat16


def grouped():
    return lax.axis_size("seq") == 4 and lax.axis_size("dp") == 8


def coordinates():
    seq, dp = lax.axis_index("seq"), lax.axis_index("dp")
    return seq // 2, seq % 2, dp // 2, dp % 2


def slot_of(y, c, z, x):
    return (y * 2 + c) * 8 + z * 2 + x


def device_of(y, c, z, x):
    return (y * 2 + c, z * 2 + x)


def greet(peers):
    barrier = pltpu.get_barrier_semaphore()
    for peer in peers:
        pl.semaphore_signal(barrier, inc=1, device_id=peer, device_id_type=MESH)
    pl.semaphore_wait(barrier, len(peers))


def six_peers(y, c, z, x):
    return [device_of(y, c, (z + k) % 4, x) for k in (1, 2, 3)] + [
        device_of(y, c, z, 1 - x),
        device_of(1 - y, c, z, x),
        device_of(y, 1 - c, z, x),
    ]


class Gather:
    def __init__(self, parts, sources, gathered, local_sem, send_sem, recv_sem, ahead=None):
        self.parts, self.sources, self.gathered = parts, sources, gathered
        self.send_sem, self.recv_sem, self.ahead = send_sem, recv_sem, ahead or AHEAD
        self.y, self.c, self.z, self.x = y, c, z, x = coordinates()
        self.me = slot_of(y, c, z, x)
        self.across_x = device_of(y, c, z, 1 - x)
        self.across_y = device_of(1 - y, c, z, x)
        self.other_core = device_of(y, 1 - c, z, x)
        self.own = [
            pltpu.make_async_copy(sources[i], gathered[i].at[self.me], local_sem.at[i])
            for i in range(len(sources))
        ]
        self.done = 0

    def place(self, p, slot):
        i, row, rows, column, columns, _ = self.parts[p]
        return self.gathered[i].at[slot, pl.ds(row, rows), pl.ds(column, columns)]

    def send(self, p, slot, target, first=False):
        i, row, rows, column, columns, _ = self.parts[p]
        source = self.sources[i].at[pl.ds(row, rows), pl.ds(column, columns)]
        pltpu.make_async_remote_copy(
            src_ref=source if first else self.place(p, slot),
            dst_ref=self.place(p, slot),
            send_sem=self.send_sem.at[p],
            recv_sem=self.recv_sem.at[p, slot],
            device_id=target,
            device_id_type=MESH,
        ).start()

    def arrived(self, p, slot):
        place = self.place(p, slot)
        pltpu.make_async_copy(place, place, self.recv_sem.at[p, slot]).wait()

    def first(self, p):
        for k in (1, 3, 2):
            self.send(p, self.me, device_of(self.y, self.c, (self.z + k) % 4, self.x), True)
        self.send(p, self.me, self.across_x, True)
        self.send(p, self.me, self.across_y, True)
        self.send(p, self.me, self.other_core, True)

    def start(self):
        for copy in self.own:
            copy.start()
        for p in range(min(self.ahead, len(self.parts))):
            self.first(p)

    def after_z(self, p):
        for k in (3, 1, 2):
            slot = slot_of(self.y, self.c, (self.z + k) % 4, self.x)
            self.arrived(p, slot)
            self.send(p, slot, self.across_x)
            self.send(p, slot, self.across_y)
            self.send(p, slot, self.other_core)

    def after_first(self, p):
        x_first = self.parts[p][5]
        for k in (0, 3, 1, 2):
            by_x = slot_of(self.y, self.c, (self.z + k) % 4, 1 - self.x)
            by_y = slot_of(1 - self.y, self.c, (self.z + k) % 4, self.x)
            self.arrived(p, by_x)
            if x_first:
                self.send(p, by_x, self.across_y)
            self.send(p, by_x, self.other_core)
            self.arrived(p, by_y)
            if not x_first:
                self.send(p, by_y, self.across_x)
            self.send(p, by_y, self.other_core)

    def after_second(self, p):
        for k in (0, 3, 1, 2):
            slot = slot_of(1 - self.y, self.c, (self.z + k) % 4, 1 - self.x)
            self.arrived(p, slot)
            self.send(p, slot, self.other_core)

    def whole(self, p):
        for side in (0, 1):
            for zz in range(4):
                for xx in (0, 1):
                    self.arrived(p, slot_of(side, 1 - self.c, zz, xx))

    def steps(self):
        return len(self.parts) + 3

    def run(self, until):
        while self.done < min(until, self.steps()):
            s, count = self.done, len(self.parts)
            if self.ahead <= s + self.ahead < count:
                self.first(s + self.ahead)
            for stage, act in enumerate(
                (self.after_z, self.after_first, self.after_second, self.whole)
            ):
                if 0 <= s - stage < count:
                    act(s - stage)
            self.done += 1

    def own_arrived(self, indices):
        for i in indices:
            self.own[i].wait()

    def finish(self):
        self.run(self.steps())
        for p, (i, row, rows, column, columns, _) in enumerate(self.parts):
            sent = self.gathered[i].at[pl.ds(0, 31), pl.ds(row, rows), pl.ds(column, columns)]
            pltpu.make_async_copy(sent, sent, self.send_sem.at[p]).wait()


def cut(arrays):
    parts = []
    for i, (rows, columns) in enumerate(arrays):
        if columns > 1536:
            width = 1536 if columns % 1536 == 0 else 768
            pieces = [(0, rows, w, width) for w in range(0, columns, width)]
        elif rows > 48:
            pieces = [(r, 48, 0, columns) for r in range(0, rows, 48)]
        else:
            pieces = [(0, rows, 0, columns)]
        for piece in pieces:
            parts.append((i,) + piece + (len(parts) % 2 == 0,))
    return parts


class Reduce:
    def __init__(self, parts, terms, totals, buffers, mine, send_sem, recv_sem, mine_sem):
        self.parts, self.terms, self.totals, self.buffers = parts, terms, totals, buffers
        self.send_sem, self.recv_sem, self.mine_sem = send_sem, recv_sem, mine_sem
        self.y, self.c, self.z, self.x = coordinates()
        self.mine, self.kinds = mine, {}
        for p, part in enumerate(parts):
            if part[0] < len(mine[0]):
                self.kinds.setdefault((part[2], part[4]), []).append(p)
        self.done = 0

    def term(self, p, core):
        i, row, rows, column, columns, _ = self.parts[p]
        return self.terms[i].at[:, core, :, :, pl.ds(row, rows), pl.ds(column, columns)]

    def fetch(self, p):
        kind = (self.parts[p][2], self.parts[p][4])
        place = self.kinds[kind].index(p)
        held = self.mine[1][kind].at[place % 2]
        return pltpu.make_async_copy(self.term(p, self.c), held, self.mine_sem.at[p]), held

    def copies(self, p, stage):
        one, two, three, four = self.buffers[4 * p : 4 * p + 4]
        y, c, z, x = self.y, self.c, self.z, self.x
        across_x, across_y = device_of(y, c, z, 1 - x), device_of(1 - y, c, z, x)
        x_last = self.parts[p][5]
        if stage == 0:
            pairs = [(self.term(p, 1 - c), one, device_of(y, 1 - c, z, x))]
        elif stage == 1 and x_last:
            pairs = [(one.at[1 - y], two, across_y)]
        elif stage == 1:
            pairs = [(one.at[:, :, 1 - x], two, across_x)]
        elif stage == 2 and x_last:
            pairs = [(two.at[:, 1 - x], three, across_x)]
        elif stage == 2:
            pairs = [(two.at[1 - y], three, across_y)]
        else:
            pairs = [
                (three.at[(z + k) % 4], four.at[k - 1], device_of(y, c, (z + k) % 4, x))
                for k in (1, 2, 3)
            ]
        return [
            pltpu.make_async_remote_copy(
                src_ref=src,
                dst_ref=dst,
                send_sem=self.send_sem.at[p, stage + n],
                recv_sem=self.recv_sem.at[p, stage + n],
                device_id=target,
                device_id_type=MESH,
            )
            for n, (src, dst, target) in enumerate(pairs)
        ]

    def add(self, p, stage):
        one, two, three, four = self.buffers[4 * p : 4 * p + 4]
        y, c, z, x = self.y, self.c, self.z, self.x
        i, row, rows, column, columns, x_last = self.parts[p]

        def total(a, b):
            return (a.astype(F32) + b.astype(F32)).astype(a.dtype)

        if stage == 0:
            if i < len(self.mine[0]):
                copy, held = self.fetch(p)
                copy.wait()
            else:
                held = self.term(p, c)

            def add_one(k, _):
                b, zz = k // 4, k % 4
                for xx in (0, 1):
                    one[b, zz, xx] = total(one[b, zz, xx], held[b, zz, xx])
                return 0

            lax.fori_loop(0, 8, add_one, 0)
            if i < len(self.mine[0]):
                same = self.kinds[(rows, columns)]
                later = same.index(p) + 2
                if later < len(same):
                    self.fetch(same[later])[0].start()
        elif stage == 1:

            def add_two(k, _):
                for h in (0, 1):
                    if x_last:
                        two[k, h] = total(two[k, h], one[y, k, h])
                    else:
                        two[h, k] = total(two[h, k], one[h, k, x])
                return 0

            lax.fori_loop(0, 4, add_two, 0)
        elif stage == 2:

            def add_three(k, _):
                three[k] = total(three[k], two[k, x] if x_last else two[y, k])
                return 0

            lax.fori_loop(0, 4, add_three, 0)
        else:
            self.totals[i][pl.ds(row, rows), pl.ds(column, columns)] = (
                three[z].astype(F32)
                + four[0].astype(F32)
                + four[1].astype(F32)
                + four[2].astype(F32)
            )

    def start(self, arrays):
        for p, part in enumerate(self.parts):
            if part[0] in arrays:
                for copy in self.copies(p, 0):
                    copy.start()

    def fetch_first(self):
        for same in self.kinds.values():
            for p in same[:2]:
                self.fetch(p)[0].start()

    def steps(self):
        return len(self.parts) + LAGS[3]

    def run(self, until):
        while self.done < min(until, self.steps()):
            for stage in range(4):
                p = self.done - LAGS[stage]
                if 0 <= p < len(self.parts):
                    for copy in self.copies(p, stage):
                        copy.wait_recv()
                    self.add(p, stage)
                    if stage < 3:
                        for copy in self.copies(p, stage + 1):
                            copy.start()
            self.done += 1

    def finish(self):
        self.run(self.steps())
        for p in range(len(self.parts)):
            for stage in range(4):
                for copy in self.copies(p, stage):
                    copy.wait_send()


def all_others():
    rows, groups = lax.axis_size("seq"), lax.axis_size("dp")
    count = rows * groups
    me = lax.axis_index("seq") * groups + lax.axis_index("dp")
    others = [lax.rem(me + k, count) for k in range(1, count)]
    return me, others, [(o // groups, lax.rem(o, groups)) for o in others]


class Swap:
    def __init__(self, src, dst, send_sem, recv_sem):
        self.src, self.dst, self.send_sem, self.recv_sem = src, dst, send_sem, recv_sem

    def start(self):
        me, others, places = all_others()
        for o, place in zip(others, places):
            pltpu.make_async_remote_copy(
                src_ref=self.src.at[o],
                dst_ref=self.dst.at[me],
                send_sem=self.send_sem,
                recv_sem=self.recv_sem,
                device_id=place,
                device_id_type=MESH,
            ).start()

    def wait(self):
        most = pl.ds(0, self.src.shape[0] - 1)
        me = all_others()[0]
        pltpu.make_async_copy(self.src.at[most], self.dst.at[most], self.recv_sem).wait()
        pltpu.make_async_copy(self.src.at[most], self.dst.at[most], self.send_sem).wait()
        self.dst[me] = self.src[me]


def line_body(src, dst, local_sem, send_sem, recv_sem):
    y, c, z, x = coordinates()
    me, mate, far, last = y * 2 + c, y * 2 + 1 - c, (1 - y) * 2 + c, (1 - y) * 2 + 1 - c
    own = pltpu.make_async_copy(src, dst.at[me], local_sem)
    own.start()
    core, side = device_of(y, 1 - c, z, x), device_of(1 - y, c, z, x)
    greet([core, side])

    def copy(n, source, slot, target):
        return pltpu.make_async_remote_copy(
            src_ref=source,
            dst_ref=dst.at[slot],
            send_sem=send_sem.at[n],
            recv_sem=recv_sem.at[n],
            device_id=target,
            device_id_type=MESH,
        )

    first = copy(0, src, me, side)
    second = copy(1, src, me, core)
    third = copy(2, dst.at[far], far, core)
    first.start()
    second.start()
    first.wait_recv()
    third.start()
    second.wait_recv()
    third.wait_recv()
    for each in (first, second, third):
        each.wait_send()
    own.wait()


def gather_line(value, collective_id):
    if not grouped():
        return lax.all_gather(value, "seq", axis=0)
    return pl.pallas_call(
        line_body,
        out_shape=jax.ShapeDtypeStruct((4,) + value.shape, value.dtype),
        in_specs=[pl.BlockSpec(memory_space=pltpu.VMEM)],
        out_specs=pl.BlockSpec(memory_space=pltpu.VMEM),
        scratch_shapes=[
            pltpu.SemaphoreType.DMA(()),
            pltpu.SemaphoreType.DMA((3,)),
            pltpu.SemaphoreType.DMA((3,)),
        ],
        compiler_params=pltpu.CompilerParams(
            collective_id=collective_id, has_side_effects=True
        ),
    )(value)


def line_sum_body(src, dst, one, two, send_sem, recv_sem):
    y, c, z, x = coordinates()
    core, side = device_of(y, 1 - c, z, x), device_of(1 - y, c, z, x)
    greet([core, side])

    def copy(n, source, target, where):
        return pltpu.make_async_remote_copy(
            src_ref=source,
            dst_ref=where,
            send_sem=send_sem.at[n],
            recv_sem=recv_sem.at[n],
            device_id=target,
            device_id_type=MESH,
        )

    far = copy(0, src.at[1 - y, 1 - c], core, one.at[1 - y])
    near = copy(1, src.at[y, 1 - c], core, one.at[y])
    far.start()
    near.start()
    far.wait_recv()
    one[1 - y] = (one[1 - y].astype(F32) + src[1 - y, c].astype(F32)).astype(one.dtype)
    onward = copy(2, one.at[1 - y], side, two)
    onward.start()
    near.wait_recv()
    onward.wait_recv()
    dst[...] = (one[y].astype(F32) + src[y, c].astype(F32)) + two[...].astype(F32)
    for each in (far, near, onward):
        each.wait_send()


def sum_line(value, collective_id):
    if not grouped():
        return lax.psum_scatter(value, "seq", scatter_dimension=0).astype(F32)
    return pl.pallas_call(
        line_sum_body,
        out_shape=jax.ShapeDtypeStruct(value.shape[1:], F32),
        in_specs=[pl.BlockSpec(memory_space=pltpu.VMEM)],
        out_specs=pl.BlockSpec(memory_space=pltpu.VMEM),
        scratch_shapes=[
            pltpu.VMEM((2,) + value.shape[1:], value.dtype),
            pltpu.VMEM(value.shape[1:], value.dtype),
            pltpu.SemaphoreType.DMA((3,)),
            pltpu.SemaphoreType.DMA((3,)),
        ],
        compiler_params=pltpu.CompilerParams(
            collective_id=collective_id, has_side_effects=True, vmem_limit_bytes=32 * MIB
        ),
    )(value.reshape((2, 2) + value.shape[1:]))


def layer_norm(residual, scale_gain):
    average = jnp.mean(residual, axis=-1, keepdims=True)
    centered = residual - average
    variance = jnp.mean(centered * centered, axis=-1, keepdims=True)
    return centered * lax.rsqrt(variance + EPSILON) * scale_gain


def contract(left_side, right_side, left_dim, right_dim):
    return lax.dot_general(
        left_side,
        right_side,
        (((left_dim,), (right_dim,)), ((), ())),
        preferred_element_type=F32,
    )


def product(left_side, right_side):
    return contract(left_side, right_side, 1, 0)


def product_back(left_side, right_side):
    return contract(left_side, right_side, 1, 1)


def product_sum(left_side, right_side):
    return contract(left_side, right_side, 0, 0)


def feed_forward(residual, scale_gain, up_weight, down_weight):
    normed = layer_norm(residual, scale_gain).astype(BF16)
    pre_act = product(normed, up_weight)
    activated = jax.nn.gelu(pre_act).astype(BF16)
    return (residual + product(activated, down_weight), (normed, pre_act, activated))


def feed_back(residual, scale_gain, up_weight, down_weight, stored, grad_residual):
    normed, pre_act, activated = stored
    grad_branch = grad_residual.astype(BF16)
    grad_down = product_sum(activated, grad_branch)
    grad_activated = product_back(grad_branch, down_weight)
    gelu_pull = jax.vjp(jax.nn.gelu, pre_act)[1]
    grad_pre = gelu_pull(grad_activated)[0].astype(BF16)
    grad_up = product_sum(normed, grad_pre)
    grad_normed = product_back(grad_pre, up_weight)
    norm_pull = jax.vjp(layer_norm, residual, scale_gain)[1]
    grad_input, grad_gain = norm_pull(grad_normed)
    return (grad_residual + grad_input, grad_gain, grad_up, grad_down)


def ssm_kernel(decay_log, turn_angle, mix_real, mix_imag, length):
    rate = jnp.exp(decay_log)[:, :, None]
    angle = turn_angle[:, :, None]
    step = 32

    def powers(times):
        return (
            jnp.exp(-times * rate) * jnp.cos(times * angle),
            jnp.exp(-times * rate) * jnp.sin(times * angle),
        )

    low_real, low_imag = powers(jnp.arange(step, dtype=F32)[None, None])
    high_real, high_imag = powers(
        (step * jnp.arange(length // step, dtype=jnp.int32)).astype(F32)[None, None]
    )
    real, imag = mix_real[:, :, None], mix_imag[:, :, None]
    high = jnp.concatenate(
        [real * high_real - imag * high_imag, -(real * high_imag + imag * high_real)], axis=1
    )
    low = jnp.concatenate([low_real, low_imag], axis=1)
    kernel = jnp.einsum("cna,cnb->cab", high, low, precision=HIGHEST)
    return kernel.reshape(decay_log.shape[0], length)


def toeplitz(row, rows):
    spread = jnp.broadcast_to(row, (rows, row.shape[1]))
    return pltpu.roll(spread, 0, 1, stride=1, stride_axis=0)


def block_sum(mixed, blocks, groups, rows):
    total = mixed[:, :rows]
    for d in range(1, blocks):
        piece = mixed[: (blocks - d) * groups, d * rows : (d + 1) * rows]
        total = total + jnp.concatenate(
            [jnp.zeros((d * groups, rows), piece.dtype), piece], axis=0
        )
    return total


def block_spread(value, blocks, lags, groups, rows):
    pieces = [value]
    for d in range(1, lags):
        pieces.append(
            jnp.concatenate(
                [value[d * groups :], jnp.zeros((d * groups, rows), value.dtype)], axis=0
            )
        )
    return jnp.concatenate(pieces, axis=1)


def mix(blocks, groups, rows, keys, values, tap_row, kernel_row, skip):
    span = blocks * rows
    taps = toeplitz(tap_row, rows)[:, : 2 * rows].astype(BF16)
    longer = toeplitz(kernel_row, rows)[:, :span].astype(BF16)
    near = product(keys, taps)
    shifted = near[:, :rows] + jnp.concatenate(
        [jnp.zeros((groups, rows), F32), near[: (blocks - 1) * groups, rows:]], axis=0
    )
    signal = shifted * values.astype(F32)
    mixed = product(signal.astype(BF16), longer)
    return shifted, block_sum(mixed, blocks, groups, rows) + skip * signal


def mixer_body(blocks, groups, rows, k_ref, v_ref, taps_ref, kernel_ref, skip_ref, shifted_ref, out_ref):
    for ch in range(k_ref.shape[0]):
        row = slice(ch, ch + 1)
        shifted_ref[ch], out = mix(
            blocks, groups, rows, k_ref[ch], v_ref[ch],
            taps_ref[row, :], kernel_ref[row, :], skip_ref[row, :1],
        )
        out_ref[ch] = out.astype(BF16)


def flat_weight(ref):
    wide = ref[...].astype(F32)
    return wide.reshape(wide.shape[0] * wide.shape[1], wide.shape[2]).astype(BF16)


def first_body(
    parts, count, *refs,
):
    sources = refs[:count]
    tokens, live, taps_ref, kernel_ref, skip_ref = refs[count : count + 5]
    refs = refs[count + 5 :]
    gathered = refs[:count]
    (
        residual_ref, standard_ref, inverse_ref, normed_ref, queries_ref, ssm_ref, gated_ref,
        k_ref, v_ref, shifted_ref,
    ) = refs[count : count + 10]
    (
        wide, sent_kv, came_kv, sent_y, came_y,
        local_sem, send_sem, recv_sem, swap_sem,
    ) = refs[count + 10 :]
    gains, key_all, value_all, query_all, out_all = gathered[:5]
    devices, channels = key_all.shape[0], key_all.shape[1]
    rows, features = tokens.shape
    blocks, groups = lax.axis_size("seq"), lax.axis_size("dp")
    greet(all_others()[2])
    gather = Gather(parts, sources, gathered, local_sem, send_sem, recv_sem)
    gather.start()

    turned = tokens[...].astype(F32).T
    centered = turned - jnp.mean(turned, axis=0, keepdims=True)
    inverse = lax.rsqrt(jnp.mean(centered * centered, axis=0, keepdims=True) + EPSILON)
    inverse_ref[...] = jnp.broadcast_to(inverse, inverse_ref.shape)
    standard_ref[...] = centered * inverse

    gather.run(RUNS[0])
    gather.own_arrived(range(5))
    gain = gains[...].reshape(features, 128)[:, :1]
    normed_ref[...] = (standard_ref[...] * gain).astype(BF16)

    def projected(weight):
        return contract(flat_weight(weight), normed_ref[...], 0, 0)

    wide[:, :channels, :] = projected(key_all).reshape(devices, channels, rows)
    wide[:, channels:, :] = (projected(value_all) * live[...]).reshape(devices, channels, rows)
    sent_kv[...] = wide[...].astype(BF16)
    over = Swap(sent_kv, came_kv, swap_sem.at[0], swap_sem.at[1])
    over.start()
    queries_ref[...] = projected(query_all)
    gather.run(RUNS[1])
    over.wait()
    wide[...] = came_kv[...].astype(F32)
    for ch in range(channels):
        row = slice(ch, ch + 1)
        k_ref[ch] = wide[:, ch, :].astype(BF16)
        v_ref[ch] = wide[:, channels + ch, :].astype(BF16)
        shifted_ref[ch], out = mix(
            blocks, groups, rows, k_ref[ch], v_ref[ch],
            taps_ref[row, :], kernel_ref[row, :], skip_ref[row, :1],
        )
        wide[:, ch, :] = out
        if ch == channels // 2:
            gather.run(RUNS[2])
    sent_y[...] = wide[:, :channels, :].astype(BF16)
    back = Swap(sent_y, came_y, swap_sem.at[2], swap_sem.at[3])
    back.start()
    gather.run(RUNS[3])
    back.wait()
    ssm = came_y[...].astype(F32).reshape(features, rows)
    ssm_ref[...] = ssm.astype(BF16)
    gated_ref[...] = (queries_ref[...] * ssm).astype(BF16)
    residual_ref[...] = tokens[...].astype(F32) + contract(
        gated_ref[...], flat_weight(out_all), 0, 0
    )
    gather.own_arrived(range(5, count))
    gather.finish()


def first_layer(weights, tokens, live, tap_row, kernel_row, skip_row, collective_id):
    count = len(weights)
    blocks, groups = lax.axis_size("seq"), lax.axis_size("dp")
    devices = blocks * groups
    rows, features = tokens.shape
    channels = features // devices
    parts = cut([a.shape for a in weights])
    vmem, anywhere = pl.BlockSpec(memory_space=pltpu.VMEM), pl.BlockSpec(memory_space=pl.ANY)
    turned = (features, rows)
    per_channel = (channels, devices, rows)
    results = [
        ((rows, features), F32), (turned, F32), ((8, rows), F32), (turned, BF16), (turned, F32),
        (turned, BF16), (turned, BF16), (per_channel, BF16), (per_channel, BF16), (per_channel, F32),
    ]
    out = pl.pallas_call(
        partial(first_body, parts, count),
        out_shape=[jax.ShapeDtypeStruct((devices,) + a.shape, a.dtype) for a in weights]
        + [jax.ShapeDtypeStruct(*r) for r in results],
        in_specs=[anywhere] * count + [vmem] * 5,
        out_specs=[vmem] * 5 + [anywhere] * (count - 5) + [vmem] * len(results),
        scratch_shapes=[
            pltpu.VMEM((devices, 2 * channels, rows), F32),
            pltpu.VMEM((devices, 2 * channels, rows), BF16),
            pltpu.VMEM((devices, 2 * channels, rows), BF16),
            pltpu.VMEM((devices, channels, rows), BF16),
            pltpu.VMEM((devices, channels, rows), BF16),
            pltpu.SemaphoreType.DMA((count,)),
            pltpu.SemaphoreType.DMA((len(parts),)),
            pltpu.SemaphoreType.DMA((len(parts), devices)),
            pltpu.SemaphoreType.DMA((4,)),
        ],
        compiler_params=pltpu.CompilerParams(
            collective_id=collective_id, has_side_effects=True, vmem_limit_bytes=48 * MIB
        ),
    )(*weights, tokens, live, tap_row, kernel_row, skip_row)
    return out[:count], out[count:]


def first_layer_apart(weights, tokens, live, tap_row, kernel_row, skip_row):
    blocks, groups = lax.axis_size("seq"), lax.axis_size("dp")
    devices = blocks * groups
    rows, features = tokens.shape
    channels = features // devices
    every = [lax.all_gather(a, BOTH, axis=0) for a in weights]
    gain = every[0][:, :, 0].reshape(features, 1)
    key_all, value_all, query_all, out_all = [a.reshape(features, -1) for a in every[1:5]]
    turned = tokens.astype(F32).T
    centered = turned - jnp.mean(turned, axis=0, keepdims=True)
    inverse = lax.rsqrt(jnp.mean(centered * centered, axis=0, keepdims=True) + EPSILON)
    standard = centered * inverse
    normed = (standard * gain).astype(BF16)
    queries = contract(query_all, normed, 0, 0)
    keys = contract(key_all, normed, 0, 0).astype(BF16)
    values = (contract(value_all, normed, 0, 0) * live).astype(BF16)
    sent = jnp.stack([a.reshape(devices, channels, rows) for a in (keys, values)], axis=1)
    k_own, v_own = lax.all_to_all(sent, BOTH, 0, 0, tiled=True).transpose(1, 2, 0, 3)
    per_channel = (channels, devices, rows)
    shifted, mixed = local_call(
        partial(mixer_body, blocks, groups, rows),
        [jax.ShapeDtypeStruct(per_channel, F32), jax.ShapeDtypeStruct(per_channel, BF16)],
        k_own, v_own, tap_row, kernel_row, skip_row,
    )
    ssm = lax.all_to_all(mixed.transpose(1, 0, 2), BOTH, 0, 0, tiled=True)
    ssm = ssm.reshape(features, rows)
    gated = (queries * ssm.astype(F32)).astype(BF16)
    residual = tokens.astype(F32) + contract(gated, out_all, 0, 0)
    inverse = jnp.broadcast_to(inverse, (8, rows))
    return every, [residual, standard, inverse, normed, queries, ssm, gated, k_own, v_own, shifted]


def mix_back(
    blocks, groups, rows, out_grad, keys, values, shifted, tap_row, kernel_row, skip
):
    span = blocks * rows
    turned = (
        lax.broadcasted_iota(jnp.int32, (rows, rows), 0)
        + lax.broadcasted_iota(jnp.int32, (rows, rows), 1)
        == rows - 1
    ).astype(BF16)

    def lag_sums(earlier, spread, lanes):
        backward = product(earlier, turned).astype(BF16)
        pairs = product_sum(backward, spread)
        padded = jnp.concatenate(
            [pairs, jnp.zeros((rows, lanes - pairs.shape[1]), F32)], axis=1
        )
        return jnp.sum(
            pltpu.roll(padded, lanes - rows + 1, 1, stride=1, stride_axis=0),
            axis=0,
            keepdims=True,
        )

    taps = toeplitz(tap_row, rows)[:, : 2 * rows].astype(BF16)
    longer = toeplitz(kernel_row, rows)[:, :span].astype(BF16)
    values = values.astype(F32)
    signal = shifted * values
    later = block_spread(out_grad, blocks, blocks, groups, rows).astype(BF16)
    signal_grad = product_back(later, longer) + skip * out_grad
    kernel_grad = lag_sums(signal.astype(BF16), later, kernel_row.shape[1])
    skip_grad = jnp.sum(jnp.sum(signal * out_grad, axis=0, keepdims=True), axis=1, keepdims=True)
    shifted_grad = values * signal_grad
    next_two = block_spread(shifted_grad, blocks, 2, groups, rows).astype(BF16)
    return (
        product_back(next_two, taps),
        shifted * signal_grad,
        kernel_grad,
        lag_sums(keys, next_two, tap_row.shape[1]),
        skip_grad,
    )


def mixer_back_body(
    blocks, groups, rows,
    grad_ref, k_ref, v_ref, shifted_ref, taps_ref, kernel_ref, skip_ref,
    grad_k_ref, grad_v_ref, kernel_grad_ref, taps_grad_ref, skip_grad_ref,
):
    for ch in range(k_ref.shape[0]):
        row = slice(ch, ch + 1)
        grad_k, grad_v, kernel_grad_ref[row, :], taps_grad_ref[row, :], skip_grad = mix_back(
            blocks, groups, rows, grad_ref[ch].astype(F32), k_ref[ch], v_ref[ch], shifted_ref[ch],
            taps_ref[row, :], kernel_ref[row, :], skip_ref[row, :1],
        )
        grad_k_ref[ch], grad_v_ref[ch] = grad_k.astype(BF16), grad_v.astype(BF16)
        skip_grad_ref[row, :] = jnp.broadcast_to(skip_grad, (1, 128))


def last_body(parts, count, kinds, *refs):
    early = refs[:count]
    (
        gain_in, branch, grad_one, live, gated, normed, queries, ssm, standard, inverse,
        gains, key_all, value_all, query_all, out_all,
        k_ref, v_ref, shifted_ref, taps_ref, kernel_ref, skip_ref,
    ) = refs[count : count + 21]
    refs = refs[count + 21 :]
    totals = refs[: count + 5]
    input_grad, kernel_grad_ref, taps_grad_ref, skip_grad_ref = refs[count + 5 : count + 9]
    refs = refs[count + 9 :]
    out_term, query_term, key_term, value_term, gain_term = own_terms = refs[:5]
    buffers = refs[5 : 5 + 4 * len(parts)]
    refs = refs[5 + 4 * len(parts) :]
    held = dict(zip(kinds, refs[: len(kinds)]))
    (
        wide, sent_g, came_g, sent_kv, came_kv, query_grad,
        send_sem, recv_sem, mine_sem, swap_sem,
    ) = refs[len(kinds) :]
    devices, channels = key_all.shape[0], key_all.shape[1]
    rows, features = branch.shape
    blocks, groups = lax.axis_size("seq"), lax.axis_size("dp")
    greet(all_others()[2])
    reduce = Reduce(
        parts, early + own_terms, totals, buffers, (early, held), send_sem, recv_sem, mine_sem
    )
    reduce.fetch_first()

    def slots(value, columns):
        return value.reshape(2, 2, 4, 2, channels, columns)

    gated_grad = contract(flat_weight(out_all), branch[...], 1, 1)
    sent_g[...] = (gated_grad * queries[...]).reshape(devices, channels, rows).astype(BF16)
    over = Swap(sent_g, came_g, swap_sem.at[0], swap_sem.at[1])
    over.start()
    reduce.start(range(count))
    query_grad[...] = (gated_grad * ssm[...].astype(F32)).astype(BF16)
    out_term[...] = slots(product(gated[...], branch[...]), features).astype(BF16)
    query_term[...] = slots(contract(normed[...], query_grad[...], 1, 1), features).astype(BF16)
    reduce.start((count, count + 1))
    reduce.run(PLACES[0])
    over.wait()
    wide[:, :channels, :] = came_g[...].astype(F32)
    for ch in range(channels):
        row = slice(ch, ch + 1)
        grad_k, grad_v, kernel_grad_ref[row, :], taps_grad_ref[row, :], skip_grad = mix_back(
            blocks, groups, rows, wide[:, ch, :], k_ref[ch], v_ref[ch], shifted_ref[ch],
            taps_ref[row, :], kernel_ref[row, :], skip_ref[row, :1],
        )
        wide[:, ch, :], wide[:, channels + ch, :] = grad_k, grad_v
        skip_grad_ref[row, :] = jnp.broadcast_to(skip_grad, (1, 128))
        if ch % 8 == 7:
            reduce.run(PLACES[1 + ch // 8])
    sent_kv[...] = wide[...].astype(BF16)
    back = Swap(sent_kv, came_kv, swap_sem.at[2], swap_sem.at[3])
    back.start()
    reduce.run(PLACES[4])
    back.wait()
    wide[...] = came_kv[...].astype(F32)
    key_grad = wide[:, :channels, :].reshape(features, rows).astype(BF16)
    value_grad = (wide[:, channels:, :].reshape(features, rows) * live[...]).astype(BF16)
    key_term[...] = slots(contract(normed[...], key_grad, 1, 1), features).astype(BF16)
    value_term[...] = slots(contract(normed[...], value_grad, 1, 1), features).astype(BF16)
    reduce.start((count + 2, count + 3))
    normed_grad = product(flat_weight(query_all), query_grad[...])
    normed_grad += product(flat_weight(key_all), key_grad)
    normed_grad += product(flat_weight(value_all), value_grad)
    gain_grad = jnp.sum(normed_grad * standard[...], axis=1, keepdims=True)
    lane = lax.broadcasted_iota(jnp.int32, (features, 128), 1)
    gain_term[...] = slots(jnp.where(lane == 0, gain_grad, gain_in[...]), 128)
    reduce.start((count + 4,))
    scaled = normed_grad * gains[...].reshape(features, 128)[:, :1]
    scaled = (
        scaled
        - jnp.mean(scaled, axis=0, keepdims=True)
        - standard[...] * jnp.mean(scaled * standard[...], axis=0, keepdims=True)
    )
    input_grad[...] = grad_one[...] + (scaled * inverse[:1, :]).T
    reduce.finish()


def last_layer(terms, gain_in, branch, grad_one, live, kept, weights, mixer_rows, collective_id):
    standard, inverse, normed, queries, ssm, gated, k_own, v_own, shifted = kept
    gains, key_all, value_all, query_all, out_all = weights
    devices, channels, features = key_all.shape
    rows = branch.shape[0]
    count = len(terms)
    square = (channels, features)
    shapes = [a.shape[1:] for a in terms] + [square] * 4 + [(channels, 128)]
    types = [BF16] * (count + 4) + [F32]
    parts = cut(shapes)
    kinds = sorted({(part[2], part[4]) for part in parts if part[0] < count})
    scratch = [pltpu.VMEM((2, 2, 4, 2) + s, t) for s, t in zip(shapes[count:], types[count:])]
    for i, _, part_rows, _, columns, x_last in parts:
        for lead in ((2, 4, 2), (4, 2) if x_last else (2, 4), (4,), (3,)):
            scratch.append(pltpu.VMEM(lead + (part_rows, columns), types[i]))
    scratch += [pltpu.VMEM((2, 2, 4, 2) + kind, BF16) for kind in kinds]
    scratch += [
        pltpu.VMEM((devices, 2 * channels, rows), F32),
        pltpu.VMEM((devices, channels, rows), BF16),
        pltpu.VMEM((devices, channels, rows), BF16),
        pltpu.VMEM((devices, 2 * channels, rows), BF16),
        pltpu.VMEM((devices, 2 * channels, rows), BF16),
        pltpu.VMEM((features, rows), BF16),
        pltpu.SemaphoreType.DMA((len(parts), 6)),
        pltpu.SemaphoreType.DMA((len(parts), 6)),
        pltpu.SemaphoreType.DMA((len(parts),)),
        pltpu.SemaphoreType.DMA((4,)),
    ]
    vmem, anywhere = pl.BlockSpec(memory_space=pltpu.VMEM), pl.BlockSpec(memory_space=pl.ANY)
    results = [jax.ShapeDtypeStruct(s, F32) for s in shapes]
    results.append(jax.ShapeDtypeStruct((rows, features), F32))
    results += [jax.ShapeDtypeStruct(a.shape, F32) for a in (mixer_rows[1], mixer_rows[0])]
    results.append(jax.ShapeDtypeStruct((channels, 128), F32))
    out = pl.pallas_call(
        partial(last_body, parts, count, kinds),
        out_shape=results,
        in_specs=[anywhere] * count + [vmem] * 21,
        out_specs=[vmem] * len(results),
        scratch_shapes=scratch,
        compiler_params=pltpu.CompilerParams(
            collective_id=collective_id, has_side_effects=True, vmem_limit_bytes=62 * MIB
        ),
    )(
        *[a.reshape((2, 2, 4, 2) + a.shape[1:]) for a in terms],
        gain_in, branch, grad_one, live, gated, normed, queries, ssm, standard, inverse,
        gains, key_all, value_all, query_all, out_all,
        k_own, v_own, shifted, *mixer_rows,
    )
    return out[: count + 5], out[count + 5 :]


def last_layer_apart(terms, gain_in, branch, grad_one, live, kept, weights, mixer_rows):
    standard, inverse, normed, queries, ssm, gated, k_own, v_own, shifted = kept
    gains, key_all, value_all, query_all, out_all = weights
    devices, channels, features = key_all.shape
    rows = branch.shape[0]
    blocks, groups = lax.axis_size("seq"), lax.axis_size("dp")
    key_all, value_all, query_all, out_all = [
        a.reshape(features, features) for a in (key_all, value_all, query_all, out_all)
    ]
    gated_grad = contract(out_all, branch, 1, 1)
    query_grad = (gated_grad * ssm.astype(F32)).astype(BF16)
    sent = (gated_grad * queries).reshape(devices, channels, rows).astype(BF16)
    own = lax.all_to_all(sent, BOTH, 0, 0, tiled=True).transpose(1, 0, 2)
    per_channel = jax.ShapeDtypeStruct(own.shape, BF16)
    grad_k, grad_v, kernel_grad, taps_grad, skip_grad = local_call(
        partial(mixer_back_body, blocks, groups, rows),
        [per_channel, per_channel]
        + [jax.ShapeDtypeStruct(a.shape, F32) for a in (mixer_rows[1], mixer_rows[0])]
        + [jax.ShapeDtypeStruct((channels, 128), F32)],
        own, k_own, v_own, shifted, *mixer_rows,
    )
    sent = jnp.stack([grad_k.transpose(1, 0, 2), grad_v.transpose(1, 0, 2)], axis=1)
    came = lax.all_to_all(sent, BOTH, 0, 0, tiled=True)
    key_grad = came[:, 0].reshape(features, rows)
    value_grad = (came[:, 1].reshape(features, rows) * live).astype(BF16)
    normed_grad = (
        product(query_all, query_grad) + product(key_all, key_grad) + product(value_all, value_grad)
    )
    gain_grad = jnp.sum(normed_grad * standard, axis=1, keepdims=True)
    lane = lax.broadcasted_iota(jnp.int32, (features, 128), 1)
    gain_term = jnp.where(lane == 0, gain_grad, gain_in)
    scaled = normed_grad * gains.reshape(features, 128)[:, :1]
    scaled = (
        scaled
        - jnp.mean(scaled, axis=0, keepdims=True)
        - standard * jnp.mean(scaled * standard, axis=0, keepdims=True)
    )
    input_grad = grad_one + (scaled * inverse[:1]).T
    last = [product(gated, branch)]
    last += [contract(normed, g, 1, 1) for g in (query_grad, key_grad, value_grad)]
    last = [a.reshape(devices, channels, features).astype(BF16) for a in last]
    last.append(gain_term.reshape(devices, channels, 128))
    sums = [
        lax.psum_scatter(a, BOTH, scatter_dimension=0, tiled=False).astype(F32)
        for a in list(terms) + last
    ]
    return sums, [input_grad, kernel_grad, taps_grad, skip_grad]


def allowed_keys(place, length, rows, keys):
    row_places = place * rows + lax.broadcasted_iota(jnp.int32, (rows, keys), 0)
    key_places = lax.broadcasted_iota(jnp.int32, (rows, keys), 1)
    return (key_places <= row_places) & (key_places < length)


def attend_body(where_ref, q_ref, kv_ref, out_ref, log_ref):
    rows, features = q_ref.shape
    keys = kv_ref.shape[0]
    allowed = allowed_keys(where_ref[0], where_ref[1], rows, keys)
    for head in range(HEADS):
        own = slice(head * HDIM, (head + 1) * HDIM)
        values = slice(features + head * HDIM, features + (head + 1) * HDIM)
        scores = product_back(q_ref[:, own], kv_ref[:, own]) * HDIM ** (-0.5)
        scores = jnp.where(allowed, scores, MASKED)
        most = jnp.max(scores, axis=1, keepdims=True)
        powers = jnp.exp(scores - most)
        total = jnp.sum(powers, axis=1, keepdims=True)
        weights = (powers * (1.0 / total)).astype(BF16)
        out_ref[:, own] = product(weights, kv_ref[:, values]).astype(BF16)
        log_ref[:, head : head + 1] = most + jnp.log(total)


def attend_back_body(where_ref, q_ref, kv_ref, log_ref, grad_ref, grad_q_ref, grad_kv_ref):
    rows, features = q_ref.shape
    keys = kv_ref.shape[0]
    allowed = allowed_keys(where_ref[0], where_ref[1], rows, keys)
    scale = HDIM ** (-0.5)
    for head in range(HEADS):
        own = slice(head * HDIM, (head + 1) * HDIM)
        values = slice(features + head * HDIM, features + (head + 1) * HDIM)
        queries, grads = q_ref[:, own], grad_ref[:, own]
        scores = product_back(queries, kv_ref[:, own]) * scale
        probs = jnp.where(allowed, jnp.exp(scores - log_ref[:, head : head + 1]), 0.0)
        prob_grad = product_back(grads, kv_ref[:, values])
        delta = jnp.sum(probs * prob_grad, axis=1, keepdims=True)
        grad_scores = (probs * (prob_grad - delta)).astype(BF16)
        grad_q_ref[:, own] = (product(grad_scores, kv_ref[:, own]) * scale).astype(BF16)
        grad_kv_ref[:, own] = (product_sum(grad_scores, queries) * scale).astype(BF16)
        grad_kv_ref[:, values] = product_sum(probs.astype(BF16), grads).astype(BF16)


def local_call(body, out_shape, *operands, scalars=0, limit=48):
    vmem = pl.BlockSpec(memory_space=pltpu.VMEM)
    smem = pl.BlockSpec(memory_space=pltpu.SMEM)
    return pl.pallas_call(
        body,
        out_shape=out_shape,
        in_specs=[smem] * scalars + [vmem] * (len(operands) - scalars),
        out_specs=jax.tree.map(lambda _: vmem, out_shape),
        compiler_params=pltpu.CompilerParams(vmem_limit_bytes=limit * MIB),
    )(*operands)


def shards(
    tokens, lengths, norm_one, query_one, key_one, value_one, shift_taps, decay_log,
    turn_angle, mix_real, mix_imag, skip_gain, out_one, norm_two, up_one, down_one,
    norm_three, qkv_weight, out_two, norm_four, up_two, down_two, cotangent,
):
    blocks, groups = lax.axis_size("seq"), lax.axis_size("dp")
    devices = blocks * groups
    rows, features = tokens.shape[1], tokens.shape[2]
    channels = features // devices
    place = lax.axis_index("seq")
    length = lengths[0]
    row_places = place * rows + jnp.arange(rows, dtype=jnp.int32)
    live_mask = (row_places < length).astype(F32)[:, None]
    live_lane = (row_places < length).astype(F32)[None, :]

    kernel, kernel_pull = jax.vjp(
        partial(ssm_kernel, length=rows * blocks),
        *[a.astype(F32) for a in (decay_log, turn_angle, mix_real, mix_imag)],
    )
    wide = -(-(blocks + 1) * rows // 128) * 128
    kernel_row = jnp.pad(kernel, ((0, 0), (0, wide - kernel.shape[1])))
    narrow = -(-3 * rows // 128) * 128
    tap_row = jnp.pad(
        shift_taps.astype(F32), ((0, 0), (0, narrow - shift_taps.shape[1]))
    )
    skip_row = jnp.broadcast_to(skip_gain.astype(F32)[:, None], (channels, 128))

    gains = jnp.stack([norm_one, norm_two, norm_three, norm_four], axis=1).astype(F32)
    gains = jnp.pad(gains, ((0, 0), (0, 124)))
    weights = [
        gains, key_one, value_one, query_one, out_one, up_one, down_one, qkv_weight, out_two,
        up_two, down_two,
    ]
    mixer_rows = (tap_row, kernel_row, skip_row)
    if grouped():
        every, kept = first_layer(weights, tokens[0], live_lane, *mixer_rows, 1)
    else:
        every, kept = first_layer_apart(weights, tokens[0], live_lane, *mixer_rows)
    residual_one = kept[0]
    gain_one, gain_two, gain_three, gain_four = [
        every[0][:, :, n].reshape(features) for n in range(4)
    ]
    up_one_all, down_one_all, qkv_all, out_two_all, late_up, late_down = [
        g.reshape((-1, g.shape[2])) for g in every[5:]
    ]

    residual_two, stored_two = feed_forward(residual_one, gain_two, up_one_all, down_one_all)
    normed_three = layer_norm(residual_two, gain_three).astype(BF16)
    joint = product(normed_three, qkv_all).astype(BF16)
    att_q = joint[:, :features]
    kv = gather_line(joint[:, features:], 4).reshape(blocks * rows, 2 * features)
    where = jnp.stack([place.astype(jnp.int32), length])
    attended, log_total = local_call(
        attend_body,
        [jax.ShapeDtypeStruct((rows, features), BF16), jax.ShapeDtypeStruct((rows, 128), F32)],
        where, att_q, kv, scalars=1,
    )
    residual_three = residual_two + product(attended, out_two_all)
    residual_four, stored_four = feed_forward(residual_three, gain_four, late_up, late_down)
    activations = (live_mask * residual_four).astype(BF16)

    grad_four = live_mask * cotangent[0].astype(F32)
    grad_three, grad_norm_four, grad_up_two, grad_down_two = feed_back(
        residual_three, gain_four, late_up, late_down, stored_four, grad_four
    )
    branch_three = grad_three.astype(BF16)
    grad_out_two = product_sum(attended, branch_three)
    grad_attended = product_back(branch_three, out_two_all).astype(BF16)
    grad_q, grad_kv = local_call(
        attend_back_body,
        [
            jax.ShapeDtypeStruct((rows, features), BF16),
            jax.ShapeDtypeStruct((blocks * rows, 2 * features), BF16),
        ],
        where, att_q, kv, log_total, grad_attended, scalars=1,
    )
    grad_kv = sum_line(grad_kv.reshape(blocks, rows, 2 * features), 5)
    grad_joint = jnp.concatenate([grad_q, grad_kv.astype(BF16)], axis=1)
    grad_qkv_weight = product_sum(normed_three, grad_joint)
    grad_normed_three = product_back(grad_joint, qkv_all)
    grad_from_three, grad_norm_three = jax.vjp(layer_norm, residual_two, gain_three)[1](
        grad_normed_three
    )
    grad_two = grad_three + grad_from_three
    grad_one, grad_norm_two, grad_up_one, grad_down_one = feed_back(
        residual_one, gain_two, up_one_all, down_one_all, stored_two, grad_two
    )
    branch_one = grad_one.astype(BF16)
    gain_in = jnp.stack(
        [jnp.zeros_like(grad_norm_two), grad_norm_two, grad_norm_three, grad_norm_four], axis=1
    )
    gain_in = jnp.pad(gain_in, ((0, 0), (0, 124)))
    terms = [
        g.astype(BF16).reshape(devices, -1, g.shape[1])
        for g in (
            grad_up_two, grad_down_two, grad_qkv_weight, grad_out_two, grad_up_one, grad_down_one
        )
    ]
    last = (terms, gain_in, branch_one, grad_one, live_lane, kept[1:], every[:5], mixer_rows)
    if grouped():
        sums, rest = last_layer(*last, 2)
    else:
        sums, rest = last_layer_apart(*last)
    grad_up_two, grad_down_two, grad_qkv_weight, grad_out_two, grad_up_one, grad_down_one = sums[:6]
    grad_out_one, grad_query_one, grad_key_one, grad_value_one, gain_grads = sums[6:]
    gain_grads = gain_grads[:, :4].T
    input_grad, kernel_grad, taps_grad, skip_grad = rest
    grad_decay_log, grad_turn_angle, grad_mix_real, grad_mix_imag = kernel_pull(
        kernel_grad[:, : rows * blocks]
    )
    grad_shift_taps = taps_grad[:, : shift_taps.shape[1]]
    grad_skip_gain = skip_grad[:, 0]
    return (
        activations[None], input_grad[None],
        gain_grads[0], grad_query_one, grad_key_one, grad_value_one,
        grad_shift_taps, grad_decay_log, grad_turn_angle, grad_mix_real, grad_mix_imag,
        grad_skip_gain, grad_out_one,
        gain_grads[1], grad_up_one, grad_down_one,
        gain_grads[2], grad_qkv_weight, grad_out_two,
        gain_grads[3], grad_up_two, grad_down_two,
    )


def solution(mesh):
    row, vector = P(BOTH, None), P(BOTH)
    whole = P("dp", "seq", None)
    weights = (
        vector, row, row, row, row, row, row, row, row, vector, row,
        vector, row, row, vector, row, row, vector, row, row,
    )
    return jax.shard_map(
        shards,
        mesh=mesh,
        in_specs=(whole, P("dp")) + weights + (whole,),
        out_specs=(whole, whole) + weights,
        check_vma=False,
    )
```

```python
from functools import partial

import jax
import jax.numpy as jnp
from jax import lax
from jax.experimental import pallas as pl
from jax.experimental.pallas import tpu as pltpu
from jax.sharding import PartitionSpec as P

HEADS = 12
HDIM = 64
EPSILON = 1e-05
HIGHEST = lax.Precision.HIGHEST
MASKED = -1e30
BOTH = ("seq", "dp")
MESH = pl.DeviceIdType.MESH
MIB = 1024 * 1024
LAGS = (0, 2, 4, 6)
PLACES = (4, 5, 6, 7, 9)
MIDDLE = (1, 1, 2, 3, 4, 5, 6, 7, 8)
RUNS = (8, 11, 12, 14, 15, 17)
AHEAD = 4
F32 = jnp.float32
BF16 = jnp.bfloat16


def grouped():
    return lax.axis_size("seq") == 4 and lax.axis_size("dp") == 8


def coordinates():
    seq, dp = lax.axis_index("seq"), lax.axis_index("dp")
    return seq // 2, seq % 2, dp // 2, dp % 2


def slot_of(y, c, z, x):
    return (y * 2 + c) * 8 + z * 2 + x


def device_of(y, c, z, x):
    return (y * 2 + c, z * 2 + x)


def greet(peers):
    barrier = pltpu.get_barrier_semaphore()
    for peer in peers:
        pl.semaphore_signal(barrier, inc=1, device_id=peer, device_id_type=MESH)
    pl.semaphore_wait(barrier, len(peers))


def six_peers(y, c, z, x):
    return [device_of(y, c, (z + k) % 4, x) for k in (1, 2, 3)] + [
        device_of(y, c, z, 1 - x),
        device_of(1 - y, c, z, x),
        device_of(y, 1 - c, z, x),
    ]


class Gather:
    def __init__(self, parts, sources, gathered, local_sem, send_sem, recv_sem, ahead=None):
        self.parts, self.sources, self.gathered = parts, sources, gathered
        self.send_sem, self.recv_sem, self.ahead = send_sem, recv_sem, ahead or AHEAD
        self.y, self.c, self.z, self.x = y, c, z, x = coordinates()
        self.me = slot_of(y, c, z, x)
        self.across_x = device_of(y, c, z, 1 - x)
        self.across_y = device_of(1 - y, c, z, x)
        self.other_core = device_of(y, 1 - c, z, x)
        self.own = [
            pltpu.make_async_copy(sources[i], gathered[i].at[self.me], local_sem.at[i])
            for i in range(len(sources))
        ]
        self.done = 0

    def place(self, p, slot):
        i, row, rows, column, columns, _ = self.parts[p]
        return self.gathered[i].at[slot, pl.ds(row, rows), pl.ds(column, columns)]

    def send(self, p, slot, target, first=False):
        i, row, rows, column, columns, _ = self.parts[p]
        source = self.sources[i].at[pl.ds(row, rows), pl.ds(column, columns)]
        pltpu.make_async_remote_copy(
            src_ref=source if first else self.place(p, slot),
            dst_ref=self.place(p, slot),
            send_sem=self.send_sem.at[p],
            recv_sem=self.recv_sem.at[p, slot],
            device_id=target,
            device_id_type=MESH,
        ).start()

    def arrived(self, p, slot):
        place = self.place(p, slot)
        pltpu.make_async_copy(place, place, self.recv_sem.at[p, slot]).wait()

    def first(self, p):
        for k in (1, 3, 2):
            self.send(p, self.me, device_of(self.y, self.c, (self.z + k) % 4, self.x), True)
        self.send(p, self.me, self.across_x, True)
        self.send(p, self.me, self.across_y, True)
        self.send(p, self.me, self.other_core, True)

    def start(self):
        for copy in self.own:
            copy.start()
        for p in range(min(self.ahead, len(self.parts))):
            self.first(p)

    def after_z(self, p):
        for k in (3, 1, 2):
            slot = slot_of(self.y, self.c, (self.z + k) % 4, self.x)
            self.arrived(p, slot)
            self.send(p, slot, self.across_x)
            self.send(p, slot, self.across_y)
            self.send(p, slot, self.other_core)

    def after_first(self, p):
        x_first = self.parts[p][5]
        for k in (0, 3, 1, 2):
            by_x = slot_of(self.y, self.c, (self.z + k) % 4, 1 - self.x)
            by_y = slot_of(1 - self.y, self.c, (self.z + k) % 4, self.x)
            self.arrived(p, by_x)
            if x_first:
                self.send(p, by_x, self.across_y)
            self.send(p, by_x, self.other_core)
            self.arrived(p, by_y)
            if not x_first:
                self.send(p, by_y, self.across_x)
            self.send(p, by_y, self.other_core)

    def after_second(self, p):
        for k in (0, 3, 1, 2):
            slot = slot_of(1 - self.y, self.c, (self.z + k) % 4, 1 - self.x)
            self.arrived(p, slot)
            self.send(p, slot, self.other_core)

    def whole(self, p):
        for side in (0, 1):
            for zz in range(4):
                for xx in (0, 1):
                    self.arrived(p, slot_of(side, 1 - self.c, zz, xx))

    def steps(self):
        return len(self.parts) + 3

    def run(self, until):
        while self.done < min(until, self.steps()):
            s, count = self.done, len(self.parts)
            if self.ahead <= s + self.ahead < count:
                self.first(s + self.ahead)
            for stage, act in enumerate(
                (self.after_z, self.after_first, self.after_second, self.whole)
            ):
                if 0 <= s - stage < count:
                    act(s - stage)
            self.done += 1

    def own_arrived(self, indices):
        for i in indices:
            self.own[i].wait()

    def finish(self):
        self.run(self.steps())
        for p, (i, row, rows, column, columns, _) in enumerate(self.parts):
            sent = self.gathered[i].at[pl.ds(0, 31), pl.ds(row, rows), pl.ds(column, columns)]
            pltpu.make_async_copy(sent, sent, self.send_sem.at[p]).wait()


def cut(arrays):
    parts = []
    for i, (rows, columns) in enumerate(arrays):
        if columns > 1536:
            width = 1536 if columns % 1536 == 0 else 768
            pieces = [(0, rows, w, width) for w in range(0, columns, width)]
        elif rows > 48:
            pieces = [(r, 48, 0, columns) for r in range(0, rows, 48)]
        else:
            pieces = [(0, rows, 0, columns)]
        for piece in pieces:
            parts.append((i,) + piece + (len(parts) % 2 == 0,))
    return parts


class Reduce:
    def __init__(self, parts, terms, totals, buffers, mine, send_sem, recv_sem, mine_sem):
        self.parts, self.terms, self.totals, self.buffers = parts, terms, totals, buffers
        self.send_sem, self.recv_sem, self.mine_sem = send_sem, recv_sem, mine_sem
        self.y, self.c, self.z, self.x = coordinates()
        self.mine, self.kinds = mine, {}
        for p, part in enumerate(parts):
            if part[0] < len(mine[0]):
                self.kinds.setdefault((part[2], part[4]), []).append(p)
        self.done = 0

    def term(self, p, core):
        i, row, rows, column, columns, _ = self.parts[p]
        return self.terms[i].at[:, core, :, :, pl.ds(row, rows), pl.ds(column, columns)]

    def fetch(self, p):
        kind = (self.parts[p][2], self.parts[p][4])
        place = self.kinds[kind].index(p)
        held = self.mine[1][kind].at[place % 2]
        return pltpu.make_async_copy(self.term(p, self.c), held, self.mine_sem.at[p]), held

    def copies(self, p, stage):
        one, two, three, four = self.buffers[4 * p : 4 * p + 4]
        y, c, z, x = self.y, self.c, self.z, self.x
        across_x, across_y = device_of(y, c, z, 1 - x), device_of(1 - y, c, z, x)
        x_last = self.parts[p][5]
        if stage == 0:
            pairs = [(self.term(p, 1 - c), one, device_of(y, 1 - c, z, x))]
        elif stage == 1 and x_last:
            pairs = [(one.at[1 - y], two, across_y)]
        elif stage == 1:
            pairs = [(one.at[:, :, 1 - x], two, across_x)]
        elif stage == 2 and x_last:
            pairs = [(two.at[:, 1 - x], three, across_x)]
        elif stage == 2:
            pairs = [(two.at[1 - y], three, across_y)]
        else:
            pairs = [
                (three.at[(z + k) % 4], four.at[k - 1], device_of(y, c, (z + k) % 4, x))
                for k in (1, 2, 3)
            ]
        return [
            pltpu.make_async_remote_copy(
                src_ref=src,
                dst_ref=dst,
                send_sem=self.send_sem.at[p, stage + n],
                recv_sem=self.recv_sem.at[p, stage + n],
                device_id=target,
                device_id_type=MESH,
            )
            for n, (src, dst, target) in enumerate(pairs)
        ]

    def add(self, p, stage):
        one, two, three, four = self.buffers[4 * p : 4 * p + 4]
        y, c, z, x = self.y, self.c, self.z, self.x
        i, row, rows, column, columns, x_last = self.parts[p]

        def total(a, b):
            return (a.astype(F32) + b.astype(F32)).astype(a.dtype)

        if stage == 0:
            if i < len(self.mine[0]):
                copy, held = self.fetch(p)
                copy.wait()
            else:
                held = self.term(p, c)

            def add_one(k, _):
                b, zz = k // 4, k % 4
                for xx in (0, 1):
                    one[b, zz, xx] = total(one[b, zz, xx], held[b, zz, xx])
                return 0

            lax.fori_loop(0, 8, add_one, 0)
            if i < len(self.mine[0]):
                same = self.kinds[(rows, columns)]
                later = same.index(p) + 2
                if later < len(same):
                    self.fetch(same[later])[0].start()
        elif stage == 1:

            def add_two(k, _):
                for h in (0, 1):
                    if x_last:
                        two[k, h] = total(two[k, h], one[y, k, h])
                    else:
                        two[h, k] = total(two[h, k], one[h, k, x])
                return 0

            lax.fori_loop(0, 4, add_two, 0)
        elif stage == 2:

            def add_three(k, _):
                three[k] = total(three[k], two[k, x] if x_last else two[y, k])
                return 0

            lax.fori_loop(0, 4, add_three, 0)
        else:
            self.totals[i][pl.ds(row, rows), pl.ds(column, columns)] = (
                three[z].astype(F32)
                + four[0].astype(F32)
                + four[1].astype(F32)
                + four[2].astype(F32)
            )

    def start(self, arrays):
        for p, part in enumerate(self.parts):
            if part[0] in arrays:
                for copy in self.copies(p, 0):
                    copy.start()

    def fetch_first(self):
        for same in self.kinds.values():
            for p in same[:2]:
                self.fetch(p)[0].start()

    def steps(self):
        return len(self.parts) + LAGS[3]

    def run(self, until):
        while self.done < min(until, self.steps()):
            for stage in range(4):
                p = self.done - LAGS[stage]
                if 0 <= p < len(self.parts):
                    for copy in self.copies(p, stage):
                        copy.wait_recv()
                    self.add(p, stage)
                    if stage < 3:
                        for copy in self.copies(p, stage + 1):
                            copy.start()
            self.done += 1

    def finish(self):
        self.run(self.steps())
        for p in range(len(self.parts)):
            for stage in range(4):
                for copy in self.copies(p, stage):
                    copy.wait_send()


def all_others():
    rows, groups = lax.axis_size("seq"), lax.axis_size("dp")
    count = rows * groups
    me = lax.axis_index("seq") * groups + lax.axis_index("dp")
    others = [lax.rem(me + k, count) for k in range(1, count)]
    return me, others, [(o // groups, lax.rem(o, groups)) for o in others]


class Swap:
    def __init__(self, src, dst, send_sem, recv_sem):
        self.src, self.dst, self.send_sem, self.recv_sem = src, dst, send_sem, recv_sem

    def start(self):
        me, others, places = all_others()
        for o, place in zip(others, places):
            pltpu.make_async_remote_copy(
                src_ref=self.src.at[o],
                dst_ref=self.dst.at[me],
                send_sem=self.send_sem,
                recv_sem=self.recv_sem,
                device_id=place,
                device_id_type=MESH,
            ).start()

    def wait(self):
        most = pl.ds(0, self.src.shape[0] - 1)
        me = all_others()[0]
        pltpu.make_async_copy(self.src.at[most], self.dst.at[most], self.recv_sem).wait()
        pltpu.make_async_copy(self.src.at[most], self.dst.at[most], self.send_sem).wait()
        self.dst[me] = self.src[me]


def layer_norm(residual, scale_gain):
    average = jnp.mean(residual, axis=-1, keepdims=True)
    centered = residual - average
    variance = jnp.mean(centered * centered, axis=-1, keepdims=True)
    return centered * lax.rsqrt(variance + EPSILON) * scale_gain


def contract(left_side, right_side, left_dim, right_dim):
    return lax.dot_general(
        left_side,
        right_side,
        (((left_dim,), (right_dim,)), ((), ())),
        preferred_element_type=F32,
    )


def product(left_side, right_side):
    return contract(left_side, right_side, 1, 0)


def product_back(left_side, right_side):
    return contract(left_side, right_side, 1, 1)


def product_sum(left_side, right_side):
    return contract(left_side, right_side, 0, 0)


def feed_forward(residual, scale_gain, up_weight, down_weight):
    normed = layer_norm(residual, scale_gain).astype(BF16)
    pre_act = product(normed, up_weight)
    activated = jax.nn.gelu(pre_act).astype(BF16)
    return (residual + product(activated, down_weight), (normed, pre_act, activated))


def feed_back(residual, scale_gain, up_weight, down_weight, stored, grad_residual):
    normed, pre_act, activated = stored
    grad_branch = grad_residual.astype(BF16)
    grad_down = product_sum(activated, grad_branch)
    grad_activated = product_back(grad_branch, down_weight)
    gelu_pull = jax.vjp(jax.nn.gelu, pre_act)[1]
    grad_pre = gelu_pull(grad_activated)[0].astype(BF16)
    grad_up = product_sum(normed, grad_pre)
    grad_normed = product_back(grad_pre, up_weight)
    norm_pull = jax.vjp(layer_norm, residual, scale_gain)[1]
    grad_input, grad_gain = norm_pull(grad_normed)
    return (grad_residual + grad_input, grad_gain, grad_up, grad_down)


def ssm_kernel(decay_log, turn_angle, mix_real, mix_imag, length):
    rate = jnp.exp(decay_log)[:, :, None]
    angle = turn_angle[:, :, None]
    step = 32

    def powers(times):
        return (
            jnp.exp(-times * rate) * jnp.cos(times * angle),
            jnp.exp(-times * rate) * jnp.sin(times * angle),
        )

    low_real, low_imag = powers(jnp.arange(step, dtype=F32)[None, None])
    high_real, high_imag = powers(
        (step * jnp.arange(length // step, dtype=jnp.int32)).astype(F32)[None, None]
    )
    real, imag = mix_real[:, :, None], mix_imag[:, :, None]
    high = jnp.concatenate(
        [real * high_real - imag * high_imag, -(real * high_imag + imag * high_real)], axis=1
    )
    low = jnp.concatenate([low_real, low_imag], axis=1)
    kernel = jnp.einsum("cna,cnb->cab", high, low, precision=HIGHEST)
    return kernel.reshape(decay_log.shape[0], length)


def toeplitz(row, rows):
    spread = jnp.broadcast_to(row, (rows, row.shape[1]))
    return pltpu.roll(spread, 0, 1, stride=1, stride_axis=0)


def block_sum(mixed, blocks, groups, rows):
    total = mixed[:, :rows]
    for d in range(1, blocks):
        piece = mixed[: (blocks - d) * groups, d * rows : (d + 1) * rows]
        total = total + jnp.concatenate(
            [jnp.zeros((d * groups, rows), piece.dtype), piece], axis=0
        )
    return total


def block_spread(value, blocks, lags, groups, rows):
    pieces = [value]
    for d in range(1, lags):
        pieces.append(
            jnp.concatenate(
                [value[d * groups :], jnp.zeros((d * groups, rows), value.dtype)], axis=0
            )
        )
    return jnp.concatenate(pieces, axis=1)


def mix(blocks, groups, rows, keys, values, tap_row, kernel_row, skip):
    span = blocks * rows
    taps = toeplitz(tap_row, rows)[:, : 2 * rows].astype(BF16)
    longer = toeplitz(kernel_row, rows)[:, :span].astype(BF16)
    near = product(keys, taps)
    shifted = near[:, :rows] + jnp.concatenate(
        [jnp.zeros((groups, rows), F32), near[: (blocks - 1) * groups, rows:]], axis=0
    )
    signal = shifted * values.astype(F32)
    mixed = product(signal.astype(BF16), longer)
    return shifted, block_sum(mixed, blocks, groups, rows) + skip * signal


def mixer_body(blocks, groups, rows, k_ref, v_ref, taps_ref, kernel_ref, skip_ref, shifted_ref, out_ref):
    for ch in range(k_ref.shape[0]):
        row = slice(ch, ch + 1)
        shifted_ref[ch], out = mix(
            blocks, groups, rows, k_ref[ch], v_ref[ch],
            taps_ref[row, :], kernel_ref[row, :], skip_ref[row, :1],
        )
        out_ref[ch] = out.astype(BF16)


def flat_weight(ref):
    wide = ref[...].astype(F32)
    return wide.reshape(wide.shape[0] * wide.shape[1], wide.shape[2]).astype(BF16)


def flat_part(ref, first, width):
    wide = ref[:, :, first : first + width].astype(F32)
    return wide.reshape(wide.shape[0] * wide.shape[1], width).astype(BF16)


def first_body(parts, count, *refs):
    sources = refs[:count]
    tokens, live, key_live, taps_ref, kernel_ref, skip_ref = refs[count : count + 6]
    refs = refs[count + 6 :]
    gathered = refs[:count]
    (
        residual_ref, standard_ref, inverse_ref, normed_ref, queries_ref, ssm_ref, gated_ref,
        k_ref, v_ref, shifted_ref,
        normed_two, pre_one, act_one, residual_two, normed_three, att_q, att_kv, attended,
        log_total, residual_three,
    ) = refs[count : count + 20]
    (
        wide, sent_kv, came_kv, sent_y, came_y, up, down, qkv, out_two,
        local_sem, send_sem, recv_sem, swap_sem, load_sem, line_send, line_recv,
    ) = refs[count + 20 :]
    gains, key_all, value_all, query_all, out_all = gathered[:5]
    devices, channels = key_all.shape[0], key_all.shape[1]
    rows, features = tokens.shape
    blocks, groups = lax.axis_size("seq"), lax.axis_size("dp")
    greet(all_others()[2])
    gather = Gather(parts, sources, gathered, local_sem, send_sem, recv_sem)
    gather.start()

    turned = tokens[...].astype(F32).T
    centered = turned - jnp.mean(turned, axis=0, keepdims=True)
    inverse = lax.rsqrt(jnp.mean(centered * centered, axis=0, keepdims=True) + EPSILON)
    inverse_ref[...] = jnp.broadcast_to(inverse, inverse_ref.shape)
    standard_ref[...] = centered * inverse

    gather.run(RUNS[0])
    gather.own_arrived(range(5))
    all_gains = gains[...].reshape(features, 128)
    normed_ref[...] = (standard_ref[...] * all_gains[:, :1]).astype(BF16)

    def projected(weight):
        return contract(flat_weight(weight), normed_ref[...], 0, 0)

    wide[:, :channels, :] = projected(key_all).reshape(devices, channels, rows)
    wide[:, channels:, :] = (projected(value_all) * live[...]).reshape(devices, channels, rows)
    sent_kv[...] = wide[...].astype(BF16)
    over = Swap(sent_kv, came_kv, swap_sem.at[0], swap_sem.at[1])
    over.start()
    queries_ref[...] = projected(query_all)
    gather.run(RUNS[1])
    over.wait()
    wide[...] = came_kv[...].astype(F32)
    for ch in range(channels):
        row = slice(ch, ch + 1)
        k_ref[ch] = wide[:, ch, :].astype(BF16)
        v_ref[ch] = wide[:, channels + ch, :].astype(BF16)
        shifted_ref[ch], out = mix(
            blocks, groups, rows, k_ref[ch], v_ref[ch],
            taps_ref[row, :], kernel_ref[row, :], skip_ref[row, :1],
        )
        wide[:, ch, :] = out
        if ch == channels // 2:
            gather.run(RUNS[2])
    sent_y[...] = wide[:, :channels, :].astype(BF16)
    back = Swap(sent_y, came_y, swap_sem.at[2], swap_sem.at[3])
    back.start()
    gather.run(RUNS[3])
    gather.own_arrived(range(5, count))
    loads = [
        pltpu.make_async_copy(gathered[5 + n], held, load_sem.at[n])
        for n, held in enumerate((up, down, qkv, out_two))
    ]
    loads[0].start()
    loads[1].start()
    back.wait()
    ssm = came_y[...].astype(F32).reshape(features, rows)
    ssm_ref[...] = ssm.astype(BF16)
    gated_ref[...] = (queries_ref[...] * ssm).astype(BF16)
    residual_ref[...] = tokens[...].astype(F32) + contract(
        gated_ref[...], flat_weight(out_all), 0, 0
    )

    gain_rows = all_gains.T
    normed_two[...] = layer_norm(residual_ref[...], gain_rows[1:2]).astype(BF16)
    loads[0].wait()
    for first in range(0, up.shape[2], features):
        own = slice(first, first + features)
        pre = product(normed_two[...], flat_part(up, first, features))
        pre_one[:, own] = pre
        act_one[:, own] = jax.nn.gelu(pre).astype(BF16)
    loads[1].wait()
    down_flat = down[...].reshape(-1, features)
    residual_two[...] = residual_ref[...] + product(act_one[...], down_flat)
    normed_three[...] = layer_norm(residual_two[...], gain_rows[2:3]).astype(BF16)
    gather.run(RUNS[4])
    loads[2].start()
    loads[2].wait()
    y, c, z, x = coordinates()
    me = y * 2 + c
    for first in range(0, 2 * features, features):
        joint = product(normed_three[...], flat_part(qkv, features + first, features))
        att_kv[me, :, first : first + features] = joint.astype(BF16)
    core, side = device_of(y, 1 - c, z, x), device_of(1 - y, c, z, x)

    def pass_on(n, slot, target):
        return pltpu.make_async_remote_copy(
            src_ref=att_kv.at[slot],
            dst_ref=att_kv.at[slot],
            send_sem=line_send.at[n],
            recv_sem=line_recv.at[n],
            device_id=target,
            device_id_type=MESH,
        )

    def taken(n, slot):
        pltpu.make_async_copy(att_kv.at[slot], att_kv.at[slot], line_recv.at[n]).wait()

    far = (1 - y) * 2 + c
    passed = [pass_on(0, me, side), pass_on(1, me, core), pass_on(2, far, core)]
    passed[0].start()
    passed[1].start()
    att_q[...] = product(normed_three[...], flat_part(qkv, 0, features)).astype(BF16)
    taken(0, far)
    passed[2].start()
    gather.run(RUNS[5])
    loads[3].start()
    taken(1, y * 2 + 1 - c)
    taken(2, (1 - y) * 2 + 1 - c)
    keys = blocks * rows
    row_places = me * rows + lax.broadcasted_iota(jnp.int32, (rows, keys), 0)
    key_places = lax.broadcasted_iota(jnp.int32, (rows, keys), 1)
    hidden = jnp.where(key_places <= row_places, key_live[...], 0.0)
    attend_heads(
        hidden > 0.5, att_q, att_kv[...].reshape(keys, 2 * features), attended, log_total
    )
    loads[3].wait()
    residual_three[...] = residual_two[...] + product(attended[...], flat_weight(out_two))
    for each in passed:
        each.wait_send()
    gather.finish()


def first_layer(weights, tokens, live, key_live, tap_row, kernel_row, skip_row, collective_id):
    count = len(weights)
    blocks, groups = lax.axis_size("seq"), lax.axis_size("dp")
    devices = blocks * groups
    rows, features = tokens.shape
    channels = features // devices
    parts = cut([a.shape for a in weights])
    vmem, anywhere = pl.BlockSpec(memory_space=pltpu.VMEM), pl.BlockSpec(memory_space=pl.ANY)
    turned = (features, rows)
    per_channel = (channels, devices, rows)
    results = [
        ((rows, features), F32), (turned, F32), ((8, rows), F32), (turned, BF16), (turned, F32),
        (turned, BF16), (turned, BF16), (per_channel, BF16), (per_channel, BF16), (per_channel, F32),
    ]
    hidden = weights[5].shape[1]
    results += [
        ((rows, features), BF16), ((rows, hidden), F32), ((rows, hidden), BF16),
        ((rows, features), F32), ((rows, features), BF16), ((rows, features), BF16),
        ((blocks, rows, 2 * features), BF16), ((rows, features), BF16), ((rows, 128), F32),
        ((rows, features), F32),
    ]
    out = pl.pallas_call(
        partial(first_body, parts, count),
        out_shape=[jax.ShapeDtypeStruct((devices,) + a.shape, a.dtype) for a in weights]
        + [jax.ShapeDtypeStruct(*r) for r in results],
        in_specs=[anywhere] * count + [vmem] * 6,
        out_specs=[vmem] * 5 + [anywhere] * (count - 5) + [vmem] * len(results),
        scratch_shapes=[
            pltpu.VMEM((devices, 2 * channels, rows), F32),
            pltpu.VMEM((devices, 2 * channels, rows), BF16),
            pltpu.VMEM((devices, 2 * channels, rows), BF16),
            pltpu.VMEM((devices, channels, rows), BF16),
            pltpu.VMEM((devices, channels, rows), BF16),
        ]
        + [pltpu.VMEM((devices,) + a.shape, BF16) for a in weights[5:9]]
        + [
            pltpu.SemaphoreType.DMA((count,)),
            pltpu.SemaphoreType.DMA((len(parts),)),
            pltpu.SemaphoreType.DMA((len(parts), devices)),
            pltpu.SemaphoreType.DMA((4,)),
            pltpu.SemaphoreType.DMA((4,)),
            pltpu.SemaphoreType.DMA((3,)),
            pltpu.SemaphoreType.DMA((3,)),
        ],
        compiler_params=pltpu.CompilerParams(
            collective_id=collective_id, has_side_effects=True, vmem_limit_bytes=60 * MIB
        ),
    )(*weights, tokens, live, key_live, tap_row, kernel_row, skip_row)
    return out[:count], out[count:]


def first_layer_apart(weights, tokens, live, key_live, tap_row, kernel_row, skip_row):
    blocks, groups = lax.axis_size("seq"), lax.axis_size("dp")
    devices = blocks * groups
    rows, features = tokens.shape
    channels = features // devices
    every = [lax.all_gather(a, BOTH, axis=0) for a in weights]
    gain = every[0][:, :, 0].reshape(features, 1)
    key_all, value_all, query_all, out_all = [a.reshape(features, -1) for a in every[1:5]]
    turned = tokens.astype(F32).T
    centered = turned - jnp.mean(turned, axis=0, keepdims=True)
    inverse = lax.rsqrt(jnp.mean(centered * centered, axis=0, keepdims=True) + EPSILON)
    standard = centered * inverse
    normed = (standard * gain).astype(BF16)
    queries = contract(query_all, normed, 0, 0)
    keys = contract(key_all, normed, 0, 0).astype(BF16)
    values = (contract(value_all, normed, 0, 0) * live).astype(BF16)
    sent = jnp.stack([a.reshape(devices, channels, rows) for a in (keys, values)], axis=1)
    k_own, v_own = lax.all_to_all(sent, BOTH, 0, 0, tiled=True).transpose(1, 2, 0, 3)
    per_channel = (channels, devices, rows)
    shifted, mixed = local_call(
        partial(mixer_body, blocks, groups, rows),
        [jax.ShapeDtypeStruct(per_channel, F32), jax.ShapeDtypeStruct(per_channel, BF16)],
        k_own, v_own, tap_row, kernel_row, skip_row,
    )
    ssm = lax.all_to_all(mixed.transpose(1, 0, 2), BOTH, 0, 0, tiled=True)
    ssm = ssm.reshape(features, rows)
    gated = (queries * ssm.astype(F32)).astype(BF16)
    residual = tokens.astype(F32) + contract(gated, out_all, 0, 0)
    inverse = jnp.broadcast_to(inverse, (8, rows))
    kept = [residual, standard, inverse, normed, queries, ssm, gated, k_own, v_own, shifted]
    up, down, qkv, out_two = [a.reshape(-1, a.shape[2]) for a in every[5:9]]
    residual_two, stored = feed_forward(residual, every[0][:, :, 1].reshape(features), up, down)
    normed_three = layer_norm(residual_two, every[0][:, :, 2].reshape(features)).astype(BF16)
    joint = product(normed_three, qkv).astype(BF16)
    att_q = joint[:, :features]
    att_kv = lax.all_gather(joint[:, features:], "seq", axis=0)
    where = jnp.stack([lax.axis_index("seq").astype(F32) * rows, jnp.sum(key_live)])
    attended, log_total = local_call(
        attend_body,
        [jax.ShapeDtypeStruct((rows, features), BF16), jax.ShapeDtypeStruct((rows, 128), F32)],
        where.astype(jnp.int32), att_q, att_kv.reshape(blocks * rows, 2 * features), scalars=1,
    )
    residual_three = residual_two + product(attended, out_two)
    kept += [*stored, residual_two, normed_three, att_q, att_kv, attended, log_total]
    return every, kept + [residual_three]


def mix_back(
    blocks, groups, rows, out_grad, keys, values, shifted, tap_row, kernel_row, skip
):
    span = blocks * rows
    turned = (
        lax.broadcasted_iota(jnp.int32, (rows, rows), 0)
        + lax.broadcasted_iota(jnp.int32, (rows, rows), 1)
        == rows - 1
    ).astype(BF16)

    def lag_sums(earlier, spread, lanes):
        backward = product(earlier, turned).astype(BF16)
        pairs = product_sum(backward, spread)
        padded = jnp.concatenate(
            [pairs, jnp.zeros((rows, lanes - pairs.shape[1]), F32)], axis=1
        )
        return jnp.sum(
            pltpu.roll(padded, lanes - rows + 1, 1, stride=1, stride_axis=0),
            axis=0,
            keepdims=True,
        )

    taps = toeplitz(tap_row, rows)[:, : 2 * rows].astype(BF16)
    longer = toeplitz(kernel_row, rows)[:, :span].astype(BF16)
    values = values.astype(F32)
    signal = shifted * values
    later = block_spread(out_grad, blocks, blocks, groups, rows).astype(BF16)
    signal_grad = product_back(later, longer) + skip * out_grad
    kernel_grad = lag_sums(signal.astype(BF16), later, kernel_row.shape[1])
    skip_grad = jnp.sum(jnp.sum(signal * out_grad, axis=0, keepdims=True), axis=1, keepdims=True)
    shifted_grad = values * signal_grad
    next_two = block_spread(shifted_grad, blocks, 2, groups, rows).astype(BF16)
    return (
        product_back(next_two, taps),
        shifted * signal_grad,
        kernel_grad,
        lag_sums(keys, next_two, tap_row.shape[1]),
        skip_grad,
    )


def mixer_back_body(
    blocks, groups, rows,
    grad_ref, k_ref, v_ref, shifted_ref, taps_ref, kernel_ref, skip_ref,
    grad_k_ref, grad_v_ref, kernel_grad_ref, taps_grad_ref, skip_grad_ref,
):
    for ch in range(k_ref.shape[0]):
        row = slice(ch, ch + 1)
        grad_k, grad_v, kernel_grad_ref[row, :], taps_grad_ref[row, :], skip_grad = mix_back(
            blocks, groups, rows, grad_ref[ch].astype(F32), k_ref[ch], v_ref[ch], shifted_ref[ch],
            taps_ref[row, :], kernel_ref[row, :], skip_ref[row, :1],
        )
        grad_k_ref[ch], grad_v_ref[ch] = grad_k.astype(BF16), grad_v.astype(BF16)
        skip_grad_ref[row, :] = jnp.broadcast_to(skip_grad, (1, 128))


def last_body(parts, count, kinds, *refs):
    early = refs[:count]
    (
        gain_in, branch, grad_one, live, gated, normed, queries, ssm, standard, inverse,
        gains, key_all, value_all, query_all, out_all,
        k_ref, v_ref, shifted_ref, taps_ref, kernel_ref, skip_ref,
    ) = refs[count : count + 21]
    refs = refs[count + 21 :]
    totals = refs[: count + 5]
    input_grad, kernel_grad_ref, taps_grad_ref, skip_grad_ref = refs[count + 5 : count + 9]
    refs = refs[count + 9 :]
    out_term, query_term, key_term, value_term, gain_term = own_terms = refs[:5]
    buffers = refs[5 : 5 + 4 * len(parts)]
    refs = refs[5 + 4 * len(parts) :]
    held = dict(zip(kinds, refs[: len(kinds)]))
    (
        wide, sent_g, came_g, sent_kv, came_kv, query_grad,
        send_sem, recv_sem, mine_sem, swap_sem,
    ) = refs[len(kinds) :]
    devices, channels = key_all.shape[0], key_all.shape[1]
    rows, features = branch.shape
    blocks, groups = lax.axis_size("seq"), lax.axis_size("dp")
    greet(all_others()[2])
    reduce = Reduce(
        parts, early + own_terms, totals, buffers, (early, held), send_sem, recv_sem, mine_sem
    )
    reduce.fetch_first()

    def slots(value, columns):
        return value.reshape(2, 2, 4, 2, channels, columns)

    gated_grad = contract(flat_weight(out_all), branch[...], 1, 1)
    sent_g[...] = (gated_grad * queries[...]).reshape(devices, channels, rows).astype(BF16)
    over = Swap(sent_g, came_g, swap_sem.at[0], swap_sem.at[1])
    over.start()
    reduce.start(range(count))
    query_grad[...] = (gated_grad * ssm[...].astype(F32)).astype(BF16)
    out_term[...] = slots(product(gated[...], branch[...]), features).astype(BF16)
    query_term[...] = slots(contract(normed[...], query_grad[...], 1, 1), features).astype(BF16)
    reduce.start((count, count + 1))
    reduce.run(PLACES[0])
    over.wait()
    wide[:, :channels, :] = came_g[...].astype(F32)
    for ch in range(channels):
        row = slice(ch, ch + 1)
        grad_k, grad_v, kernel_grad_ref[row, :], taps_grad_ref[row, :], skip_grad = mix_back(
            blocks, groups, rows, wide[:, ch, :], k_ref[ch], v_ref[ch], shifted_ref[ch],
            taps_ref[row, :], kernel_ref[row, :], skip_ref[row, :1],
        )
        wide[:, ch, :], wide[:, channels + ch, :] = grad_k, grad_v
        skip_grad_ref[row, :] = jnp.broadcast_to(skip_grad, (1, 128))
        if ch % 8 == 7:
            reduce.run(PLACES[1 + ch // 8])
    sent_kv[...] = wide[...].astype(BF16)
    back = Swap(sent_kv, came_kv, swap_sem.at[2], swap_sem.at[3])
    back.start()
    reduce.run(PLACES[4])
    back.wait()
    wide[...] = came_kv[...].astype(F32)
    key_grad = wide[:, :channels, :].reshape(features, rows).astype(BF16)
    value_grad = (wide[:, channels:, :].reshape(features, rows) * live[...]).astype(BF16)
    key_term[...] = slots(contract(normed[...], key_grad, 1, 1), features).astype(BF16)
    value_term[...] = slots(contract(normed[...], value_grad, 1, 1), features).astype(BF16)
    reduce.start((count + 2, count + 3))
    normed_grad = product(flat_weight(query_all), query_grad[...])
    normed_grad += product(flat_weight(key_all), key_grad)
    normed_grad += product(flat_weight(value_all), value_grad)
    gain_grad = jnp.sum(normed_grad * standard[...], axis=1, keepdims=True)
    lane = lax.broadcasted_iota(jnp.int32, (features, 128), 1)
    gain_term[...] = slots(jnp.where(lane == 0, gain_grad, gain_in[...]), 128)
    reduce.start((count + 4,))
    scaled = normed_grad * gains[...].reshape(features, 128)[:, :1]
    scaled = (
        scaled
        - jnp.mean(scaled, axis=0, keepdims=True)
        - standard[...] * jnp.mean(scaled * standard[...], axis=0, keepdims=True)
    )
    input_grad[...] = grad_one[...] + (scaled * inverse[:1, :]).T
    reduce.finish()


def last_layer(terms, gain_in, branch, grad_one, live, kept, weights, mixer_rows, collective_id):
    standard, inverse, normed, queries, ssm, gated, k_own, v_own, shifted = kept
    gains, key_all, value_all, query_all, out_all = weights
    devices, channels, features = key_all.shape
    rows = branch.shape[0]
    count = len(terms)
    square = (channels, features)
    shapes = [a.shape[1:] for a in terms] + [square] * 4 + [(channels, 128)]
    types = [BF16] * (count + 4) + [F32]
    parts = cut(shapes)
    kinds = sorted({(part[2], part[4]) for part in parts if part[0] < count})
    scratch = [pltpu.VMEM((2, 2, 4, 2) + s, t) for s, t in zip(shapes[count:], types[count:])]
    for i, _, part_rows, _, columns, x_last in parts:
        for lead in ((2, 4, 2), (4, 2) if x_last else (2, 4), (4,), (3,)):
            scratch.append(pltpu.VMEM(lead + (part_rows, columns), types[i]))
    scratch += [pltpu.VMEM((2, 2, 4, 2) + kind, BF16) for kind in kinds]
    scratch += [
        pltpu.VMEM((devices, 2 * channels, rows), F32),
        pltpu.VMEM((devices, channels, rows), BF16),
        pltpu.VMEM((devices, channels, rows), BF16),
        pltpu.VMEM((devices, 2 * channels, rows), BF16),
        pltpu.VMEM((devices, 2 * channels, rows), BF16),
        pltpu.VMEM((features, rows), BF16),
        pltpu.SemaphoreType.DMA((len(parts), 6)),
        pltpu.SemaphoreType.DMA((len(parts), 6)),
        pltpu.SemaphoreType.DMA((len(parts),)),
        pltpu.SemaphoreType.DMA((4,)),
    ]
    vmem, anywhere = pl.BlockSpec(memory_space=pltpu.VMEM), pl.BlockSpec(memory_space=pl.ANY)
    results = [jax.ShapeDtypeStruct(s, F32) for s in shapes]
    results.append(jax.ShapeDtypeStruct((rows, features), F32))
    results += [jax.ShapeDtypeStruct(a.shape, F32) for a in (mixer_rows[1], mixer_rows[0])]
    results.append(jax.ShapeDtypeStruct((channels, 128), F32))
    out = pl.pallas_call(
        partial(last_body, parts, count, kinds),
        out_shape=results,
        in_specs=[anywhere] * count + [vmem] * 21,
        out_specs=[vmem] * len(results),
        scratch_shapes=scratch,
        compiler_params=pltpu.CompilerParams(
            collective_id=collective_id, has_side_effects=True, vmem_limit_bytes=62 * MIB
        ),
    )(
        *[a.reshape((2, 2, 4, 2) + a.shape[1:]) for a in terms],
        gain_in, branch, grad_one, live, gated, normed, queries, ssm, standard, inverse,
        gains, key_all, value_all, query_all, out_all,
        k_own, v_own, shifted, *mixer_rows,
    )
    return out[: count + 5], out[count + 5 :]


def last_layer_apart(terms, gain_in, branch, grad_one, live, kept, weights, mixer_rows):
    standard, inverse, normed, queries, ssm, gated, k_own, v_own, shifted = kept
    gains, key_all, value_all, query_all, out_all = weights
    devices, channels, features = key_all.shape
    rows = branch.shape[0]
    blocks, groups = lax.axis_size("seq"), lax.axis_size("dp")
    key_all, value_all, query_all, out_all = [
        a.reshape(features, features) for a in (key_all, value_all, query_all, out_all)
    ]
    gated_grad = contract(out_all, branch, 1, 1)
    query_grad = (gated_grad * ssm.astype(F32)).astype(BF16)
    sent = (gated_grad * queries).reshape(devices, channels, rows).astype(BF16)
    own = lax.all_to_all(sent, BOTH, 0, 0, tiled=True).transpose(1, 0, 2)
    per_channel = jax.ShapeDtypeStruct(own.shape, BF16)
    grad_k, grad_v, kernel_grad, taps_grad, skip_grad = local_call(
        partial(mixer_back_body, blocks, groups, rows),
        [per_channel, per_channel]
        + [jax.ShapeDtypeStruct(a.shape, F32) for a in (mixer_rows[1], mixer_rows[0])]
        + [jax.ShapeDtypeStruct((channels, 128), F32)],
        own, k_own, v_own, shifted, *mixer_rows,
    )
    sent = jnp.stack([grad_k.transpose(1, 0, 2), grad_v.transpose(1, 0, 2)], axis=1)
    came = lax.all_to_all(sent, BOTH, 0, 0, tiled=True)
    key_grad = came[:, 0].reshape(features, rows)
    value_grad = (came[:, 1].reshape(features, rows) * live).astype(BF16)
    normed_grad = (
        product(query_all, query_grad) + product(key_all, key_grad) + product(value_all, value_grad)
    )
    gain_grad = jnp.sum(normed_grad * standard, axis=1, keepdims=True)
    lane = lax.broadcasted_iota(jnp.int32, (features, 128), 1)
    gain_term = jnp.where(lane == 0, gain_grad, gain_in)
    scaled = normed_grad * gains.reshape(features, 128)[:, :1]
    scaled = (
        scaled
        - jnp.mean(scaled, axis=0, keepdims=True)
        - standard * jnp.mean(scaled * standard, axis=0, keepdims=True)
    )
    input_grad = grad_one + (scaled * inverse[:1]).T
    last = [product(gated, branch)]
    last += [contract(normed, g, 1, 1) for g in (query_grad, key_grad, value_grad)]
    last = [a.reshape(devices, channels, features).astype(BF16) for a in last]
    last.append(gain_term.reshape(devices, channels, 128))
    sums = [
        lax.psum_scatter(a, BOTH, scatter_dimension=0, tiled=False).astype(F32)
        for a in list(terms) + last
    ]
    return sums, [input_grad, kernel_grad, taps_grad, skip_grad]


def allowed_keys(first, length, rows, keys):
    row_places = first + lax.broadcasted_iota(jnp.int32, (rows, keys), 0)
    key_places = lax.broadcasted_iota(jnp.int32, (rows, keys), 1)
    return (key_places <= row_places) & (key_places < length)


def attend_heads(allowed, q_ref, kv, out_ref, log_ref):
    features = q_ref.shape[1]
    for head in range(HEADS):
        own = slice(head * HDIM, (head + 1) * HDIM)
        values = slice(features + head * HDIM, features + (head + 1) * HDIM)
        scores = product_back(q_ref[:, own], kv[:, own]) * HDIM ** (-0.5)
        scores = jnp.where(allowed, scores, MASKED)
        most = jnp.max(scores, axis=1, keepdims=True)
        powers = jnp.exp(scores - most)
        total = jnp.sum(powers, axis=1, keepdims=True)
        weights = (powers * (1.0 / total)).astype(BF16)
        out_ref[:, own] = product(weights, kv[:, values]).astype(BF16)
        log_ref[:, head : head + 1] = most + jnp.log(total)


def attend_body(where_ref, q_ref, kv_ref, out_ref, log_ref):
    allowed = allowed_keys(where_ref[0], where_ref[1], q_ref.shape[0], kv_ref.shape[0])
    attend_heads(allowed, q_ref, kv_ref, out_ref, log_ref)


def attend_back_head(head, allowed, q_ref, kv, log_ref, grad_ref):
    features = q_ref.shape[1]
    scale = HDIM ** (-0.5)
    own = slice(head * HDIM, (head + 1) * HDIM)
    values = slice(features + head * HDIM, features + (head + 1) * HDIM)
    queries, grads = q_ref[:, own], grad_ref[:, own]
    scores = product_back(queries, kv[:, own]) * scale
    probs = jnp.where(allowed, jnp.exp(scores - log_ref[:, head : head + 1]), 0.0)
    prob_grad = product_back(grads, kv[:, values])
    delta = jnp.sum(probs * prob_grad, axis=1, keepdims=True)
    grad_scores = (probs * (prob_grad - delta)).astype(BF16)
    return (
        (product(grad_scores, kv[:, own]) * scale).astype(BF16),
        (product_sum(grad_scores, queries) * scale).astype(BF16),
        product_sum(probs.astype(BF16), grads).astype(BF16),
    )


def attend_back_body(where_ref, q_ref, kv_ref, log_ref, grad_ref, grad_q_ref, grad_kv_ref):
    features = q_ref.shape[1]
    allowed = allowed_keys(where_ref[0], where_ref[1], q_ref.shape[0], kv_ref.shape[0])
    for head in range(HEADS):
        own = slice(head * HDIM, (head + 1) * HDIM)
        values = slice(features + head * HDIM, features + (head + 1) * HDIM)
        grad_q_ref[:, own], grad_kv_ref[:, own], grad_kv_ref[:, values] = attend_back_head(
            head, allowed, q_ref, kv_ref, log_ref, grad_ref
        )


def norm_back(residual, gain_row, grad):
    average = jnp.mean(residual, axis=-1, keepdims=True)
    centered = residual - average
    inverse = lax.rsqrt(jnp.mean(centered * centered, axis=-1, keepdims=True) + EPSILON)
    standard = centered * inverse
    scaled = grad * gain_row
    inner = jnp.mean(scaled * standard, axis=-1, keepdims=True)
    grad_input = inverse * (scaled - jnp.mean(scaled, axis=-1, keepdims=True) - standard * inner)
    return grad_input, jnp.sum(grad * standard, axis=0, keepdims=True)


def middle_body(parts, count, kinds, *refs):
    early = refs[:count]
    qkv_all, up_all, down_all = refs[count : count + 3]
    (
        att_q, att_kv, log_total, grad_attended, key_live, normed_three, residual_two,
        grad_three, gains, act_one, pre_one, normed_two, residual_one,
    ) = refs[count + 3 : count + 16]
    refs = refs[count + 16 :]
    totals = refs[:count]
    qkv_out, up_out, down_out, grad_one, gain_grads = refs[count : count + 5]
    refs = refs[count + 5 :]
    buffers = refs[: 4 * len(parts)]
    refs = refs[4 * len(parts) :]
    held = dict(zip(kinds, refs[: len(kinds)]))
    (
        qkv, up, down, grad_q, grad_kv, line_one, line_two,
        send_sem, recv_sem, mine_sem, load_sem, store_sem, line_send, line_recv,
    ) = refs[len(kinds) :]
    rows, features = att_q.shape
    keys = att_kv.shape[0] * rows
    y, c, z, x = coordinates()
    greet(six_peers(y, c, z, x))
    loads = [
        pltpu.make_async_copy(src, dst, load_sem.at[n])
        for n, (src, dst) in enumerate(((qkv_all, qkv), (up_all, up), (down_all, down)))
    ]
    stores = [
        pltpu.make_async_copy(src, dst, store_sem.at[n])
        for n, (src, dst) in enumerate(((qkv, qkv_out), (up, up_out), (down, down_out)))
    ]
    reduce = Reduce(
        parts, early, totals, buffers, (early, held), send_sem, recv_sem, mine_sem
    )
    reduce.fetch_first()
    reduce.start(range(count))
    for load in loads:
        load.start()
    gain_rows = gains[...].reshape(features, 128).T

    row_places = (y * 2 + c) * rows + lax.broadcasted_iota(jnp.int32, (rows, keys), 0)
    key_places = lax.broadcasted_iota(jnp.int32, (rows, keys), 1)
    allowed = jnp.where(key_places <= row_places, key_live[...], 0.0) > 0.5
    kv = att_kv[...].reshape(keys, 2 * features)
    for head in range(HEADS):
        own = slice(head * HDIM, (head + 1) * HDIM)
        values = slice(features + head * HDIM, features + (head + 1) * HDIM)
        grad_q[:, own], key_grad, value_grad = attend_back_head(
            head, allowed, att_q, kv, log_total, grad_attended
        )
        grad_kv[:, :, :, own] = key_grad.reshape(2, 2, rows, HDIM)
        grad_kv[:, :, :, values] = value_grad.reshape(2, 2, rows, HDIM)
        if head % 4 == 3:
            reduce.run(MIDDLE[head // 4])

    core, side = device_of(y, 1 - c, z, x), device_of(1 - y, c, z, x)

    def line_copy(n, source, target, where):
        return pltpu.make_async_remote_copy(
            src_ref=source,
            dst_ref=where,
            send_sem=line_send.at[n],
            recv_sem=line_recv.at[n],
            device_id=target,
            device_id_type=MESH,
        )

    far = line_copy(0, grad_kv.at[1 - y, 1 - c], core, line_one.at[1 - y])
    near = line_copy(1, grad_kv.at[y, 1 - c], core, line_one.at[y])
    onward = line_copy(2, line_one.at[1 - y], side, line_two)
    far.start()
    near.start()
    far.wait_recv()
    mine = line_one[1 - y].astype(F32) + grad_kv[1 - y, c].astype(F32)
    line_one[1 - y] = mine.astype(BF16)
    onward.start()
    loads[0].wait()
    query_grad = grad_q[...]
    grad_normed = product_back(query_grad, flat_part(qkv, 0, features))
    reduce.run(MIDDLE[3])
    near.wait_recv()
    onward.wait_recv()
    total = (line_one[y].astype(F32) + grad_kv[y, c].astype(F32)) + line_two[...].astype(F32)
    joint = [query_grad, total[:, :features].astype(BF16), total[:, features:].astype(BF16)]
    for n in (1, 2):
        grad_normed += product_back(joint[n], flat_part(qkv, n * features, features))
    grad_from, gain_grad = norm_back(residual_two[...], gain_rows[2:3], grad_normed)
    grad_two = grad_three[...] + grad_from
    gain_grads[...] = jnp.zeros_like(gain_grads)
    gain_grads[2:3, :] = gain_grad
    slots, shard = qkv.shape[0], qkv.shape[1]
    for n in range(3):
        term = product_sum(normed_three[...], joint[n]).reshape(slots, shard, features)
        qkv[:, :, n * features : (n + 1) * features] = term.astype(BF16)
    stores[0].start()
    reduce.run(MIDDLE[4])

    branch = grad_two.astype(BF16)
    loads[1].wait()
    loads[2].wait()
    deep = down.shape[1]
    few = features // deep
    grad_normed = jnp.zeros((rows, features), F32)
    for n in range(up.shape[2] // features):
        own = slice(n * features, (n + 1) * features)
        some = pl.ds(n * few, few)
        gate_grad = product_back(branch, down[some].reshape(features, features))
        pre_grad = jax.vjp(jax.nn.gelu, pre_one[:, own])[1](gate_grad)[0].astype(BF16)
        grad_normed += product_back(pre_grad, flat_part(up, n * features, features))
        term = product_sum(act_one[:, own], branch)
        down[some] = term.astype(BF16).reshape(few, deep, features)
        term = product_sum(normed_two[...], pre_grad).reshape(slots, shard, features)
        up[:, :, own] = term.astype(BF16)
        reduce.run(MIDDLE[5 + n])
    stores[1].start()
    stores[2].start()
    grad_from, gain_grad = norm_back(residual_one[...], gain_rows[1:2], grad_normed)
    grad_one[...] = grad_two + grad_from
    gain_grads[1:2, :] = gain_grad
    reduce.finish()
    for each in (far, near, onward):
        each.wait_send()
    for store in stores:
        store.wait()


def middle_layers(terms, weights, kept, collective_id):
    count = len(terms)
    att_q, act_one = kept[0], kept[9]
    rows, features = att_q.shape
    shapes = [a.shape[1:] for a in terms]
    parts = cut(shapes)
    kinds = sorted({(part[2], part[4]) for part in parts})
    scratch = []
    for _, _, part_rows, _, columns, x_last in parts:
        for lead in ((2, 4, 2), (4, 2) if x_last else (2, 4), (4,), (3,)):
            scratch.append(pltpu.VMEM(lead + (part_rows, columns), BF16))
    scratch += [pltpu.VMEM((2, 2, 4, 2) + kind, BF16) for kind in kinds]
    scratch += [pltpu.VMEM(a.shape, BF16) for a in weights]
    scratch += [
        pltpu.VMEM((rows, features), BF16),
        pltpu.VMEM((2, 2, rows, 2 * features), BF16),
        pltpu.VMEM((2, rows, 2 * features), BF16),
        pltpu.VMEM((rows, 2 * features), BF16),
        pltpu.SemaphoreType.DMA((len(parts), 6)),
        pltpu.SemaphoreType.DMA((len(parts), 6)),
        pltpu.SemaphoreType.DMA((len(parts),)),
        pltpu.SemaphoreType.DMA((3,)),
        pltpu.SemaphoreType.DMA((3,)),
        pltpu.SemaphoreType.DMA((3,)),
        pltpu.SemaphoreType.DMA((3,)),
    ]
    vmem, anywhere = pl.BlockSpec(memory_space=pltpu.VMEM), pl.BlockSpec(memory_space=pl.ANY)
    results = [jax.ShapeDtypeStruct(s, F32) for s in shapes]
    results += [jax.ShapeDtypeStruct(a.shape, BF16) for a in weights]
    results += [
        jax.ShapeDtypeStruct((rows, features), F32),
        jax.ShapeDtypeStruct((8, features), F32),
    ]
    out = pl.pallas_call(
        partial(middle_body, parts, count, kinds),
        out_shape=results,
        in_specs=[anywhere] * (count + 3) + [vmem] * 13,
        out_specs=[vmem] * count + [anywhere] * 3 + [vmem] * 2,
        scratch_shapes=scratch,
        compiler_params=pltpu.CompilerParams(
            collective_id=collective_id, has_side_effects=True, vmem_limit_bytes=60 * MIB
        ),
    )(*[a.reshape((2, 2, 4, 2) + a.shape[1:]) for a in terms], *weights, *kept)
    return out[:count], out[count : count + 3], out[count + 3], out[count + 4]


def local_call(body, out_shape, *operands, scalars=0, limit=48):
    vmem = pl.BlockSpec(memory_space=pltpu.VMEM)
    smem = pl.BlockSpec(memory_space=pltpu.SMEM)
    return pl.pallas_call(
        body,
        out_shape=out_shape,
        in_specs=[smem] * scalars + [vmem] * (len(operands) - scalars),
        out_specs=jax.tree.map(lambda _: vmem, out_shape),
        compiler_params=pltpu.CompilerParams(vmem_limit_bytes=limit * MIB),
    )(*operands)


def shards(
    tokens, lengths, norm_one, query_one, key_one, value_one, shift_taps, decay_log,
    turn_angle, mix_real, mix_imag, skip_gain, out_one, norm_two, up_one, down_one,
    norm_three, qkv_weight, out_two, norm_four, up_two, down_two, cotangent,
):
    blocks, groups = lax.axis_size("seq"), lax.axis_size("dp")
    devices = blocks * groups
    rows, features = tokens.shape[1], tokens.shape[2]
    channels = features // devices
    place = lax.axis_index("seq")
    length = lengths[0]
    row_places = place * rows + jnp.arange(rows, dtype=jnp.int32)
    live_mask = (row_places < length).astype(F32)[:, None]
    live_lane = (row_places < length).astype(F32)[None, :]

    kernel, kernel_pull = jax.vjp(
        partial(ssm_kernel, length=rows * blocks),
        *[a.astype(F32) for a in (decay_log, turn_angle, mix_real, mix_imag)],
    )
    wide = -(-(blocks + 1) * rows // 128) * 128
    kernel_row = jnp.pad(kernel, ((0, 0), (0, wide - kernel.shape[1])))
    narrow = -(-3 * rows // 128) * 128
    tap_row = jnp.pad(
        shift_taps.astype(F32), ((0, 0), (0, narrow - shift_taps.shape[1]))
    )
    skip_row = jnp.broadcast_to(skip_gain.astype(F32)[:, None], (channels, 128))

    gains = jnp.stack([norm_one, norm_two, norm_three, norm_four], axis=1).astype(F32)
    gains = jnp.pad(gains, ((0, 0), (0, 124)))
    weights = [
        gains, key_one, value_one, query_one, out_one, up_one, down_one, qkv_weight, out_two,
        up_two, down_two,
    ]
    mixer_rows = (tap_row, kernel_row, skip_row)
    key_live = (jnp.arange(blocks * rows, dtype=jnp.int32) < length).astype(F32)[None, :]
    if grouped():
        every, kept = first_layer(weights, tokens[0], live_lane, key_live, *mixer_rows, 1)
    else:
        every, kept = first_layer_apart(weights, tokens[0], live_lane, key_live, *mixer_rows)
    residual_one = kept[0]
    gain_one, gain_two, gain_three, gain_four = [
        every[0][:, :, n].reshape(features) for n in range(4)
    ]
    up_one_all, down_one_all, qkv_all, out_two_all, late_up, late_down = [
        g.reshape((-1, g.shape[2])) for g in every[5:]
    ]

    normed_two, pre_one, act_one, residual_two, normed_three, att_q, kv = kept[10:17]
    attended, log_total, residual_three = kept[17:]
    residual_four, stored_four = feed_forward(residual_three, gain_four, late_up, late_down)
    activations = (live_mask * residual_four).astype(BF16)

    grad_four = live_mask * cotangent[0].astype(F32)
    grad_three, grad_norm_four, grad_up_two, grad_down_two = feed_back(
        residual_three, gain_four, late_up, late_down, stored_four, grad_four
    )
    branch_three = grad_three.astype(BF16)
    grad_out_two = product_sum(attended, branch_three)
    grad_attended = product_back(branch_three, out_two_all).astype(BF16)
    slots = (devices, -1)
    terms = [
        g.astype(BF16).reshape(slots + g.shape[1:])
        for g in (grad_up_two, grad_down_two, grad_out_two)
    ]
    if grouped():
        done, terms, grad_one, gain_grads = middle_layers(
            terms,
            every[7:8] + every[5:7],
            [
                att_q, kv, log_total, grad_attended, key_live, normed_three, residual_two,
                grad_three, every[0], act_one, pre_one, normed_two, residual_one,
            ],
            3,
        )
        grad_norm_two, grad_norm_three = gain_grads[1], gain_grads[2]
    else:
        grad_q, grad_kv = local_call(
            attend_back_body,
            [
                jax.ShapeDtypeStruct((rows, features), BF16),
                jax.ShapeDtypeStruct((blocks * rows, 2 * features), BF16),
            ],
            jnp.stack([place.astype(jnp.int32) * rows, length]), att_q,
            kv.reshape(blocks * rows, 2 * features), log_total, grad_attended, scalars=1,
        )
        grad_kv = lax.psum_scatter(
            grad_kv.reshape(blocks, rows, 2 * features), "seq", scatter_dimension=0
        )
        grad_joint = jnp.concatenate([grad_q, grad_kv.astype(BF16)], axis=1)
        grad_qkv_weight = product_sum(normed_three, grad_joint)
        grad_normed_three = product_back(grad_joint, qkv_all)
        grad_from_three, grad_norm_three = jax.vjp(layer_norm, residual_two, gain_three)[1](
            grad_normed_three
        )
        grad_one, grad_norm_two, grad_up_one, grad_down_one = feed_back(
            residual_one, gain_two, up_one_all, down_one_all, (normed_two, pre_one, act_one),
            grad_three + grad_from_three,
        )
        done = []
        terms += [
            g.astype(BF16).reshape(slots + g.shape[1:])
            for g in (grad_qkv_weight, grad_up_one, grad_down_one)
        ]
    branch_one = grad_one.astype(BF16)
    gain_in = jnp.stack(
        [jnp.zeros_like(grad_norm_two), grad_norm_two, grad_norm_three, grad_norm_four], axis=1
    )
    gain_in = jnp.pad(gain_in, ((0, 0), (0, 124)))
    last = (terms, gain_in, branch_one, grad_one, live_lane, kept[1:10], every[:5], mixer_rows)
    if grouped():
        sums, rest = last_layer(*last, 2)
        sums = list(done) + list(sums)
    else:
        sums, rest = last_layer_apart(*last)
    grad_up_two, grad_down_two, grad_out_two, grad_qkv_weight, grad_up_one, grad_down_one = sums[:6]
    grad_out_one, grad_query_one, grad_key_one, grad_value_one, gain_grads = sums[6:]
    gain_grads = gain_grads[:, :4].T
    input_grad, kernel_grad, taps_grad, skip_grad = rest
    grad_decay_log, grad_turn_angle, grad_mix_real, grad_mix_imag = kernel_pull(
        kernel_grad[:, : rows * blocks]
    )
    grad_shift_taps = taps_grad[:, : shift_taps.shape[1]]
    grad_skip_gain = skip_grad[:, 0]
    return (
        activations[None], input_grad[None],
        gain_grads[0], grad_query_one, grad_key_one, grad_value_one,
        grad_shift_taps, grad_decay_log, grad_turn_angle, grad_mix_real, grad_mix_imag,
        grad_skip_gain, grad_out_one,
        gain_grads[1], grad_up_one, grad_down_one,
        gain_grads[2], grad_qkv_weight, grad_out_two,
        gain_grads[3], grad_up_two, grad_down_two,
    )


def solution(mesh):
    row, vector = P(BOTH, None), P(BOTH)
    whole = P("dp", "seq", None)
    weights = (
        vector, row, row, row, row, row, row, row, row, vector, row,
        vector, row, row, vector, row, row, vector, row, row,
    )
    return jax.shard_map(
        shards,
        mesh=mesh,
        in_specs=(whole, P("dp")) + weights + (whole,),
        out_specs=(whole, whole) + weights,
        check_vma=False,
    )
```

```python
from functools import partial

import jax
import jax.numpy as jnp
from jax import lax
from jax.experimental import pallas as pl
from jax.experimental.pallas import tpu as pltpu
from jax.sharding import PartitionSpec as P

HEADS = 12
HDIM = 64
EPSILON = 1e-05
HIGHEST = lax.Precision.HIGHEST
MASKED = -1e30
BOTH = ("seq", "dp")
MESH = pl.DeviceIdType.MESH
MIB = 1024 * 1024
LAGS = (0, 2, 4, 6)
PLACES = (4, 5, 6, 7, 9)
MIDDLE = (1, 1, 2, 3, 4, 5, 6, 7, 8)
EARLY = 2
RUNS = (8, 11, 12, 14, 15, 17)
AHEAD = 4
F32 = jnp.float32
BF16 = jnp.bfloat16


def grouped():
    return lax.axis_size("seq") == 4 and lax.axis_size("dp") == 8


def coordinates():
    seq, dp = lax.axis_index("seq"), lax.axis_index("dp")
    return seq // 2, seq % 2, dp // 2, dp % 2


def slot_of(y, c, z, x):
    return (y * 2 + c) * 8 + z * 2 + x


def device_of(y, c, z, x):
    return (y * 2 + c, z * 2 + x)


def greet(peers):
    barrier = pltpu.get_barrier_semaphore()
    for peer in peers:
        pl.semaphore_signal(barrier, inc=1, device_id=peer, device_id_type=MESH)
    pl.semaphore_wait(barrier, len(peers))


def six_peers(y, c, z, x):
    return [device_of(y, c, (z + k) % 4, x) for k in (1, 2, 3)] + [
        device_of(y, c, z, 1 - x),
        device_of(1 - y, c, z, x),
        device_of(y, 1 - c, z, x),
    ]


class Gather:
    def __init__(self, parts, sources, gathered, local_sem, send_sem, recv_sem, ahead=None):
        self.parts, self.sources, self.gathered = parts, sources, gathered
        self.send_sem, self.recv_sem, self.ahead = send_sem, recv_sem, ahead or AHEAD
        self.y, self.c, self.z, self.x = y, c, z, x = coordinates()
        self.me = slot_of(y, c, z, x)
        self.across_x = device_of(y, c, z, 1 - x)
        self.across_y = device_of(1 - y, c, z, x)
        self.other_core = device_of(y, 1 - c, z, x)
        self.own = [
            pltpu.make_async_copy(sources[i], gathered[i].at[self.me], local_sem.at[i])
            for i in range(len(sources))
        ]
        self.done = 0

    def place(self, p, slot):
        i, row, rows, column, columns, _ = self.parts[p]
        return self.gathered[i].at[slot, pl.ds(row, rows), pl.ds(column, columns)]

    def send(self, p, slot, target, first=False):
        i, row, rows, column, columns, _ = self.parts[p]
        source = self.sources[i].at[pl.ds(row, rows), pl.ds(column, columns)]
        pltpu.make_async_remote_copy(
            src_ref=source if first else self.place(p, slot),
            dst_ref=self.place(p, slot),
            send_sem=self.send_sem.at[p],
            recv_sem=self.recv_sem.at[p, slot],
            device_id=target,
            device_id_type=MESH,
        ).start()

    def arrived(self, p, slot):
        place = self.place(p, slot)
        pltpu.make_async_copy(place, place, self.recv_sem.at[p, slot]).wait()

    def first(self, p):
        for k in (1, 3, 2):
            self.send(p, self.me, device_of(self.y, self.c, (self.z + k) % 4, self.x), True)
        self.send(p, self.me, self.across_x, True)
        self.send(p, self.me, self.across_y, True)
        self.send(p, self.me, self.other_core, True)

    def start(self):
        for copy in self.own:
            copy.start()
        for p in range(min(self.ahead, len(self.parts))):
            self.first(p)

    def after_z(self, p):
        for k in (3, 1, 2):
            slot = slot_of(self.y, self.c, (self.z + k) % 4, self.x)
            self.arrived(p, slot)
            self.send(p, slot, self.across_x)
            self.send(p, slot, self.across_y)
            self.send(p, slot, self.other_core)

    def after_first(self, p):
        x_first = self.parts[p][5]
        for k in (0, 3, 1, 2):
            by_x = slot_of(self.y, self.c, (self.z + k) % 4, 1 - self.x)
            by_y = slot_of(1 - self.y, self.c, (self.z + k) % 4, self.x)
            self.arrived(p, by_x)
            if x_first:
                self.send(p, by_x, self.across_y)
            self.send(p, by_x, self.other_core)
            self.arrived(p, by_y)
            if not x_first:
                self.send(p, by_y, self.across_x)
            self.send(p, by_y, self.other_core)

    def after_second(self, p):
        for k in (0, 3, 1, 2):
            slot = slot_of(1 - self.y, self.c, (self.z + k) % 4, 1 - self.x)
            self.arrived(p, slot)
            self.send(p, slot, self.other_core)

    def whole(self, p):
        for side in (0, 1):
            for zz in range(4):
                for xx in (0, 1):
                    self.arrived(p, slot_of(side, 1 - self.c, zz, xx))

    def steps(self):
        return len(self.parts) + 3

    def run(self, until):
        while self.done < min(until, self.steps()):
            s, count = self.done, len(self.parts)
            if self.ahead <= s + self.ahead < count:
                self.first(s + self.ahead)
            for stage, act in enumerate(
                (self.after_z, self.after_first, self.after_second, self.whole)
            ):
                if 0 <= s - stage < count:
                    act(s - stage)
            self.done += 1

    def own_arrived(self, indices):
        for i in indices:
            self.own[i].wait()

    def finish(self):
        self.run(self.steps())
        for p, (i, row, rows, column, columns, _) in enumerate(self.parts):
            sent = self.gathered[i].at[pl.ds(0, 31), pl.ds(row, rows), pl.ds(column, columns)]
            pltpu.make_async_copy(sent, sent, self.send_sem.at[p]).wait()


def cut(arrays):
    parts = []
    for i, (rows, columns) in enumerate(arrays):
        if columns > 1536:
            width = 1536 if columns % 1536 == 0 else 768
            pieces = [(0, rows, w, width) for w in range(0, columns, width)]
        elif rows > 48:
            pieces = [(r, 48, 0, columns) for r in range(0, rows, 48)]
        else:
            pieces = [(0, rows, 0, columns)]
        for piece in pieces:
            parts.append((i,) + piece + (len(parts) % 2 == 0,))
    return parts


class Reduce:
    def __init__(self, parts, terms, totals, buffers, mine, send_sem, recv_sem, mine_sem):
        self.parts, self.terms, self.totals, self.buffers = parts, terms, totals, buffers
        self.send_sem, self.recv_sem, self.mine_sem = send_sem, recv_sem, mine_sem
        self.y, self.c, self.z, self.x = coordinates()
        self.mine, self.kinds = mine, {}
        for p, part in enumerate(parts):
            if part[0] < len(mine[0]):
                self.kinds.setdefault((part[2], part[4]), []).append(p)
        self.done = 0

    def term(self, p, core):
        i, row, rows, column, columns, _ = self.parts[p]
        return self.terms[i].at[:, core, :, :, pl.ds(row, rows), pl.ds(column, columns)]

    def fetch(self, p):
        kind = (self.parts[p][2], self.parts[p][4])
        place = self.kinds[kind].index(p)
        held = self.mine[1][kind].at[place % 2]
        return pltpu.make_async_copy(self.term(p, self.c), held, self.mine_sem.at[p]), held

    def copies(self, p, stage):
        one, two, three, four = self.buffers[4 * p : 4 * p + 4]
        y, c, z, x = self.y, self.c, self.z, self.x
        across_x, across_y = device_of(y, c, z, 1 - x), device_of(1 - y, c, z, x)
        x_last = self.parts[p][5]
        if stage == 0:
            pairs = [(self.term(p, 1 - c), one, device_of(y, 1 - c, z, x))]
        elif stage == 1 and x_last:
            pairs = [(one.at[1 - y], two, across_y)]
        elif stage == 1:
            pairs = [(one.at[:, :, 1 - x], two, across_x)]
        elif stage == 2 and x_last:
            pairs = [(two.at[:, 1 - x], three, across_x)]
        elif stage == 2:
            pairs = [(two.at[1 - y], three, across_y)]
        else:
            pairs = [
                (three.at[(z + k) % 4], four.at[k - 1], device_of(y, c, (z + k) % 4, x))
                for k in (1, 2, 3)
            ]
        return [
            pltpu.make_async_remote_copy(
                src_ref=src,
                dst_ref=dst,
                send_sem=self.send_sem.at[p, stage + n],
                recv_sem=self.recv_sem.at[p, stage + n],
                device_id=target,
                device_id_type=MESH,
            )
            for n, (src, dst, target) in enumerate(pairs)
        ]

    def add(self, p, stage):
        one, two, three, four = self.buffers[4 * p : 4 * p + 4]
        y, c, z, x = self.y, self.c, self.z, self.x
        i, row, rows, column, columns, x_last = self.parts[p]

        def total(a, b):
            return (a.astype(F32) + b.astype(F32)).astype(a.dtype)

        if stage == 0:
            if i < len(self.mine[0]):
                copy, held = self.fetch(p)
                copy.wait()
            else:
                held = self.term(p, c)

            def add_one(k, _):
                b, zz = k // 4, k % 4
                for xx in (0, 1):
                    one[b, zz, xx] = total(one[b, zz, xx], held[b, zz, xx])
                return 0

            lax.fori_loop(0, 8, add_one, 0)
            if i < len(self.mine[0]):
                same = self.kinds[(rows, columns)]
                later = same.index(p) + 2
                if later < len(same):
                    self.fetch(same[later])[0].start()
        elif stage == 1:

            def add_two(k, _):
                for h in (0, 1):
                    if x_last:
                        two[k, h] = total(two[k, h], one[y, k, h])
                    else:
                        two[h, k] = total(two[h, k], one[h, k, x])
                return 0

            lax.fori_loop(0, 4, add_two, 0)
        elif stage == 2:

            def add_three(k, _):
                three[k] = total(three[k], two[k, x] if x_last else two[y, k])
                return 0

            lax.fori_loop(0, 4, add_three, 0)
        else:
            self.totals[i][pl.ds(row, rows), pl.ds(column, columns)] = (
                three[z].astype(F32)
                + four[0].astype(F32)
                + four[1].astype(F32)
                + four[2].astype(F32)
            )

    def start(self, arrays):
        for p, part in enumerate(self.parts):
            if part[0] in arrays:
                for copy in self.copies(p, 0):
                    copy.start()

    def fetch_first(self):
        for same in self.kinds.values():
            for p in same[:2]:
                self.fetch(p)[0].start()

    def steps(self):
        return len(self.parts) + LAGS[3]

    def run(self, until):
        while self.done < min(until, self.steps()):
            for stage in range(4):
                p = self.done - LAGS[stage]
                if 0 <= p < len(self.parts):
                    for copy in self.copies(p, stage):
                        copy.wait_recv()
                    self.add(p, stage)
                    if stage < 3:
                        for copy in self.copies(p, stage + 1):
                            copy.start()
            self.done += 1

    def finish(self):
        self.run(self.steps())
        for p in range(len(self.parts)):
            for stage in range(4):
                for copy in self.copies(p, stage):
                    copy.wait_send()


def all_others():
    rows, groups = lax.axis_size("seq"), lax.axis_size("dp")
    count = rows * groups
    me = lax.axis_index("seq") * groups + lax.axis_index("dp")
    others = [lax.rem(me + k, count) for k in range(1, count)]
    return me, others, [(o // groups, lax.rem(o, groups)) for o in others]


class Swap:
    def __init__(self, src, dst, send_sem, recv_sem):
        self.src, self.dst, self.send_sem, self.recv_sem = src, dst, send_sem, recv_sem

    def start(self):
        me, others, places = all_others()
        for o, place in zip(others, places):
            pltpu.make_async_remote_copy(
                src_ref=self.src.at[o],
                dst_ref=self.dst.at[me],
                send_sem=self.send_sem,
                recv_sem=self.recv_sem,
                device_id=place,
                device_id_type=MESH,
            ).start()

    def wait(self):
        most = pl.ds(0, self.src.shape[0] - 1)
        me = all_others()[0]
        pltpu.make_async_copy(self.src.at[most], self.dst.at[most], self.recv_sem).wait()
        pltpu.make_async_copy(self.src.at[most], self.dst.at[most], self.send_sem).wait()
        self.dst[me] = self.src[me]


def layer_norm(residual, scale_gain):
    average = jnp.mean(residual, axis=-1, keepdims=True)
    centered = residual - average
    variance = jnp.mean(centered * centered, axis=-1, keepdims=True)
    return centered * lax.rsqrt(variance + EPSILON) * scale_gain


def contract(left_side, right_side, left_dim, right_dim):
    return lax.dot_general(
        left_side,
        right_side,
        (((left_dim,), (right_dim,)), ((), ())),
        preferred_element_type=F32,
    )


def product(left_side, right_side):
    return contract(left_side, right_side, 1, 0)


def product_back(left_side, right_side):
    return contract(left_side, right_side, 1, 1)


def product_sum(left_side, right_side):
    return contract(left_side, right_side, 0, 0)


def feed_forward(residual, scale_gain, up_weight, down_weight):
    normed = layer_norm(residual, scale_gain).astype(BF16)
    pre_act = product(normed, up_weight)
    activated = jax.nn.gelu(pre_act).astype(BF16)
    return (residual + product(activated, down_weight), (normed, pre_act, activated))


def feed_back(residual, scale_gain, up_weight, down_weight, stored, grad_residual):
    normed, pre_act, activated = stored
    grad_branch = grad_residual.astype(BF16)
    grad_down = product_sum(activated, grad_branch)
    grad_activated = product_back(grad_branch, down_weight)
    gelu_pull = jax.vjp(jax.nn.gelu, pre_act)[1]
    grad_pre = gelu_pull(grad_activated)[0].astype(BF16)
    grad_up = product_sum(normed, grad_pre)
    grad_normed = product_back(grad_pre, up_weight)
    norm_pull = jax.vjp(layer_norm, residual, scale_gain)[1]
    grad_input, grad_gain = norm_pull(grad_normed)
    return (grad_residual + grad_input, grad_gain, grad_up, grad_down)


def ssm_kernel(decay_log, turn_angle, mix_real, mix_imag, length):
    rate = jnp.exp(decay_log)[:, :, None]
    angle = turn_angle[:, :, None]
    step = 32

    def powers(times):
        return (
            jnp.exp(-times * rate) * jnp.cos(times * angle),
            jnp.exp(-times * rate) * jnp.sin(times * angle),
        )

    low_real, low_imag = powers(jnp.arange(step, dtype=F32)[None, None])
    high_real, high_imag = powers(
        (step * jnp.arange(length // step, dtype=jnp.int32)).astype(F32)[None, None]
    )
    real, imag = mix_real[:, :, None], mix_imag[:, :, None]
    high = jnp.concatenate(
        [real * high_real - imag * high_imag, -(real * high_imag + imag * high_real)], axis=1
    )
    low = jnp.concatenate([low_real, low_imag], axis=1)
    kernel = jnp.einsum("cna,cnb->cab", high, low, precision=HIGHEST)
    return kernel.reshape(decay_log.shape[0], length)


def state_columns(decay, turn, real, imag, cols):
    states = decay.shape[1]
    size = jnp.exp(-jnp.exp(decay))
    turned = [a.T for a in (size * jnp.cos(turn), size * jnp.sin(turn), real, imag)]
    for ch in range(decay.shape[0]):
        for n, a in enumerate(turned):
            cols[ch * states : (ch + 1) * states, n : n + 1] = a[:, ch : ch + 1]


def state_powers(cols, ch, states):
    own = cols[pl.ds(pl.multiple_of(ch * states, states), states), :]
    base_real, base_imag = own[:, :1], own[:, 1:2]
    lane = lax.broadcasted_iota(jnp.int32, (states, 128), 1)
    real, imag = jnp.ones((states, 128), F32), jnp.zeros((states, 128), F32)
    for bit in range(7):
        taken = lane % (2 << bit) >= (1 << bit)
        step_real = jnp.where(taken, base_real, 1.0)
        step_imag = jnp.where(taken, base_imag, 0.0)
        real, imag = real * step_real - imag * step_imag, real * step_imag + imag * step_real
        base_real, base_imag = (
            base_real * base_real - base_imag * base_imag, 2.0 * base_real * base_imag
        )
    return real, imag, base_real, base_imag, own[:, 2:3], own[:, 3:4]


def kernel_rows(decay, turn, real_mix, imag_mix, cols, kernel_ref, length):
    states = decay.shape[1]
    state_columns(decay, turn, real_mix, imag_mix, cols)
    kernel_ref[...] = jnp.zeros_like(kernel_ref)

    def one(ch, _):
        real, imag, jump_real, jump_imag, mix_real, mix_imag = state_powers(cols, ch, states)
        for first in range(0, length, 128):
            terms = mix_real * real - mix_imag * imag
            kernel_ref[ch, :, first : first + 128] = jnp.sum(terms, axis=0, keepdims=True)
            real, imag = (
                real * jump_real - imag * jump_imag, real * jump_imag + imag * jump_real
            )
        return 0

    lax.fori_loop(0, decay.shape[0], one, 0)


def kernel_rows_back(decay, turn, real_mix, imag_mix, cols, sums, grad_ref, length):
    channels, states = decay.shape
    state_columns(decay, turn, real_mix, imag_mix, cols)
    lane = lax.broadcasted_iota(jnp.int32, (states, 128), 1)

    def one(ch, _):
        real, imag, jump_real, jump_imag, _, _ = state_powers(cols, ch, states)
        totals = [jnp.zeros((states, 128), F32)] * 4
        for first in range(0, length, 128):
            grad = grad_ref[ch, :, first : first + 128]
            times = (first + lax.broadcasted_iota(jnp.int32, (1, 128), 1)).astype(F32)
            parts = (grad * real, grad * imag, grad * times * real, grad * times * imag)
            totals = [a + b for a, b in zip(totals, parts)]
            real, imag = (
                real * jump_real - imag * jump_imag, real * jump_imag + imag * jump_real
            )
        kept = jnp.zeros((states, 128), F32)
        for n, a in enumerate(totals):
            kept = jnp.where(lane == n, jnp.sum(a, axis=1, keepdims=True), kept)
        sums[pl.ds(pl.multiple_of(ch * states, states), states), :] = kept
        return 0

    lax.fori_loop(0, channels, one, 0)
    plain_real, plain_imag, timed_real, timed_imag = [
        jnp.concatenate(
            [sums[ch * states : (ch + 1) * states, n : n + 1] for ch in range(channels)], axis=1
        ).T
        for n in range(4)
    ]
    return (
        -jnp.exp(decay) * (real_mix * timed_real - imag_mix * timed_imag),
        -(real_mix * timed_imag + imag_mix * timed_real),
        plain_real,
        -plain_imag,
    )


def toeplitz(row, rows):
    spread = jnp.broadcast_to(row, (rows, row.shape[1]))
    return pltpu.roll(spread, 0, 1, stride=1, stride_axis=0)


def block_sum(mixed, blocks, groups, rows):
    total = mixed[:, :rows]
    for d in range(1, blocks):
        piece = mixed[: (blocks - d) * groups, d * rows : (d + 1) * rows]
        total = total + jnp.concatenate(
            [jnp.zeros((d * groups, rows), piece.dtype), piece], axis=0
        )
    return total


def block_spread(value, blocks, lags, groups, rows):
    pieces = [value]
    for d in range(1, lags):
        pieces.append(
            jnp.concatenate(
                [value[d * groups :], jnp.zeros((d * groups, rows), value.dtype)], axis=0
            )
        )
    return jnp.concatenate(pieces, axis=1)


def mix(blocks, groups, rows, keys, values, tap_row, kernel_row, skip):
    span = blocks * rows
    taps = toeplitz(tap_row, rows)[:, : 2 * rows].astype(BF16)
    longer = toeplitz(kernel_row, rows)[:, :span].astype(BF16)
    near = product(keys, taps)
    shifted = near[:, :rows] + jnp.concatenate(
        [jnp.zeros((groups, rows), F32), near[: (blocks - 1) * groups, rows:]], axis=0
    )
    signal = shifted * values.astype(F32)
    mixed = product(signal.astype(BF16), longer)
    return shifted, block_sum(mixed, blocks, groups, rows) + skip * signal


def mixer_body(blocks, groups, rows, k_ref, v_ref, taps_ref, kernel_ref, skip_ref, shifted_ref, out_ref):
    for ch in range(k_ref.shape[0]):
        row = slice(ch, ch + 1)
        shifted_ref[ch], out = mix(
            blocks, groups, rows, k_ref[ch], v_ref[ch],
            taps_ref[row, :], kernel_ref[row, :], skip_ref[row, :1],
        )
        out_ref[ch] = out.astype(BF16)


def flat_weight(ref):
    wide = ref[...].astype(F32)
    return wide.reshape(wide.shape[0] * wide.shape[1], wide.shape[2]).astype(BF16)


def flat_part(ref, first, width):
    wide = ref[:, :, first : first + width].astype(F32)
    return wide.reshape(wide.shape[0] * wide.shape[1], width).astype(BF16)


def first_body(parts, count, *refs):
    sources = refs[:count]
    tokens, live, key_live, small, taps = refs[count : count + 5]
    states = refs[count + 5 : count + 9]
    refs = refs[count + 9 :]
    gathered = refs[:count]
    (
        residual_ref, standard_ref, inverse_ref, normed_ref, queries_ref, ssm_ref, gated_ref,
        k_ref, v_ref, shifted_ref,
        normed_two, pre_one, act_one, residual_two, normed_three, att_q, att_kv, attended,
        log_total, residual_three, taps_ref, kernel_ref,
    ) = refs[count : count + 22]
    (
        wide, sent_kv, came_kv, sent_y, came_y, up, down, qkv, out_two, cols,
        local_sem, send_sem, recv_sem, swap_sem, load_sem, line_send, line_recv,
    ) = refs[count + 22 :]
    gains, key_all, value_all, query_all, out_all = gathered[:5]
    devices, channels = key_all.shape[0], key_all.shape[1]
    rows, features = tokens.shape
    blocks, groups = lax.axis_size("seq"), lax.axis_size("dp")
    greet(all_others()[2])
    gather = Gather(parts, sources, gathered, local_sem, send_sem, recv_sem)
    gather.start()

    turned = tokens[...].astype(F32).T
    centered = turned - jnp.mean(turned, axis=0, keepdims=True)
    inverse = lax.rsqrt(jnp.mean(centered * centered, axis=0, keepdims=True) + EPSILON)
    inverse_ref[...] = jnp.broadcast_to(inverse, inverse_ref.shape)
    standard_ref[...] = centered * inverse
    tap_count = taps.shape[1]
    taps_ref[...] = jnp.zeros_like(taps_ref)
    taps_ref[:, :tap_count] = taps[...].astype(F32)
    gather.run(EARLY)
    kernel_rows(*[a[...].astype(F32) for a in states], cols, kernel_ref, blocks * rows)
    gather.run(RUNS[0])
    gather.own_arrived(range(5))
    all_gains = gains[...].reshape(features, 128)
    normed_ref[...] = (standard_ref[...] * all_gains[:, :1]).astype(BF16)

    def projected(weight):
        return contract(flat_weight(weight), normed_ref[...], 0, 0)

    wide[:, :channels, :] = projected(key_all).reshape(devices, channels, rows)
    wide[:, channels:, :] = (projected(value_all) * live[...]).reshape(devices, channels, rows)
    sent_kv[...] = wide[...].astype(BF16)
    over = Swap(sent_kv, came_kv, swap_sem.at[0], swap_sem.at[1])
    over.start()
    queries_ref[...] = projected(query_all)
    gather.run(RUNS[1])
    over.wait()
    wide[...] = came_kv[...].astype(F32)
    for ch in range(channels):
        row = slice(ch, ch + 1)
        k_ref[ch] = wide[:, ch, :].astype(BF16)
        v_ref[ch] = wide[:, channels + ch, :].astype(BF16)
        shifted_ref[ch], out = mix(
            blocks, groups, rows, k_ref[ch], v_ref[ch],
            taps_ref[row, :], kernel_ref[ch], small[row, 4:5],
        )
        wide[:, ch, :] = out
        if ch == channels // 2:
            gather.run(RUNS[2])
    sent_y[...] = wide[:, :channels, :].astype(BF16)
    back = Swap(sent_y, came_y, swap_sem.at[2], swap_sem.at[3])
    back.start()
    gather.run(RUNS[3])
    gather.own_arrived(range(5, count))
    loads = [
        pltpu.make_async_copy(gathered[5 + n], held, load_sem.at[n])
        for n, held in enumerate((up, down, qkv, out_two))
    ]
    loads[0].start()
    loads[1].start()
    back.wait()
    ssm = came_y[...].astype(F32).reshape(features, rows)
    ssm_ref[...] = ssm.astype(BF16)
    gated_ref[...] = (queries_ref[...] * ssm).astype(BF16)
    residual_ref[...] = tokens[...].astype(F32) + contract(
        gated_ref[...], flat_weight(out_all), 0, 0
    )

    gain_rows = all_gains.T
    normed_two[...] = layer_norm(residual_ref[...], gain_rows[1:2]).astype(BF16)
    loads[0].wait()
    for first in range(0, up.shape[2], features):
        own = slice(first, first + features)
        pre = product(normed_two[...], flat_part(up, first, features))
        pre_one[:, own] = pre
        act_one[:, own] = jax.nn.gelu(pre).astype(BF16)
    loads[1].wait()
    down_flat = down[...].reshape(-1, features)
    residual_two[...] = residual_ref[...] + product(act_one[...], down_flat)
    normed_three[...] = layer_norm(residual_two[...], gain_rows[2:3]).astype(BF16)
    gather.run(RUNS[4])
    loads[2].start()
    loads[2].wait()
    y, c, z, x = coordinates()
    me = y * 2 + c
    for first in range(0, 2 * features, features):
        joint = product(normed_three[...], flat_part(qkv, features + first, features))
        att_kv[me, :, first : first + features] = joint.astype(BF16)
    core, side = device_of(y, 1 - c, z, x), device_of(1 - y, c, z, x)

    def pass_on(n, slot, target):
        return pltpu.make_async_remote_copy(
            src_ref=att_kv.at[slot],
            dst_ref=att_kv.at[slot],
            send_sem=line_send.at[n],
            recv_sem=line_recv.at[n],
            device_id=target,
            device_id_type=MESH,
        )

    def taken(n, slot):
        pltpu.make_async_copy(att_kv.at[slot], att_kv.at[slot], line_recv.at[n]).wait()

    far = (1 - y) * 2 + c
    passed = [pass_on(0, me, side), pass_on(1, me, core), pass_on(2, far, core)]
    passed[0].start()
    passed[1].start()
    att_q[...] = product(normed_three[...], flat_part(qkv, 0, features)).astype(BF16)
    taken(0, far)
    passed[2].start()
    gather.run(RUNS[5])
    loads[3].start()
    taken(1, y * 2 + 1 - c)
    taken(2, (1 - y) * 2 + 1 - c)
    keys = blocks * rows
    row_places = me * rows + lax.broadcasted_iota(jnp.int32, (rows, keys), 0)
    key_places = lax.broadcasted_iota(jnp.int32, (rows, keys), 1)
    hidden = jnp.where(key_places <= row_places, key_live[...], 0.0)
    attend_heads(
        hidden > 0.5, att_q, att_kv[...].reshape(keys, 2 * features), attended, log_total
    )
    loads[3].wait()
    residual_three[...] = residual_two[...] + product(attended[...], flat_weight(out_two))
    for each in passed:
        each.wait_send()
    gather.finish()


def first_layer(weights, tokens, live, key_live, mixer, collective_id):
    count = len(weights)
    blocks, groups = lax.axis_size("seq"), lax.axis_size("dp")
    devices = blocks * groups
    rows, features = tokens.shape
    channels = features // devices
    parts = cut([a.shape for a in weights])
    vmem, anywhere = pl.BlockSpec(memory_space=pltpu.VMEM), pl.BlockSpec(memory_space=pl.ANY)
    turned = (features, rows)
    per_channel = (channels, devices, rows)
    results = [
        ((rows, features), F32), (turned, F32), ((8, rows), F32), (turned, BF16), (turned, F32),
        (turned, BF16), (turned, BF16), (per_channel, BF16), (per_channel, BF16), (per_channel, F32),
    ]
    hidden = weights[5].shape[1]
    results += [
        ((rows, features), BF16), ((rows, hidden), F32), ((rows, hidden), BF16),
        ((rows, features), F32), ((rows, features), BF16), ((rows, features), BF16),
        ((blocks, rows, 2 * features), BF16), ((rows, features), BF16), ((rows, 128), F32),
        ((rows, features), F32), ((channels, -(-3 * rows // 128) * 128), F32),
        ((channels, 1, -(-(blocks + 1) * rows // 128) * 128), F32),
    ]
    out = pl.pallas_call(
        partial(first_body, parts, count),
        out_shape=[jax.ShapeDtypeStruct((devices,) + a.shape, a.dtype) for a in weights]
        + [jax.ShapeDtypeStruct(*r) for r in results],
        in_specs=[anywhere] * count + [vmem] * 9,
        out_specs=[vmem] * 5 + [anywhere] * (count - 5) + [vmem] * len(results),
        scratch_shapes=[
            pltpu.VMEM((devices, 2 * channels, rows), F32),
            pltpu.VMEM((devices, 2 * channels, rows), BF16),
            pltpu.VMEM((devices, 2 * channels, rows), BF16),
            pltpu.VMEM((devices, channels, rows), BF16),
            pltpu.VMEM((devices, channels, rows), BF16),
        ]
        + [pltpu.VMEM((devices,) + a.shape, BF16) for a in weights[5:9]]
        + [
            pltpu.VMEM((channels * mixer[1].shape[1], 128), F32),
            pltpu.SemaphoreType.DMA((count,)),
            pltpu.SemaphoreType.DMA((len(parts),)),
            pltpu.SemaphoreType.DMA((len(parts), devices)),
            pltpu.SemaphoreType.DMA((4,)),
            pltpu.SemaphoreType.DMA((4,)),
            pltpu.SemaphoreType.DMA((3,)),
            pltpu.SemaphoreType.DMA((3,)),
        ],
        compiler_params=pltpu.CompilerParams(
            collective_id=collective_id, has_side_effects=True, vmem_limit_bytes=60 * MIB
        ),
    )(*weights, tokens, live, key_live, weights[0], *mixer)
    return out[:count], out[count:]


def mixer_rows(small, mixer, rows, blocks):
    taps, *states = mixer
    kernel, pull = jax.vjp(
        partial(ssm_kernel, length=rows * blocks), *[a.astype(F32) for a in states]
    )
    wide = -(-(blocks + 1) * rows // 128) * 128
    kernel_row = jnp.pad(kernel, ((0, 0), (0, wide - kernel.shape[1])))
    narrow = -(-3 * rows // 128) * 128
    tap_row = jnp.pad(taps.astype(F32), ((0, 0), (0, narrow - taps.shape[1])))
    skip_row = jnp.broadcast_to(small[:, 4:5], small.shape)
    return (tap_row, kernel_row, skip_row), pull


def first_layer_apart(weights, tokens, live, key_live, mixer):
    blocks, groups = lax.axis_size("seq"), lax.axis_size("dp")
    devices = blocks * groups
    rows, features = tokens.shape
    channels = features // devices
    every = [lax.all_gather(a, BOTH, axis=0) for a in weights]
    gain = every[0][:, :, 0].reshape(features, 1)
    key_all, value_all, query_all, out_all = [a.reshape(features, -1) for a in every[1:5]]
    turned = tokens.astype(F32).T
    centered = turned - jnp.mean(turned, axis=0, keepdims=True)
    inverse = lax.rsqrt(jnp.mean(centered * centered, axis=0, keepdims=True) + EPSILON)
    standard = centered * inverse
    normed = (standard * gain).astype(BF16)
    queries = contract(query_all, normed, 0, 0)
    keys = contract(key_all, normed, 0, 0).astype(BF16)
    values = (contract(value_all, normed, 0, 0) * live).astype(BF16)
    sent = jnp.stack([a.reshape(devices, channels, rows) for a in (keys, values)], axis=1)
    k_own, v_own = lax.all_to_all(sent, BOTH, 0, 0, tiled=True).transpose(1, 2, 0, 3)
    per_channel = (channels, devices, rows)
    shifted, mixed = local_call(
        partial(mixer_body, blocks, groups, rows),
        [jax.ShapeDtypeStruct(per_channel, F32), jax.ShapeDtypeStruct(per_channel, BF16)],
        k_own, v_own, *mixer_rows(weights[0], mixer, rows, blocks)[0],
    )
    ssm = lax.all_to_all(mixed.transpose(1, 0, 2), BOTH, 0, 0, tiled=True)
    ssm = ssm.reshape(features, rows)
    gated = (queries * ssm.astype(F32)).astype(BF16)
    residual = tokens.astype(F32) + contract(gated, out_all, 0, 0)
    inverse = jnp.broadcast_to(inverse, (8, rows))
    kept = [residual, standard, inverse, normed, queries, ssm, gated, k_own, v_own, shifted]
    up, down, qkv, out_two = [a.reshape(-1, a.shape[2]) for a in every[5:9]]
    residual_two, stored = feed_forward(residual, every[0][:, :, 1].reshape(features), up, down)
    normed_three = layer_norm(residual_two, every[0][:, :, 2].reshape(features)).astype(BF16)
    joint = product(normed_three, qkv).astype(BF16)
    att_q = joint[:, :features]
    att_kv = lax.all_gather(joint[:, features:], "seq", axis=0)
    where = jnp.stack([lax.axis_index("seq").astype(F32) * rows, jnp.sum(key_live)])
    attended, log_total = local_call(
        attend_body,
        [jax.ShapeDtypeStruct((rows, features), BF16), jax.ShapeDtypeStruct((rows, 128), F32)],
        where.astype(jnp.int32), att_q, att_kv.reshape(blocks * rows, 2 * features), scalars=1,
    )
    residual_three = residual_two + product(attended, out_two)
    kept += [*stored, residual_two, normed_three, att_q, att_kv, attended, log_total]
    return every, kept + [residual_three, None, None]


def mix_back(
    blocks, groups, rows, out_grad, keys, values, shifted, tap_row, kernel_row, skip
):
    span = blocks * rows
    turned = (
        lax.broadcasted_iota(jnp.int32, (rows, rows), 0)
        + lax.broadcasted_iota(jnp.int32, (rows, rows), 1)
        == rows - 1
    ).astype(BF16)

    def lag_sums(earlier, spread, lanes):
        backward = product(earlier, turned).astype(BF16)
        pairs = product_sum(backward, spread)
        padded = jnp.concatenate(
            [pairs, jnp.zeros((rows, lanes - pairs.shape[1]), F32)], axis=1
        )
        return jnp.sum(
            pltpu.roll(padded, lanes - rows + 1, 1, stride=1, stride_axis=0),
            axis=0,
            keepdims=True,
        )

    taps = toeplitz(tap_row, rows)[:, : 2 * rows].astype(BF16)
    longer = toeplitz(kernel_row, rows)[:, :span].astype(BF16)
    values = values.astype(F32)
    signal = shifted * values
    later = block_spread(out_grad, blocks, blocks, groups, rows).astype(BF16)
    signal_grad = product_back(later, longer) + skip * out_grad
    kernel_grad = lag_sums(signal.astype(BF16), later, kernel_row.shape[1])
    skip_grad = jnp.sum(jnp.sum(signal * out_grad, axis=0, keepdims=True), axis=1, keepdims=True)
    shifted_grad = values * signal_grad
    next_two = block_spread(shifted_grad, blocks, 2, groups, rows).astype(BF16)
    return (
        product_back(next_two, taps),
        shifted * signal_grad,
        kernel_grad,
        lag_sums(keys, next_two, tap_row.shape[1]),
        skip_grad,
    )


def mixer_back_body(
    blocks, groups, rows,
    grad_ref, k_ref, v_ref, shifted_ref, taps_ref, kernel_ref, skip_ref,
    grad_k_ref, grad_v_ref, kernel_grad_ref, taps_grad_ref, skip_grad_ref,
):
    for ch in range(k_ref.shape[0]):
        row = slice(ch, ch + 1)
        grad_k, grad_v, kernel_grad_ref[row, :], taps_grad_ref[row, :], skip_grad = mix_back(
            blocks, groups, rows, grad_ref[ch].astype(F32), k_ref[ch], v_ref[ch], shifted_ref[ch],
            taps_ref[row, :], kernel_ref[row, :], skip_ref[row, :1],
        )
        grad_k_ref[ch], grad_v_ref[ch] = grad_k.astype(BF16), grad_v.astype(BF16)
        skip_grad_ref[row, :] = jnp.broadcast_to(skip_grad, (1, 128))


def packed(ref, channels, residual_shape):
    rows, width = residual_shape
    top = 2 * channels

    def at(row, column, height, columns):
        return ref.at[pl.ds(row, height), pl.ds(column, columns)]

    return (
        [
            at(channels, 0, channels, 3 * width),
            at(0, 0, channels, 4 * width),
            at(top, 0, 4 * channels, width),
        ]
        + [at(top + n * channels, width, channels, width) for n in range(4)]
        + [at(top + 5 * channels, width, channels, 128)]
        + [at(top, 2 * width, rows, width)]
        + [at(top + (4 + n) * channels, 0, channels, 64) for n in range(4)]
        + [at(top + 4 * channels, width, channels, 64)]
        + [at(top + 6 * channels, width, channels, 128)]
    )


def last_body(parts, count, kinds, *refs):
    early = refs[:count]
    (
        gain_in, branch, grad_one, live, gated, normed, queries, ssm, standard, inverse,
        gains, key_all, value_all, query_all, out_all,
        k_ref, v_ref, shifted_ref, taps_ref, kernel_ref, small,
    ) = refs[count : count + 21]
    states = refs[count + 21 : count + 25]
    refs = refs[count + 25 :]
    *totals, input_grad, taps_out, s0, s1, s2, s3, skip_grad_ref = packed(
        refs[0], key_all.shape[1], branch.shape
    )
    state_grads = (s0, s1, s2, s3)
    refs = refs[1:]
    out_term, query_term, key_term, value_term, gain_term = own_terms = refs[:5]
    buffers = refs[5 : 5 + 4 * len(parts)]
    refs = refs[5 + 4 * len(parts) :]
    held = dict(zip(kinds, refs[: len(kinds)]))
    (
        wide, sent_g, came_g, sent_kv, came_kv, query_grad, cols, state_sums, kernel_grad_ref,
        taps_grad_ref, send_sem, recv_sem, mine_sem, swap_sem,
    ) = refs[len(kinds) :]
    devices, channels = key_all.shape[0], key_all.shape[1]
    rows, features = branch.shape
    blocks, groups = lax.axis_size("seq"), lax.axis_size("dp")
    greet(all_others()[2])
    reduce = Reduce(
        parts, early + own_terms, totals, buffers, (early, held), send_sem, recv_sem, mine_sem
    )
    reduce.fetch_first()

    def slots(value, columns):
        return value.reshape(2, 2, 4, 2, channels, columns)

    gated_grad = contract(flat_weight(out_all), branch[...], 1, 1)
    sent_g[...] = (gated_grad * queries[...]).reshape(devices, channels, rows).astype(BF16)
    over = Swap(sent_g, came_g, swap_sem.at[0], swap_sem.at[1])
    over.start()
    reduce.start(range(count))
    query_grad[...] = (gated_grad * ssm[...].astype(F32)).astype(BF16)
    out_term[...] = slots(product(gated[...], branch[...]), features).astype(BF16)
    query_term[...] = slots(contract(normed[...], query_grad[...], 1, 1), features).astype(BF16)
    reduce.start((count, count + 1))
    reduce.run(PLACES[0])
    over.wait()
    wide[:, :channels, :] = came_g[...].astype(F32)
    for ch in range(channels):
        row = slice(ch, ch + 1)
        grad_k, grad_v, kernel_grad_ref[ch], taps_grad_ref[row, :], skip_grad = mix_back(
            blocks, groups, rows, wide[:, ch, :], k_ref[ch], v_ref[ch], shifted_ref[ch],
            taps_ref[row, :], kernel_ref[ch], small[row, 4:5],
        )
        wide[:, ch, :], wide[:, channels + ch, :] = grad_k, grad_v
        skip_grad_ref[row, :] = jnp.broadcast_to(skip_grad, (1, 128))
        if ch % 8 == 7:
            reduce.run(PLACES[1 + ch // 8])
    sent_kv[...] = wide[...].astype(BF16)
    back = Swap(sent_kv, came_kv, swap_sem.at[2], swap_sem.at[3])
    back.start()
    taps_out[...] = taps_grad_ref[:, : taps_out.shape[1]]
    grads = kernel_rows_back(
        *[a[...].astype(F32) for a in states], cols, state_sums, kernel_grad_ref, blocks * rows
    )
    for place, grad in zip(state_grads, grads):
        place[...] = grad
    reduce.run(PLACES[4])
    back.wait()
    wide[...] = came_kv[...].astype(F32)
    key_grad = wide[:, :channels, :].reshape(features, rows).astype(BF16)
    value_grad = (wide[:, channels:, :].reshape(features, rows) * live[...]).astype(BF16)
    key_term[...] = slots(contract(normed[...], key_grad, 1, 1), features).astype(BF16)
    value_term[...] = slots(contract(normed[...], value_grad, 1, 1), features).astype(BF16)
    reduce.start((count + 2, count + 3))
    normed_grad = product(flat_weight(query_all), query_grad[...])
    normed_grad += product(flat_weight(key_all), key_grad)
    normed_grad += product(flat_weight(value_all), value_grad)
    gain_grad = jnp.sum(normed_grad * standard[...], axis=1, keepdims=True)
    lane = lax.broadcasted_iota(jnp.int32, (features, 128), 1)
    gain_term[...] = slots(jnp.where(lane == 0, gain_grad, gain_in[...]), 128)
    reduce.start((count + 4,))
    scaled = normed_grad * gains[...].reshape(features, 128)[:, :1]
    scaled = (
        scaled
        - jnp.mean(scaled, axis=0, keepdims=True)
        - standard[...] * jnp.mean(scaled * standard[...], axis=0, keepdims=True)
    )
    input_grad[...] = grad_one[...] + (scaled * inverse[:1, :]).T
    reduce.finish()


def last_layer(
    terms, gain_in, branch, grad_one, live, kept, weights, small, mixer, done, collective_id
):
    standard, inverse, normed, queries, ssm, gated, k_own, v_own, shifted = kept[:9]
    tap_row, kernel_row = kept[9:]
    gains, key_all, value_all, query_all, out_all = weights
    devices, channels, features = key_all.shape
    rows = branch.shape[0]
    count = len(terms)
    square = (channels, features)
    shapes = [a.shape[1:] for a in terms] + [square] * 4 + [(channels, 128)]
    types = [BF16] * (count + 4) + [F32]
    parts = cut(shapes)
    kinds = sorted({(part[2], part[4]) for part in parts if part[0] < count})
    scratch = [pltpu.VMEM((2, 2, 4, 2) + s, t) for s, t in zip(shapes[count:], types[count:])]
    for i, _, part_rows, _, columns, x_last in parts:
        for lead in ((2, 4, 2), (4, 2) if x_last else (2, 4), (4,), (3,)):
            scratch.append(pltpu.VMEM(lead + (part_rows, columns), types[i]))
    scratch += [pltpu.VMEM((2, 2, 4, 2) + kind, BF16) for kind in kinds]
    scratch += [
        pltpu.VMEM((devices, 2 * channels, rows), F32),
        pltpu.VMEM((devices, channels, rows), BF16),
        pltpu.VMEM((devices, channels, rows), BF16),
        pltpu.VMEM((devices, 2 * channels, rows), BF16),
        pltpu.VMEM((devices, 2 * channels, rows), BF16),
        pltpu.VMEM((features, rows), BF16),
        pltpu.VMEM((channels * mixer[1].shape[1], 128), F32),
        pltpu.VMEM((channels * mixer[1].shape[1], 128), F32),
        pltpu.VMEM(kernel_row.shape, F32),
        pltpu.VMEM(tap_row.shape, F32),
        pltpu.SemaphoreType.DMA((len(parts), 6)),
        pltpu.SemaphoreType.DMA((len(parts), 6)),
        pltpu.SemaphoreType.DMA((len(parts),)),
        pltpu.SemaphoreType.DMA((4,)),
    ]
    vmem, anywhere = pl.BlockSpec(memory_space=pltpu.VMEM), pl.BlockSpec(memory_space=pl.ANY)
    height = 2 * channels + max(rows, 8 * channels)
    results = [jax.ShapeDtypeStruct((height, 4 * features), F32)]
    out = pl.pallas_call(
        partial(last_body, parts, count, kinds),
        out_shape=results,
        in_specs=[anywhere] * count + [vmem] * 25,
        out_specs=[vmem] * len(results),
        scratch_shapes=scratch,
        compiler_params=pltpu.CompilerParams(
            collective_id=collective_id, has_side_effects=True, vmem_limit_bytes=62 * MIB
        ),
    )(
        *[a.reshape((2, 2, 4, 2) + a.shape[1:]) for a in terms],
        gain_in, branch, grad_one, live, gated, normed, queries, ssm, standard, inverse,
        gains, key_all, value_all, query_all, out_all,
        k_own, v_own, shifted, tap_row, kernel_row, small, *mixer[1:],
    )
    return settle(done, out[0], channels, (rows, features))


def last_layer_apart(terms, gain_in, branch, grad_one, live, kept, weights, small, mixer):
    standard, inverse, normed, queries, ssm, gated, k_own, v_own, shifted = kept[:9]
    gains, key_all, value_all, query_all, out_all = weights
    devices, channels, features = key_all.shape
    rows = branch.shape[0]
    blocks, groups = lax.axis_size("seq"), lax.axis_size("dp")
    key_all, value_all, query_all, out_all = [
        a.reshape(features, features) for a in (key_all, value_all, query_all, out_all)
    ]
    made, pull = mixer_rows(small, mixer, rows, blocks)
    gated_grad = contract(out_all, branch, 1, 1)
    query_grad = (gated_grad * ssm.astype(F32)).astype(BF16)
    sent = (gated_grad * queries).reshape(devices, channels, rows).astype(BF16)
    own = lax.all_to_all(sent, BOTH, 0, 0, tiled=True).transpose(1, 0, 2)
    per_channel = jax.ShapeDtypeStruct(own.shape, BF16)
    grad_k, grad_v, kernel_grad, taps_grad, skip_grad = local_call(
        partial(mixer_back_body, blocks, groups, rows),
        [per_channel, per_channel]
        + [jax.ShapeDtypeStruct(a.shape, F32) for a in (made[1], made[0])]
        + [jax.ShapeDtypeStruct((channels, 128), F32)],
        own, k_own, v_own, shifted, *made,
    )
    sent = jnp.stack([grad_k.transpose(1, 0, 2), grad_v.transpose(1, 0, 2)], axis=1)
    came = lax.all_to_all(sent, BOTH, 0, 0, tiled=True)
    key_grad = came[:, 0].reshape(features, rows)
    value_grad = (came[:, 1].reshape(features, rows) * live).astype(BF16)
    normed_grad = (
        product(query_all, query_grad) + product(key_all, key_grad) + product(value_all, value_grad)
    )
    gain_grad = jnp.sum(normed_grad * standard, axis=1, keepdims=True)
    lane = lax.broadcasted_iota(jnp.int32, (features, 128), 1)
    gain_term = jnp.where(lane == 0, gain_grad, gain_in)
    scaled = normed_grad * gains.reshape(features, 128)[:, :1]
    scaled = (
        scaled
        - jnp.mean(scaled, axis=0, keepdims=True)
        - standard * jnp.mean(scaled * standard, axis=0, keepdims=True)
    )
    input_grad = grad_one + (scaled * inverse[:1]).T
    last = [product(gated, branch)]
    last += [contract(normed, g, 1, 1) for g in (query_grad, key_grad, value_grad)]
    last = [a.reshape(devices, channels, features).astype(BF16) for a in last]
    last.append(gain_term.reshape(devices, channels, 128))
    sums = [
        lax.psum_scatter(a, BOTH, scatter_dimension=0, tiled=False).astype(F32)
        for a in list(terms) + last
    ]
    taps_grad = taps_grad[:, : mixer[0].shape[1]]
    return sums, [input_grad, taps_grad, *pull(kernel_grad[:, : rows * blocks]), skip_grad]


def allowed_keys(first, length, rows, keys):
    row_places = first + lax.broadcasted_iota(jnp.int32, (rows, keys), 0)
    key_places = lax.broadcasted_iota(jnp.int32, (rows, keys), 1)
    return (key_places <= row_places) & (key_places < length)


def attend_heads(allowed, q_ref, kv, out_ref, log_ref):
    features = q_ref.shape[1]
    for head in range(HEADS):
        own = slice(head * HDIM, (head + 1) * HDIM)
        values = slice(features + head * HDIM, features + (head + 1) * HDIM)
        scores = product_back(q_ref[:, own], kv[:, own]) * HDIM ** (-0.5)
        scores = jnp.where(allowed, scores, MASKED)
        most = jnp.max(scores, axis=1, keepdims=True)
        powers = jnp.exp(scores - most)
        total = jnp.sum(powers, axis=1, keepdims=True)
        weights = (powers * (1.0 / total)).astype(BF16)
        out_ref[:, own] = product(weights, kv[:, values]).astype(BF16)
        log_ref[:, head : head + 1] = most + jnp.log(total)


def attend_body(where_ref, q_ref, kv_ref, out_ref, log_ref):
    allowed = allowed_keys(where_ref[0], where_ref[1], q_ref.shape[0], kv_ref.shape[0])
    attend_heads(allowed, q_ref, kv_ref, out_ref, log_ref)


def attend_back_head(head, allowed, q_ref, kv, log_ref, grad_ref):
    features = q_ref.shape[1]
    scale = HDIM ** (-0.5)
    own = slice(head * HDIM, (head + 1) * HDIM)
    values = slice(features + head * HDIM, features + (head + 1) * HDIM)
    queries, grads = q_ref[:, own], grad_ref[:, own]
    scores = product_back(queries, kv[:, own]) * scale
    probs = jnp.where(allowed, jnp.exp(scores - log_ref[:, head : head + 1]), 0.0)
    prob_grad = product_back(grads, kv[:, values])
    delta = jnp.sum(probs * prob_grad, axis=1, keepdims=True)
    grad_scores = (probs * (prob_grad - delta)).astype(BF16)
    return (
        (product(grad_scores, kv[:, own]) * scale).astype(BF16),
        (product_sum(grad_scores, queries) * scale).astype(BF16),
        product_sum(probs.astype(BF16), grads).astype(BF16),
    )


def attend_back_body(where_ref, q_ref, kv_ref, log_ref, grad_ref, grad_q_ref, grad_kv_ref):
    features = q_ref.shape[1]
    allowed = allowed_keys(where_ref[0], where_ref[1], q_ref.shape[0], kv_ref.shape[0])
    for head in range(HEADS):
        own = slice(head * HDIM, (head + 1) * HDIM)
        values = slice(features + head * HDIM, features + (head + 1) * HDIM)
        grad_q_ref[:, own], grad_kv_ref[:, own], grad_kv_ref[:, values] = attend_back_head(
            head, allowed, q_ref, kv_ref, log_ref, grad_ref
        )


def norm_back(residual, gain_row, grad):
    average = jnp.mean(residual, axis=-1, keepdims=True)
    centered = residual - average
    inverse = lax.rsqrt(jnp.mean(centered * centered, axis=-1, keepdims=True) + EPSILON)
    standard = centered * inverse
    scaled = grad * gain_row
    inner = jnp.mean(scaled * standard, axis=-1, keepdims=True)
    grad_input = inverse * (scaled - jnp.mean(scaled, axis=-1, keepdims=True) - standard * inner)
    return grad_input, jnp.sum(grad * standard, axis=0, keepdims=True)


def middle_body(parts, count, kinds, *refs):
    early = refs[:count]
    qkv_all, up_all, down_all = refs[count : count + 3]
    (
        att_q, att_kv, log_total, grad_attended, key_live, normed_three, residual_two,
        grad_three, gains, act_one, pre_one, normed_two, residual_one,
    ) = refs[count + 3 : count + 16]
    refs = refs[count + 16 :]
    totals = refs[:count]
    qkv_out, up_out, down_out, grad_one, gain_grads = refs[count : count + 5]
    refs = refs[count + 5 :]
    buffers = refs[: 4 * len(parts)]
    refs = refs[4 * len(parts) :]
    held = dict(zip(kinds, refs[: len(kinds)]))
    (
        qkv, up, down, grad_q, grad_kv, line_one, line_two,
        send_sem, recv_sem, mine_sem, load_sem, store_sem, line_send, line_recv,
    ) = refs[len(kinds) :]
    rows, features = att_q.shape
    keys = att_kv.shape[0] * rows
    y, c, z, x = coordinates()
    greet(six_peers(y, c, z, x))
    loads = [
        pltpu.make_async_copy(src, dst, load_sem.at[n])
        for n, (src, dst) in enumerate(((qkv_all, qkv), (up_all, up), (down_all, down)))
    ]
    stores = [
        pltpu.make_async_copy(src, dst, store_sem.at[n])
        for n, (src, dst) in enumerate(((qkv, qkv_out), (up, up_out), (down, down_out)))
    ]
    reduce = Reduce(
        parts, early, totals, buffers, (early, held), send_sem, recv_sem, mine_sem
    )
    reduce.fetch_first()
    reduce.start(range(count))
    for load in loads:
        load.start()
    gain_rows = gains[...].reshape(features, 128).T

    row_places = (y * 2 + c) * rows + lax.broadcasted_iota(jnp.int32, (rows, keys), 0)
    key_places = lax.broadcasted_iota(jnp.int32, (rows, keys), 1)
    allowed = jnp.where(key_places <= row_places, key_live[...], 0.0) > 0.5
    kv = att_kv[...].reshape(keys, 2 * features)
    for head in range(HEADS):
        own = slice(head * HDIM, (head + 1) * HDIM)
        values = slice(features + head * HDIM, features + (head + 1) * HDIM)
        grad_q[:, own], key_grad, value_grad = attend_back_head(
            head, allowed, att_q, kv, log_total, grad_attended
        )
        grad_kv[:, :, :, own] = key_grad.reshape(2, 2, rows, HDIM)
        grad_kv[:, :, :, values] = value_grad.reshape(2, 2, rows, HDIM)
        if head % 4 == 3:
            reduce.run(MIDDLE[head // 4])

    core, side = device_of(y, 1 - c, z, x), device_of(1 - y, c, z, x)

    def line_copy(n, source, target, where):
        return pltpu.make_async_remote_copy(
            src_ref=source,
            dst_ref=where,
            send_sem=line_send.at[n],
            recv_sem=line_recv.at[n],
            device_id=target,
            device_id_type=MESH,
        )

    far = line_copy(0, grad_kv.at[1 - y, 1 - c], core, line_one.at[1 - y])
    near = line_copy(1, grad_kv.at[y, 1 - c], core, line_one.at[y])
    onward = line_copy(2, line_one.at[1 - y], side, line_two)
    far.start()
    near.start()
    far.wait_recv()
    mine = line_one[1 - y].astype(F32) + grad_kv[1 - y, c].astype(F32)
    line_one[1 - y] = mine.astype(BF16)
    onward.start()
    loads[0].wait()
    query_grad = grad_q[...]
    grad_normed = product_back(query_grad, flat_part(qkv, 0, features))
    reduce.run(MIDDLE[3])
    near.wait_recv()
    onward.wait_recv()
    total = (line_one[y].astype(F32) + grad_kv[y, c].astype(F32)) + line_two[...].astype(F32)
    joint = [query_grad, total[:, :features].astype(BF16), total[:, features:].astype(BF16)]
    for n in (1, 2):
        grad_normed += product_back(joint[n], flat_part(qkv, n * features, features))
    grad_from, gain_grad = norm_back(residual_two[...], gain_rows[2:3], grad_normed)
    grad_two = grad_three[...] + grad_from
    gain_grads[...] = jnp.zeros_like(gain_grads)
    gain_grads[2:3, :] = gain_grad
    slots, shard = qkv.shape[0], qkv.shape[1]
    for n in range(3):
        term = product_sum(normed_three[...], joint[n]).reshape(slots, shard, features)
        qkv[:, :, n * features : (n + 1) * features] = term.astype(BF16)
    stores[0].start()
    reduce.run(MIDDLE[4])

    branch = grad_two.astype(BF16)
    loads[1].wait()
    loads[2].wait()
    deep = down.shape[1]
    few = features // deep
    grad_normed = jnp.zeros((rows, features), F32)
    for n in range(up.shape[2] // features):
        own = slice(n * features, (n + 1) * features)
        some = pl.ds(n * few, few)
        gate_grad = product_back(branch, down[some].reshape(features, features))
        pre_grad = jax.vjp(jax.nn.gelu, pre_one[:, own])[1](gate_grad)[0].astype(BF16)
        grad_normed += product_back(pre_grad, flat_part(up, n * features, features))
        term = product_sum(act_one[:, own], branch)
        down[some] = term.astype(BF16).reshape(few, deep, features)
        term = product_sum(normed_two[...], pre_grad).reshape(slots, shard, features)
        up[:, :, own] = term.astype(BF16)
        reduce.run(MIDDLE[5 + n])
    stores[1].start()
    stores[2].start()
    grad_from, gain_grad = norm_back(residual_one[...], gain_rows[1:2], grad_normed)
    grad_one[...] = grad_two + grad_from
    gain_grads[1:2, :] = gain_grad
    reduce.finish()
    for each in (far, near, onward):
        each.wait_send()
    for store in stores:
        store.wait()


def middle_layers(terms, weights, kept, collective_id):
    count = len(terms)
    att_q, act_one = kept[0], kept[9]
    rows, features = att_q.shape
    shapes = [a.shape[1:] for a in terms]
    parts = cut(shapes)
    kinds = sorted({(part[2], part[4]) for part in parts})
    scratch = []
    for _, _, part_rows, _, columns, x_last in parts:
        for lead in ((2, 4, 2), (4, 2) if x_last else (2, 4), (4,), (3,)):
            scratch.append(pltpu.VMEM(lead + (part_rows, columns), BF16))
    scratch += [pltpu.VMEM((2, 2, 4, 2) + kind, BF16) for kind in kinds]
    scratch += [pltpu.VMEM(a.shape, BF16) for a in weights]
    scratch += [
        pltpu.VMEM((rows, features), BF16),
        pltpu.VMEM((2, 2, rows, 2 * features), BF16),
        pltpu.VMEM((2, rows, 2 * features), BF16),
        pltpu.VMEM((rows, 2 * features), BF16),
        pltpu.SemaphoreType.DMA((len(parts), 6)),
        pltpu.SemaphoreType.DMA((len(parts), 6)),
        pltpu.SemaphoreType.DMA((len(parts),)),
        pltpu.SemaphoreType.DMA((3,)),
        pltpu.SemaphoreType.DMA((3,)),
        pltpu.SemaphoreType.DMA((3,)),
        pltpu.SemaphoreType.DMA((3,)),
    ]
    vmem, anywhere = pl.BlockSpec(memory_space=pltpu.VMEM), pl.BlockSpec(memory_space=pl.ANY)
    results = [jax.ShapeDtypeStruct(s, F32) for s in shapes]
    results += [jax.ShapeDtypeStruct(a.shape, BF16) for a in weights]
    results += [
        jax.ShapeDtypeStruct((rows, features), F32),
        jax.ShapeDtypeStruct((8, features), F32),
    ]
    out = pl.pallas_call(
        partial(middle_body, parts, count, kinds),
        out_shape=results,
        in_specs=[anywhere] * (count + 3) + [vmem] * 13,
        out_specs=[vmem] * count + [anywhere] * 3 + [vmem] * 2,
        scratch_shapes=scratch,
        compiler_params=pltpu.CompilerParams(
            collective_id=collective_id, has_side_effects=True, vmem_limit_bytes=60 * MIB
        ),
    )(*[a.reshape((2, 2, 4, 2) + a.shape[1:]) for a in terms], *weights, *kept)
    return out[:count], out[count : count + 3], out[count + 3], out[count + 4]


def local_call(body, out_shape, *operands, scalars=0, limit=48):
    vmem = pl.BlockSpec(memory_space=pltpu.VMEM)
    smem = pl.BlockSpec(memory_space=pltpu.SMEM)
    return pl.pallas_call(
        body,
        out_shape=out_shape,
        in_specs=[smem] * scalars + [vmem] * (len(operands) - scalars),
        out_specs=jax.tree.map(lambda _: vmem, out_shape),
        compiler_params=pltpu.CompilerParams(vmem_limit_bytes=limit * MIB),
    )(*operands)


def settle(done, everything, channels, residual_shape):
    width = residual_shape[1]
    shapes = [a.shape for a in done]
    shapes += [(channels, 3 * width), (channels, 4 * width), (4 * channels, width)]
    shapes += [(channels, width)] * 4 + [(channels, 128), residual_shape]
    shapes += [(channels, 64)] * 5 + [(channels, 128)]
    count = len(done)

    def body(*refs):
        sources = [*refs[:count], *packed(refs[count], channels, residual_shape)]
        for source, place in zip(sources, refs[count + 1 :]):
            place[...] = source[...]

    out = local_call(
        body, [jax.ShapeDtypeStruct(s, F32) for s in shapes], *done, everything
    )
    return out[: count + 8], out[count + 8 :]


def shards(
    tokens, lengths, norm_one, query_one, key_one, value_one, shift_taps, decay_log,
    turn_angle, mix_real, mix_imag, skip_gain, out_one, norm_two, up_one, down_one,
    norm_three, qkv_weight, out_two, norm_four, up_two, down_two, cotangent,
):
    blocks, groups = lax.axis_size("seq"), lax.axis_size("dp")
    devices = blocks * groups
    rows, features = tokens.shape[1], tokens.shape[2]
    channels = features // devices
    place = lax.axis_index("seq")
    length = lengths[0]
    row_places = place * rows + jnp.arange(rows, dtype=jnp.int32)
    live_mask = (row_places < length).astype(F32)[:, None]
    live_lane = (row_places < length).astype(F32)[None, :]

    small = jnp.stack([norm_one, norm_two, norm_three, norm_four, skip_gain], axis=1)
    small = jnp.pad(small.astype(F32), ((0, 0), (0, 123)))
    mixer = [shift_taps, decay_log, turn_angle, mix_real, mix_imag]
    weights = [
        small, key_one, value_one, query_one, out_one, up_one, down_one, qkv_weight, out_two,
        up_two, down_two,
    ]
    key_live = (jnp.arange(blocks * rows, dtype=jnp.int32) < length).astype(F32)[None, :]
    if grouped():
        every, kept = first_layer(weights, tokens[0], live_lane, key_live, mixer, 1)
    else:
        every, kept = first_layer_apart(weights, tokens[0], live_lane, key_live, mixer)
    residual_one = kept[0]
    gain_one, gain_two, gain_three, gain_four = [
        every[0][:, :, n].reshape(features) for n in range(4)
    ]
    up_one_all, down_one_all, qkv_all, out_two_all, late_up, late_down = [
        g.reshape((-1, g.shape[2])) for g in every[5:]
    ]

    normed_two, pre_one, act_one, residual_two, normed_three, att_q, kv = kept[10:17]
    attended, log_total, residual_three = kept[17:20]
    residual_four, stored_four = feed_forward(residual_three, gain_four, late_up, late_down)
    activations = (live_mask * residual_four).astype(BF16)

    grad_four = live_mask * cotangent[0].astype(F32)
    grad_three, grad_norm_four, grad_up_two, grad_down_two = feed_back(
        residual_three, gain_four, late_up, late_down, stored_four, grad_four
    )
    branch_three = grad_three.astype(BF16)
    grad_out_two = product_sum(attended, branch_three)
    grad_attended = product_back(branch_three, out_two_all).astype(BF16)
    slots = (devices, -1)
    terms = [
        g.astype(BF16).reshape(slots + g.shape[1:])
        for g in (grad_up_two, grad_down_two, grad_out_two)
    ]
    if grouped():
        done, terms, grad_one, gain_grads = middle_layers(
            terms,
            every[7:8] + every[5:7],
            [
                att_q, kv, log_total, grad_attended, key_live, normed_three, residual_two,
                grad_three, every[0], act_one, pre_one, normed_two, residual_one,
            ],
            3,
        )
        grad_norm_two, grad_norm_three = gain_grads[1], gain_grads[2]
    else:
        grad_q, grad_kv = local_call(
            attend_back_body,
            [
                jax.ShapeDtypeStruct((rows, features), BF16),
                jax.ShapeDtypeStruct((blocks * rows, 2 * features), BF16),
            ],
            jnp.stack([place.astype(jnp.int32) * rows, length]), att_q,
            kv.reshape(blocks * rows, 2 * features), log_total, grad_attended, scalars=1,
        )
        grad_kv = lax.psum_scatter(
            grad_kv.reshape(blocks, rows, 2 * features), "seq", scatter_dimension=0
        )
        grad_joint = jnp.concatenate([grad_q, grad_kv.astype(BF16)], axis=1)
        grad_qkv_weight = product_sum(normed_three, grad_joint)
        grad_normed_three = product_back(grad_joint, qkv_all)
        grad_from_three, grad_norm_three = jax.vjp(layer_norm, residual_two, gain_three)[1](
            grad_normed_three
        )
        grad_one, grad_norm_two, grad_up_one, grad_down_one = feed_back(
            residual_one, gain_two, up_one_all, down_one_all, (normed_two, pre_one, act_one),
            grad_three + grad_from_three,
        )
        done = []
        terms += [
            g.astype(BF16).reshape(slots + g.shape[1:])
            for g in (grad_qkv_weight, grad_up_one, grad_down_one)
        ]
    branch_one = grad_one.astype(BF16)
    gain_in = jnp.stack(
        [jnp.zeros_like(grad_norm_two), grad_norm_two, grad_norm_three, grad_norm_four], axis=1
    )
    gain_in = jnp.pad(gain_in, ((0, 0), (0, 124)))
    last = (
        terms, gain_in, branch_one, grad_one, live_lane, kept[1:10] + kept[20:], every[:5], small,
        mixer,
    )
    if grouped():
        sums, rest = last_layer(*last, done, 2)
    else:
        sums, rest = last_layer_apart(*last)
    grad_up_two, grad_down_two, grad_out_two, grad_qkv_weight, grad_up_one, grad_down_one = sums[:6]
    grad_out_one, grad_query_one, grad_key_one, grad_value_one, gain_grads = sums[6:]
    gain_grads = gain_grads[:, :4].T
    input_grad, grad_shift_taps, grad_decay_log, grad_turn_angle, grad_mix_real = rest[:5]
    grad_mix_imag, skip_grad = rest[5:]
    grad_skip_gain = skip_grad[:, 0]
    return (
        activations[None], input_grad[None],
        gain_grads[0], grad_query_one, grad_key_one, grad_value_one,
        grad_shift_taps, grad_decay_log, grad_turn_angle, grad_mix_real, grad_mix_imag,
        grad_skip_gain, grad_out_one,
        gain_grads[1], grad_up_one, grad_down_one,
        gain_grads[2], grad_qkv_weight, grad_out_two,
        gain_grads[3], grad_up_two, grad_down_two,
    )


def solution(mesh):
    row, vector = P(BOTH, None), P(BOTH)
    whole = P("dp", "seq", None)
    weights = (
        vector, row, row, row, row, row, row, row, row, vector, row,
        vector, row, row, vector, row, row, vector, row, row,
    )
    return jax.shard_map(
        shards,
        mesh=mesh,
        in_specs=(whole, P("dp")) + weights + (whole,),
        out_specs=(whole, whole) + weights,
        check_vma=False,
    )
```

```python
from functools import partial

import jax
import jax.numpy as jnp
from jax import lax
from jax.experimental import pallas as pl
from jax.experimental.pallas import tpu as pltpu
from jax.sharding import PartitionSpec as P

HEADS = 12
HDIM = 64
EPSILON = 1e-05
HIGHEST = lax.Precision.HIGHEST
MASKED = -1e30
BOTH = ("seq", "dp")
MESH = pl.DeviceIdType.MESH
MIB = 1024 * 1024
LAGS = (0, 2, 4, 6)
PLACES = (4, 5, 6, 7, 9)
MIDDLE = (1, 1, 2, 3, 4, 5, 6, 7, 8)
EARLY = 2
RUNS = (8, 9, 9, 10, 11, 12)
AHEAD = 5
F32 = jnp.float32
BF16 = jnp.bfloat16


def grouped():
    return lax.axis_size("seq") == 4 and lax.axis_size("dp") == 8


def coordinates():
    seq, dp = lax.axis_index("seq"), lax.axis_index("dp")
    return seq // 2, seq % 2, dp // 2, dp % 2


def slot_of(y, c, z, x):
    return (y * 2 + c) * 8 + z * 2 + x


def device_of(y, c, z, x):
    return (y * 2 + c, z * 2 + x)


def greet(peers):
    barrier = pltpu.get_barrier_semaphore()
    for peer in peers:
        pl.semaphore_signal(barrier, inc=1, device_id=peer, device_id_type=MESH)
    pl.semaphore_wait(barrier, len(peers))


def six_peers(y, c, z, x):
    return [device_of(y, c, (z + k) % 4, x) for k in (1, 2, 3)] + [
        device_of(y, c, z, 1 - x),
        device_of(1 - y, c, z, x),
        device_of(y, 1 - c, z, x),
    ]


class Gather:
    def __init__(self, parts, sources, gathered, local_sem, send_sem, recv_sem, ahead=None):
        self.parts, self.sources, self.gathered = parts, sources, gathered
        self.send_sem, self.recv_sem, self.ahead = send_sem, recv_sem, ahead or AHEAD
        self.y, self.c, self.z, self.x = y, c, z, x = coordinates()
        self.me = slot_of(y, c, z, x)
        self.across_x = device_of(y, c, z, 1 - x)
        self.across_y = device_of(1 - y, c, z, x)
        self.other_core = device_of(y, 1 - c, z, x)
        self.own = [
            pltpu.make_async_copy(sources[i], gathered[i].at[self.me], local_sem.at[i])
            for i in range(len(sources))
        ]
        self.done = 0

    def place(self, p, slot):
        i, row, rows, column, columns, _ = self.parts[p]
        return self.gathered[i].at[slot, pl.ds(row, rows), pl.ds(column, columns)]

    def send(self, p, slot, target, first=False):
        i, row, rows, column, columns, _ = self.parts[p]
        source = self.sources[i].at[pl.ds(row, rows), pl.ds(column, columns)]
        pltpu.make_async_remote_copy(
            src_ref=source if first else self.place(p, slot),
            dst_ref=self.place(p, slot),
            send_sem=self.send_sem.at[p],
            recv_sem=self.recv_sem.at[p, slot],
            device_id=target,
            device_id_type=MESH,
        ).start()

    def arrived(self, p, slot):
        place = self.place(p, slot)
        pltpu.make_async_copy(place, place, self.recv_sem.at[p, slot]).wait()

    def first(self, p):
        for k in (1, 3, 2):
            self.send(p, self.me, device_of(self.y, self.c, (self.z + k) % 4, self.x), True)
        self.send(p, self.me, self.across_x, True)
        self.send(p, self.me, self.across_y, True)
        self.send(p, self.me, self.other_core, True)

    def start(self):
        for copy in self.own:
            copy.start()
        for p in range(min(self.ahead, len(self.parts))):
            self.first(p)

    def after_z(self, p):
        for k in (3, 1, 2):
            slot = slot_of(self.y, self.c, (self.z + k) % 4, self.x)
            self.arrived(p, slot)
            self.send(p, slot, self.across_x)
            self.send(p, slot, self.across_y)
            self.send(p, slot, self.other_core)

    def after_first(self, p):
        x_first = self.parts[p][5]
        for k in (0, 3, 1, 2):
            by_x = slot_of(self.y, self.c, (self.z + k) % 4, 1 - self.x)
            by_y = slot_of(1 - self.y, self.c, (self.z + k) % 4, self.x)
            self.arrived(p, by_x)
            if x_first:
                self.send(p, by_x, self.across_y)
            self.send(p, by_x, self.other_core)
            self.arrived(p, by_y)
            if not x_first:
                self.send(p, by_y, self.across_x)
            self.send(p, by_y, self.other_core)

    def after_second(self, p):
        for k in (0, 3, 1, 2):
            slot = slot_of(1 - self.y, self.c, (self.z + k) % 4, 1 - self.x)
            self.arrived(p, slot)
            self.send(p, slot, self.other_core)

    def whole(self, p):
        for side in (0, 1):
            for zz in range(4):
                for xx in (0, 1):
                    self.arrived(p, slot_of(side, 1 - self.c, zz, xx))

    def steps(self):
        return len(self.parts) + 3

    def run(self, until):
        while self.done < min(until, self.steps()):
            s, count = self.done, len(self.parts)
            if self.ahead <= s + self.ahead < count:
                self.first(s + self.ahead)
            for stage, act in enumerate(
                (self.after_z, self.after_first, self.after_second, self.whole)
            ):
                if 0 <= s - stage < count:
                    act(s - stage)
            self.done += 1

    def own_arrived(self, indices):
        for i in indices:
            self.own[i].wait()

    def finish(self):
        self.run(self.steps())
        for p, (i, row, rows, column, columns, _) in enumerate(self.parts):
            sent = self.gathered[i].at[pl.ds(0, 31), pl.ds(row, rows), pl.ds(column, columns)]
            pltpu.make_async_copy(sent, sent, self.send_sem.at[p]).wait()


def cut(arrays):
    parts = []
    for i, (rows, columns) in enumerate(arrays):
        if columns > 1536:
            width = 1536 if columns % 1536 == 0 else 768
            pieces = [(0, rows, w, width) for w in range(0, columns, width)]
        elif rows > 48:
            pieces = [(r, 48, 0, columns) for r in range(0, rows, 48)]
        else:
            pieces = [(0, rows, 0, columns)]
        for piece in pieces:
            parts.append((i,) + piece + (len(parts) % 2 == 0,))
    return parts


class Reduce:
    def __init__(self, parts, terms, totals, buffers, mine, send_sem, recv_sem, mine_sem):
        self.parts, self.terms, self.totals, self.buffers = parts, terms, totals, buffers
        self.send_sem, self.recv_sem, self.mine_sem = send_sem, recv_sem, mine_sem
        self.y, self.c, self.z, self.x = coordinates()
        self.mine, self.kinds = mine, {}
        for p, part in enumerate(parts):
            if part[0] < len(mine[0]):
                self.kinds.setdefault((part[2], part[4]), []).append(p)
        self.done = 0

    def term(self, p, core):
        i, row, rows, column, columns, _ = self.parts[p]
        return self.terms[i].at[:, core, :, :, pl.ds(row, rows), pl.ds(column, columns)]

    def fetch(self, p):
        kind = (self.parts[p][2], self.parts[p][4])
        place = self.kinds[kind].index(p)
        held = self.mine[1][kind].at[place % 2]
        return pltpu.make_async_copy(self.term(p, self.c), held, self.mine_sem.at[p]), held

    def copies(self, p, stage):
        one, two, three, four = self.buffers[4 * p : 4 * p + 4]
        y, c, z, x = self.y, self.c, self.z, self.x
        across_x, across_y = device_of(y, c, z, 1 - x), device_of(1 - y, c, z, x)
        x_last = self.parts[p][5]
        if stage == 0:
            pairs = [(self.term(p, 1 - c), one, device_of(y, 1 - c, z, x))]
        elif stage == 1 and x_last:
            pairs = [(one.at[1 - y], two, across_y)]
        elif stage == 1:
            pairs = [(one.at[:, :, 1 - x], two, across_x)]
        elif stage == 2 and x_last:
            pairs = [(two.at[:, 1 - x], three, across_x)]
        elif stage == 2:
            pairs = [(two.at[1 - y], three, across_y)]
        else:
            pairs = [
                (three.at[(z + k) % 4], four.at[k - 1], device_of(y, c, (z + k) % 4, x))
                for k in (1, 2, 3)
            ]
        return [
            pltpu.make_async_remote_copy(
                src_ref=src,
                dst_ref=dst,
                send_sem=self.send_sem.at[p, stage + n],
                recv_sem=self.recv_sem.at[p, stage + n],
                device_id=target,
                device_id_type=MESH,
            )
            for n, (src, dst, target) in enumerate(pairs)
        ]

    def add(self, p, stage):
        one, two, three, four = self.buffers[4 * p : 4 * p + 4]
        y, c, z, x = self.y, self.c, self.z, self.x
        i, row, rows, column, columns, x_last = self.parts[p]

        def total(a, b):
            return (a.astype(F32) + b.astype(F32)).astype(a.dtype)

        if stage == 0:
            if i < len(self.mine[0]):
                copy, held = self.fetch(p)
                copy.wait()
            else:
                held = self.term(p, c)

            def add_one(k, _):
                b, zz = k // 4, k % 4
                for xx in (0, 1):
                    one[b, zz, xx] = total(one[b, zz, xx], held[b, zz, xx])
                return 0

            lax.fori_loop(0, 8, add_one, 0)
            if i < len(self.mine[0]):
                same = self.kinds[(rows, columns)]
                later = same.index(p) + 2
                if later < len(same):
                    self.fetch(same[later])[0].start()
        elif stage == 1:

            def add_two(k, _):
                for h in (0, 1):
                    if x_last:
                        two[k, h] = total(two[k, h], one[y, k, h])
                    else:
                        two[h, k] = total(two[h, k], one[h, k, x])
                return 0

            lax.fori_loop(0, 4, add_two, 0)
        elif stage == 2:

            def add_three(k, _):
                three[k] = total(three[k], two[k, x] if x_last else two[y, k])
                return 0

            lax.fori_loop(0, 4, add_three, 0)
        else:
            self.totals[i][pl.ds(row, rows), pl.ds(column, columns)] = (
                three[z].astype(F32)
                + four[0].astype(F32)
                + four[1].astype(F32)
                + four[2].astype(F32)
            )

    def start(self, arrays):
        for p, part in enumerate(self.parts):
            if part[0] in arrays:
                for copy in self.copies(p, 0):
                    copy.start()

    def fetch_first(self):
        for same in self.kinds.values():
            for p in same[:2]:
                self.fetch(p)[0].start()

    def steps(self):
        return len(self.parts) + LAGS[3]

    def run(self, until):
        while self.done < min(until, self.steps()):
            for stage in range(4):
                p = self.done - LAGS[stage]
                if 0 <= p < len(self.parts):
                    for copy in self.copies(p, stage):
                        copy.wait_recv()
                    self.add(p, stage)
                    if stage < 3:
                        for copy in self.copies(p, stage + 1):
                            copy.start()
            self.done += 1

    def finish(self):
        self.run(self.steps())
        for p in range(len(self.parts)):
            for stage in range(4):
                for copy in self.copies(p, stage):
                    copy.wait_send()


def all_others():
    rows, groups = lax.axis_size("seq"), lax.axis_size("dp")
    count = rows * groups
    me = lax.axis_index("seq") * groups + lax.axis_index("dp")
    others = [lax.rem(me + k, count) for k in range(1, count)]
    return me, others, [(o // groups, lax.rem(o, groups)) for o in others]


class Swap:
    def __init__(self, src, dst, send_sem, recv_sem):
        self.src, self.dst, self.send_sem, self.recv_sem = src, dst, send_sem, recv_sem

    def start(self):
        me, others, places = all_others()
        for o, place in zip(others, places):
            pltpu.make_async_remote_copy(
                src_ref=self.src.at[o],
                dst_ref=self.dst.at[me],
                send_sem=self.send_sem,
                recv_sem=self.recv_sem,
                device_id=place,
                device_id_type=MESH,
            ).start()

    def wait(self):
        most = pl.ds(0, self.src.shape[0] - 1)
        me = all_others()[0]
        pltpu.make_async_copy(self.src.at[most], self.dst.at[most], self.recv_sem).wait()
        pltpu.make_async_copy(self.src.at[most], self.dst.at[most], self.send_sem).wait()
        self.dst[me] = self.src[me]


def layer_norm(residual, scale_gain):
    average = jnp.mean(residual, axis=-1, keepdims=True)
    centered = residual - average
    variance = jnp.mean(centered * centered, axis=-1, keepdims=True)
    return centered * lax.rsqrt(variance + EPSILON) * scale_gain


def contract(left_side, right_side, left_dim, right_dim):
    return lax.dot_general(
        left_side,
        right_side,
        (((left_dim,), (right_dim,)), ((), ())),
        preferred_element_type=F32,
    )


def product(left_side, right_side):
    return contract(left_side, right_side, 1, 0)


def product_back(left_side, right_side):
    return contract(left_side, right_side, 1, 1)


def product_sum(left_side, right_side):
    return contract(left_side, right_side, 0, 0)


def feed_forward(residual, scale_gain, up_weight, down_weight):
    normed = layer_norm(residual, scale_gain).astype(BF16)
    pre_act = product(normed, up_weight)
    activated = jax.nn.gelu(pre_act).astype(BF16)
    return (residual + product(activated, down_weight), (normed, pre_act, activated))


def feed_back(residual, scale_gain, up_weight, down_weight, stored, grad_residual):
    normed, pre_act, activated = stored
    grad_branch = grad_residual.astype(BF16)
    grad_down = product_sum(activated, grad_branch)
    grad_activated = product_back(grad_branch, down_weight)
    gelu_pull = jax.vjp(jax.nn.gelu, pre_act)[1]
    grad_pre = gelu_pull(grad_activated)[0].astype(BF16)
    grad_up = product_sum(normed, grad_pre)
    grad_normed = product_back(grad_pre, up_weight)
    norm_pull = jax.vjp(layer_norm, residual, scale_gain)[1]
    grad_input, grad_gain = norm_pull(grad_normed)
    return (grad_residual + grad_input, grad_gain, grad_up, grad_down)


def ssm_kernel(decay_log, turn_angle, mix_real, mix_imag, length):
    rate = jnp.exp(decay_log)[:, :, None]
    angle = turn_angle[:, :, None]
    step = 32

    def powers(times):
        return (
            jnp.exp(-times * rate) * jnp.cos(times * angle),
            jnp.exp(-times * rate) * jnp.sin(times * angle),
        )

    low_real, low_imag = powers(jnp.arange(step, dtype=F32)[None, None])
    high_real, high_imag = powers(
        (step * jnp.arange(length // step, dtype=jnp.int32)).astype(F32)[None, None]
    )
    real, imag = mix_real[:, :, None], mix_imag[:, :, None]
    high = jnp.concatenate(
        [real * high_real - imag * high_imag, -(real * high_imag + imag * high_real)], axis=1
    )
    low = jnp.concatenate([low_real, low_imag], axis=1)
    kernel = jnp.einsum("cna,cnb->cab", high, low, precision=HIGHEST)
    return kernel.reshape(decay_log.shape[0], length)


def state_columns(decay, turn, real, imag, cols):
    states = decay.shape[1]
    size = jnp.exp(-jnp.exp(decay))
    turned = [a.T for a in (size * jnp.cos(turn), size * jnp.sin(turn), real, imag)]
    for ch in range(decay.shape[0]):
        for n, a in enumerate(turned):
            cols[ch * states : (ch + 1) * states, n : n + 1] = a[:, ch : ch + 1]


def state_powers(cols, ch, states):
    own = cols[pl.ds(pl.multiple_of(ch * states, states), states), :]
    base_real, base_imag = own[:, :1], own[:, 1:2]
    lane = lax.broadcasted_iota(jnp.int32, (states, 128), 1)
    real, imag = jnp.ones((states, 128), F32), jnp.zeros((states, 128), F32)
    for bit in range(7):
        taken = lane % (2 << bit) >= (1 << bit)
        step_real = jnp.where(taken, base_real, 1.0)
        step_imag = jnp.where(taken, base_imag, 0.0)
        real, imag = real * step_real - imag * step_imag, real * step_imag + imag * step_real
        base_real, base_imag = (
            base_real * base_real - base_imag * base_imag, 2.0 * base_real * base_imag
        )
    return real, imag, base_real, base_imag, own[:, 2:3], own[:, 3:4]


def kernel_rows(decay, turn, real_mix, imag_mix, cols, kernel_ref, length):
    states = decay.shape[1]
    state_columns(decay, turn, real_mix, imag_mix, cols)
    kernel_ref[...] = jnp.zeros_like(kernel_ref)

    def one(ch, _):
        real, imag, jump_real, jump_imag, mix_real, mix_imag = state_powers(cols, ch, states)
        for first in range(0, length, 128):
            terms = mix_real * real - mix_imag * imag
            kernel_ref[ch, :, first : first + 128] = jnp.sum(terms, axis=0, keepdims=True)
            real, imag = (
                real * jump_real - imag * jump_imag, real * jump_imag + imag * jump_real
            )
        return 0

    lax.fori_loop(0, decay.shape[0], one, 0)


def kernel_rows_back(decay, turn, real_mix, imag_mix, cols, sums, grad_ref, length):
    channels, states = decay.shape
    state_columns(decay, turn, real_mix, imag_mix, cols)
    lane = lax.broadcasted_iota(jnp.int32, (states, 128), 1)

    def one(ch, _):
        real, imag, jump_real, jump_imag, _, _ = state_powers(cols, ch, states)
        totals = [jnp.zeros((states, 128), F32)] * 4
        for first in range(0, length, 128):
            grad = grad_ref[ch, :, first : first + 128]
            times = (first + lax.broadcasted_iota(jnp.int32, (1, 128), 1)).astype(F32)
            parts = (grad * real, grad * imag, grad * times * real, grad * times * imag)
            totals = [a + b for a, b in zip(totals, parts)]
            real, imag = (
                real * jump_real - imag * jump_imag, real * jump_imag + imag * jump_real
            )
        kept = jnp.zeros((states, 128), F32)
        for n, a in enumerate(totals):
            kept = jnp.where(lane == n, jnp.sum(a, axis=1, keepdims=True), kept)
        sums[pl.ds(pl.multiple_of(ch * states, states), states), :] = kept
        return 0

    lax.fori_loop(0, channels, one, 0)
    plain_real, plain_imag, timed_real, timed_imag = [
        jnp.concatenate(
            [sums[ch * states : (ch + 1) * states, n : n + 1] for ch in range(channels)], axis=1
        ).T
        for n in range(4)
    ]
    return (
        -jnp.exp(decay) * (real_mix * timed_real - imag_mix * timed_imag),
        -(real_mix * timed_imag + imag_mix * timed_real),
        plain_real,
        -plain_imag,
    )


def toeplitz(row, rows):
    spread = jnp.broadcast_to(row, (rows, row.shape[1]))
    return pltpu.roll(spread, 0, 1, stride=1, stride_axis=0)


def block_sum(mixed, blocks, groups, rows):
    total = mixed[:, :rows]
    for d in range(1, blocks):
        piece = mixed[: (blocks - d) * groups, d * rows : (d + 1) * rows]
        total = total + jnp.concatenate(
            [jnp.zeros((d * groups, rows), piece.dtype), piece], axis=0
        )
    return total


def block_spread(value, blocks, lags, groups, rows):
    pieces = [value]
    for d in range(1, lags):
        pieces.append(
            jnp.concatenate(
                [value[d * groups :], jnp.zeros((d * groups, rows), value.dtype)], axis=0
            )
        )
    return jnp.concatenate(pieces, axis=1)


def mix(blocks, groups, rows, keys, values, tap_row, kernel_row, skip):
    span = blocks * rows
    taps = toeplitz(tap_row, rows)[:, : 2 * rows].astype(BF16)
    longer = toeplitz(kernel_row, rows)[:, :span].astype(BF16)
    near = product(keys, taps)
    shifted = near[:, :rows] + jnp.concatenate(
        [jnp.zeros((groups, rows), F32), near[: (blocks - 1) * groups, rows:]], axis=0
    )
    signal = shifted * values.astype(F32)
    mixed = product(signal.astype(BF16), longer)
    return shifted, block_sum(mixed, blocks, groups, rows) + skip * signal


def mixer_body(blocks, groups, rows, k_ref, v_ref, taps_ref, kernel_ref, skip_ref, shifted_ref, out_ref):
    for ch in range(k_ref.shape[0]):
        row = slice(ch, ch + 1)
        shifted_ref[ch], out = mix(
            blocks, groups, rows, k_ref[ch], v_ref[ch],
            taps_ref[row, :], kernel_ref[row, :], skip_ref[row, :1],
        )
        out_ref[ch] = out.astype(BF16)


def flat_weight(ref):
    wide = ref[...].astype(F32)
    return wide.reshape(wide.shape[0] * wide.shape[1], wide.shape[2]).astype(BF16)


def flat_part(ref, first, width):
    wide = ref[:, :, first : first + width].astype(F32)
    return wide.reshape(wide.shape[0] * wide.shape[1], width).astype(BF16)


def first_body(parts, count, *refs):
    sources = refs[:count]
    tokens, live, key_live, small, taps = refs[count : count + 5]
    states = refs[count + 5 : count + 9]
    refs = refs[count + 9 :]
    gathered = refs[:count]
    (
        residual_ref, standard_ref, inverse_ref, normed_ref, queries_ref, ssm_ref, gated_ref,
        k_ref, v_ref, shifted_ref,
        normed_two, pre_one, act_one, residual_two, normed_three, att_q, att_kv, attended,
        log_total, residual_three, taps_ref, kernel_ref, gain_out,
    ) = refs[count : count + 23]
    (
        wide, sent_kv, came_kv, sent_y, came_y, up, down, qkv, out_two, cols,
        local_sem, send_sem, recv_sem, swap_sem, load_sem, line_send, line_recv,
    ) = refs[count + 23 :]
    gains, key_all, value_all, query_all, out_all = gathered[:5]
    devices, channels = key_all.shape[0], key_all.shape[1]
    rows, features = tokens.shape
    blocks, groups = lax.axis_size("seq"), lax.axis_size("dp")
    greet(all_others()[2])
    gather = Gather(parts, sources, gathered, local_sem, send_sem, recv_sem)
    gather.start()

    turned = tokens[...].astype(F32).T
    centered = turned - jnp.mean(turned, axis=0, keepdims=True)
    inverse = lax.rsqrt(jnp.mean(centered * centered, axis=0, keepdims=True) + EPSILON)
    inverse_ref[...] = jnp.broadcast_to(inverse, inverse_ref.shape)
    standard_ref[...] = centered * inverse
    tap_count = taps.shape[1]
    taps_ref[...] = jnp.zeros_like(taps_ref)
    taps_ref[:, :tap_count] = taps[...].astype(F32)
    gather.run(EARLY)
    kernel_rows(*[a[...].astype(F32) for a in states], cols, kernel_ref, blocks * rows)
    gather.run(RUNS[0])
    gather.own_arrived(range(5))
    all_gains = gains[...].reshape(features, 128)
    normed_ref[...] = (standard_ref[...] * all_gains[:, :1]).astype(BF16)

    def projected(weight):
        return contract(flat_weight(weight), normed_ref[...], 0, 0)

    wide[:, :channels, :] = projected(key_all).reshape(devices, channels, rows)
    wide[:, channels:, :] = (projected(value_all) * live[...]).reshape(devices, channels, rows)
    sent_kv[...] = wide[...].astype(BF16)
    over = Swap(sent_kv, came_kv, swap_sem.at[0], swap_sem.at[1])
    over.start()
    queries_ref[...] = projected(query_all)
    gather.run(RUNS[1])
    over.wait()
    wide[...] = came_kv[...].astype(F32)
    for ch in range(channels):
        row = slice(ch, ch + 1)
        k_ref[ch] = wide[:, ch, :].astype(BF16)
        v_ref[ch] = wide[:, channels + ch, :].astype(BF16)
        shifted_ref[ch], out = mix(
            blocks, groups, rows, k_ref[ch], v_ref[ch],
            taps_ref[row, :], kernel_ref[ch], small[row, 4:5],
        )
        wide[:, ch, :] = out
        if ch == channels // 2:
            gather.run(RUNS[2])
    sent_y[...] = wide[:, :channels, :].astype(BF16)
    back = Swap(sent_y, came_y, swap_sem.at[2], swap_sem.at[3])
    back.start()
    gather.run(RUNS[3])
    gather.own_arrived(range(5, count))
    loads = [
        pltpu.make_async_copy(gathered[5 + n], held, load_sem.at[n])
        for n, held in enumerate((up, down, qkv, out_two))
    ]
    loads[0].start()
    loads[1].start()
    back.wait()
    ssm = came_y[...].astype(F32).reshape(features, rows)
    ssm_ref[...] = ssm.astype(BF16)
    gated_ref[...] = (queries_ref[...] * ssm).astype(BF16)
    residual_ref[...] = tokens[...].astype(F32) + contract(
        gated_ref[...], flat_weight(out_all), 0, 0
    )

    gain_rows = all_gains.T
    gain_out[...] = gain_rows[:8]
    normed_two[...] = layer_norm(residual_ref[...], gain_rows[1:2]).astype(BF16)
    loads[0].wait()
    for first in range(0, up.shape[2], features):
        own = slice(first, first + features)
        pre = product(normed_two[...], flat_part(up, first, features))
        pre_one[:, own] = pre
        act_one[:, own] = jax.nn.gelu(pre).astype(BF16)
    loads[1].wait()
    down_flat = down[...].reshape(-1, features)
    residual_two[...] = residual_ref[...] + product(act_one[...], down_flat)
    normed_three[...] = layer_norm(residual_two[...], gain_rows[2:3]).astype(BF16)
    gather.run(RUNS[4])
    loads[2].start()
    loads[2].wait()
    y, c, z, x = coordinates()
    me = y * 2 + c
    for first in range(0, 2 * features, features):
        joint = product(normed_three[...], flat_part(qkv, features + first, features))
        att_kv[me, :, first : first + features] = joint.astype(BF16)
    core, side = device_of(y, 1 - c, z, x), device_of(1 - y, c, z, x)

    def pass_on(n, slot, target):
        return pltpu.make_async_remote_copy(
            src_ref=att_kv.at[slot],
            dst_ref=att_kv.at[slot],
            send_sem=line_send.at[n],
            recv_sem=line_recv.at[n],
            device_id=target,
            device_id_type=MESH,
        )

    def taken(n, slot):
        pltpu.make_async_copy(att_kv.at[slot], att_kv.at[slot], line_recv.at[n]).wait()

    far = (1 - y) * 2 + c
    passed = [pass_on(0, me, side), pass_on(1, me, core), pass_on(2, far, core)]
    passed[0].start()
    passed[1].start()
    att_q[...] = product(normed_three[...], flat_part(qkv, 0, features)).astype(BF16)
    taken(0, far)
    passed[2].start()
    gather.run(RUNS[5])
    loads[3].start()
    taken(1, y * 2 + 1 - c)
    taken(2, (1 - y) * 2 + 1 - c)
    keys = blocks * rows
    row_places = me * rows + lax.broadcasted_iota(jnp.int32, (rows, keys), 0)
    key_places = lax.broadcasted_iota(jnp.int32, (rows, keys), 1)
    hidden = jnp.where(key_places <= row_places, key_live[...], 0.0)
    attend_heads(
        hidden > 0.5, att_q, att_kv[...].reshape(keys, 2 * features), attended, log_total
    )
    loads[3].wait()
    residual_three[...] = residual_two[...] + product(attended[...], flat_weight(out_two))
    for each in passed:
        each.wait_send()
    gather.finish()


def first_layer(weights, tokens, live, key_live, mixer, collective_id):
    count = len(weights)
    blocks, groups = lax.axis_size("seq"), lax.axis_size("dp")
    devices = blocks * groups
    rows, features = tokens.shape
    channels = features // devices
    parts = [
        (n, 0, a.shape[0], 0, a.shape[1], n % 2 == 0) for n, a in enumerate(weights)
    ]
    vmem, anywhere = pl.BlockSpec(memory_space=pltpu.VMEM), pl.BlockSpec(memory_space=pl.ANY)
    turned = (features, rows)
    per_channel = (channels, devices, rows)
    results = [
        ((rows, features), F32), (turned, F32), ((8, rows), F32), (turned, BF16), (turned, F32),
        (turned, BF16), (turned, BF16), (per_channel, BF16), (per_channel, BF16), (per_channel, F32),
    ]
    hidden = weights[5].shape[1]
    results += [
        ((rows, features), BF16), ((rows, hidden), F32), ((rows, hidden), BF16),
        ((rows, features), F32), ((rows, features), BF16), ((rows, features), BF16),
        ((blocks, rows, 2 * features), BF16), ((rows, features), BF16), ((rows, 128), F32),
        ((rows, features), F32), ((channels, -(-3 * rows // 128) * 128), F32),
        ((channels, 1, -(-(blocks + 1) * rows // 128) * 128), F32), ((8, features), F32),
    ]
    out = pl.pallas_call(
        partial(first_body, parts, count),
        out_shape=[jax.ShapeDtypeStruct((devices,) + a.shape, a.dtype) for a in weights]
        + [jax.ShapeDtypeStruct(*r) for r in results],
        in_specs=[anywhere] * count + [vmem] * 9,
        out_specs=[vmem] * 5 + [anywhere] * (count - 5) + [vmem] * len(results),
        scratch_shapes=[
            pltpu.VMEM((devices, 2 * channels, rows), F32),
            pltpu.VMEM((devices, 2 * channels, rows), BF16),
            pltpu.VMEM((devices, 2 * channels, rows), BF16),
            pltpu.VMEM((devices, channels, rows), BF16),
            pltpu.VMEM((devices, channels, rows), BF16),
        ]
        + [pltpu.VMEM((devices,) + a.shape, BF16) for a in weights[5:9]]
        + [
            pltpu.VMEM((channels * mixer[1].shape[1], 128), F32),
            pltpu.SemaphoreType.DMA((count,)),
            pltpu.SemaphoreType.DMA((len(parts),)),
            pltpu.SemaphoreType.DMA((len(parts), devices)),
            pltpu.SemaphoreType.DMA((4,)),
            pltpu.SemaphoreType.DMA((4,)),
            pltpu.SemaphoreType.DMA((3,)),
            pltpu.SemaphoreType.DMA((3,)),
        ],
        compiler_params=pltpu.CompilerParams(
            collective_id=collective_id, has_side_effects=True, vmem_limit_bytes=60 * MIB
        ),
    )(*weights, tokens, live, key_live, weights[0], *mixer)
    return out[:count], out[count:]


def mixer_rows(small, mixer, rows, blocks):
    taps, *states = mixer
    kernel, pull = jax.vjp(
        partial(ssm_kernel, length=rows * blocks), *[a.astype(F32) for a in states]
    )
    wide = -(-(blocks + 1) * rows // 128) * 128
    kernel_row = jnp.pad(kernel, ((0, 0), (0, wide - kernel.shape[1])))
    narrow = -(-3 * rows // 128) * 128
    tap_row = jnp.pad(taps.astype(F32), ((0, 0), (0, narrow - taps.shape[1])))
    skip_row = jnp.broadcast_to(small[:, 4:5], small.shape)
    return (tap_row, kernel_row, skip_row), pull


def first_layer_apart(weights, tokens, live, key_live, mixer):
    blocks, groups = lax.axis_size("seq"), lax.axis_size("dp")
    devices = blocks * groups
    rows, features = tokens.shape
    channels = features // devices
    every = [lax.all_gather(a, BOTH, axis=0) for a in weights]
    gain = every[0][:, :, 0].reshape(features, 1)
    key_all, value_all, query_all, out_all = [a.reshape(features, -1) for a in every[1:5]]
    turned = tokens.astype(F32).T
    centered = turned - jnp.mean(turned, axis=0, keepdims=True)
    inverse = lax.rsqrt(jnp.mean(centered * centered, axis=0, keepdims=True) + EPSILON)
    standard = centered * inverse
    normed = (standard * gain).astype(BF16)
    queries = contract(query_all, normed, 0, 0)
    keys = contract(key_all, normed, 0, 0).astype(BF16)
    values = (contract(value_all, normed, 0, 0) * live).astype(BF16)
    sent = jnp.stack([a.reshape(devices, channels, rows) for a in (keys, values)], axis=1)
    k_own, v_own = lax.all_to_all(sent, BOTH, 0, 0, tiled=True).transpose(1, 2, 0, 3)
    per_channel = (channels, devices, rows)
    shifted, mixed = local_call(
        partial(mixer_body, blocks, groups, rows),
        [jax.ShapeDtypeStruct(per_channel, F32), jax.ShapeDtypeStruct(per_channel, BF16)],
        k_own, v_own, *mixer_rows(weights[0], mixer, rows, blocks)[0],
    )
    ssm = lax.all_to_all(mixed.transpose(1, 0, 2), BOTH, 0, 0, tiled=True)
    ssm = ssm.reshape(features, rows)
    gated = (queries * ssm.astype(F32)).astype(BF16)
    residual = tokens.astype(F32) + contract(gated, out_all, 0, 0)
    inverse = jnp.broadcast_to(inverse, (8, rows))
    kept = [residual, standard, inverse, normed, queries, ssm, gated, k_own, v_own, shifted]
    up, down, qkv, out_two = [a.reshape(-1, a.shape[2]) for a in every[5:9]]
    residual_two, stored = feed_forward(residual, every[0][:, :, 1].reshape(features), up, down)
    normed_three = layer_norm(residual_two, every[0][:, :, 2].reshape(features)).astype(BF16)
    joint = product(normed_three, qkv).astype(BF16)
    att_q = joint[:, :features]
    att_kv = lax.all_gather(joint[:, features:], "seq", axis=0)
    where = jnp.stack([lax.axis_index("seq").astype(F32) * rows, jnp.sum(key_live)])
    attended, log_total = local_call(
        attend_body,
        [jax.ShapeDtypeStruct((rows, features), BF16), jax.ShapeDtypeStruct((rows, 128), F32)],
        where.astype(jnp.int32), att_q, att_kv.reshape(blocks * rows, 2 * features), scalars=1,
    )
    residual_three = residual_two + product(attended, out_two)
    kept += [*stored, residual_two, normed_three, att_q, att_kv, attended, log_total]
    gain_rows = every[0][:, :, :8].reshape(features, 8).T
    return every, kept + [residual_three, None, None, gain_rows]


def mix_back(
    blocks, groups, rows, out_grad, keys, values, shifted, tap_row, kernel_row, skip
):
    span = blocks * rows
    turned = (
        lax.broadcasted_iota(jnp.int32, (rows, rows), 0)
        + lax.broadcasted_iota(jnp.int32, (rows, rows), 1)
        == rows - 1
    ).astype(BF16)

    def lag_sums(earlier, spread, lanes):
        backward = product(earlier, turned).astype(BF16)
        pairs = product_sum(backward, spread)
        padded = jnp.concatenate(
            [pairs, jnp.zeros((rows, lanes - pairs.shape[1]), F32)], axis=1
        )
        return jnp.sum(
            pltpu.roll(padded, lanes - rows + 1, 1, stride=1, stride_axis=0),
            axis=0,
            keepdims=True,
        )

    taps = toeplitz(tap_row, rows)[:, : 2 * rows].astype(BF16)
    longer = toeplitz(kernel_row, rows)[:, :span].astype(BF16)
    values = values.astype(F32)
    signal = shifted * values
    later = block_spread(out_grad, blocks, blocks, groups, rows).astype(BF16)
    signal_grad = product_back(later, longer) + skip * out_grad
    kernel_grad = lag_sums(signal.astype(BF16), later, kernel_row.shape[1])
    skip_grad = jnp.sum(jnp.sum(signal * out_grad, axis=0, keepdims=True), axis=1, keepdims=True)
    shifted_grad = values * signal_grad
    next_two = block_spread(shifted_grad, blocks, 2, groups, rows).astype(BF16)
    return (
        product_back(next_two, taps),
        shifted * signal_grad,
        kernel_grad,
        lag_sums(keys, next_two, tap_row.shape[1]),
        skip_grad,
    )


def mixer_back_body(
    blocks, groups, rows,
    grad_ref, k_ref, v_ref, shifted_ref, taps_ref, kernel_ref, skip_ref,
    grad_k_ref, grad_v_ref, kernel_grad_ref, taps_grad_ref, skip_grad_ref,
):
    for ch in range(k_ref.shape[0]):
        row = slice(ch, ch + 1)
        grad_k, grad_v, kernel_grad_ref[row, :], taps_grad_ref[row, :], skip_grad = mix_back(
            blocks, groups, rows, grad_ref[ch].astype(F32), k_ref[ch], v_ref[ch], shifted_ref[ch],
            taps_ref[row, :], kernel_ref[row, :], skip_ref[row, :1],
        )
        grad_k_ref[ch], grad_v_ref[ch] = grad_k.astype(BF16), grad_v.astype(BF16)
        skip_grad_ref[row, :] = jnp.broadcast_to(skip_grad, (1, 128))


def packed(ref, channels, residual_shape):
    rows, width = residual_shape
    top = 2 * channels

    def at(row, column, height, columns):
        return ref.at[pl.ds(row, height), pl.ds(column, columns)]

    return (
        [
            at(channels, 0, channels, 3 * width),
            at(0, 0, channels, 4 * width),
            at(top, 0, 4 * channels, width),
        ]
        + [at(top + n * channels, width, channels, width) for n in range(4)]
        + [at(top + 5 * channels, width, channels, 128)]
        + [at(top, 2 * width, rows, width)]
        + [at(top + (4 + n) * channels, 0, channels, 64) for n in range(4)]
        + [at(top + 4 * channels, width, channels, 64)]
        + [at(top + 6 * channels, width, channels, 128)]
    )


def last_body(parts, count, kinds, *refs):
    early = refs[:count]
    (
        gain_in, branch, grad_one, live, gated, normed, queries, ssm, standard, inverse,
        gains, key_all, value_all, query_all, out_all,
        k_ref, v_ref, shifted_ref, taps_ref, kernel_ref, small,
    ) = refs[count : count + 21]
    states = refs[count + 21 : count + 25]
    refs = refs[count + 25 :]
    *totals, input_grad, taps_out, s0, s1, s2, s3, skip_grad_ref = packed(
        refs[0], key_all.shape[1], branch.shape
    )
    state_grads = (s0, s1, s2, s3)
    refs = refs[1:]
    out_term, query_term, key_term, value_term, gain_term = own_terms = refs[:5]
    buffers = refs[5 : 5 + 4 * len(parts)]
    refs = refs[5 + 4 * len(parts) :]
    held = dict(zip(kinds, refs[: len(kinds)]))
    (
        wide, sent_g, came_g, sent_kv, came_kv, query_grad, cols, state_sums, kernel_grad_ref,
        taps_grad_ref, send_sem, recv_sem, mine_sem, swap_sem,
    ) = refs[len(kinds) :]
    devices, channels = key_all.shape[0], key_all.shape[1]
    rows, features = branch.shape
    blocks, groups = lax.axis_size("seq"), lax.axis_size("dp")
    greet(all_others()[2])
    reduce = Reduce(
        parts, early + own_terms, totals, buffers, (early, held), send_sem, recv_sem, mine_sem
    )
    reduce.fetch_first()

    def slots(value, columns):
        return value.reshape(2, 2, 4, 2, channels, columns)

    gated_grad = contract(flat_weight(out_all), branch[...], 1, 1)
    sent_g[...] = (gated_grad * queries[...]).reshape(devices, channels, rows).astype(BF16)
    over = Swap(sent_g, came_g, swap_sem.at[0], swap_sem.at[1])
    over.start()
    reduce.start(range(count))
    query_grad[...] = (gated_grad * ssm[...].astype(F32)).astype(BF16)
    out_term[...] = slots(product(gated[...], branch[...]), features).astype(BF16)
    query_term[...] = slots(contract(normed[...], query_grad[...], 1, 1), features).astype(BF16)
    reduce.start((count, count + 1))
    reduce.run(PLACES[0])
    over.wait()
    wide[:, :channels, :] = came_g[...].astype(F32)
    for ch in range(channels):
        row = slice(ch, ch + 1)
        grad_k, grad_v, kernel_grad_ref[ch], taps_grad_ref[row, :], skip_grad = mix_back(
            blocks, groups, rows, wide[:, ch, :], k_ref[ch], v_ref[ch], shifted_ref[ch],
            taps_ref[row, :], kernel_ref[ch], small[row, 4:5],
        )
        wide[:, ch, :], wide[:, channels + ch, :] = grad_k, grad_v
        skip_grad_ref[row, :] = jnp.broadcast_to(skip_grad, (1, 128))
        if ch % 8 == 7:
            reduce.run(PLACES[1 + ch // 8])
    sent_kv[...] = wide[...].astype(BF16)
    back = Swap(sent_kv, came_kv, swap_sem.at[2], swap_sem.at[3])
    back.start()
    taps_out[...] = taps_grad_ref[:, : taps_out.shape[1]]
    grads = kernel_rows_back(
        *[a[...].astype(F32) for a in states], cols, state_sums, kernel_grad_ref, blocks * rows
    )
    for place, grad in zip(state_grads, grads):
        place[...] = grad
    reduce.run(PLACES[4])
    back.wait()
    wide[...] = came_kv[...].astype(F32)
    key_grad = wide[:, :channels, :].reshape(features, rows).astype(BF16)
    value_grad = (wide[:, channels:, :].reshape(features, rows) * live[...]).astype(BF16)
    key_term[...] = slots(contract(normed[...], key_grad, 1, 1), features).astype(BF16)
    value_term[...] = slots(contract(normed[...], value_grad, 1, 1), features).astype(BF16)
    reduce.start((count + 2, count + 3))
    normed_grad = product(flat_weight(query_all), query_grad[...])
    normed_grad += product(flat_weight(key_all), key_grad)
    normed_grad += product(flat_weight(value_all), value_grad)
    gain_grad = jnp.sum(normed_grad * standard[...], axis=1, keepdims=True)
    lane = lax.broadcasted_iota(jnp.int32, (features, 128), 1)
    others = jnp.concatenate([gain_in[...].T, jnp.zeros((features, 120), F32)], axis=1)
    gain_term[...] = slots(jnp.where(lane == 0, gain_grad, others), 128)
    reduce.start((count + 4,))
    scaled = normed_grad * gains[...].reshape(features, 128)[:, :1]
    scaled = (
        scaled
        - jnp.mean(scaled, axis=0, keepdims=True)
        - standard[...] * jnp.mean(scaled * standard[...], axis=0, keepdims=True)
    )
    input_grad[...] = grad_one[...] + (scaled * inverse[:1, :]).T
    reduce.finish()


def last_layer(
    terms, gain_in, branch, grad_one, live, kept, weights, small, mixer, done, collective_id
):
    standard, inverse, normed, queries, ssm, gated, k_own, v_own, shifted = kept[:9]
    tap_row, kernel_row = kept[9:]
    gains, key_all, value_all, query_all, out_all = weights
    devices, channels, features = key_all.shape
    rows = branch.shape[0]
    count = len(terms)
    square = (channels, features)
    shapes = [a.shape[1:] for a in terms] + [square] * 4 + [(channels, 128)]
    types = [BF16] * (count + 4) + [F32]
    parts = cut(shapes)
    kinds = sorted({(part[2], part[4]) for part in parts if part[0] < count})
    scratch = [pltpu.VMEM((2, 2, 4, 2) + s, t) for s, t in zip(shapes[count:], types[count:])]
    for i, _, part_rows, _, columns, x_last in parts:
        for lead in ((2, 4, 2), (4, 2) if x_last else (2, 4), (4,), (3,)):
            scratch.append(pltpu.VMEM(lead + (part_rows, columns), types[i]))
    scratch += [pltpu.VMEM((2, 2, 4, 2) + kind, BF16) for kind in kinds]
    scratch += [
        pltpu.VMEM((devices, 2 * channels, rows), F32),
        pltpu.VMEM((devices, channels, rows), BF16),
        pltpu.VMEM((devices, channels, rows), BF16),
        pltpu.VMEM((devices, 2 * channels, rows), BF16),
        pltpu.VMEM((devices, 2 * channels, rows), BF16),
        pltpu.VMEM((features, rows), BF16),
        pltpu.VMEM((channels * mixer[1].shape[1], 128), F32),
        pltpu.VMEM((channels * mixer[1].shape[1], 128), F32),
        pltpu.VMEM(kernel_row.shape, F32),
        pltpu.VMEM(tap_row.shape, F32),
        pltpu.SemaphoreType.DMA((len(parts), 6)),
        pltpu.SemaphoreType.DMA((len(parts), 6)),
        pltpu.SemaphoreType.DMA((len(parts),)),
        pltpu.SemaphoreType.DMA((4,)),
    ]
    vmem, anywhere = pl.BlockSpec(memory_space=pltpu.VMEM), pl.BlockSpec(memory_space=pl.ANY)
    height = 2 * channels + max(rows, 8 * channels)
    results = [jax.ShapeDtypeStruct((height, 4 * features), F32)]
    out = pl.pallas_call(
        partial(last_body, parts, count, kinds),
        out_shape=results,
        in_specs=[anywhere] * count + [vmem] * 25,
        out_specs=[vmem] * len(results),
        scratch_shapes=scratch,
        compiler_params=pltpu.CompilerParams(
            collective_id=collective_id, has_side_effects=True, vmem_limit_bytes=62 * MIB
        ),
    )(
        *[a.reshape((2, 2, 4, 2) + a.shape[1:]) for a in terms],
        gain_in, branch, grad_one, live, gated, normed, queries, ssm, standard, inverse,
        gains, key_all, value_all, query_all, out_all,
        k_own, v_own, shifted, tap_row, kernel_row, small, *mixer[1:],
    )
    return settle(done, out[0], channels, (rows, features))


def last_layer_apart(terms, gain_in, branch, grad_one, live, kept, weights, small, mixer):
    standard, inverse, normed, queries, ssm, gated, k_own, v_own, shifted = kept[:9]
    gains, key_all, value_all, query_all, out_all = weights
    devices, channels, features = key_all.shape
    rows = branch.shape[0]
    blocks, groups = lax.axis_size("seq"), lax.axis_size("dp")
    key_all, value_all, query_all, out_all = [
        a.reshape(features, features) for a in (key_all, value_all, query_all, out_all)
    ]
    made, pull = mixer_rows(small, mixer, rows, blocks)
    gated_grad = contract(out_all, branch, 1, 1)
    query_grad = (gated_grad * ssm.astype(F32)).astype(BF16)
    sent = (gated_grad * queries).reshape(devices, channels, rows).astype(BF16)
    own = lax.all_to_all(sent, BOTH, 0, 0, tiled=True).transpose(1, 0, 2)
    per_channel = jax.ShapeDtypeStruct(own.shape, BF16)
    grad_k, grad_v, kernel_grad, taps_grad, skip_grad = local_call(
        partial(mixer_back_body, blocks, groups, rows),
        [per_channel, per_channel]
        + [jax.ShapeDtypeStruct(a.shape, F32) for a in (made[1], made[0])]
        + [jax.ShapeDtypeStruct((channels, 128), F32)],
        own, k_own, v_own, shifted, *made,
    )
    sent = jnp.stack([grad_k.transpose(1, 0, 2), grad_v.transpose(1, 0, 2)], axis=1)
    came = lax.all_to_all(sent, BOTH, 0, 0, tiled=True)
    key_grad = came[:, 0].reshape(features, rows)
    value_grad = (came[:, 1].reshape(features, rows) * live).astype(BF16)
    normed_grad = (
        product(query_all, query_grad) + product(key_all, key_grad) + product(value_all, value_grad)
    )
    gain_grad = jnp.sum(normed_grad * standard, axis=1, keepdims=True)
    lane = lax.broadcasted_iota(jnp.int32, (features, 128), 1)
    gain_term = jnp.where(lane == 0, gain_grad, jnp.pad(gain_in.T, ((0, 0), (0, 120))))
    scaled = normed_grad * gains.reshape(features, 128)[:, :1]
    scaled = (
        scaled
        - jnp.mean(scaled, axis=0, keepdims=True)
        - standard * jnp.mean(scaled * standard, axis=0, keepdims=True)
    )
    input_grad = grad_one + (scaled * inverse[:1]).T
    last = [product(gated, branch)]
    last += [contract(normed, g, 1, 1) for g in (query_grad, key_grad, value_grad)]
    last = [a.reshape(devices, channels, features).astype(BF16) for a in last]
    last.append(gain_term.reshape(devices, channels, 128))
    sums = [
        lax.psum_scatter(a, BOTH, scatter_dimension=0, tiled=False).astype(F32)
        for a in list(terms) + last
    ]
    taps_grad = taps_grad[:, : mixer[0].shape[1]]
    return sums, [input_grad, taps_grad, *pull(kernel_grad[:, : rows * blocks]), skip_grad]


def allowed_keys(first, length, rows, keys):
    row_places = first + lax.broadcasted_iota(jnp.int32, (rows, keys), 0)
    key_places = lax.broadcasted_iota(jnp.int32, (rows, keys), 1)
    return (key_places <= row_places) & (key_places < length)


def attend_heads(allowed, q_ref, kv, out_ref, log_ref):
    features = q_ref.shape[1]
    for head in range(HEADS):
        own = slice(head * HDIM, (head + 1) * HDIM)
        values = slice(features + head * HDIM, features + (head + 1) * HDIM)
        scores = product_back(q_ref[:, own], kv[:, own]) * HDIM ** (-0.5)
        scores = jnp.where(allowed, scores, MASKED)
        most = jnp.max(scores, axis=1, keepdims=True)
        powers = jnp.exp(scores - most)
        total = jnp.sum(powers, axis=1, keepdims=True)
        weights = (powers * (1.0 / total)).astype(BF16)
        out_ref[:, own] = product(weights, kv[:, values]).astype(BF16)
        log_ref[:, head : head + 1] = most + jnp.log(total)


def attend_body(where_ref, q_ref, kv_ref, out_ref, log_ref):
    allowed = allowed_keys(where_ref[0], where_ref[1], q_ref.shape[0], kv_ref.shape[0])
    attend_heads(allowed, q_ref, kv_ref, out_ref, log_ref)


def attend_back_head(head, allowed, q_ref, kv, log_ref, grad_ref):
    features = q_ref.shape[1]
    scale = HDIM ** (-0.5)
    own = slice(head * HDIM, (head + 1) * HDIM)
    values = slice(features + head * HDIM, features + (head + 1) * HDIM)
    queries, grads = q_ref[:, own], grad_ref[:, own]
    scores = product_back(queries, kv[:, own]) * scale
    probs = jnp.where(allowed, jnp.exp(scores - log_ref[:, head : head + 1]), 0.0)
    prob_grad = product_back(grads, kv[:, values])
    delta = jnp.sum(probs * prob_grad, axis=1, keepdims=True)
    grad_scores = (probs * (prob_grad - delta)).astype(BF16)
    return (
        (product(grad_scores, kv[:, own]) * scale).astype(BF16),
        (product_sum(grad_scores, queries) * scale).astype(BF16),
        product_sum(probs.astype(BF16), grads).astype(BF16),
    )


def attend_back_body(where_ref, q_ref, kv_ref, log_ref, grad_ref, grad_q_ref, grad_kv_ref):
    features = q_ref.shape[1]
    allowed = allowed_keys(where_ref[0], where_ref[1], q_ref.shape[0], kv_ref.shape[0])
    for head in range(HEADS):
        own = slice(head * HDIM, (head + 1) * HDIM)
        values = slice(features + head * HDIM, features + (head + 1) * HDIM)
        grad_q_ref[:, own], grad_kv_ref[:, own], grad_kv_ref[:, values] = attend_back_head(
            head, allowed, q_ref, kv_ref, log_ref, grad_ref
        )


def norm_back(residual, gain_row, grad):
    average = jnp.mean(residual, axis=-1, keepdims=True)
    centered = residual - average
    inverse = lax.rsqrt(jnp.mean(centered * centered, axis=-1, keepdims=True) + EPSILON)
    standard = centered * inverse
    scaled = grad * gain_row
    inner = jnp.mean(scaled * standard, axis=-1, keepdims=True)
    grad_input = inverse * (scaled - jnp.mean(scaled, axis=-1, keepdims=True) - standard * inner)
    return grad_input, jnp.sum(grad * standard, axis=0, keepdims=True)


def middle_body(parts, count, kinds, *refs):
    early = refs[:count]
    qkv_all, up_all, down_all = refs[count : count + 3]
    (
        att_q, att_kv, log_total, grad_attended, key_live, normed_three, residual_two,
        grad_three, gain_rows, act_one, pre_one, normed_two, residual_one, fourth,
    ) = refs[count + 3 : count + 17]
    refs = refs[count + 17 :]
    totals = refs[:count]
    qkv_out, up_out, down_out, grad_one, gain_grads, branch_out = refs[count : count + 6]
    refs = refs[count + 6 :]
    buffers = refs[: 4 * len(parts)]
    refs = refs[4 * len(parts) :]
    held = dict(zip(kinds, refs[: len(kinds)]))
    (
        qkv, up, down, grad_q, grad_kv, line_one, line_two,
        send_sem, recv_sem, mine_sem, load_sem, store_sem, line_send, line_recv,
    ) = refs[len(kinds) :]
    rows, features = att_q.shape
    keys = att_kv.shape[0] * rows
    y, c, z, x = coordinates()
    greet(six_peers(y, c, z, x))
    loads = [
        pltpu.make_async_copy(src, dst, load_sem.at[n])
        for n, (src, dst) in enumerate(((qkv_all, qkv), (up_all, up), (down_all, down)))
    ]
    stores = [
        pltpu.make_async_copy(src, dst, store_sem.at[n])
        for n, (src, dst) in enumerate(((qkv, qkv_out), (up, up_out), (down, down_out)))
    ]
    reduce = Reduce(
        parts, early, totals, buffers, (early, held), send_sem, recv_sem, mine_sem
    )
    reduce.fetch_first()
    reduce.start(range(count))
    for load in loads:
        load.start()
    row_places = (y * 2 + c) * rows + lax.broadcasted_iota(jnp.int32, (rows, keys), 0)
    key_places = lax.broadcasted_iota(jnp.int32, (rows, keys), 1)
    allowed = jnp.where(key_places <= row_places, key_live[...], 0.0) > 0.5
    kv = att_kv[...].reshape(keys, 2 * features)
    for head in range(HEADS):
        own = slice(head * HDIM, (head + 1) * HDIM)
        values = slice(features + head * HDIM, features + (head + 1) * HDIM)
        grad_q[:, own], key_grad, value_grad = attend_back_head(
            head, allowed, att_q, kv, log_total, grad_attended
        )
        grad_kv[:, :, :, own] = key_grad.reshape(2, 2, rows, HDIM)
        grad_kv[:, :, :, values] = value_grad.reshape(2, 2, rows, HDIM)
        if head % 4 == 3:
            reduce.run(MIDDLE[head // 4])

    core, side = device_of(y, 1 - c, z, x), device_of(1 - y, c, z, x)

    def line_copy(n, source, target, where):
        return pltpu.make_async_remote_copy(
            src_ref=source,
            dst_ref=where,
            send_sem=line_send.at[n],
            recv_sem=line_recv.at[n],
            device_id=target,
            device_id_type=MESH,
        )

    far = line_copy(0, grad_kv.at[1 - y, 1 - c], core, line_one.at[1 - y])
    near = line_copy(1, grad_kv.at[y, 1 - c], core, line_one.at[y])
    onward = line_copy(2, line_one.at[1 - y], side, line_two)
    far.start()
    near.start()
    far.wait_recv()
    mine = line_one[1 - y].astype(F32) + grad_kv[1 - y, c].astype(F32)
    line_one[1 - y] = mine.astype(BF16)
    onward.start()
    loads[0].wait()
    query_grad = grad_q[...]
    grad_normed = product_back(query_grad, flat_part(qkv, 0, features))
    reduce.run(MIDDLE[3])
    near.wait_recv()
    onward.wait_recv()
    total = (line_one[y].astype(F32) + grad_kv[y, c].astype(F32)) + line_two[...].astype(F32)
    joint = [query_grad, total[:, :features].astype(BF16), total[:, features:].astype(BF16)]
    for n in (1, 2):
        grad_normed += product_back(joint[n], flat_part(qkv, n * features, features))
    grad_from, gain_grad = norm_back(residual_two[...], gain_rows[2:3], grad_normed)
    grad_two = grad_three[...] + grad_from
    gain_grads[...] = jnp.zeros_like(gain_grads)
    gain_grads[3:4, :] = fourth[...]
    gain_grads[2:3, :] = gain_grad
    slots, shard = qkv.shape[0], qkv.shape[1]
    for n in range(3):
        term = product_sum(normed_three[...], joint[n]).reshape(slots, shard, features)
        qkv[:, :, n * features : (n + 1) * features] = term.astype(BF16)
    stores[0].start()
    reduce.run(MIDDLE[4])

    branch = grad_two.astype(BF16)
    loads[1].wait()
    loads[2].wait()
    deep = down.shape[1]
    few = features // deep
    grad_normed = jnp.zeros((rows, features), F32)
    for n in range(up.shape[2] // features):
        own = slice(n * features, (n + 1) * features)
        some = pl.ds(n * few, few)
        gate_grad = product_back(branch, down[some].reshape(features, features))
        pre_grad = jax.vjp(jax.nn.gelu, pre_one[:, own])[1](gate_grad)[0].astype(BF16)
        grad_normed += product_back(pre_grad, flat_part(up, n * features, features))
        term = product_sum(act_one[:, own], branch)
        down[some] = term.astype(BF16).reshape(few, deep, features)
        term = product_sum(normed_two[...], pre_grad).reshape(slots, shard, features)
        up[:, :, own] = term.astype(BF16)
        reduce.run(MIDDLE[5 + n])
    stores[1].start()
    stores[2].start()
    grad_from, gain_grad = norm_back(residual_one[...], gain_rows[1:2], grad_normed)
    grad_one[...] = grad_two + grad_from
    branch_out[...] = grad_one[...].astype(BF16)
    gain_grads[1:2, :] = gain_grad
    reduce.finish()
    for each in (far, near, onward):
        each.wait_send()
    for store in stores:
        store.wait()


def middle_layers(terms, weights, kept, collective_id):
    count = len(terms)
    att_q, act_one = kept[0], kept[9]
    rows, features = att_q.shape
    shapes = [a.shape[1:] for a in terms]
    parts = cut(shapes)
    kinds = sorted({(part[2], part[4]) for part in parts})
    scratch = []
    for _, _, part_rows, _, columns, x_last in parts:
        for lead in ((2, 4, 2), (4, 2) if x_last else (2, 4), (4,), (3,)):
            scratch.append(pltpu.VMEM(lead + (part_rows, columns), BF16))
    scratch += [pltpu.VMEM((2, 2, 4, 2) + kind, BF16) for kind in kinds]
    scratch += [pltpu.VMEM(a.shape, BF16) for a in weights]
    scratch += [
        pltpu.VMEM((rows, features), BF16),
        pltpu.VMEM((2, 2, rows, 2 * features), BF16),
        pltpu.VMEM((2, rows, 2 * features), BF16),
        pltpu.VMEM((rows, 2 * features), BF16),
        pltpu.SemaphoreType.DMA((len(parts), 6)),
        pltpu.SemaphoreType.DMA((len(parts), 6)),
        pltpu.SemaphoreType.DMA((len(parts),)),
        pltpu.SemaphoreType.DMA((3,)),
        pltpu.SemaphoreType.DMA((3,)),
        pltpu.SemaphoreType.DMA((3,)),
        pltpu.SemaphoreType.DMA((3,)),
    ]
    vmem, anywhere = pl.BlockSpec(memory_space=pltpu.VMEM), pl.BlockSpec(memory_space=pl.ANY)
    results = [jax.ShapeDtypeStruct(s, F32) for s in shapes]
    results += [jax.ShapeDtypeStruct(a.shape, BF16) for a in weights]
    results += [
        jax.ShapeDtypeStruct((rows, features), F32),
        jax.ShapeDtypeStruct((8, features), F32),
        jax.ShapeDtypeStruct((rows, features), BF16),
    ]
    out = pl.pallas_call(
        partial(middle_body, parts, count, kinds),
        out_shape=results,
        in_specs=[anywhere] * (count + 3) + [vmem] * 14,
        out_specs=[vmem] * count + [anywhere] * 3 + [vmem] * 3,
        scratch_shapes=scratch,
        compiler_params=pltpu.CompilerParams(
            collective_id=collective_id, has_side_effects=True, vmem_limit_bytes=60 * MIB
        ),
    )(*[a.reshape((2, 2, 4, 2) + a.shape[1:]) for a in terms], *weights, *kept)
    return out[:count], out[count : count + 3], *out[count + 3 :]


def local_call(body, out_shape, *operands, scalars=0, limit=48):
    vmem = pl.BlockSpec(memory_space=pltpu.VMEM)
    smem = pl.BlockSpec(memory_space=pltpu.SMEM)
    return pl.pallas_call(
        body,
        out_shape=out_shape,
        in_specs=[smem] * scalars + [vmem] * (len(operands) - scalars),
        out_specs=jax.tree.map(lambda _: vmem, out_shape),
        compiler_params=pltpu.CompilerParams(vmem_limit_bytes=limit * MIB),
    )(*operands)


def settle(done, everything, channels, residual_shape):
    width = residual_shape[1]
    shapes = [a.shape for a in done]
    shapes += [(channels, 3 * width), (channels, 4 * width), (4 * channels, width)]
    shapes += [(channels, width)] * 4 + [(channels, 128), residual_shape]
    shapes += [(channels, 64)] * 5 + [(channels, 128)]
    count = len(done)

    def body(*refs):
        sources = [*refs[:count], *packed(refs[count], channels, residual_shape)]
        for source, place in zip(sources, refs[count + 1 :]):
            place[...] = source[...]

    out = local_call(
        body, [jax.ShapeDtypeStruct(s, F32) for s in shapes], *done, everything
    )
    return out[: count + 8], out[count + 8 :]


def shards(
    tokens, lengths, norm_one, query_one, key_one, value_one, shift_taps, decay_log,
    turn_angle, mix_real, mix_imag, skip_gain, out_one, norm_two, up_one, down_one,
    norm_three, qkv_weight, out_two, norm_four, up_two, down_two, cotangent,
):
    blocks, groups = lax.axis_size("seq"), lax.axis_size("dp")
    devices = blocks * groups
    rows, features = tokens.shape[1], tokens.shape[2]
    channels = features // devices
    place = lax.axis_index("seq")
    length = lengths[0]
    row_places = place * rows + jnp.arange(rows, dtype=jnp.int32)
    live_mask = (row_places < length).astype(F32)[:, None]
    live_lane = (row_places < length).astype(F32)[None, :]

    small = jnp.stack([norm_one, norm_two, norm_three, norm_four, skip_gain], axis=1)
    small = jnp.pad(small.astype(F32), ((0, 0), (0, 123)))
    mixer = [shift_taps, decay_log, turn_angle, mix_real, mix_imag]
    weights = [
        small, key_one, value_one, query_one, out_one, up_one, down_one, qkv_weight, out_two,
        up_two, down_two,
    ]
    key_live = (jnp.arange(blocks * rows, dtype=jnp.int32) < length).astype(F32)[None, :]
    if grouped():
        every, kept = first_layer(weights, tokens[0], live_lane, key_live, mixer, 1)
    else:
        every, kept = first_layer_apart(weights, tokens[0], live_lane, key_live, mixer)
    residual_one = kept[0]
    gain_rows = kept[22]
    gain_two, gain_three, gain_four = gain_rows[1], gain_rows[2], gain_rows[3]
    up_one_all, down_one_all, qkv_all, out_two_all, late_up, late_down = [
        g.reshape((-1, g.shape[2])) for g in every[5:]
    ]

    normed_two, pre_one, act_one, residual_two, normed_three, att_q, kv = kept[10:17]
    attended, log_total, residual_three = kept[17:20]
    residual_four, stored_four = feed_forward(residual_three, gain_four, late_up, late_down)
    activations = (live_mask * residual_four).astype(BF16)

    grad_four = live_mask * cotangent[0].astype(F32)
    grad_three, grad_norm_four, grad_up_two, grad_down_two = feed_back(
        residual_three, gain_four, late_up, late_down, stored_four, grad_four
    )
    branch_three = grad_three.astype(BF16)
    grad_out_two = product_sum(attended, branch_three)
    grad_attended = product_back(branch_three, out_two_all).astype(BF16)
    slots = (devices, -1)
    terms = [
        g.astype(BF16).reshape(slots + g.shape[1:])
        for g in (grad_up_two, grad_down_two, grad_out_two)
    ]
    if grouped():
        done, terms, grad_one, gain_in, branch_one = middle_layers(
            terms,
            every[7:8] + every[5:7],
            [
                att_q, kv, log_total, grad_attended, key_live, normed_three, residual_two,
                grad_three, gain_rows, act_one, pre_one, normed_two, residual_one,
                grad_norm_four[None],
            ],
            3,
        )
    else:
        grad_q, grad_kv = local_call(
            attend_back_body,
            [
                jax.ShapeDtypeStruct((rows, features), BF16),
                jax.ShapeDtypeStruct((blocks * rows, 2 * features), BF16),
            ],
            jnp.stack([place.astype(jnp.int32) * rows, length]), att_q,
            kv.reshape(blocks * rows, 2 * features), log_total, grad_attended, scalars=1,
        )
        grad_kv = lax.psum_scatter(
            grad_kv.reshape(blocks, rows, 2 * features), "seq", scatter_dimension=0
        )
        grad_joint = jnp.concatenate([grad_q, grad_kv.astype(BF16)], axis=1)
        grad_qkv_weight = product_sum(normed_three, grad_joint)
        grad_normed_three = product_back(grad_joint, qkv_all)
        grad_from_three, grad_norm_three = jax.vjp(layer_norm, residual_two, gain_three)[1](
            grad_normed_three
        )
        grad_one, grad_norm_two, grad_up_one, grad_down_one = feed_back(
            residual_one, gain_two, up_one_all, down_one_all, (normed_two, pre_one, act_one),
            grad_three + grad_from_three,
        )
        done = []
        terms += [
            g.astype(BF16).reshape(slots + g.shape[1:])
            for g in (grad_qkv_weight, grad_up_one, grad_down_one)
        ]
        branch_one = grad_one.astype(BF16)
        gain_in = jnp.stack(
            [jnp.zeros_like(grad_norm_two), grad_norm_two, grad_norm_three, grad_norm_four]
        )
        gain_in = jnp.pad(gain_in, ((0, 4), (0, 0)))
    last = (
        terms, gain_in, branch_one, grad_one, live_lane, kept[1:10] + kept[20:22], every[:5], small,
        mixer,
    )
    if grouped():
        sums, rest = last_layer(*last, done, 2)
    else:
        sums, rest = last_layer_apart(*last)
    grad_up_two, grad_down_two, grad_out_two, grad_qkv_weight, grad_up_one, grad_down_one = sums[:6]
    grad_out_one, grad_query_one, grad_key_one, grad_value_one, gain_grads = sums[6:]
    gain_grads = gain_grads[:, :4].T
    input_grad, grad_shift_taps, grad_decay_log, grad_turn_angle, grad_mix_real = rest[:5]
    grad_mix_imag, skip_grad = rest[5:]
    grad_skip_gain = skip_grad[:, 0]
    return (
        activations[None], input_grad[None],
        gain_grads[0], grad_query_one, grad_key_one, grad_value_one,
        grad_shift_taps, grad_decay_log, grad_turn_angle, grad_mix_real, grad_mix_imag,
        grad_skip_gain, grad_out_one,
        gain_grads[1], grad_up_one, grad_down_one,
        gain_grads[2], grad_qkv_weight, grad_out_two,
        gain_grads[3], grad_up_two, grad_down_two,
    )


def solution(mesh):
    row, vector = P(BOTH, None), P(BOTH)
    whole = P("dp", "seq", None)
    weights = (
        vector, row, row, row, row, row, row, row, row, vector, row,
        vector, row, row, vector, row, row, vector, row, row,
    )
    return jax.shard_map(
        shards,
        mesh=mesh,
        in_specs=(whole, P("dp")) + weights + (whole,),
        out_specs=(whole, whole) + weights,
        check_vma=False,
    )
```

```python
from functools import partial

import jax
import jax.numpy as jnp
from jax import lax
from jax.experimental import pallas as pl
from jax.experimental.pallas import tpu as pltpu
from jax.sharding import PartitionSpec as P

HEADS = 12
HDIM = 64
EPSILON = 1e-05
HIGHEST = lax.Precision.HIGHEST
MASKED = -1e30
BOTH = ("seq", "dp")
MESH = pl.DeviceIdType.MESH
MIB = 1024 * 1024
LAGS = (0, 2, 4, 6)
PLACES = (4, 5, 6, 7, 9)
MIDDLE = (1, 1, 2, 3, 4, 5, 6, 7, 8)
EARLY = 2
RUNS = (6, 9, 9, 10, 11, 12)
AHEAD = 4
F32 = jnp.float32
BF16 = jnp.bfloat16


def grouped():
    return lax.axis_size("seq") == 4 and lax.axis_size("dp") == 8


def coordinates():
    seq, dp = lax.axis_index("seq"), lax.axis_index("dp")
    return seq // 2, seq % 2, dp // 2, dp % 2


def slot_of(y, c, z, x):
    return (y * 2 + c) * 8 + z * 2 + x


def device_of(y, c, z, x):
    return (y * 2 + c, z * 2 + x)


def greet(peers):
    barrier = pltpu.get_barrier_semaphore()
    for peer in peers:
        pl.semaphore_signal(barrier, inc=1, device_id=peer, device_id_type=MESH)
    pl.semaphore_wait(barrier, len(peers))


def six_peers(y, c, z, x):
    return [device_of(y, c, (z + k) % 4, x) for k in (1, 2, 3)] + [
        device_of(y, c, z, 1 - x),
        device_of(1 - y, c, z, x),
        device_of(y, 1 - c, z, x),
    ]


class Gather:
    def __init__(self, parts, sources, gathered, local_sem, send_sem, recv_sem, ahead=None):
        self.parts, self.sources, self.gathered = parts, sources, gathered
        self.send_sem, self.recv_sem, self.ahead = send_sem, recv_sem, ahead or AHEAD
        self.y, self.c, self.z, self.x = y, c, z, x = coordinates()
        self.me = slot_of(y, c, z, x)
        self.across_x = device_of(y, c, z, 1 - x)
        self.across_y = device_of(1 - y, c, z, x)
        self.other_core = device_of(y, 1 - c, z, x)
        self.own = [
            pltpu.make_async_copy(sources[i], gathered[i].at[self.me], local_sem.at[i])
            for i in range(len(sources))
        ]
        self.done = 0

    def place(self, p, slot):
        i, row, rows, column, columns, _ = self.parts[p]
        return self.gathered[i].at[slot, pl.ds(row, rows), pl.ds(column, columns)]

    def send(self, p, slot, target, first=False):
        i, row, rows, column, columns, _ = self.parts[p]
        source = self.sources[i].at[pl.ds(row, rows), pl.ds(column, columns)]
        pltpu.make_async_remote_copy(
            src_ref=source if first else self.place(p, slot),
            dst_ref=self.place(p, slot),
            send_sem=self.send_sem.at[p],
            recv_sem=self.recv_sem.at[p, slot],
            device_id=target,
            device_id_type=MESH,
        ).start()

    def arrived(self, p, slot):
        place = self.place(p, slot)
        pltpu.make_async_copy(place, place, self.recv_sem.at[p, slot]).wait()

    def first(self, p):
        for k in (1, 3, 2):
            self.send(p, self.me, device_of(self.y, self.c, (self.z + k) % 4, self.x), True)
        self.send(p, self.me, self.across_x, True)
        self.send(p, self.me, self.across_y, True)
        self.send(p, self.me, self.other_core, True)

    def start(self):
        for copy in self.own:
            copy.start()
        for p in range(min(self.ahead, len(self.parts))):
            self.first(p)

    def after_z(self, p):
        for k in (3, 1, 2):
            slot = slot_of(self.y, self.c, (self.z + k) % 4, self.x)
            self.arrived(p, slot)
            self.send(p, slot, self.across_x)
            self.send(p, slot, self.across_y)
            self.send(p, slot, self.other_core)

    def after_first(self, p):
        x_first = self.parts[p][5]
        for k in (0, 3, 1, 2):
            by_x = slot_of(self.y, self.c, (self.z + k) % 4, 1 - self.x)
            by_y = slot_of(1 - self.y, self.c, (self.z + k) % 4, self.x)
            self.arrived(p, by_x)
            if x_first:
                self.send(p, by_x, self.across_y)
            self.send(p, by_x, self.other_core)
            self.arrived(p, by_y)
            if not x_first:
                self.send(p, by_y, self.across_x)
            self.send(p, by_y, self.other_core)

    def after_second(self, p):
        for k in (0, 3, 1, 2):
            slot = slot_of(1 - self.y, self.c, (self.z + k) % 4, 1 - self.x)
            self.arrived(p, slot)
            self.send(p, slot, self.other_core)

    def whole(self, p):
        for side in (0, 1):
            for zz in range(4):
                for xx in (0, 1):
                    self.arrived(p, slot_of(side, 1 - self.c, zz, xx))

    def steps(self):
        return len(self.parts) + 3

    def run(self, until):
        while self.done < min(until, self.steps()):
            s, count = self.done, len(self.parts)
            if self.ahead <= s + self.ahead < count:
                self.first(s + self.ahead)
            for stage, act in enumerate(
                (self.after_z, self.after_first, self.after_second, self.whole)
            ):
                if 0 <= s - stage < count:
                    act(s - stage)
            self.done += 1

    def own_arrived(self, indices):
        for i in indices:
            self.own[i].wait()

    def finish(self):
        self.run(self.steps())
        for p, (i, row, rows, column, columns, _) in enumerate(self.parts):
            sent = self.gathered[i].at[pl.ds(0, 31), pl.ds(row, rows), pl.ds(column, columns)]
            pltpu.make_async_copy(sent, sent, self.send_sem.at[p]).wait()


def cut(arrays):
    parts = []
    for i, (rows, columns) in enumerate(arrays):
        if columns > 1536:
            width = 1536 if columns % 1536 == 0 else 768
            pieces = [(0, rows, w, width) for w in range(0, columns, width)]
        elif rows > 48:
            pieces = [(r, 48, 0, columns) for r in range(0, rows, 48)]
        else:
            pieces = [(0, rows, 0, columns)]
        for piece in pieces:
            parts.append((i,) + piece + (len(parts) % 2 == 0,))
    return parts


class Reduce:
    def __init__(self, parts, terms, totals, buffers, mine, send_sem, recv_sem, mine_sem):
        self.parts, self.terms, self.totals, self.buffers = parts, terms, totals, buffers
        self.send_sem, self.recv_sem, self.mine_sem = send_sem, recv_sem, mine_sem
        self.y, self.c, self.z, self.x = coordinates()
        self.mine, self.kinds = mine, {}
        for p, part in enumerate(parts):
            if part[0] < len(mine[0]):
                self.kinds.setdefault((part[2], part[4]), []).append(p)
        self.done = 0

    def term(self, p, core):
        i, row, rows, column, columns, _ = self.parts[p]
        return self.terms[i].at[:, core, :, :, pl.ds(row, rows), pl.ds(column, columns)]

    def fetch(self, p):
        kind = (self.parts[p][2], self.parts[p][4])
        place = self.kinds[kind].index(p)
        held = self.mine[1][kind].at[place % 2]
        return pltpu.make_async_copy(self.term(p, self.c), held, self.mine_sem.at[p]), held

    def copies(self, p, stage):
        one, two, three, four = self.buffers[4 * p : 4 * p + 4]
        y, c, z, x = self.y, self.c, self.z, self.x
        across_x, across_y = device_of(y, c, z, 1 - x), device_of(1 - y, c, z, x)
        x_last = self.parts[p][5]
        if stage == 0:
            pairs = [(self.term(p, 1 - c), one, device_of(y, 1 - c, z, x))]
        elif stage == 1 and x_last:
            pairs = [(one.at[1 - y], two, across_y)]
        elif stage == 1:
            pairs = [(one.at[:, :, 1 - x], two, across_x)]
        elif stage == 2 and x_last:
            pairs = [(two.at[:, 1 - x], three, across_x)]
        elif stage == 2:
            pairs = [(two.at[1 - y], three, across_y)]
        else:
            pairs = [
                (three.at[(z + k) % 4], four.at[k - 1], device_of(y, c, (z + k) % 4, x))
                for k in (1, 2, 3)
            ]
        return [
            pltpu.make_async_remote_copy(
                src_ref=src,
                dst_ref=dst,
                send_sem=self.send_sem.at[p, stage + n],
                recv_sem=self.recv_sem.at[p, stage + n],
                device_id=target,
                device_id_type=MESH,
            )
            for n, (src, dst, target) in enumerate(pairs)
        ]

    def add(self, p, stage):
        one, two, three, four = self.buffers[4 * p : 4 * p + 4]
        y, c, z, x = self.y, self.c, self.z, self.x
        i, row, rows, column, columns, x_last = self.parts[p]

        def total(a, b):
            return (a.astype(F32) + b.astype(F32)).astype(a.dtype)

        if stage == 0:
            if i < len(self.mine[0]):
                copy, held = self.fetch(p)
                copy.wait()
            else:
                held = self.term(p, c)

            def add_one(k, _):
                b, zz = k // 4, k % 4
                for xx in (0, 1):
                    one[b, zz, xx] = total(one[b, zz, xx], held[b, zz, xx])
                return 0

            lax.fori_loop(0, 8, add_one, 0)
            if i < len(self.mine[0]):
                same = self.kinds[(rows, columns)]
                later = same.index(p) + 2
                if later < len(same):
                    self.fetch(same[later])[0].start()
        elif stage == 1:

            def add_two(k, _):
                for h in (0, 1):
                    if x_last:
                        two[k, h] = total(two[k, h], one[y, k, h])
                    else:
                        two[h, k] = total(two[h, k], one[h, k, x])
                return 0

            lax.fori_loop(0, 4, add_two, 0)
        elif stage == 2:

            def add_three(k, _):
                three[k] = total(three[k], two[k, x] if x_last else two[y, k])
                return 0

            lax.fori_loop(0, 4, add_three, 0)
        else:
            self.totals[i][pl.ds(row, rows), pl.ds(column, columns)] = (
                three[z].astype(F32)
                + four[0].astype(F32)
                + four[1].astype(F32)
                + four[2].astype(F32)
            )

    def start(self, arrays):
        for p, part in enumerate(self.parts):
            if part[0] in arrays:
                for copy in self.copies(p, 0):
                    copy.start()

    def fetch_first(self):
        for same in self.kinds.values():
            for p in same[:2]:
                self.fetch(p)[0].start()

    def steps(self):
        return len(self.parts) + LAGS[3]

    def run(self, until):
        while self.done < min(until, self.steps()):
            for stage in range(4):
                p = self.done - LAGS[stage]
                if 0 <= p < len(self.parts):
                    for copy in self.copies(p, stage):
                        copy.wait_recv()
                    self.add(p, stage)
                    if stage < 3:
                        for copy in self.copies(p, stage + 1):
                            copy.start()
            self.done += 1

    def finish(self):
        self.run(self.steps())
        for p in range(len(self.parts)):
            for stage in range(4):
                for copy in self.copies(p, stage):
                    copy.wait_send()


def all_others():
    rows, groups = lax.axis_size("seq"), lax.axis_size("dp")
    count = rows * groups
    me = lax.axis_index("seq") * groups + lax.axis_index("dp")
    others = [lax.rem(me + k, count) for k in range(1, count)]
    return me, others, [(o // groups, lax.rem(o, groups)) for o in others]


class Swap:
    def __init__(self, src, dst, send_sem, recv_sem):
        self.src, self.dst, self.send_sem, self.recv_sem = src, dst, send_sem, recv_sem

    def start(self):
        me, others, places = all_others()
        for o, place in zip(others, places):
            pltpu.make_async_remote_copy(
                src_ref=self.src.at[o],
                dst_ref=self.dst.at[me],
                send_sem=self.send_sem,
                recv_sem=self.recv_sem,
                device_id=place,
                device_id_type=MESH,
            ).start()

    def wait(self):
        most = pl.ds(0, self.src.shape[0] - 1)
        me = all_others()[0]
        pltpu.make_async_copy(self.src.at[most], self.dst.at[most], self.recv_sem).wait()
        pltpu.make_async_copy(self.src.at[most], self.dst.at[most], self.send_sem).wait()
        self.dst[me] = self.src[me]


def layer_norm(residual, scale_gain):
    average = jnp.mean(residual, axis=-1, keepdims=True)
    centered = residual - average
    variance = jnp.mean(centered * centered, axis=-1, keepdims=True)
    return centered * lax.rsqrt(variance + EPSILON) * scale_gain


def contract(left_side, right_side, left_dim, right_dim):
    return lax.dot_general(
        left_side,
        right_side,
        (((left_dim,), (right_dim,)), ((), ())),
        preferred_element_type=F32,
    )


def product(left_side, right_side):
    return contract(left_side, right_side, 1, 0)


def product_back(left_side, right_side):
    return contract(left_side, right_side, 1, 1)


def product_sum(left_side, right_side):
    return contract(left_side, right_side, 0, 0)


def feed_forward(residual, scale_gain, up_weight, down_weight):
    normed = layer_norm(residual, scale_gain).astype(BF16)
    pre_act = product(normed, up_weight)
    activated = jax.nn.gelu(pre_act).astype(BF16)
    return (residual + product(activated, down_weight), (normed, pre_act, activated))


def feed_back(residual, scale_gain, up_weight, down_weight, stored, grad_residual):
    normed, pre_act, activated = stored
    grad_branch = grad_residual.astype(BF16)
    grad_down = product_sum(activated, grad_branch)
    grad_activated = product_back(grad_branch, down_weight)
    gelu_pull = jax.vjp(jax.nn.gelu, pre_act)[1]
    grad_pre = gelu_pull(grad_activated)[0].astype(BF16)
    grad_up = product_sum(normed, grad_pre)
    grad_normed = product_back(grad_pre, up_weight)
    norm_pull = jax.vjp(layer_norm, residual, scale_gain)[1]
    grad_input, grad_gain = norm_pull(grad_normed)
    return (grad_residual + grad_input, grad_gain, grad_up, grad_down)


def ssm_kernel(decay_log, turn_angle, mix_real, mix_imag, length):
    rate = jnp.exp(decay_log)[:, :, None]
    angle = turn_angle[:, :, None]
    step = 32

    def powers(times):
        return (
            jnp.exp(-times * rate) * jnp.cos(times * angle),
            jnp.exp(-times * rate) * jnp.sin(times * angle),
        )

    low_real, low_imag = powers(jnp.arange(step, dtype=F32)[None, None])
    high_real, high_imag = powers(
        (step * jnp.arange(length // step, dtype=jnp.int32)).astype(F32)[None, None]
    )
    real, imag = mix_real[:, :, None], mix_imag[:, :, None]
    high = jnp.concatenate(
        [real * high_real - imag * high_imag, -(real * high_imag + imag * high_real)], axis=1
    )
    low = jnp.concatenate([low_real, low_imag], axis=1)
    kernel = jnp.einsum("cna,cnb->cab", high, low, precision=HIGHEST)
    return kernel.reshape(decay_log.shape[0], length)


def state_columns(decay, turn, real, imag, cols):
    states = decay.shape[1]
    size = jnp.exp(-jnp.exp(decay))
    turned = [a.T for a in (size * jnp.cos(turn), size * jnp.sin(turn), real, imag)]
    for ch in range(decay.shape[0]):
        for n, a in enumerate(turned):
            cols[ch * states : (ch + 1) * states, n : n + 1] = a[:, ch : ch + 1]


def state_powers(cols, ch, states):
    own = cols[pl.ds(pl.multiple_of(ch * states, states), states), :]
    base_real, base_imag = own[:, :1], own[:, 1:2]
    lane = lax.broadcasted_iota(jnp.int32, (states, 128), 1)
    real, imag = jnp.ones((states, 128), F32), jnp.zeros((states, 128), F32)
    for bit in range(7):
        taken = lane % (2 << bit) >= (1 << bit)
        step_real = jnp.where(taken, base_real, 1.0)
        step_imag = jnp.where(taken, base_imag, 0.0)
        real, imag = real * step_real - imag * step_imag, real * step_imag + imag * step_real
        base_real, base_imag = (
            base_real * base_real - base_imag * base_imag, 2.0 * base_real * base_imag
        )
    return real, imag, base_real, base_imag, own[:, 2:3], own[:, 3:4]


def kernel_rows(decay, turn, real_mix, imag_mix, cols, kernel_ref, length):
    states = decay.shape[1]
    state_columns(decay, turn, real_mix, imag_mix, cols)
    kernel_ref[...] = jnp.zeros_like(kernel_ref)

    def one(ch, _):
        real, imag, jump_real, jump_imag, mix_real, mix_imag = state_powers(cols, ch, states)
        for first in range(0, length, 128):
            terms = mix_real * real - mix_imag * imag
            kernel_ref[ch, :, first : first + 128] = jnp.sum(terms, axis=0, keepdims=True)
            real, imag = (
                real * jump_real - imag * jump_imag, real * jump_imag + imag * jump_real
            )
        return 0

    lax.fori_loop(0, decay.shape[0], one, 0)


def kernel_rows_back(decay, turn, real_mix, imag_mix, cols, sums, grad_ref, length):
    channels, states = decay.shape
    state_columns(decay, turn, real_mix, imag_mix, cols)
    lane = lax.broadcasted_iota(jnp.int32, (states, 128), 1)

    def one(ch, _):
        real, imag, jump_real, jump_imag, _, _ = state_powers(cols, ch, states)
        totals = [jnp.zeros((states, 128), F32)] * 4
        for first in range(0, length, 128):
            grad = grad_ref[ch, :, first : first + 128]
            times = (first + lax.broadcasted_iota(jnp.int32, (1, 128), 1)).astype(F32)
            parts = (grad * real, grad * imag, grad * times * real, grad * times * imag)
            totals = [a + b for a, b in zip(totals, parts)]
            real, imag = (
                real * jump_real - imag * jump_imag, real * jump_imag + imag * jump_real
            )
        kept = jnp.zeros((states, 128), F32)
        for n, a in enumerate(totals):
            kept = jnp.where(lane == n, jnp.sum(a, axis=1, keepdims=True), kept)
        sums[pl.ds(pl.multiple_of(ch * states, states), states), :] = kept
        return 0

    lax.fori_loop(0, channels, one, 0)
    plain_real, plain_imag, timed_real, timed_imag = [
        jnp.concatenate(
            [sums[ch * states : (ch + 1) * states, n : n + 1] for ch in range(channels)], axis=1
        ).T
        for n in range(4)
    ]
    return (
        -jnp.exp(decay) * (real_mix * timed_real - imag_mix * timed_imag),
        -(real_mix * timed_imag + imag_mix * timed_real),
        plain_real,
        -plain_imag,
    )


def toeplitz(row, rows):
    spread = jnp.broadcast_to(row, (rows, row.shape[1]))
    return pltpu.roll(spread, 0, 1, stride=1, stride_axis=0)


def block_sum(mixed, blocks, groups, rows):
    total = mixed[:, :rows]
    for d in range(1, blocks):
        piece = mixed[: (blocks - d) * groups, d * rows : (d + 1) * rows]
        total = total + jnp.concatenate(
            [jnp.zeros((d * groups, rows), piece.dtype), piece], axis=0
        )
    return total


def block_spread(value, blocks, lags, groups, rows):
    pieces = [value]
    for d in range(1, lags):
        pieces.append(
            jnp.concatenate(
                [value[d * groups :], jnp.zeros((d * groups, rows), value.dtype)], axis=0
            )
        )
    return jnp.concatenate(pieces, axis=1)


def mix(blocks, groups, rows, keys, values, tap_row, kernel_row, skip):
    span = blocks * rows
    taps = toeplitz(tap_row, rows)[:, : 2 * rows].astype(BF16)
    longer = toeplitz(kernel_row, rows)[:, :span].astype(BF16)
    near = product(keys, taps)
    shifted = near[:, :rows] + jnp.concatenate(
        [jnp.zeros((groups, rows), F32), near[: (blocks - 1) * groups, rows:]], axis=0
    )
    signal = shifted * values.astype(F32)
    mixed = product(signal.astype(BF16), longer)
    return shifted, block_sum(mixed, blocks, groups, rows) + skip * signal


def mixer_body(blocks, groups, rows, k_ref, v_ref, taps_ref, kernel_ref, skip_ref, shifted_ref, out_ref):
    for ch in range(k_ref.shape[0]):
        row = slice(ch, ch + 1)
        shifted_ref[ch], out = mix(
            blocks, groups, rows, k_ref[ch], v_ref[ch],
            taps_ref[row, :], kernel_ref[row, :], skip_ref[row, :1],
        )
        out_ref[ch] = out.astype(BF16)


def flat_weight(ref):
    wide = ref[...].astype(F32)
    return wide.reshape(wide.shape[0] * wide.shape[1], wide.shape[2]).astype(BF16)


def flat_part(ref, first, width):
    wide = ref[:, :, first : first + width].astype(F32)
    return wide.reshape(wide.shape[0] * wide.shape[1], width).astype(BF16)


def first_body(parts, count, *refs):
    sources = refs[:count]
    tokens, live, key_live, small, taps = refs[count : count + 5]
    states = refs[count + 5 : count + 9]
    refs = refs[count + 9 :]
    gathered = refs[:count]
    (
        residual_ref, standard_ref, inverse_ref, normed_ref, queries_ref, ssm_ref, gated_ref,
        k_ref, v_ref, shifted_ref,
        normed_two, pre_one, act_one, residual_two, normed_three, att_q, att_kv, attended,
        log_total, residual_three, taps_ref, kernel_ref, gain_out,
    ) = refs[count : count + 23]
    (
        wide, sent_kv, came_kv, sent_y, came_y, up, down, qkv, out_two, cols,
        local_sem, send_sem, recv_sem, swap_sem, load_sem, line_send, line_recv,
    ) = refs[count + 23 :]
    gains, key_all, value_all, query_all, out_all = gathered[:5]
    devices, channels = key_all.shape[0], key_all.shape[1]
    rows, features = tokens.shape
    blocks, groups = lax.axis_size("seq"), lax.axis_size("dp")
    greet(all_others()[2])
    gather = Gather(parts, sources, gathered, local_sem, send_sem, recv_sem)
    gather.start()

    turned = tokens[...].astype(F32).T
    centered = turned - jnp.mean(turned, axis=0, keepdims=True)
    inverse = lax.rsqrt(jnp.mean(centered * centered, axis=0, keepdims=True) + EPSILON)
    inverse_ref[...] = jnp.broadcast_to(inverse, inverse_ref.shape)
    standard_ref[...] = centered * inverse
    tap_count = taps.shape[1]
    taps_ref[...] = jnp.zeros_like(taps_ref)
    taps_ref[:, :tap_count] = taps[...].astype(F32)
    gather.run(EARLY)
    kernel_rows(*[a[...].astype(F32) for a in states], cols, kernel_ref, blocks * rows)
    gather.run(RUNS[0])
    gather.own_arrived(range(3))
    all_gains = gains[...].reshape(features, 128)
    normed_ref[...] = (standard_ref[...] * all_gains[:, :1]).astype(BF16)

    def projected(weight):
        return contract(flat_weight(weight), normed_ref[...], 0, 0)

    wide[:, :channels, :] = projected(key_all).reshape(devices, channels, rows)
    wide[:, channels:, :] = (projected(value_all) * live[...]).reshape(devices, channels, rows)
    sent_kv[...] = wide[...].astype(BF16)
    over = Swap(sent_kv, came_kv, swap_sem.at[0], swap_sem.at[1])
    over.start()
    gather.run(RUNS[1])
    gather.own_arrived(range(3, 5))
    queries_ref[...] = projected(query_all)
    over.wait()
    wide[...] = came_kv[...].astype(F32)
    for ch in range(channels):
        row = slice(ch, ch + 1)
        k_ref[ch] = wide[:, ch, :].astype(BF16)
        v_ref[ch] = wide[:, channels + ch, :].astype(BF16)
        shifted_ref[ch], out = mix(
            blocks, groups, rows, k_ref[ch], v_ref[ch],
            taps_ref[row, :], kernel_ref[ch], small[row, 4:5],
        )
        wide[:, ch, :] = out
        if ch == channels // 2:
            gather.run(RUNS[2])
    sent_y[...] = wide[:, :channels, :].astype(BF16)
    back = Swap(sent_y, came_y, swap_sem.at[2], swap_sem.at[3])
    back.start()
    gather.run(RUNS[3])
    gather.own_arrived(range(5, count))
    loads = [
        pltpu.make_async_copy(gathered[5 + n], held, load_sem.at[n])
        for n, held in enumerate((up, down, qkv, out_two))
    ]
    loads[0].start()
    loads[1].start()
    back.wait()
    ssm = came_y[...].astype(F32).reshape(features, rows)
    ssm_ref[...] = ssm.astype(BF16)
    gated_ref[...] = (queries_ref[...] * ssm).astype(BF16)
    residual_ref[...] = tokens[...].astype(F32) + contract(
        gated_ref[...], flat_weight(out_all), 0, 0
    )

    gain_rows = all_gains.T
    gain_out[...] = gain_rows[:8]
    normed_two[...] = layer_norm(residual_ref[...], gain_rows[1:2]).astype(BF16)
    loads[0].wait()
    for first in range(0, up.shape[2], features):
        own = slice(first, first + features)
        pre = product(normed_two[...], flat_part(up, first, features))
        pre_one[:, own] = pre
        act_one[:, own] = jax.nn.gelu(pre).astype(BF16)
    loads[1].wait()
    down_flat = down[...].reshape(-1, features)
    residual_two[...] = residual_ref[...] + product(act_one[...], down_flat)
    normed_three[...] = layer_norm(residual_two[...], gain_rows[2:3]).astype(BF16)
    gather.run(RUNS[4])
    loads[2].start()
    loads[2].wait()
    y, c, z, x = coordinates()
    me = y * 2 + c
    for first in range(0, 2 * features, features):
        joint = product(normed_three[...], flat_part(qkv, features + first, features))
        att_kv[me, :, first : first + features] = joint.astype(BF16)
    core, side = device_of(y, 1 - c, z, x), device_of(1 - y, c, z, x)

    def pass_on(n, slot, target):
        return pltpu.make_async_remote_copy(
            src_ref=att_kv.at[slot],
            dst_ref=att_kv.at[slot],
            send_sem=line_send.at[n],
            recv_sem=line_recv.at[n],
            device_id=target,
            device_id_type=MESH,
        )

    def taken(n, slot):
        pltpu.make_async_copy(att_kv.at[slot], att_kv.at[slot], line_recv.at[n]).wait()

    far = (1 - y) * 2 + c
    passed = [pass_on(0, me, side), pass_on(1, me, core), pass_on(2, far, core)]
    passed[0].start()
    passed[1].start()
    att_q[...] = product(normed_three[...], flat_part(qkv, 0, features)).astype(BF16)
    taken(0, far)
    passed[2].start()
    gather.run(RUNS[5])
    loads[3].start()
    taken(1, y * 2 + 1 - c)
    taken(2, (1 - y) * 2 + 1 - c)
    keys = blocks * rows
    row_places = me * rows + lax.broadcasted_iota(jnp.int32, (rows, keys), 0)
    key_places = lax.broadcasted_iota(jnp.int32, (rows, keys), 1)
    hidden = jnp.where(key_places <= row_places, key_live[...], 0.0)
    attend_heads(
        hidden > 0.5, att_q, att_kv[...].reshape(keys, 2 * features), attended, log_total
    )
    loads[3].wait()
    residual_three[...] = residual_two[...] + product(attended[...], flat_weight(out_two))
    for each in passed:
        each.wait_send()
    gather.finish()


def first_layer(weights, tokens, live, key_live, mixer, collective_id):
    count = len(weights)
    blocks, groups = lax.axis_size("seq"), lax.axis_size("dp")
    devices = blocks * groups
    rows, features = tokens.shape
    channels = features // devices
    parts = [
        (n, 0, a.shape[0], 0, a.shape[1], n % 2 == 0) for n, a in enumerate(weights)
    ]
    vmem, anywhere = pl.BlockSpec(memory_space=pltpu.VMEM), pl.BlockSpec(memory_space=pl.ANY)
    turned = (features, rows)
    per_channel = (channels, devices, rows)
    results = [
        ((rows, features), F32), (turned, F32), ((8, rows), F32), (turned, BF16), (turned, F32),
        (turned, BF16), (turned, BF16), (per_channel, BF16), (per_channel, BF16), (per_channel, F32),
    ]
    hidden = weights[5].shape[1]
    results += [
        ((rows, features), BF16), ((rows, hidden), F32), ((rows, hidden), BF16),
        ((rows, features), F32), ((rows, features), BF16), ((rows, features), BF16),
        ((blocks, rows, 2 * features), BF16), ((rows, features), BF16), ((rows, 128), F32),
        ((rows, features), F32), ((channels, -(-3 * rows // 128) * 128), F32),
        ((channels, 1, -(-(blocks + 1) * rows // 128) * 128), F32), ((8, features), F32),
    ]
    out = pl.pallas_call(
        partial(first_body, parts, count),
        out_shape=[jax.ShapeDtypeStruct((devices,) + a.shape, a.dtype) for a in weights]
        + [jax.ShapeDtypeStruct(*r) for r in results],
        in_specs=[anywhere] * count + [vmem] * 9,
        out_specs=[vmem] * 5 + [anywhere] * (count - 5) + [vmem] * len(results),
        scratch_shapes=[
            pltpu.VMEM((devices, 2 * channels, rows), F32),
            pltpu.VMEM((devices, 2 * channels, rows), BF16),
            pltpu.VMEM((devices, 2 * channels, rows), BF16),
            pltpu.VMEM((devices, channels, rows), BF16),
            pltpu.VMEM((devices, channels, rows), BF16),
        ]
        + [pltpu.VMEM((devices,) + a.shape, BF16) for a in weights[5:9]]
        + [
            pltpu.VMEM((channels * mixer[1].shape[1], 128), F32),
            pltpu.SemaphoreType.DMA((count,)),
            pltpu.SemaphoreType.DMA((len(parts),)),
            pltpu.SemaphoreType.DMA((len(parts), devices)),
            pltpu.SemaphoreType.DMA((4,)),
            pltpu.SemaphoreType.DMA((4,)),
            pltpu.SemaphoreType.DMA((3,)),
            pltpu.SemaphoreType.DMA((3,)),
        ],
        compiler_params=pltpu.CompilerParams(
            collective_id=collective_id, has_side_effects=True, vmem_limit_bytes=60 * MIB
        ),
    )(*weights, tokens, live, key_live, weights[0], *mixer)
    return out[:count], out[count:]


def mixer_rows(small, mixer, rows, blocks):
    taps, *states = mixer
    kernel, pull = jax.vjp(
        partial(ssm_kernel, length=rows * blocks), *[a.astype(F32) for a in states]
    )
    wide = -(-(blocks + 1) * rows // 128) * 128
    kernel_row = jnp.pad(kernel, ((0, 0), (0, wide - kernel.shape[1])))
    narrow = -(-3 * rows // 128) * 128
    tap_row = jnp.pad(taps.astype(F32), ((0, 0), (0, narrow - taps.shape[1])))
    skip_row = jnp.broadcast_to(small[:, 4:5], small.shape)
    return (tap_row, kernel_row, skip_row), pull


def first_layer_apart(weights, tokens, live, key_live, mixer):
    blocks, groups = lax.axis_size("seq"), lax.axis_size("dp")
    devices = blocks * groups
    rows, features = tokens.shape
    channels = features // devices
    every = [lax.all_gather(a, BOTH, axis=0) for a in weights]
    gain = every[0][:, :, 0].reshape(features, 1)
    key_all, value_all, query_all, out_all = [a.reshape(features, -1) for a in every[1:5]]
    turned = tokens.astype(F32).T
    centered = turned - jnp.mean(turned, axis=0, keepdims=True)
    inverse = lax.rsqrt(jnp.mean(centered * centered, axis=0, keepdims=True) + EPSILON)
    standard = centered * inverse
    normed = (standard * gain).astype(BF16)
    queries = contract(query_all, normed, 0, 0)
    keys = contract(key_all, normed, 0, 0).astype(BF16)
    values = (contract(value_all, normed, 0, 0) * live).astype(BF16)
    sent = jnp.stack([a.reshape(devices, channels, rows) for a in (keys, values)], axis=1)
    k_own, v_own = lax.all_to_all(sent, BOTH, 0, 0, tiled=True).transpose(1, 2, 0, 3)
    per_channel = (channels, devices, rows)
    shifted, mixed = local_call(
        partial(mixer_body, blocks, groups, rows),
        [jax.ShapeDtypeStruct(per_channel, F32), jax.ShapeDtypeStruct(per_channel, BF16)],
        k_own, v_own, *mixer_rows(weights[0], mixer, rows, blocks)[0],
    )
    ssm = lax.all_to_all(mixed.transpose(1, 0, 2), BOTH, 0, 0, tiled=True)
    ssm = ssm.reshape(features, rows)
    gated = (queries * ssm.astype(F32)).astype(BF16)
    residual = tokens.astype(F32) + contract(gated, out_all, 0, 0)
    inverse = jnp.broadcast_to(inverse, (8, rows))
    kept = [residual, standard, inverse, normed, queries, ssm, gated, k_own, v_own, shifted]
    up, down, qkv, out_two = [a.reshape(-1, a.shape[2]) for a in every[5:9]]
    residual_two, stored = feed_forward(residual, every[0][:, :, 1].reshape(features), up, down)
    normed_three = layer_norm(residual_two, every[0][:, :, 2].reshape(features)).astype(BF16)
    joint = product(normed_three, qkv).astype(BF16)
    att_q = joint[:, :features]
    att_kv = lax.all_gather(joint[:, features:], "seq", axis=0)
    where = jnp.stack([lax.axis_index("seq").astype(F32) * rows, jnp.sum(key_live)])
    attended, log_total = local_call(
        attend_body,
        [jax.ShapeDtypeStruct((rows, features), BF16), jax.ShapeDtypeStruct((rows, 128), F32)],
        where.astype(jnp.int32), att_q, att_kv.reshape(blocks * rows, 2 * features), scalars=1,
    )
    residual_three = residual_two + product(attended, out_two)
    kept += [*stored, residual_two, normed_three, att_q, att_kv, attended, log_total]
    gain_rows = every[0][:, :, :8].reshape(features, 8).T
    return every, kept + [residual_three, None, None, gain_rows]


def mix_back(
    blocks, groups, rows, out_grad, keys, values, shifted, tap_row, kernel_row, skip
):
    span = blocks * rows
    turned = (
        lax.broadcasted_iota(jnp.int32, (rows, rows), 0)
        + lax.broadcasted_iota(jnp.int32, (rows, rows), 1)
        == rows - 1
    ).astype(BF16)

    def lag_sums(earlier, spread, lanes):
        backward = product(earlier, turned).astype(BF16)
        pairs = product_sum(backward, spread)
        padded = jnp.concatenate(
            [pairs, jnp.zeros((rows, lanes - pairs.shape[1]), F32)], axis=1
        )
        return jnp.sum(
            pltpu.roll(padded, lanes - rows + 1, 1, stride=1, stride_axis=0),
            axis=0,
            keepdims=True,
        )

    taps = toeplitz(tap_row, rows)[:, : 2 * rows].astype(BF16)
    longer = toeplitz(kernel_row, rows)[:, :span].astype(BF16)
    values = values.astype(F32)
    signal = shifted * values
    later = block_spread(out_grad, blocks, blocks, groups, rows).astype(BF16)
    signal_grad = product_back(later, longer) + skip * out_grad
    kernel_grad = lag_sums(signal.astype(BF16), later, kernel_row.shape[1])
    skip_grad = jnp.sum(jnp.sum(signal * out_grad, axis=0, keepdims=True), axis=1, keepdims=True)
    shifted_grad = values * signal_grad
    next_two = block_spread(shifted_grad, blocks, 2, groups, rows).astype(BF16)
    return (
        product_back(next_two, taps),
        shifted * signal_grad,
        kernel_grad,
        lag_sums(keys, next_two, tap_row.shape[1]),
        skip_grad,
    )


def mixer_back_body(
    blocks, groups, rows,
    grad_ref, k_ref, v_ref, shifted_ref, taps_ref, kernel_ref, skip_ref,
    grad_k_ref, grad_v_ref, kernel_grad_ref, taps_grad_ref, skip_grad_ref,
):
    for ch in range(k_ref.shape[0]):
        row = slice(ch, ch + 1)
        grad_k, grad_v, kernel_grad_ref[row, :], taps_grad_ref[row, :], skip_grad = mix_back(
            blocks, groups, rows, grad_ref[ch].astype(F32), k_ref[ch], v_ref[ch], shifted_ref[ch],
            taps_ref[row, :], kernel_ref[row, :], skip_ref[row, :1],
        )
        grad_k_ref[ch], grad_v_ref[ch] = grad_k.astype(BF16), grad_v.astype(BF16)
        skip_grad_ref[row, :] = jnp.broadcast_to(skip_grad, (1, 128))


def packed(ref, channels, residual_shape):
    rows, width = residual_shape
    top = 2 * channels

    def at(row, column, height, columns):
        return ref.at[pl.ds(row, height), pl.ds(column, columns)]

    return (
        [
            at(channels, 0, channels, 3 * width),
            at(0, 0, channels, 4 * width),
            at(top, 0, 4 * channels, width),
        ]
        + [at(top + n * channels, width, channels, width) for n in range(4)]
        + [at(top + 5 * channels, width, channels, 128)]
        + [at(top, 2 * width, rows, width)]
        + [at(top + (4 + n) * channels, 0, channels, 64) for n in range(4)]
        + [at(top + 4 * channels, width, channels, 64)]
        + [at(top + 6 * channels, width, channels, 128)]
    )


def last_body(parts, count, kinds, *refs):
    early = refs[:count]
    (
        gain_in, branch, grad_one, live, gated, normed, queries, ssm, standard, inverse,
        gains, key_all, value_all, query_all, out_all,
        k_ref, v_ref, shifted_ref, taps_ref, kernel_ref, small,
    ) = refs[count : count + 21]
    states = refs[count + 21 : count + 25]
    refs = refs[count + 25 :]
    *totals, input_grad, taps_out, s0, s1, s2, s3, skip_grad_ref = packed(
        refs[0], key_all.shape[1], branch.shape
    )
    state_grads = (s0, s1, s2, s3)
    refs = refs[1:]
    out_term, query_term, key_term, value_term, gain_term = own_terms = refs[:5]
    buffers = refs[5 : 5 + 4 * len(parts)]
    refs = refs[5 + 4 * len(parts) :]
    held = dict(zip(kinds, refs[: len(kinds)]))
    (
        wide, sent_g, came_g, sent_kv, came_kv, query_grad, cols, state_sums, kernel_grad_ref,
        taps_grad_ref, send_sem, recv_sem, mine_sem, swap_sem,
    ) = refs[len(kinds) :]
    devices, channels = key_all.shape[0], key_all.shape[1]
    rows, features = branch.shape
    blocks, groups = lax.axis_size("seq"), lax.axis_size("dp")
    greet(all_others()[2])
    reduce = Reduce(
        parts, early + own_terms, totals, buffers, (early, held), send_sem, recv_sem, mine_sem
    )
    reduce.fetch_first()

    def slots(value, columns):
        return value.reshape(2, 2, 4, 2, channels, columns)

    gated_grad = contract(flat_weight(out_all), branch[...], 1, 1)
    sent_g[...] = (gated_grad * queries[...]).reshape(devices, channels, rows).astype(BF16)
    over = Swap(sent_g, came_g, swap_sem.at[0], swap_sem.at[1])
    over.start()
    reduce.start(range(count))
    query_grad[...] = (gated_grad * ssm[...].astype(F32)).astype(BF16)
    out_term[...] = slots(product(gated[...], branch[...]), features).astype(BF16)
    query_term[...] = slots(contract(normed[...], query_grad[...], 1, 1), features).astype(BF16)
    reduce.start((count, count + 1))
    reduce.run(PLACES[0])
    over.wait()
    wide[:, :channels, :] = came_g[...].astype(F32)
    for ch in range(channels):
        row = slice(ch, ch + 1)
        grad_k, grad_v, kernel_grad_ref[ch], taps_grad_ref[row, :], skip_grad = mix_back(
            blocks, groups, rows, wide[:, ch, :], k_ref[ch], v_ref[ch], shifted_ref[ch],
            taps_ref[row, :], kernel_ref[ch], small[row, 4:5],
        )
        wide[:, ch, :], wide[:, channels + ch, :] = grad_k, grad_v
        skip_grad_ref[row, :] = jnp.broadcast_to(skip_grad, (1, 128))
        if ch % 8 == 7:
            reduce.run(PLACES[1 + ch // 8])
    sent_kv[...] = wide[...].astype(BF16)
    back = Swap(sent_kv, came_kv, swap_sem.at[2], swap_sem.at[3])
    back.start()
    taps_out[...] = taps_grad_ref[:, : taps_out.shape[1]]
    grads = kernel_rows_back(
        *[a[...].astype(F32) for a in states], cols, state_sums, kernel_grad_ref, blocks * rows
    )
    for place, grad in zip(state_grads, grads):
        place[...] = grad
    reduce.run(PLACES[4])
    back.wait()
    wide[...] = came_kv[...].astype(F32)
    key_grad = wide[:, :channels, :].reshape(features, rows).astype(BF16)
    value_grad = (wide[:, channels:, :].reshape(features, rows) * live[...]).astype(BF16)
    key_term[...] = slots(contract(normed[...], key_grad, 1, 1), features).astype(BF16)
    value_term[...] = slots(contract(normed[...], value_grad, 1, 1), features).astype(BF16)
    reduce.start((count + 2, count + 3))
    normed_grad = product(flat_weight(query_all), query_grad[...])
    normed_grad += product(flat_weight(key_all), key_grad)
    normed_grad += product(flat_weight(value_all), value_grad)
    gain_grad = jnp.sum(normed_grad * standard[...], axis=1, keepdims=True)
    lane = lax.broadcasted_iota(jnp.int32, (features, 128), 1)
    others = jnp.concatenate([gain_in[...].T, jnp.zeros((features, 120), F32)], axis=1)
    gain_term[...] = slots(jnp.where(lane == 0, gain_grad, others), 128)
    reduce.start((count + 4,))
    scaled = normed_grad * gains[...].reshape(features, 128)[:, :1]
    scaled = (
        scaled
        - jnp.mean(scaled, axis=0, keepdims=True)
        - standard[...] * jnp.mean(scaled * standard[...], axis=0, keepdims=True)
    )
    input_grad[...] = grad_one[...] + (scaled * inverse[:1, :]).T
    reduce.finish()


def last_layer(
    terms, gain_in, branch, grad_one, live, kept, weights, small, mixer, done, collective_id
):
    standard, inverse, normed, queries, ssm, gated, k_own, v_own, shifted = kept[:9]
    tap_row, kernel_row = kept[9:]
    gains, key_all, value_all, query_all, out_all = weights
    devices, channels, features = key_all.shape
    rows = branch.shape[0]
    count = len(terms)
    square = (channels, features)
    shapes = [a.shape[1:] for a in terms] + [square] * 4 + [(channels, 128)]
    types = [BF16] * (count + 4) + [F32]
    parts = cut(shapes)
    kinds = sorted({(part[2], part[4]) for part in parts if part[0] < count})
    scratch = [pltpu.VMEM((2, 2, 4, 2) + s, t) for s, t in zip(shapes[count:], types[count:])]
    for i, _, part_rows, _, columns, x_last in parts:
        for lead in ((2, 4, 2), (4, 2) if x_last else (2, 4), (4,), (3,)):
            scratch.append(pltpu.VMEM(lead + (part_rows, columns), types[i]))
    scratch += [pltpu.VMEM((2, 2, 4, 2) + kind, BF16) for kind in kinds]
    scratch += [
        pltpu.VMEM((devices, 2 * channels, rows), F32),
        pltpu.VMEM((devices, channels, rows), BF16),
        pltpu.VMEM((devices, channels, rows), BF16),
        pltpu.VMEM((devices, 2 * channels, rows), BF16),
        pltpu.VMEM((devices, 2 * channels, rows), BF16),
        pltpu.VMEM((features, rows), BF16),
        pltpu.VMEM((channels * mixer[1].shape[1], 128), F32),
        pltpu.VMEM((channels * mixer[1].shape[1], 128), F32),
        pltpu.VMEM(kernel_row.shape, F32),
        pltpu.VMEM(tap_row.shape, F32),
        pltpu.SemaphoreType.DMA((len(parts), 6)),
        pltpu.SemaphoreType.DMA((len(parts), 6)),
        pltpu.SemaphoreType.DMA((len(parts),)),
        pltpu.SemaphoreType.DMA((4,)),
    ]
    vmem, anywhere = pl.BlockSpec(memory_space=pltpu.VMEM), pl.BlockSpec(memory_space=pl.ANY)
    height = 2 * channels + max(rows, 8 * channels)
    results = [jax.ShapeDtypeStruct((height, 4 * features), F32)]
    out = pl.pallas_call(
        partial(last_body, parts, count, kinds),
        out_shape=results,
        in_specs=[anywhere] * count + [vmem] * 25,
        out_specs=[vmem] * len(results),
        scratch_shapes=scratch,
        compiler_params=pltpu.CompilerParams(
            collective_id=collective_id, has_side_effects=True, vmem_limit_bytes=62 * MIB
        ),
    )(
        *[a.reshape((2, 2, 4, 2) + a.shape[1:]) for a in terms],
        gain_in, branch, grad_one, live, gated, normed, queries, ssm, standard, inverse,
        gains, key_all, value_all, query_all, out_all,
        k_own, v_own, shifted, tap_row, kernel_row, small, *mixer[1:],
    )
    return settle(done, out[0], channels, (rows, features))


def last_layer_apart(terms, gain_in, branch, grad_one, live, kept, weights, small, mixer):
    standard, inverse, normed, queries, ssm, gated, k_own, v_own, shifted = kept[:9]
    gains, key_all, value_all, query_all, out_all = weights
    devices, channels, features = key_all.shape
    rows = branch.shape[0]
    blocks, groups = lax.axis_size("seq"), lax.axis_size("dp")
    key_all, value_all, query_all, out_all = [
        a.reshape(features, features) for a in (key_all, value_all, query_all, out_all)
    ]
    made, pull = mixer_rows(small, mixer, rows, blocks)
    gated_grad = contract(out_all, branch, 1, 1)
    query_grad = (gated_grad * ssm.astype(F32)).astype(BF16)
    sent = (gated_grad * queries).reshape(devices, channels, rows).astype(BF16)
    own = lax.all_to_all(sent, BOTH, 0, 0, tiled=True).transpose(1, 0, 2)
    per_channel = jax.ShapeDtypeStruct(own.shape, BF16)
    grad_k, grad_v, kernel_grad, taps_grad, skip_grad = local_call(
        partial(mixer_back_body, blocks, groups, rows),
        [per_channel, per_channel]
        + [jax.ShapeDtypeStruct(a.shape, F32) for a in (made[1], made[0])]
        + [jax.ShapeDtypeStruct((channels, 128), F32)],
        own, k_own, v_own, shifted, *made,
    )
    sent = jnp.stack([grad_k.transpose(1, 0, 2), grad_v.transpose(1, 0, 2)], axis=1)
    came = lax.all_to_all(sent, BOTH, 0, 0, tiled=True)
    key_grad = came[:, 0].reshape(features, rows)
    value_grad = (came[:, 1].reshape(features, rows) * live).astype(BF16)
    normed_grad = (
        product(query_all, query_grad) + product(key_all, key_grad) + product(value_all, value_grad)
    )
    gain_grad = jnp.sum(normed_grad * standard, axis=1, keepdims=True)
    lane = lax.broadcasted_iota(jnp.int32, (features, 128), 1)
    gain_term = jnp.where(lane == 0, gain_grad, jnp.pad(gain_in.T, ((0, 0), (0, 120))))
    scaled = normed_grad * gains.reshape(features, 128)[:, :1]
    scaled = (
        scaled
        - jnp.mean(scaled, axis=0, keepdims=True)
        - standard * jnp.mean(scaled * standard, axis=0, keepdims=True)
    )
    input_grad = grad_one + (scaled * inverse[:1]).T
    last = [product(gated, branch)]
    last += [contract(normed, g, 1, 1) for g in (query_grad, key_grad, value_grad)]
    last = [a.reshape(devices, channels, features).astype(BF16) for a in last]
    last.append(gain_term.reshape(devices, channels, 128))
    sums = [
        lax.psum_scatter(a, BOTH, scatter_dimension=0, tiled=False).astype(F32)
        for a in list(terms) + last
    ]
    taps_grad = taps_grad[:, : mixer[0].shape[1]]
    return sums, [input_grad, taps_grad, *pull(kernel_grad[:, : rows * blocks]), skip_grad]


def allowed_keys(first, length, rows, keys):
    row_places = first + lax.broadcasted_iota(jnp.int32, (rows, keys), 0)
    key_places = lax.broadcasted_iota(jnp.int32, (rows, keys), 1)
    return (key_places <= row_places) & (key_places < length)


def attend_heads(allowed, q_ref, kv, out_ref, log_ref):
    features = q_ref.shape[1]
    for head in range(HEADS):
        own = slice(head * HDIM, (head + 1) * HDIM)
        values = slice(features + head * HDIM, features + (head + 1) * HDIM)
        scores = product_back(q_ref[:, own], kv[:, own]) * HDIM ** (-0.5)
        scores = jnp.where(allowed, scores, MASKED)
        most = jnp.max(scores, axis=1, keepdims=True)
        powers = jnp.exp(scores - most)
        total = jnp.sum(powers, axis=1, keepdims=True)
        weights = (powers * (1.0 / total)).astype(BF16)
        out_ref[:, own] = product(weights, kv[:, values]).astype(BF16)
        log_ref[:, head : head + 1] = most + jnp.log(total)


def attend_body(where_ref, q_ref, kv_ref, out_ref, log_ref):
    allowed = allowed_keys(where_ref[0], where_ref[1], q_ref.shape[0], kv_ref.shape[0])
    attend_heads(allowed, q_ref, kv_ref, out_ref, log_ref)


def attend_back_head(head, allowed, q_ref, kv, log_ref, grad_ref):
    features = q_ref.shape[1]
    scale = HDIM ** (-0.5)
    own = slice(head * HDIM, (head + 1) * HDIM)
    values = slice(features + head * HDIM, features + (head + 1) * HDIM)
    queries, grads = q_ref[:, own], grad_ref[:, own]
    scores = product_back(queries, kv[:, own]) * scale
    probs = jnp.where(allowed, jnp.exp(scores - log_ref[:, head : head + 1]), 0.0)
    prob_grad = product_back(grads, kv[:, values])
    delta = jnp.sum(probs * prob_grad, axis=1, keepdims=True)
    grad_scores = (probs * (prob_grad - delta)).astype(BF16)
    return (
        (product(grad_scores, kv[:, own]) * scale).astype(BF16),
        (product_sum(grad_scores, queries) * scale).astype(BF16),
        product_sum(probs.astype(BF16), grads).astype(BF16),
    )


def attend_back_body(where_ref, q_ref, kv_ref, log_ref, grad_ref, grad_q_ref, grad_kv_ref):
    features = q_ref.shape[1]
    allowed = allowed_keys(where_ref[0], where_ref[1], q_ref.shape[0], kv_ref.shape[0])
    for head in range(HEADS):
        own = slice(head * HDIM, (head + 1) * HDIM)
        values = slice(features + head * HDIM, features + (head + 1) * HDIM)
        grad_q_ref[:, own], grad_kv_ref[:, own], grad_kv_ref[:, values] = attend_back_head(
            head, allowed, q_ref, kv_ref, log_ref, grad_ref
        )


def norm_back(residual, gain_row, grad):
    average = jnp.mean(residual, axis=-1, keepdims=True)
    centered = residual - average
    inverse = lax.rsqrt(jnp.mean(centered * centered, axis=-1, keepdims=True) + EPSILON)
    standard = centered * inverse
    scaled = grad * gain_row
    inner = jnp.mean(scaled * standard, axis=-1, keepdims=True)
    grad_input = inverse * (scaled - jnp.mean(scaled, axis=-1, keepdims=True) - standard * inner)
    return grad_input, jnp.sum(grad * standard, axis=0, keepdims=True)


def middle_body(parts, count, kinds, *refs):
    early = refs[:count]
    qkv_all, up_all, down_all = refs[count : count + 3]
    (
        att_q, att_kv, log_total, grad_attended, key_live, normed_three, residual_two,
        grad_three, gain_rows, act_one, pre_one, normed_two, residual_one, fourth,
    ) = refs[count + 3 : count + 17]
    refs = refs[count + 17 :]
    totals = refs[:count]
    qkv_out, up_out, down_out, grad_one, gain_grads, branch_out = refs[count : count + 6]
    refs = refs[count + 6 :]
    buffers = refs[: 4 * len(parts)]
    refs = refs[4 * len(parts) :]
    held = dict(zip(kinds, refs[: len(kinds)]))
    (
        qkv, up, down, grad_q, grad_kv, line_one, line_two,
        send_sem, recv_sem, mine_sem, load_sem, store_sem, line_send, line_recv,
    ) = refs[len(kinds) :]
    rows, features = att_q.shape
    keys = att_kv.shape[0] * rows
    y, c, z, x = coordinates()
    greet(six_peers(y, c, z, x))
    loads = [
        pltpu.make_async_copy(src, dst, load_sem.at[n])
        for n, (src, dst) in enumerate(((qkv_all, qkv), (up_all, up), (down_all, down)))
    ]
    stores = [
        pltpu.make_async_copy(src, dst, store_sem.at[n])
        for n, (src, dst) in enumerate(((qkv, qkv_out), (up, up_out), (down, down_out)))
    ]
    reduce = Reduce(
        parts, early, totals, buffers, (early, held), send_sem, recv_sem, mine_sem
    )
    reduce.fetch_first()
    reduce.start(range(count))
    for load in loads:
        load.start()
    row_places = (y * 2 + c) * rows + lax.broadcasted_iota(jnp.int32, (rows, keys), 0)
    key_places = lax.broadcasted_iota(jnp.int32, (rows, keys), 1)
    allowed = jnp.where(key_places <= row_places, key_live[...], 0.0) > 0.5
    kv = att_kv[...].reshape(keys, 2 * features)
    for head in range(HEADS):
        own = slice(head * HDIM, (head + 1) * HDIM)
        values = slice(features + head * HDIM, features + (head + 1) * HDIM)
        grad_q[:, own], key_grad, value_grad = attend_back_head(
            head, allowed, att_q, kv, log_total, grad_attended
        )
        grad_kv[:, :, :, own] = key_grad.reshape(2, 2, rows, HDIM)
        grad_kv[:, :, :, values] = value_grad.reshape(2, 2, rows, HDIM)
        if head % 4 == 3:
            reduce.run(MIDDLE[head // 4])

    core, side = device_of(y, 1 - c, z, x), device_of(1 - y, c, z, x)

    def line_copy(n, source, target, where):
        return pltpu.make_async_remote_copy(
            src_ref=source,
            dst_ref=where,
            send_sem=line_send.at[n],
            recv_sem=line_recv.at[n],
            device_id=target,
            device_id_type=MESH,
        )

    far = line_copy(0, grad_kv.at[1 - y, 1 - c], core, line_one.at[1 - y])
    near = line_copy(1, grad_kv.at[y, 1 - c], core, line_one.at[y])
    onward = line_copy(2, line_one.at[1 - y], side, line_two)
    far.start()
    near.start()
    far.wait_recv()
    mine = line_one[1 - y].astype(F32) + grad_kv[1 - y, c].astype(F32)
    line_one[1 - y] = mine.astype(BF16)
    onward.start()
    loads[0].wait()
    query_grad = grad_q[...]
    grad_normed = product_back(query_grad, flat_part(qkv, 0, features))
    reduce.run(MIDDLE[3])
    near.wait_recv()
    onward.wait_recv()
    total = (line_one[y].astype(F32) + grad_kv[y, c].astype(F32)) + line_two[...].astype(F32)
    joint = [query_grad, total[:, :features].astype(BF16), total[:, features:].astype(BF16)]
    for n in (1, 2):
        grad_normed += product_back(joint[n], flat_part(qkv, n * features, features))
    grad_from, gain_grad = norm_back(residual_two[...], gain_rows[2:3], grad_normed)
    grad_two = grad_three[...] + grad_from
    gain_grads[...] = jnp.zeros_like(gain_grads)
    gain_grads[3:4, :] = fourth[...]
    gain_grads[2:3, :] = gain_grad
    slots, shard = qkv.shape[0], qkv.shape[1]
    for n in range(3):
        term = product_sum(normed_three[...], joint[n]).reshape(slots, shard, features)
        qkv[:, :, n * features : (n + 1) * features] = term.astype(BF16)
    stores[0].start()
    reduce.run(MIDDLE[4])

    branch = grad_two.astype(BF16)
    loads[1].wait()
    loads[2].wait()
    deep = down.shape[1]
    few = features // deep
    grad_normed = jnp.zeros((rows, features), F32)
    for n in range(up.shape[2] // features):
        own = slice(n * features, (n + 1) * features)
        some = pl.ds(n * few, few)
        gate_grad = product_back(branch, down[some].reshape(features, features))
        pre_grad = jax.vjp(jax.nn.gelu, pre_one[:, own])[1](gate_grad)[0].astype(BF16)
        grad_normed += product_back(pre_grad, flat_part(up, n * features, features))
        term = product_sum(act_one[:, own], branch)
        down[some] = term.astype(BF16).reshape(few, deep, features)
        term = product_sum(normed_two[...], pre_grad).reshape(slots, shard, features)
        up[:, :, own] = term.astype(BF16)
        reduce.run(MIDDLE[5 + n])
    stores[1].start()
    stores[2].start()
    grad_from, gain_grad = norm_back(residual_one[...], gain_rows[1:2], grad_normed)
    grad_one[...] = grad_two + grad_from
    branch_out[...] = grad_one[...].astype(BF16)
    gain_grads[1:2, :] = gain_grad
    reduce.finish()
    for each in (far, near, onward):
        each.wait_send()
    for store in stores:
        store.wait()


def middle_layers(terms, weights, kept, collective_id):
    count = len(terms)
    att_q, act_one = kept[0], kept[9]
    rows, features = att_q.shape
    shapes = [a.shape[1:] for a in terms]
    parts = cut(shapes)
    kinds = sorted({(part[2], part[4]) for part in parts})
    scratch = []
    for _, _, part_rows, _, columns, x_last in parts:
        for lead in ((2, 4, 2), (4, 2) if x_last else (2, 4), (4,), (3,)):
            scratch.append(pltpu.VMEM(lead + (part_rows, columns), BF16))
    scratch += [pltpu.VMEM((2, 2, 4, 2) + kind, BF16) for kind in kinds]
    scratch += [pltpu.VMEM(a.shape, BF16) for a in weights]
    scratch += [
        pltpu.VMEM((rows, features), BF16),
        pltpu.VMEM((2, 2, rows, 2 * features), BF16),
        pltpu.VMEM((2, rows, 2 * features), BF16),
        pltpu.VMEM((rows, 2 * features), BF16),
        pltpu.SemaphoreType.DMA((len(parts), 6)),
        pltpu.SemaphoreType.DMA((len(parts), 6)),
        pltpu.SemaphoreType.DMA((len(parts),)),
        pltpu.SemaphoreType.DMA((3,)),
        pltpu.SemaphoreType.DMA((3,)),
        pltpu.SemaphoreType.DMA((3,)),
        pltpu.SemaphoreType.DMA((3,)),
    ]
    vmem, anywhere = pl.BlockSpec(memory_space=pltpu.VMEM), pl.BlockSpec(memory_space=pl.ANY)
    results = [jax.ShapeDtypeStruct(s, F32) for s in shapes]
    results += [jax.ShapeDtypeStruct(a.shape, BF16) for a in weights]
    results += [
        jax.ShapeDtypeStruct((rows, features), F32),
        jax.ShapeDtypeStruct((8, features), F32),
        jax.ShapeDtypeStruct((rows, features), BF16),
    ]
    out = pl.pallas_call(
        partial(middle_body, parts, count, kinds),
        out_shape=results,
        in_specs=[anywhere] * (count + 3) + [vmem] * 14,
        out_specs=[vmem] * count + [anywhere] * 3 + [vmem] * 3,
        scratch_shapes=scratch,
        compiler_params=pltpu.CompilerParams(
            collective_id=collective_id, has_side_effects=True, vmem_limit_bytes=60 * MIB
        ),
    )(*[a.reshape((2, 2, 4, 2) + a.shape[1:]) for a in terms], *weights, *kept)
    return out[:count], out[count : count + 3], *out[count + 3 :]


def local_call(body, out_shape, *operands, scalars=0, limit=48):
    vmem = pl.BlockSpec(memory_space=pltpu.VMEM)
    smem = pl.BlockSpec(memory_space=pltpu.SMEM)
    return pl.pallas_call(
        body,
        out_shape=out_shape,
        in_specs=[smem] * scalars + [vmem] * (len(operands) - scalars),
        out_specs=jax.tree.map(lambda _: vmem, out_shape),
        compiler_params=pltpu.CompilerParams(vmem_limit_bytes=limit * MIB),
    )(*operands)


def settle(done, everything, channels, residual_shape):
    width = residual_shape[1]
    shapes = [a.shape for a in done]
    shapes += [(channels, 3 * width), (channels, 4 * width), (4 * channels, width)]
    shapes += [(channels, width)] * 4 + [(channels, 128), residual_shape]
    shapes += [(channels, 64)] * 5 + [(channels, 128)]
    count = len(done)

    def body(*refs):
        sources = [*refs[:count], *packed(refs[count], channels, residual_shape)]
        for source, place in zip(sources, refs[count + 1 :]):
            place[...] = source[...]

    out = local_call(
        body, [jax.ShapeDtypeStruct(s, F32) for s in shapes], *done, everything
    )
    return out[: count + 8], out[count + 8 :]


def shards(
    tokens, lengths, norm_one, query_one, key_one, value_one, shift_taps, decay_log,
    turn_angle, mix_real, mix_imag, skip_gain, out_one, norm_two, up_one, down_one,
    norm_three, qkv_weight, out_two, norm_four, up_two, down_two, cotangent,
):
    blocks, groups = lax.axis_size("seq"), lax.axis_size("dp")
    devices = blocks * groups
    rows, features = tokens.shape[1], tokens.shape[2]
    channels = features // devices
    place = lax.axis_index("seq")
    length = lengths[0]
    row_places = place * rows + jnp.arange(rows, dtype=jnp.int32)
    live_mask = (row_places < length).astype(F32)[:, None]
    live_lane = (row_places < length).astype(F32)[None, :]

    small = jnp.stack([norm_one, norm_two, norm_three, norm_four, skip_gain], axis=1)
    small = jnp.pad(small.astype(F32), ((0, 0), (0, 123)))
    mixer = [shift_taps, decay_log, turn_angle, mix_real, mix_imag]
    weights = [
        small, key_one, value_one, query_one, out_one, up_one, down_one, qkv_weight, out_two,
        up_two, down_two,
    ]
    key_live = (jnp.arange(blocks * rows, dtype=jnp.int32) < length).astype(F32)[None, :]
    if grouped():
        every, kept = first_layer(weights, tokens[0], live_lane, key_live, mixer, 1)
    else:
        every, kept = first_layer_apart(weights, tokens[0], live_lane, key_live, mixer)
    residual_one = kept[0]
    gain_rows = kept[22]
    gain_two, gain_three, gain_four = gain_rows[1], gain_rows[2], gain_rows[3]
    up_one_all, down_one_all, qkv_all, out_two_all, late_up, late_down = [
        g.reshape((-1, g.shape[2])) for g in every[5:]
    ]

    normed_two, pre_one, act_one, residual_two, normed_three, att_q, kv = kept[10:17]
    attended, log_total, residual_three = kept[17:20]
    residual_four, stored_four = feed_forward(residual_three, gain_four, late_up, late_down)
    activations = (live_mask * residual_four).astype(BF16)

    grad_four = live_mask * cotangent[0].astype(F32)
    grad_three, grad_norm_four, grad_up_two, grad_down_two = feed_back(
        residual_three, gain_four, late_up, late_down, stored_four, grad_four
    )
    branch_three = grad_three.astype(BF16)
    grad_out_two = product_sum(attended, branch_three)
    grad_attended = product_back(branch_three, out_two_all).astype(BF16)
    slots = (devices, -1)
    terms = [
        g.astype(BF16).reshape(slots + g.shape[1:])
        for g in (grad_up_two, grad_down_two, grad_out_two)
    ]
    if grouped():
        done, terms, grad_one, gain_in, branch_one = middle_layers(
            terms,
            every[7:8] + every[5:7],
            [
                att_q, kv, log_total, grad_attended, key_live, normed_three, residual_two,
                grad_three, gain_rows, act_one, pre_one, normed_two, residual_one,
                grad_norm_four[None],
            ],
            3,
        )
    else:
        grad_q, grad_kv = local_call(
            attend_back_body,
            [
                jax.ShapeDtypeStruct((rows, features), BF16),
                jax.ShapeDtypeStruct((blocks * rows, 2 * features), BF16),
            ],
            jnp.stack([place.astype(jnp.int32) * rows, length]), att_q,
            kv.reshape(blocks * rows, 2 * features), log_total, grad_attended, scalars=1,
        )
        grad_kv = lax.psum_scatter(
            grad_kv.reshape(blocks, rows, 2 * features), "seq", scatter_dimension=0
        )
        grad_joint = jnp.concatenate([grad_q, grad_kv.astype(BF16)], axis=1)
        grad_qkv_weight = product_sum(normed_three, grad_joint)
        grad_normed_three = product_back(grad_joint, qkv_all)
        grad_from_three, grad_norm_three = jax.vjp(layer_norm, residual_two, gain_three)[1](
            grad_normed_three
        )
        grad_one, grad_norm_two, grad_up_one, grad_down_one = feed_back(
            residual_one, gain_two, up_one_all, down_one_all, (normed_two, pre_one, act_one),
            grad_three + grad_from_three,
        )
        done = []
        terms += [
            g.astype(BF16).reshape(slots + g.shape[1:])
            for g in (grad_qkv_weight, grad_up_one, grad_down_one)
        ]
        branch_one = grad_one.astype(BF16)
        gain_in = jnp.stack(
            [jnp.zeros_like(grad_norm_two), grad_norm_two, grad_norm_three, grad_norm_four]
        )
        gain_in = jnp.pad(gain_in, ((0, 4), (0, 0)))
    last = (
        terms, gain_in, branch_one, grad_one, live_lane, kept[1:10] + kept[20:22], every[:5], small,
        mixer,
    )
    if grouped():
        sums, rest = last_layer(*last, done, 2)
    else:
        sums, rest = last_layer_apart(*last)
    grad_up_two, grad_down_two, grad_out_two, grad_qkv_weight, grad_up_one, grad_down_one = sums[:6]
    grad_out_one, grad_query_one, grad_key_one, grad_value_one, gain_grads = sums[6:]
    gain_grads = gain_grads[:, :4].T
    input_grad, grad_shift_taps, grad_decay_log, grad_turn_angle, grad_mix_real = rest[:5]
    grad_mix_imag, skip_grad = rest[5:]
    grad_skip_gain = skip_grad[:, 0]
    return (
        activations[None], input_grad[None],
        gain_grads[0], grad_query_one, grad_key_one, grad_value_one,
        grad_shift_taps, grad_decay_log, grad_turn_angle, grad_mix_real, grad_mix_imag,
        grad_skip_gain, grad_out_one,
        gain_grads[1], grad_up_one, grad_down_one,
        gain_grads[2], grad_qkv_weight, grad_out_two,
        gain_grads[3], grad_up_two, grad_down_two,
    )


def solution(mesh):
    row, vector = P(BOTH, None), P(BOTH)
    whole = P("dp", "seq", None)
    weights = (
        vector, row, row, row, row, row, row, row, row, vector, row,
        vector, row, row, vector, row, row, vector, row, row,
    )
    return jax.shard_map(
        shards,
        mesh=mesh,
        in_specs=(whole, P("dp")) + weights + (whole,),
        out_specs=(whole, whole) + weights,
        check_vma=False,
    )
```
